32 devices in a mesh: ctx: 4 (over z), fsdp: 8 (over y, x, core).
Axes of the slice: x: 2, y: 2, z: 4, core: 2. Of those that a mesh axis runs over, the one named last changes fastest.
Arguments:
- hidden_in: bfloat16 [8, 1024, 1536], P('fsdp', 'ctx'), may hold values from -6 to 6
- w_qkv: bfloat16 [1536, 2048], P('fsdp'), may hold values from -0.15625 to 0.15625
- b_qkv: bfloat16 [2048], P('fsdp'), may hold values from -3 to 3
- w_out: bfloat16 [1536, 1536], P('fsdp'), may hold values from -1 to 1
- w_gate_up: bfloat16 [1536, 17920], P('fsdp'), may hold values from -0.15625 to 0.15625
- w_down: bfloat16 [8960, 1536], P('fsdp'), may hold values from -0.0625 to 0.0625
- gain_attn: bfloat16 [1536], P('fsdp'), may hold values from 0.5 to 1.5
- gain_mlp: bfloat16 [1536], P('fsdp'), may hold values from 0.5 to 1.5
- block_order: int32 [8, 8], P('fsdp'), may hold values from 0 to 7, as said below
- cotangent: bfloat16 [8, 1024, 1536], P('fsdp', 'ctx'), may hold values from -6 to 6
Outputs:
- hidden_out: bfloat16 [8, 1024, 1536], P('fsdp', 'ctx')
- grad_hidden: bfloat16 [8, 1024, 1536], P('fsdp', 'ctx')
- grad_w_qkv: float32 [1536, 2048], P('fsdp')
- grad_b_qk: float32 [1792], P('fsdp')
- grad_b_v: float32 [256], P('fsdp')
- grad_w_out: float32 [1536, 1536], P('fsdp')
- grad_w_gate_up: float32 [1536, 17920], P('fsdp')
- grad_w_down: float32 [8960, 1536], P('fsdp')
- grad_gain_attn: float32 [1536], P('fsdp')
- grad_gain_mlp: float32 [1536], P('fsdp')
The draws below stay inside these ranges and needn't reach their ends.
Inputs may be any that keep to these rules, and one draw needn't show every extreme that they name: `block_order`: each row holds every number below 8 once: the places of the stored blocks of a sequence of 128 tokens each.
All inputs are finite; a program needn't handle non-finite values.
Results may differ from the reference program's by a relative error of at most 0.025.
Values may be sent and summed in bfloat16 or wider, within the bound.
A program may use at most 448 MiB of HBM per device.

```python
import jax
import jax.numpy as jnp
from jax import lax

D = 1536
HEADS = 12
KV_HEADS = 2
HEAD_DIM = 128
FF = 8960
PIECE = 128
PIECES = 8
LEN = 1024
SEQS = 8
QKV = 2048


def draw_block_order(key, part):
    key = jax.random.fold_in(key, 11)
    seeds = jax.random.split(key, SEQS)
    return jax.vmap(lambda single: jax.random.permutation(single, PIECES))(seeds).astype(jnp.int32)


def block_scale(rng, extent, shards, least, largest):
    level = 1.0
    for position, parts in shards:
        steps = jax.random.uniform(jax.random.fold_in(jax.random.fold_in(rng, 6), position), (parts,), jnp.float32, least / len(shards), largest / len(shards))
        level = level * jnp.repeat(jnp.exp(steps), extent[position] // parts).reshape((-1,) + (1,) * (len(extent) - 1 - position))
    return level


def centred(rng, dims, spread, reach, pieces=(), held_as=jnp.bfloat16):
    values = spread * jax.random.normal(rng, dims, jnp.float32)
    if pieces:
        values = values * block_scale(rng, dims, pieces, -0.22, 0.18)
    return jnp.clip(values, -reach, reach).astype(held_as)


def setup_inputs(seed: int = 0) -> dict:
    key_list = jax.random.split(jax.random.key(seed), 11)
    hidden_in = centred(key_list[0], (SEQS, LEN, D), 1.0, 6.0, ((0, 8), (1, 4)))
    w_qkv = centred(key_list[1], (D, QKV), D ** -0.5, 0.15625, ((0, 8),))
    b_qkv = centred(key_list[2], (QKV,), 0.5, 3.0, ((0, 8),))
    w_out = centred(key_list[3], (HEADS * HEAD_DIM, D), 32 ** -0.5, 1.0, ((0, 8),))
    w_gate_up = centred(key_list[4], (D, 2 * FF), D ** -0.5, 0.15625, ((0, 8),))
    w_down = centred(key_list[5], (FF, D), FF ** -0.5, 0.0625, ((0, 8),))
    gain_attn = jnp.clip(1.0 + 0.1 * jax.random.normal(key_list[6], (D,), jnp.float32), 0.5, 1.5).astype(jnp.bfloat16)
    gain_mlp = jnp.clip(1.0 + 0.1 * jax.random.normal(key_list[7], (D,), jnp.float32), 0.5, 1.5).astype(jnp.bfloat16)
    block_order = draw_block_order(jax.random.fold_in(key_list[10], 71), 0)
    cotangent = centred(key_list[9], (SEQS, LEN, D), 1.0, 6.0, ((0, 8), (1, 4)))
    return {"hidden_in": hidden_in, "w_qkv": w_qkv, "b_qkv": b_qkv, "w_out": w_out, "w_gate_up": w_gate_up, "w_down": w_down, "gain_attn": gain_attn, "gain_mlp": gain_mlp, "block_order": block_order, "cotangent": cotangent}


EPSILON = 1e-06
THETA = 1000000.0
MASKED = -1e+30

@jax.custom_vjp
def low(v):
    return lax.optimization_barrier(v.astype(jnp.bfloat16)).astype(jnp.float32)

@jax.custom_vjp
def low_back(v):
    return v

def low_keep(v):
    return (low(v), None)

def low_pass(kept, grad):
    return (grad,)

def back_keep(v):
    return (v, None)

def back_low(kept, grad):
    return (low(grad),)
low.defvjp(low_keep, low_pass)
low_back.defvjp(back_keep, back_low)

def normalize(values_in, gain):
    inverse = lax.rsqrt(lax.optimization_barrier(jnp.mean(values_in * values_in, -1, keepdims=True)) + EPSILON)
    return values_in * inverse * gain

def angle_tables(places):
    half_dim = HEAD_DIM // 2
    freqs = THETA ** (-(jnp.arange(half_dim).astype(jnp.float32) * 2.0 / HEAD_DIM))
    angles = places.astype(jnp.float32)[:, None] * freqs[None, :]
    return (jnp.cos(angles), jnp.sin(angles))

def rotate(values_in, cosine, sine_table):
    half_dim = HEAD_DIM // 2
    shape = (cosine.shape[0],) + (1,) * (values_in.ndim - 2) + (half_dim,)
    cos_b = cosine.reshape(shape)
    sin_b = sine_table.reshape(shape)
    first = values_in[..., :half_dim]
    second = values_in[..., half_dim:]
    return jnp.concatenate([first * cos_b - second * sin_b, second * cos_b + first * sin_b], -1)

def attend(queries, keys_in, values_in, places):
    high = lax.Precision.HIGHEST
    width = min(512, LEN)
    count = LEN // width
    groups = HEADS // KV_HEADS
    query_blocks = queries.reshape(count, width, KV_HEADS, groups, HEAD_DIM)
    place_blocks = places.reshape(count, width)

    def one_block(pair):
        block_q, block_places = pair
        scores = jnp.einsum('qkgd,tkd->kgqt', block_q, keys_in, precision=high) * HEAD_DIM ** (-0.5)
        scores = low_back(scores)
        visible = places[None, :] <= block_places[:, None]
        scores = jnp.where(visible, scores, MASKED)
        row_top = lax.optimization_barrier(jnp.max(scores, -1, keepdims=True))
        expd = jnp.exp(scores - row_top)
        probs = low(expd / lax.optimization_barrier(jnp.sum(expd, -1, keepdims=True)))
        return jnp.einsum('kgqt,tkd->qkgd', probs, values_in, precision=high)
    result = lax.map(jax.checkpoint(one_block), (query_blocks, place_blocks))
    return result.reshape(LEN, HEADS * HEAD_DIM)

def layer(inputs, w_qkv, b_qkv, w_out, w_gate_up, w_down, gain_attn, gain_mlp, places):
    high = lax.Precision.HIGHEST
    query_width = HEADS * HEAD_DIM
    key_width = KV_HEADS * HEAD_DIM
    groups = HEADS // KV_HEADS
    normed = low(normalize(inputs, gain_attn))
    projected = low_back(jnp.dot(normed, w_qkv, precision=high) + b_qkv)
    cosine, sine_table = angle_tables(places)
    queries = projected[:, :query_width].reshape(LEN, KV_HEADS, groups, HEAD_DIM)
    keys_in = projected[:, query_width:query_width + key_width].reshape(LEN, KV_HEADS, HEAD_DIM)
    values_in = low(projected[:, query_width + key_width:].reshape(LEN, KV_HEADS, HEAD_DIM))
    queries = low(rotate(queries, cosine, sine_table))
    keys_in = low(rotate(keys_in, cosine, sine_table))
    attn_rows = low_back(low(attend(queries, keys_in, values_in, places)))
    branch = low_back(jnp.dot(attn_rows, w_out, precision=high))
    middle = inputs + branch
    normed_two = low(normalize(middle, gain_mlp))
    mixed = low_back(jnp.dot(normed_two, w_gate_up, precision=high))
    activated = low(jax.nn.silu(mixed[:, :FF]) * mixed[:, FF:])
    return middle + jnp.dot(activated, w_down, precision=high)

def reference(hidden_in, w_qkv, b_qkv, w_out, w_gate_up, w_down, gain_attn, gain_mlp, block_order, cotangent):
    params = tuple((item.astype(jnp.float32) for item in (w_qkv, b_qkv, w_out, w_gate_up, w_down, gain_attn, gain_mlp)))
    row_ids = jnp.arange(LEN).astype(jnp.int32)
    split_at = (HEADS + KV_HEADS) * HEAD_DIM

    def one_sequence(carry, item):
        inputs, grad_in, order_row = item
        places = (order_row[row_ids // PIECE] * PIECE + row_ids % PIECE).astype(jnp.int32)
        result, pull = jax.vjp(lambda first, *rest: layer(first, *rest, places), inputs.astype(jnp.float32), *params)
        grads = pull(grad_in.astype(jnp.float32))
        summed = tuple((old + new for old, new in zip(carry, grads[1:])))
        return (summed, (result.astype(jnp.bfloat16), grads[0].astype(jnp.bfloat16)))
    start = tuple((jnp.zeros(item.shape, jnp.float32) for item in params))
    totals, (outputs, grad_inputs) = lax.scan(one_sequence, start, (hidden_in, cotangent, block_order))
    return (outputs, grad_inputs, totals[0], totals[1][:split_at], totals[1][split_at:], totals[2], totals[3], totals[4], totals[5], totals[6])
```

```python
import functools

import jax
import jax.numpy as jnp
from jax import lax
from jax.experimental import pallas as pl
from jax.experimental.pallas import tpu as pltpu
from jax.sharding import PartitionSpec as P

HEADS = 12
KV_HEADS = 2
HEAD_DIM = 128
EPSILON = 1e-06
THETA = 1000000.0
MASKED = -1e30
BF = jnp.bfloat16
F32 = jnp.float32


def dot(a, b):
    return jnp.dot(a, b, preferred_element_type=F32)


def dot_bt(a, b):
    return lax.dot_general(a, b, (((1,), (1,)), ((), ())), preferred_element_type=F32)


def dot_at(a, b):
    return lax.dot_general(a, b, (((0,), (0,)), ((), ())), preferred_element_type=F32)


def angle_tables(places):
    half_dim = HEAD_DIM // 2
    freqs = THETA ** (-(jnp.arange(half_dim).astype(F32) * 2.0 / HEAD_DIM))
    angles = places.astype(F32)[:, None] * freqs[None, :]
    return (jnp.cos(angles), jnp.sin(angles))


def rotate(values_in, cosine, sine_table):
    half_dim = HEAD_DIM // 2
    shape = (cosine.shape[0],) + (1,) * (values_in.ndim - 2) + (half_dim,)
    cos_b = cosine.reshape(shape)
    sin_b = sine_table.reshape(shape)
    first = values_in[..., :half_dim]
    second = values_in[..., half_dim:]
    return jnp.concatenate([first * cos_b - second * sin_b, second * cos_b + first * sin_b], -1)


def flip(x, bit):
    n = lax.axis_size("fsdp")
    return lax.ppermute(x, "fsdp", [(i, i ^ bit) for i in range(n)])


def shift(x, distance):
    n = lax.axis_size("ctx")
    return lax.ppermute(x, "ctx", [(i, (i + distance) % n) for i in range(n)])


def place(pieces, index, total):
    rows = pieces[0][1].shape[0]
    out = jnp.zeros((total * rows,) + pieces[0][1].shape[1:], pieces[0][1].dtype)
    for block, piece in pieces:
        start = (block * rows,) + (0,) * (piece.ndim - 1)
        out = lax.dynamic_update_slice(out, piece, start)
    return out


def half_rows(rows):
    return -(-rows // 32) * 16


def plane_gather(shard):
    n = lax.axis_size("fsdp")
    me = lax.axis_index("fsdp")
    pieces = {0: shard}
    if n == 8:
        cut = half_rows(shard.shape[0])
        along_x, along_y = flip(shard, 2), flip(shard, 4)
        pieces[2], pieces[4] = along_x, along_y
        pieces[6] = jnp.concatenate([flip(along_x[:cut], 4), flip(along_y[cut:], 2)], 0)
    else:
        for k in range(2, n, 2):
            pieces[k] = flip(shard, k)
    for k in range(0, n, 2):
        pieces[k + 1] = flip(pieces[k], 1)
    return place([(me ^ k, piece) for k, piece in pieces.items()], me, n)


def plane_scatter(blocks):
    n = lax.axis_size("fsdp")
    me = lax.axis_index("fsdp")
    chip, core = me // 2, me % 2
    low = blocks.astype(BF).reshape((n // 2, 2) + blocks.shape[1:])
    kept = lax.dynamic_index_in_dim(low, core, 1, keepdims=False)
    given = lax.dynamic_index_in_dim(low, 1 - core, 1, keepdims=False)
    acc = (kept.astype(F32) + flip(given, 1).astype(F32)).astype(BF)

    def pick(k):
        return lax.dynamic_index_in_dim(acc, chip ^ k, 0, keepdims=False)

    if n == 8:
        rows = blocks.shape[1]
        cut = half_rows(rows) if rows > 1 else 0
        to_x, to_y, to_far = pick(1), pick(2), pick(3)
        if cut:
            first = flip(to_far[:cut], 2)
            from_x = [flip(to_x[:cut], 2)]
            second = flip(to_far[cut:], 4)
            from_y = [flip(to_y[cut:], 4)]
            from_x.append(flip((to_x[cut:].astype(F32) + second.astype(F32)).astype(BF), 2))
            from_y.insert(0, flip((to_y[:cut].astype(F32) + first.astype(F32)).astype(BF), 4))
            from_x, from_y = jnp.concatenate(from_x, 0), jnp.concatenate(from_y, 0)
            return pick(0).astype(F32) + from_x.astype(F32) + from_y.astype(F32)
    total = pick(0).astype(F32)
    for k in range(1, n // 2):
        total = total + flip(pick(k), 2 * k).astype(F32)
    return total


def ctx_gather(block):
    n = lax.axis_size("ctx")
    me = lax.axis_index("ctx")
    pieces = [(me, block)]
    for d in range(1, n):
        pieces.append(((me - d) % n, shift(block, d)))
    return place(pieces, me, n)


def ctx_chain(block):
    n = lax.axis_size("ctx")
    me = lax.axis_index("ctx")
    up, down = [block], [block]
    for t in range(1, n):
        up.append(lax.ppermute(up[-1], "ctx", [(i, i + 1) for i in range(t - 1, n - 1)]))
        down.append(lax.ppermute(down[-1], "ctx", [(i, i - 1) for i in range(1, n - t + 1)]))
    parts = []
    for j in range(n):
        part = block
        for i in range(n):
            if i != j:
                held = up[i - j] if i > j else down[j - i]
                part = jnp.where(me == i, held, part)
        parts.append(part)
    return parts


def ctx_scatter(blocks):
    n = lax.axis_size("ctx")
    me = lax.axis_index("ctx")
    total = lax.dynamic_index_in_dim(blocks, me, 0, keepdims=False).astype(F32)
    low = blocks.astype(BF)
    for d in range(1, n):
        part = lax.dynamic_index_in_dim(low, (me + d) % n, 0, keepdims=False)
        total = total + shift(part, d).astype(F32)
    return total


def ctx_sum(block):
    n = lax.axis_size("ctx")
    part = ctx_scatter(block.reshape((n, block.shape[0] // n) + block.shape[1:]))
    return ctx_gather(part.astype(BF)).astype(F32)


def lane_pad(n):
    return -(-n // 128) * 128


def pack_kernel(nz, nf, ff, wide, z_ref, w_ref, out_ref):
    unit = ff // (nf * nz)
    pad = wide - nf * unit
    for k in range(nz):

        @pl.when(z_ref[0] == k)
        def _():
            for h in range(2):
                for f in range(nf):
                    src = h * ff + f * (ff // nf) + k * unit
                    dst = h * wide + f * unit
                    out_ref[:, dst : dst + unit] = w_ref[:, src : src + unit]
                if pad:
                    out_ref[:, (h + 1) * wide - pad : (h + 1) * wide] = jnp.zeros(
                        (out_ref.shape[0], pad), out_ref.dtype
                    )


def pack(w, nz, nf, z):
    rows, ff = w.shape[0], w.shape[1] // 2
    wide = lane_pad(ff // nz)
    step = 32
    return pl.pallas_call(
        functools.partial(pack_kernel, nz, nf, ff, wide),
        grid=(rows // step,),
        in_specs=[
            pl.BlockSpec(memory_space=pltpu.SMEM),
            pl.BlockSpec((step, 2 * ff), lambda i: (i, 0)),
        ],
        out_specs=pl.BlockSpec((step, 2 * wide), lambda i: (i, 0)),
        out_shape=jax.ShapeDtypeStruct((rows, 2 * wide), w.dtype),
    )(z.reshape(1).astype(jnp.int32), w)


def unpack_kernel(nz, nf, ff, wide, *refs):
    unit = ff // (nf * nz)
    out_ref = refs[-1]
    for k in range(nz):
        for h in range(2):
            for f in range(nf):
                src = h * wide + f * unit
                dst = h * ff + f * (ff // nf) + k * unit
                out_ref[:, dst : dst + unit] = refs[k][:, src : src + unit].astype(F32)


def unpack(parts, nz, nf, ff):
    rows, wide = parts[0].shape[0], parts[0].shape[1] // 2
    step = 32
    return pl.pallas_call(
        functools.partial(unpack_kernel, nz, nf, ff, wide),
        grid=(rows // step,),
        in_specs=[pl.BlockSpec((step, 2 * wide), lambda i: (i, 0))] * nz,
        out_specs=pl.BlockSpec((step, 2 * ff), lambda i: (i, 0)),
        out_shape=jax.ShapeDtypeStruct((rows, 2 * ff), F32),
    )(*parts)


def shards(
    hidden_in, w_qkv, b_qkv, w_out, w_gate_up, w_down, gain_attn, gain_mlp, block_order, cotangent
):
    nz, nf = lax.axis_size("ctx"), lax.axis_size("fsdp")
    z, me = lax.axis_index("ctx"), lax.axis_index("fsdp")
    groups = HEADS // KV_HEADS
    q_width, k_width = HEADS * HEAD_DIM, KV_HEADS * HEAD_DIM
    rows = hidden_in.shape[1]
    piece_len = rows // 2
    ff = w_gate_up.shape[1] // 2
    unit = ff // (nf * nz)
    quarter = ff // nz
    wide = lane_pad(quarter)
    scale = HEAD_DIM ** (-0.5)
    order_row = block_order[0]
    all_places = (
        order_row[:, None] * piece_len + jnp.arange(piece_len, dtype=jnp.int32)[None, :]
    ).reshape(-1)
    my_places = lax.dynamic_slice_in_dim(all_places, z * rows, rows)
    visible = all_places[None, :] <= my_places[:, None]
    cosine, sine_table = angle_tables(my_places)

    whole_qkv = plane_gather(w_qkv)
    small = jnp.concatenate([b_qkv, gain_attn, gain_mlp]).reshape(1, -1)
    smalls = plane_gather(small)
    nb, ng = b_qkv.shape[0], gain_attn.shape[0]
    bias = smalls[:, :nb].reshape(-1).astype(F32)
    gain_first = smalls[:, nb : nb + ng].reshape(-1).astype(F32)
    gain_second = smalls[:, nb + ng :].reshape(-1).astype(F32)

    packed = pack(w_gate_up, nz, nf, z)
    down_mine = lax.dynamic_slice_in_dim(w_down, z * unit, unit)
    packed, down_mine, w_out, whole_qkv = lax.optimization_barrier(
        (packed, down_mine, w_out, whole_qkv)
    )
    whole_out = plane_gather(w_out)
    gu = plane_gather(packed)
    down = jnp.pad(plane_gather(down_mine), ((0, wide - quarter), (0, 0)))
    grad_low = cotangent[0]
    grad_all = ctx_gather(grad_low)

    inputs = hidden_in[0].astype(F32)
    inverse_one = lax.rsqrt(jnp.mean(inputs * inputs, -1, keepdims=True) + EPSILON)
    normed = (inputs * inverse_one * gain_first).astype(BF)
    projected = dot(normed, whole_qkv) + bias
    queries = rotate(
        projected[:, :q_width].reshape(rows, KV_HEADS, groups, HEAD_DIM), cosine, sine_table
    ).astype(BF)
    keys = rotate(
        projected[:, q_width : q_width + k_width].reshape(rows, KV_HEADS, HEAD_DIM),
        cosine,
        sine_table,
    ).astype(BF)
    kv = jnp.concatenate(
        [keys.reshape(rows, k_width), projected[:, q_width + k_width :].astype(BF)], 1
    )
    kv_all = ctx_gather(kv)
    keys_all = kv_all[:, :k_width].reshape(-1, KV_HEADS, HEAD_DIM)
    values_all = kv_all[:, k_width:].reshape(-1, KV_HEADS, HEAD_DIM)
    scores = jnp.einsum("qkgd,tkd->kgqt", queries, keys_all, preferred_element_type=F32) * scale
    scores = jnp.where(visible, scores, MASKED)
    row_top = jnp.max(scores, -1, keepdims=True)
    weights = jnp.exp(scores - row_top)
    row_total = jnp.sum(weights, -1, keepdims=True)
    attn_heads = (
        jnp.einsum("kgqt,tkd->kgqd", weights.astype(BF), values_all, preferred_element_type=F32)
        / row_total
    )
    log_total = row_top + jnp.log(row_total)
    attn_low = attn_heads.transpose(2, 0, 1, 3).reshape(rows, q_width).astype(BF)
    middle = inputs + dot(attn_low, whole_out)
    inverse_two = lax.rsqrt(jnp.mean(middle * middle, -1, keepdims=True) + EPSILON)
    normed_two = (middle * inverse_two * gain_second).astype(BF)

    x_all = ctx_gather(normed_two)
    gate = dot(x_all, gu[:, :wide])
    up = dot(x_all, gu[:, wide:])
    sigmoid_gate = jax.nn.sigmoid(gate)
    act = (gate * sigmoid_gate * up).astype(BF)
    grad_act = dot_bt(grad_all, down)
    grad_gate = grad_act * up * (sigmoid_gate * (1.0 + gate * (1.0 - sigmoid_gate)))
    grad_up = grad_act * gate * sigmoid_gate
    grad_mixed = jnp.concatenate([grad_gate, grad_up], 1).astype(BF)
    grad_normed_two = ctx_scatter(dot_bt(grad_mixed, gu).reshape(nz, rows, -1))
    down_sum = ctx_scatter(dot(act, down).reshape(nz, rows, -1))
    hidden_out = (middle + down_sum).astype(BF)[None]

    down_local = dot_at(act, grad_all)[:quarter].reshape(nf, unit, -1)
    gate_up_local = dot_at(x_all, grad_mixed).reshape(nf, -1, 2 * wide)
    grad_down = jnp.concatenate(ctx_chain(plane_scatter(down_local).astype(BF)), 0).astype(F32)
    grad_gate_up = unpack(ctx_chain(plane_scatter(gate_up_local).astype(BF)), nz, nf, ff)

    grad_full = grad_low.astype(F32)
    scaled_two = gain_second * grad_normed_two
    gain_two_local = jnp.sum(grad_normed_two * middle * inverse_two, 0)
    grad_middle = (
        grad_full
        + inverse_two * scaled_two
        - middle
        * (inverse_two * inverse_two * inverse_two)
        * jnp.mean(scaled_two * middle, -1, keepdims=True)
    )
    grad_branch = grad_middle.astype(BF)
    out_local = dot_at(attn_low, grad_branch)
    grad_out = ctx_sum(plane_scatter(out_local.reshape(nf, -1, out_local.shape[1])))
    grad_attn = dot_bt(grad_branch, whole_out).astype(BF)
    grad_heads = grad_attn.reshape(rows, KV_HEADS, groups, HEAD_DIM).transpose(1, 2, 0, 3)
    row_delta = jnp.sum(grad_heads.astype(F32) * attn_heads, -1, keepdims=True)
    scores = jnp.einsum("qkgd,tkd->kgqt", queries, keys_all, preferred_element_type=F32) * scale
    probs = jnp.where(visible, jnp.exp(scores - log_total), 0.0)
    grad_values = jnp.einsum(
        "kgqt,kgqd->tkd", probs.astype(BF), grad_heads, preferred_element_type=F32
    )
    grad_probs = jnp.einsum("kgqd,tkd->kgqt", grad_heads, values_all, preferred_element_type=F32)
    grad_scores = (probs * (grad_probs - row_delta)).astype(BF)
    grad_queries = (
        jnp.einsum("kgqt,tkd->kgqd", grad_scores, keys_all, preferred_element_type=F32) * scale
    )
    grad_keys = (
        jnp.einsum("kgqt,qkgd->tkd", grad_scores, queries, preferred_element_type=F32) * scale
    )
    kv_grads = jnp.concatenate(
        [grad_keys.reshape(nz, rows, k_width), grad_values.reshape(nz, rows, k_width)], -1
    )
    kv_grad = ctx_scatter(kv_grads)
    query_back = rotate(grad_queries.transpose(2, 0, 1, 3), cosine, -sine_table).reshape(
        rows, q_width
    )
    key_back = rotate(
        kv_grad[:, :k_width].reshape(rows, KV_HEADS, HEAD_DIM), cosine, -sine_table
    ).reshape(rows, k_width)
    grad_projected = jnp.concatenate([query_back, key_back, kv_grad[:, k_width:]], 1).astype(BF)
    bias_local = jnp.sum(grad_projected.astype(F32), 0)
    qkv_local = dot_at(normed, grad_projected)
    grad_qkv = ctx_sum(plane_scatter(qkv_local.reshape(nf, -1, qkv_local.shape[1])))
    grad_normed = dot_bt(grad_projected, whole_qkv)
    scaled_one = gain_first * grad_normed
    gain_one_local = jnp.sum(grad_normed * inputs * inverse_one, 0)
    grad_inputs = (
        grad_middle
        + inverse_one * scaled_one
        - inputs
        * (inverse_one * inverse_one * inverse_one)
        * jnp.mean(scaled_one * inputs, -1, keepdims=True)
    )
    cut = q_width + k_width
    tiny = jnp.concatenate(
        [
            bias_local[:cut].reshape(nf, -1),
            bias_local[cut:].reshape(nf, -1),
            gain_one_local.reshape(nf, -1),
            gain_two_local.reshape(nf, -1),
        ],
        1,
    ).reshape(nf, 1, -1)
    tiny = plane_scatter(tiny).reshape(nz, -1)
    tiny = ctx_sum(tiny).reshape(-1)
    e1 = cut // nf
    e2 = e1 + k_width // nf
    e3 = e2 + ng
    return (
        hidden_out,
        grad_inputs.astype(BF)[None],
        grad_qkv,
        tiny[:e1],
        tiny[e1:e2],
        grad_out,
        grad_gate_up,
        grad_down,
        tiny[e2:e3],
        tiny[e3:],
    )


def solution(mesh):
    placed = (
        P("fsdp", "ctx", None),
        P("fsdp", None),
        P("fsdp"),
        P("fsdp", None),
        P("fsdp", None),
        P("fsdp", None),
        P("fsdp"),
        P("fsdp"),
        P("fsdp", None),
        P("fsdp", "ctx", None),
    )
    return jax.shard_map(
        shards,
        mesh=mesh,
        in_specs=placed,
        out_specs=(
            P("fsdp", "ctx", None),
            P("fsdp", "ctx", None),
            P("fsdp", None),
            P("fsdp"),
            P("fsdp"),
            P("fsdp", None),
            P("fsdp", None),
            P("fsdp", None),
            P("fsdp"),
            P("fsdp"),
        ),
        check_vma=False,
    )
```

```python
import functools

import jax
import jax.numpy as jnp
from jax import lax
from jax.experimental import pallas as pl
from jax.experimental.pallas import tpu as pltpu
from jax.sharding import PartitionSpec as P

HEADS = 12
KV_HEADS = 2
HEAD_DIM = 128
EPSILON = 1e-06
THETA = 1000000.0
MASKED = -1e30
BF = jnp.bfloat16
F32 = jnp.float32


def dot(a, b):
    return jnp.dot(a, b, preferred_element_type=F32)


def dot_bt(a, b):
    return lax.dot_general(a, b, (((1,), (1,)), ((), ())), preferred_element_type=F32)


def dot_at(a, b):
    return lax.dot_general(a, b, (((0,), (0,)), ((), ())), preferred_element_type=F32)


def angle_tables(places):
    half_dim = HEAD_DIM // 2
    freqs = THETA ** (-(jnp.arange(half_dim).astype(F32) * 2.0 / HEAD_DIM))
    angles = places.astype(F32)[:, None] * freqs[None, :]
    return (jnp.cos(angles), jnp.sin(angles))


def rotate(values_in, cosine, sine_table):
    half_dim = HEAD_DIM // 2
    shape = (cosine.shape[0],) + (1,) * (values_in.ndim - 2) + (half_dim,)
    cos_b = cosine.reshape(shape)
    sin_b = sine_table.reshape(shape)
    first = values_in[..., :half_dim]
    second = values_in[..., half_dim:]
    return jnp.concatenate([first * cos_b - second * sin_b, second * cos_b + first * sin_b], -1)


def flip(x, bit):
    n = lax.axis_size("fsdp")
    return lax.ppermute(x, "fsdp", [(i, i ^ bit) for i in range(n)])


def shift(x, distance):
    n = lax.axis_size("ctx")
    return lax.ppermute(x, "ctx", [(i, (i + distance) % n) for i in range(n)])


def place(pieces, index, total):
    rows = pieces[0][1].shape[0]
    out = jnp.zeros((total * rows,) + pieces[0][1].shape[1:], pieces[0][1].dtype)
    for block, piece in pieces:
        start = (block * rows,) + (0,) * (piece.ndim - 1)
        out = lax.dynamic_update_slice(out, piece, start)
    return out


def half_rows(rows):
    return -(-rows // 32) * 16


def plane_gather(shard):
    n = lax.axis_size("fsdp")
    me = lax.axis_index("fsdp")
    pieces = {0: shard}
    if n == 8:
        cut = half_rows(shard.shape[0])
        along_x, along_y = flip(shard, 2), flip(shard, 4)
        pieces[2], pieces[4] = along_x, along_y
        pieces[6] = jnp.concatenate([flip(along_x[:cut], 4), flip(along_y[cut:], 2)], 0)
    else:
        for k in range(2, n, 2):
            pieces[k] = flip(shard, k)
    for k in range(0, n, 2):
        pieces[k + 1] = flip(pieces[k], 1)
    return place([(me ^ k, piece) for k, piece in pieces.items()], me, n)


def plane_scatter(blocks):
    n = lax.axis_size("fsdp")
    me = lax.axis_index("fsdp")
    chip, core = me // 2, me % 2
    low = blocks.astype(BF).reshape((n // 2, 2) + blocks.shape[1:])
    kept = lax.dynamic_index_in_dim(low, core, 1, keepdims=False)
    given = lax.dynamic_index_in_dim(low, 1 - core, 1, keepdims=False)
    acc = (kept.astype(F32) + flip(given, 1).astype(F32)).astype(BF)

    def pick(k):
        return lax.dynamic_index_in_dim(acc, chip ^ k, 0, keepdims=False)

    if n == 8:
        rows = blocks.shape[1]
        cut = half_rows(rows) if rows > 1 else 0
        to_x, to_y, to_far = pick(1), pick(2), pick(3)
        if cut:
            first = flip(to_far[:cut], 2)
            from_x = [flip(to_x[:cut], 2)]
            second = flip(to_far[cut:], 4)
            from_y = [flip(to_y[cut:], 4)]
            from_x.append(flip((to_x[cut:].astype(F32) + second.astype(F32)).astype(BF), 2))
            from_y.insert(0, flip((to_y[:cut].astype(F32) + first.astype(F32)).astype(BF), 4))
            from_x, from_y = jnp.concatenate(from_x, 0), jnp.concatenate(from_y, 0)
            return pick(0).astype(F32) + from_x.astype(F32) + from_y.astype(F32)
    total = pick(0).astype(F32)
    for k in range(1, n // 2):
        total = total + flip(pick(k), 2 * k).astype(F32)
    return total


def ctx_gather(block):
    n = lax.axis_size("ctx")
    me = lax.axis_index("ctx")
    pieces = [(me, block)]
    for d in range(1, n):
        pieces.append(((me - d) % n, shift(block, d)))
    return place(pieces, me, n)


def ctx_chain(block):
    n = lax.axis_size("ctx")
    me = lax.axis_index("ctx")
    up, down = [block], [block]
    for t in range(1, n):
        up.append(lax.ppermute(up[-1], "ctx", [(i, i + 1) for i in range(t - 1, n - 1)]))
        down.append(lax.ppermute(down[-1], "ctx", [(i, i - 1) for i in range(1, n - t + 1)]))
    parts = []
    for j in range(n):
        part = block
        for i in range(n):
            if i != j:
                held = up[i - j] if i > j else down[j - i]
                part = jnp.where(me == i, held, part)
        parts.append(part)
    return parts


def ctx_scatter(blocks):
    n = lax.axis_size("ctx")
    me = lax.axis_index("ctx")
    total = lax.dynamic_index_in_dim(blocks, me, 0, keepdims=False).astype(F32)
    low = blocks.astype(BF)
    for d in range(1, n):
        part = lax.dynamic_index_in_dim(low, (me + d) % n, 0, keepdims=False)
        total = total + shift(part, d).astype(F32)
    return total


def ctx_sum(block):
    n = lax.axis_size("ctx")
    part = ctx_scatter(block.reshape((n, block.shape[0] // n) + block.shape[1:]))
    return ctx_gather(part.astype(BF)).astype(F32)


def pack_kernel(nz, nf, ff, unit, upad, z_ref, w_ref, out_ref):
    for k in range(nz):

        @pl.when(z_ref[0] == k)
        def _():
            for h in range(2):
                for f in range(nf):
                    src = h * ff + f * (ff // nf) + k * unit
                    dst = (h * nf + f) * upad
                    out_ref[:, dst : dst + unit] = w_ref[:, src : src + unit]
                    out_ref[:, dst + unit : dst + upad] = jnp.zeros(
                        (out_ref.shape[0], upad - unit), out_ref.dtype
                    )


def pack(w, nz, nf, z):
    rows, ff = w.shape[0], w.shape[1] // 2
    unit = ff // (nf * nz)
    upad = -(-unit // 16) * 16
    wide = nf * upad
    step = 32
    return pl.pallas_call(
        functools.partial(pack_kernel, nz, nf, ff, unit, upad),
        grid=(rows // step,),
        in_specs=[
            pl.BlockSpec(memory_space=pltpu.SMEM),
            pl.BlockSpec((step, 2 * ff), lambda i: (i, 0)),
        ],
        out_specs=pl.BlockSpec((step, 2 * wide), lambda i: (i, 0)),
        out_shape=jax.ShapeDtypeStruct((rows, 2 * wide), w.dtype),
    )(z.reshape(1).astype(jnp.int32), w)


def unpack_kernel(nz, nf, ff, unit, upad, *refs):
    out_ref = refs[-1]
    for k in range(nz):
        for h in range(2):
            for f in range(nf):
                src = (h * nf + f) * upad
                dst = h * ff + f * (ff // nf) + k * unit
                out_ref[:, dst : dst + unit] = refs[k][:, src : src + unit].astype(F32)


def unpack(parts, nz, nf, ff):
    rows, wide = parts[0].shape[0], parts[0].shape[1] // 2
    unit, upad = ff // (nf * nz), wide // nf
    step = 32
    return pl.pallas_call(
        functools.partial(unpack_kernel, nz, nf, ff, unit, upad),
        grid=(rows // step,),
        in_specs=[pl.BlockSpec((step, 2 * wide), lambda i: (i, 0))] * nz,
        out_specs=pl.BlockSpec((step, 2 * ff), lambda i: (i, 0)),
        out_shape=jax.ShapeDtypeStruct((rows, 2 * ff), F32),
    )(*parts)


MESH = pl.DeviceIdType.MESH
VMEM_LIMIT = 63 * 2**20


def remote(src, dst, send, recv, z, f):
    return pltpu.make_async_remote_copy(
        src_ref=src, dst_ref=dst, send_sem=send, recv_sem=recv, device_id=(z, f), device_id_type=MESH
    )


def rows_at(ref, index, count):
    return ref.at[pl.ds(pl.multiple_of(index * count, count), count)]


class PlaneGather:
    def __init__(self, src, dst, rows, nf, z, me, send, recv, local, base):
        self.src, self.dst, self.rows, self.nf, self.z, self.me = src, dst, rows, nf, z, me
        self.send, self.recv, self.base = send, recv, base
        self.local = pltpu.make_async_copy(src, rows_at(dst, me, rows), local)
        self.sent = []
        self.cut = half_rows(rows)
        self.swaps = {}

    @staticmethod
    def sems(nf):
        return 2 * nf

    def slot(self, k, lo=0, hi=None):
        hi = self.rows if hi is None else hi
        start = pl.multiple_of((self.me ^ k) * self.rows, 16) + lo
        return self.dst.at[pl.ds(pl.multiple_of(start, 16), hi - lo)]

    def push(self, index, src, dst, flip_by):
        copy = remote(
            src, dst, self.send.at[self.base + index], self.recv.at[self.base + index],
            self.z, self.me ^ flip_by,
        )
        copy.start()
        self.sent.append(copy)
        return copy

    def begin(self):
        self.local.start()
        self.direct = {}
        for k in (2, 4) if self.nf == 8 else range(2, self.nf, 2):
            self.direct[k] = self.push(k, self.src, self.slot(0), k)
        self.swaps[0] = self.push(1, self.src, self.slot(0), 1)

    def swap(self, k):
        self.swaps[k] = self.push(k + 1, self.slot(k), self.slot(k), 1)

    def middle(self):
        for k, copy in self.direct.items():
            copy.wait_recv()
            if self.nf == 8:
                if k == 2:
                    self.far_a = self.push(6, self.slot(2, 0, self.cut), self.slot(2, 0, self.cut), 4)
                elif self.cut < self.rows:
                    self.far_b = self.push(
                        8, self.slot(4, self.cut), self.slot(4, self.cut), 2
                    )
            self.swap(k)

    def late(self):
        if self.nf == 8:
            self.far_a.wait_recv()
            if self.cut < self.rows:
                self.far_b.wait_recv()
            self.swap(6)

    def finish(self):
        self.local.wait()
        for copy in self.swaps.values():
            copy.wait_recv()

    def drain(self):
        for copy in self.sent:
            copy.wait_send()


class Chain:
    def __init__(self, buf, rows, nz, z, me, send, recv, base):
        self.buf, self.rows, self.nz, self.z, self.me = buf, rows, nz, z, me
        self.send, self.recv, self.base = send, recv, base

    @staticmethod
    def sems(nz):
        return nz + 2

    def copy(self, j, sem, step):
        slot = rows_at(self.buf, j, self.rows)
        return remote(
            slot, slot, self.send.at[self.base + sem], self.recv.at[self.base + j], self.z + step, self.me
        )

    def order(self, k):
        z, nz = self.z, self.nz
        below, above = z, nz - 1 - z
        m = jnp.minimum(below, above)
        near = jnp.where(k % 2 == 1, z - (k + 1) // 2, z + k // 2)
        far = jnp.where(above > below, z + (k - m), z - (k - m))
        return jnp.where(k <= 2 * m, near, far)

    def begin(self):
        z, nz = self.z, self.nz

        @pl.when(z < nz - 1)
        def _():
            self.copy(z, nz, 1).start()

        @pl.when(z > 0)
        def _():
            self.copy(z, nz + 1, -1).start()

    def passing(self, j):
        z, nz = self.z, self.nz
        return jnp.logical_and(j < z, z < nz - 1), jnp.logical_and(j > z, z > 0)

    def forward(self, k):
        j = self.order(k)
        up, down = self.passing(j)

        @pl.when(up)
        def _():
            self.copy(j, j, 1).wait_recv()
            self.copy(j, j, 1).start()

        @pl.when(down)
        def _():
            self.copy(j, j, -1).wait_recv()
            self.copy(j, j, -1).start()

    def arrive(self, k):
        j = self.order(k)
        up, down = self.passing(j)

        @pl.when(jnp.logical_not(jnp.logical_or(up, down)))
        def _():
            self.copy(j, j, 0).wait_recv()

    def drain(self):
        z, nz = self.z, self.nz

        @pl.when(z < nz - 1)
        def _():
            self.copy(z, nz, 1).wait_send()

        @pl.when(z > 0)
        def _():
            self.copy(z, nz + 1, -1).wait_send()

        def one(k, carry):
            j = self.order(k)
            up, down = self.passing(j)

            @pl.when(jnp.logical_or(up, down))
            def _():
                self.copy(j, j, 0).wait_send()

            return carry

        lax.fori_loop(1, nz, one, 0)


def greet_ctx_and_plane(nz, nf, z, me):
    barrier = pltpu.get_barrier_semaphore()
    flips = (1, 2, 4) if nf == 8 else (1,) + tuple(range(2, nf, 2))
    for k in flips:
        pl.semaphore_signal(barrier, inc=1, device_id=(z, me ^ k), device_id_type=MESH)

    @pl.when(z < nz - 1)
    def _():
        pl.semaphore_signal(barrier, inc=1, device_id=(z + 1, me), device_id_type=MESH)

    @pl.when(z > 0)
    def _():
        pl.semaphore_signal(barrier, inc=1, device_id=(z - 1, me), device_id_type=MESH)

    inner = jnp.logical_and(z > 0, z < nz - 1)

    @pl.when(inner)
    def _():
        pl.semaphore_wait(barrier, len(flips) + 2)

    @pl.when(jnp.logical_not(inner))
    def _():
        pl.semaphore_wait(barrier, len(flips) + 1)


def loop(n, body):
    def step(i, carry):
        body(i)
        return carry

    lax.fori_loop(0, n, step, 0)


def at128(i, n):
    return i * n if isinstance(i, int) else pl.multiple_of(i * n, n)


def turn(t, cos2, sin2):
    return t * cos2 + pltpu.roll(t, HEAD_DIM // 2, 1) * sin2


def front_kernel(
    dims,
    wq, sm, wo, wp, dn, x_ref, g_ref, cos_ref, sin_ref, qpos_ref, kpos_ref,
    wq_all, wo_all, q_ref, kv_out, o_ref, lse_ref, mid_ref, dx_ref, gain_ref, dwgu, dwd, dpart,
    stage, gu, dnb, g_all, x_all, act, dgu, smb, kv, bias, mask, send, recv, local,
):
    nz, nf, rows, d, wide, upad, nb, ng = dims
    z, me = lax.axis_index("ctx"), lax.axis_index("fsdp")
    q_width, k_width = HEADS * HEAD_DIM, KV_HEADS * HEAD_DIM
    qkv = q_width + 2 * k_width
    scale = HEAD_DIM ** (-0.5)
    wr = d // nf
    per = PlaneGather.sems(nf)
    plane = [
        PlaneGather(src, dst, r, nf, z, me, send, recv, local.at[i], i * per)
        for i, (src, dst, r) in enumerate(
            [(wq, wq_all, wr), (sm, smb, 16), (wo, wo_all, wr), (wp, gu, wr), (dn, dnb, upad)]
        )
    ]
    p_q, p_s, p_o, p_gu, p_d = plane
    base = len(plane) * per
    chain = [
        Chain(buf, rows, nz, z, me, send, recv, base + i * Chain.sems(nz))
        for i, buf in enumerate([g_all, kv, x_all])
    ]
    c_g, c_kv, c_x = chain
    base += len(chain) * Chain.sems(nz)
    spare = len(plane)

    g_copy = pltpu.make_async_copy(g_ref, rows_at(g_all, z, rows), local.at[spare])
    g_copy.start()
    greet_ctx_and_plane(nz, nf, z, me)
    p_s.begin()
    p_q.begin()
    g_copy.wait()
    c_g.begin()

    x = x_ref[...].astype(F32)
    inverse = lax.rsqrt(jnp.mean(x * x, -1, keepdims=True) + EPSILON)
    mask[...] = jnp.where(kpos_ref[...] <= qpos_ref[...], 0.0, MASKED)

    p_s.middle()
    p_q.middle()
    p_s.late()
    p_q.late()
    p_o.begin()
    p_s.finish()
    for f in range(nf):
        row = smb[f * 16 : (f + 1) * 16, :].astype(F32)[0:1]
        bias[0:1, f * nb : (f + 1) * nb] = row[:, :nb]
        gain_ref[0:1, f * ng : (f + 1) * ng] = row[:, nb : nb + ng]
        gain_ref[1:2, f * ng : (f + 1) * ng] = row[:, nb + ng : nb + 2 * ng]
    normed = (x * inverse * gain_ref[0:1, :]).astype(BF)
    x_all[pl.ds(at128(z, rows), rows), :] = normed
    p_q.finish()
    fetch = pltpu.make_async_copy(wq_all, stage.at[pl.ds(0, d)], local.at[spare])
    fetch.start()
    for k in range(1, nz - 1):
        c_g.forward(k)
    fetch.wait()

    def project(t):
        c0 = at128(t, 2 * HEAD_DIM)
        y = dot(
            x_all[pl.ds(at128(z, rows), rows), :], stage[pl.ds(0, d), pl.ds(c0, 2 * HEAD_DIM)]
        ) + bias[0:1, pl.ds(c0, 2 * HEAD_DIM)]
        return y, c0

    def project_v(t):
        y, c0 = project(t)
        kv[pl.ds(at128(z, rows), rows), pl.ds(pl.multiple_of(c0 - q_width, 256), 256)] = y.astype(BF)

    def turned(y):
        halves = [
            turn(y[:, h * HEAD_DIM : (h + 1) * HEAD_DIM], cos_ref[...], sin_ref[...]).astype(BF)
            for h in range(2)
        ]
        return jnp.concatenate(halves, 1)

    project_v((q_width + k_width) // 256)
    y, _ = project(q_width // 256)
    kv[pl.ds(at128(z, rows), rows), 0:k_width] = turned(y)
    c_kv.begin()
    p_gu.begin()

    def project_q(t):
        y, c0 = project(t)
        q_ref[:, pl.ds(c0, 256)] = turned(y)

    loop(q_width // 256, project_q)
    for k in range(1, nz):
        c_kv.forward(k)
        c_kv.arrive(k)
    c_g.forward(nz - 1)
    p_o.middle()

    lanes = lax.broadcasted_iota(jnp.int32, (rows, HEAD_DIM), 1)
    lse_ref[...] = jnp.zeros_like(lse_ref)

    def head(h):
        c0 = at128(h, HEAD_DIM)
        kc = at128(h // (HEADS // KV_HEADS), HEAD_DIM)
        vc = pl.multiple_of(kc + k_width, HEAD_DIM)
        s = dot_bt(q_ref[:, pl.ds(c0, HEAD_DIM)], kv[:, pl.ds(kc, HEAD_DIM)]) * scale + mask[...]
        top = jnp.max(s, -1, keepdims=True)
        p = jnp.exp(s - top)
        total = jnp.sum(p, -1, keepdims=True)
        o = dot(p.astype(BF), kv[:, pl.ds(vc, HEAD_DIM)]) / total
        o_ref[:, pl.ds(c0, HEAD_DIM)] = o.astype(BF)
        lse_ref[...] = jnp.where(lanes == h, top + jnp.log(total), lse_ref[...])

    half = HEADS // 2
    loop(half, head)
    p_o.late()
    loop(HEADS - half, lambda h: head(h + half))
    p_o.finish()
    fetch = pltpu.make_async_copy(wo_all, stage.at[pl.ds(0, q_width), pl.ds(0, d)], local.at[spare])
    fetch.start()
    p_gu.middle()
    fetch.wait()

    def out_proj(t):
        c0 = at128(t, 512)
        mid_ref[:, pl.ds(c0, 512)] = (
            dot(o_ref[...], stage[pl.ds(0, q_width), pl.ds(c0, 512)]) + x_ref[:, pl.ds(c0, 512)].astype(F32)
        )

    loop(d // 512, out_proj)
    mid = mid_ref[...]
    inverse_two = lax.rsqrt(jnp.mean(mid * mid, -1, keepdims=True) + EPSILON)
    x_all[pl.ds(at128(z, rows), rows), :] = (mid * inverse_two * gain_ref[1:2, :]).astype(BF)
    c_x.begin()
    for k in range(1, nz - 1):
        c_x.forward(k)
    p_gu.late()
    p_d.begin()
    p_gu.finish()

    cols = 768 if wide % 768 == 0 else 256

    def hidden(j):
        r0 = at128(j, rows)

        def one(t):
            c0 = at128(t, cols)
            xb = x_all[pl.ds(r0, rows), :]
            gate = dot(xb, gu[:, pl.ds(c0, cols)])
            up = dot(xb, gu[:, pl.ds(pl.multiple_of(wide + c0, 128), cols)])
            act[pl.ds(r0, rows), pl.ds(c0, cols)] = (gate * jax.nn.sigmoid(gate) * up).astype(BF)
            dgu[pl.ds(r0, rows), pl.ds(c0, cols)] = gate.astype(BF)
            dgu[pl.ds(r0, rows), pl.ds(pl.multiple_of(wide + c0, 128), cols)] = up.astype(BF)

        loop(wide // cols, one)

    hidden(z)

    def nearest(k):
        c_x.arrive(k)
        hidden(c_x.order(k))

    loop(nz - 2, lambda i: nearest(i + 1))
    c_x.forward(nz - 1)
    p_d.middle()
    nearest(nz - 1)
    for k in range(1, nz):
        c_g.arrive(k)
    p_d.late()
    p_d.finish()

    def back(j):
        r0 = at128(j, rows)

        def one(t):
            c0 = at128(t, cols)
            c1 = pl.multiple_of(wide + c0, 128)
            da = dot_bt(g_all[pl.ds(r0, rows), :], dnb[pl.ds(c0, cols), :])
            gate = dgu[pl.ds(r0, rows), pl.ds(c0, cols)].astype(F32)
            up = dgu[pl.ds(r0, rows), pl.ds(c1, cols)].astype(F32)
            sig = jax.nn.sigmoid(gate)
            dgu[pl.ds(r0, rows), pl.ds(c0, cols)] = (
                da * up * (sig * (1.0 + gate * (1.0 - sig)))
            ).astype(BF)
            dgu[pl.ds(r0, rows), pl.ds(c1, cols)] = (da * gate * sig).astype(BF)

        loop(wide // cols, one)

    rs = base

    slots = stage.at[:, pl.ds(0, d)]

    def slot_copy(src, dst, step):
        return remote(
            rows_at(slots, src, rows), rows_at(slots, dst, rows),
            send.at[rs + src], recv.at[rs + dst], z + step, me,
        )

    def give(j):
        r0 = at128(j, rows)
        back(j)
        below, above = j > z, j < z
        got = jnp.logical_or(
            jnp.logical_and(below, z > 0), jnp.logical_and(above, z < nz - 1)
        )

        @pl.when(got)
        def _():
            slot_copy(j, j, 0).wait_recv()

        def one(t):
            c0 = at128(t, 512)
            y = dot_bt(dgu[pl.ds(r0, rows), :], gu[pl.ds(c0, 512), :])
            where = (pl.ds(at128(j, rows), rows), pl.ds(c0, 512))
            y = y + jnp.where(got, stage[where].astype(F32), 0.0)
            stage[where] = y.astype(BF)

        loop(d // 512, one)

        @pl.when(below)
        def _():
            slot_copy(j, j, 1).start()

        @pl.when(above)
        def _():
            slot_copy(j, jnp.where(z - 1 == j, nz, j), -1).start()

    loop(nz - 1, lambda i: give(c_x.order(nz - 1 - i)))
    back(z)

    def own(t):
        c0 = at128(t, 512)
        dx_ref[:, pl.ds(c0, 512)] = dot_bt(
            dgu[pl.ds(at128(z, rows), rows), :], gu[pl.ds(c0, 512), :]
        )

    loop(d // 512, own)

    p_gu.drain()

    def w_gu_grad(t):
        c0 = at128(t, 256)
        gu[:, pl.ds(c0, 256)] = dot_at(x_all[...], dgu[:, pl.ds(c0, 256)]).astype(BF)

    loop(2 * wide // 256, w_gu_grad)
    out_gu = pltpu.make_async_copy(gu, dwgu, local.at[spare + 1])
    out_gu.start()

    c_x.drain()

    def down_part(t):
        c0 = at128(t, 256)
        x_all[:, pl.ds(c0, 256)] = dot(act[...], dnb[:, pl.ds(c0, 256)]).astype(BF)

    loop(d // 256, down_part)
    out_p = pltpu.make_async_copy(x_all, dpart, local.at[spare + 3])
    out_p.start()

    p_d.drain()

    def w_down_grad(t):
        c0 = at128(t, 512)
        dnb[:, pl.ds(c0, 512)] = dot_at(act[...], g_all[:, pl.ds(c0, 512)]).astype(BF)

    loop(d // 512, w_down_grad)
    out_d = pltpu.make_async_copy(dnb, dwd, local.at[spare])
    out_d.start()
    out_kv = pltpu.make_async_copy(kv, kv_out, local.at[spare + 2])
    out_kv.start()

    @pl.when(z > 0)
    def _():
        slot_copy(z, z, 0).wait_recv()
        dx_ref[...] += rows_at(slots, z, rows)[...].astype(F32)

    @pl.when(z < nz - 1)
    def _():
        slot_copy(z, nz, 0).wait_recv()
        dx_ref[...] += rows_at(slots, nz, rows)[...].astype(F32)

    for part in (p_q, p_s, p_o, c_g, c_kv):
        part.drain()

    def gave(i):
        j = c_x.order(i + 1)
        slot_copy(j, j, 0).wait_send()

    loop(nz - 1, gave)
    out_d.wait()
    out_gu.wait()
    out_kv.wait()
    out_p.wait()


def front(dims, wq, sm, wo, wp, dn, x, g, cos2, sin2, qpos, kpos):
    nz, nf, rows, d, wide, upad, nb, ng = dims
    q_width, k_width = HEADS * HEAD_DIM, KV_HEADS * HEAD_DIM
    qkv = q_width + 2 * k_width
    tokens = nz * rows
    any_, vm = pl.BlockSpec(memory_space=pl.ANY), pl.BlockSpec(memory_space=pltpu.VMEM)
    sems = 5 * PlaneGather.sems(nf) + 3 * Chain.sems(nz) + nz + 1
    out = jax.ShapeDtypeStruct
    return pl.pallas_call(
        functools.partial(front_kernel, dims),
        in_specs=[any_] * 5 + [vm, any_] + [vm] * 4,
        out_specs=[any_, any_, vm, any_] + [vm] * 5 + [any_] * 3,
        out_shape=[
            out((d, qkv), BF),
            out((q_width, d), BF),
            out((rows, q_width), BF),
            out((tokens, 2 * k_width), BF),
            out((rows, q_width), BF),
            out((rows, HEAD_DIM), F32),
            out((rows, d), F32),
            out((rows, d), F32),
            out((8, d), F32),
            out((d, 2 * wide), BF),
            out((wide, d), BF),
            out((tokens, d), BF),
        ],
        scratch_shapes=[
            pltpu.VMEM((max(d, (nz + 1) * rows), qkv), BF),
            pltpu.VMEM((d, 2 * wide), BF),
            pltpu.VMEM((wide, d), BF),
            pltpu.VMEM((tokens, d), BF),
            pltpu.VMEM((tokens, d), BF),
            pltpu.VMEM((tokens, wide), BF),
            pltpu.VMEM((tokens, 2 * wide), BF),
            pltpu.VMEM((nf * 16, sm.shape[1]), BF),
            pltpu.VMEM((tokens, 2 * k_width), BF),
            pltpu.VMEM((8, qkv), F32),
            pltpu.VMEM((rows, tokens), F32),
            pltpu.SemaphoreType.DMA((sems,)),
            pltpu.SemaphoreType.DMA((sems,)),
            pltpu.SemaphoreType.DMA((9,)),
        ],
        compiler_params=pltpu.CompilerParams(
            collective_id=0, has_side_effects=True, vmem_limit_bytes=VMEM_LIMIT
        ),
    )(wq, sm, wo, wp, dn, x, g, cos2, sin2, qpos, kpos)


def shards(
    hidden_in, w_qkv, b_qkv, w_out, w_gate_up, w_down, gain_attn, gain_mlp, block_order, cotangent
):
    nz, nf = lax.axis_size("ctx"), lax.axis_size("fsdp")
    z, me = lax.axis_index("ctx"), lax.axis_index("fsdp")
    groups = HEADS // KV_HEADS
    q_width, k_width = HEADS * HEAD_DIM, KV_HEADS * HEAD_DIM
    rows = hidden_in.shape[1]
    piece_len = rows // 2
    ff = w_gate_up.shape[1] // 2
    unit = ff // (nf * nz)
    scale = HEAD_DIM ** (-0.5)
    order_row = block_order[0]
    all_places = (
        order_row[:, None] * piece_len + jnp.arange(piece_len, dtype=jnp.int32)[None, :]
    ).reshape(-1)
    my_places = lax.dynamic_slice_in_dim(all_places, z * rows, rows)
    visible = all_places[None, :] <= my_places[:, None]
    cosine, sine_table = angle_tables(my_places)
    cos2 = jnp.concatenate([cosine, cosine], 1)
    sin2 = jnp.concatenate([-sine_table, sine_table], 1)

    packed = pack(w_gate_up, nz, nf, z)
    wide = packed.shape[1] // 2
    upad = wide // nf
    down_mine = jnp.pad(
        lax.dynamic_slice_in_dim(w_down, z * unit, unit), ((0, upad - unit), (0, 0))
    )
    nb, ng = b_qkv.shape[0], gain_attn.shape[0]
    d = hidden_in.shape[2]
    small = jnp.concatenate([b_qkv, gain_attn, gain_mlp])
    small = jnp.pad(small[None], ((0, 15), (0, -small.shape[0] % 128)))
    grad_low = cotangent[0]
    (whole_qkv, whole_out, q_low, kv_all, attn_low, lse, middle, grad_normed_two, gains, gate_up_local, down_local,
     down_part) = front(
        (nz, nf, rows, d, wide, upad, nb, ng),
        w_qkv, small, w_out, packed, down_mine, hidden_in[0], grad_low, cos2, sin2,
        my_places[:, None], all_places[None, :],
    )
    gain_first, gain_second = gains[0], gains[1]
    inputs = hidden_in[0].astype(F32)
    inverse_one = lax.rsqrt(jnp.mean(inputs * inputs, -1, keepdims=True) + EPSILON)
    normed = (inputs * inverse_one * gain_first).astype(BF)
    inverse_two = lax.rsqrt(jnp.mean(middle * middle, -1, keepdims=True) + EPSILON)
    queries = q_low.reshape(rows, KV_HEADS, groups, HEAD_DIM)
    keys_all = kv_all[:, :k_width].reshape(-1, KV_HEADS, HEAD_DIM)
    values_all = kv_all[:, k_width:].reshape(-1, KV_HEADS, HEAD_DIM)
    attn_heads = attn_low.astype(F32).reshape(rows, KV_HEADS, groups, HEAD_DIM).transpose(1, 2, 0, 3)
    log_total = lse[:, :HEADS].reshape(rows, KV_HEADS, groups).transpose(1, 2, 0)[..., None]
    down_sum = ctx_scatter(down_part.reshape(nz, rows, -1))
    hidden_out = (middle + down_sum).astype(BF)[None]
    down_sums = plane_scatter(down_local.reshape(nf, upad, -1))[:unit]
    grad_down = jnp.concatenate(ctx_chain(down_sums.astype(BF)), 0).astype(F32)
    gate_up_sums = plane_scatter(gate_up_local.reshape(nf, -1, 2 * wide))
    grad_gate_up = unpack(ctx_chain(gate_up_sums.astype(BF)), nz, nf, ff)

    grad_full = grad_low.astype(F32)
    scaled_two = gain_second * grad_normed_two
    gain_two_local = jnp.sum(grad_normed_two * middle * inverse_two, 0)
    grad_middle = (
        grad_full
        + inverse_two * scaled_two
        - middle
        * (inverse_two * inverse_two * inverse_two)
        * jnp.mean(scaled_two * middle, -1, keepdims=True)
    )
    grad_branch = grad_middle.astype(BF)
    out_local = dot_at(attn_low, grad_branch)
    grad_out = ctx_sum(plane_scatter(out_local.reshape(nf, -1, out_local.shape[1])))
    grad_attn = dot_bt(grad_branch, whole_out).astype(BF)
    grad_heads = grad_attn.reshape(rows, KV_HEADS, groups, HEAD_DIM).transpose(1, 2, 0, 3)
    row_delta = jnp.sum(grad_heads.astype(F32) * attn_heads, -1, keepdims=True)
    scores = jnp.einsum("qkgd,tkd->kgqt", queries, keys_all, preferred_element_type=F32) * scale
    probs = jnp.where(visible, jnp.exp(scores - log_total), 0.0)
    grad_values = jnp.einsum(
        "kgqt,kgqd->tkd", probs.astype(BF), grad_heads, preferred_element_type=F32
    )
    grad_probs = jnp.einsum("kgqd,tkd->kgqt", grad_heads, values_all, preferred_element_type=F32)
    grad_scores = (probs * (grad_probs - row_delta)).astype(BF)
    grad_queries = (
        jnp.einsum("kgqt,tkd->kgqd", grad_scores, keys_all, preferred_element_type=F32) * scale
    )
    grad_keys = (
        jnp.einsum("kgqt,qkgd->tkd", grad_scores, queries, preferred_element_type=F32) * scale
    )
    kv_grads = jnp.concatenate(
        [grad_keys.reshape(nz, rows, k_width), grad_values.reshape(nz, rows, k_width)], -1
    )
    kv_grad = ctx_scatter(kv_grads)
    query_back = rotate(grad_queries.transpose(2, 0, 1, 3), cosine, -sine_table).reshape(
        rows, q_width
    )
    key_back = rotate(
        kv_grad[:, :k_width].reshape(rows, KV_HEADS, HEAD_DIM), cosine, -sine_table
    ).reshape(rows, k_width)
    grad_projected = jnp.concatenate([query_back, key_back, kv_grad[:, k_width:]], 1).astype(BF)
    bias_local = jnp.sum(grad_projected.astype(F32), 0)
    qkv_local = dot_at(normed, grad_projected)
    grad_qkv = ctx_sum(plane_scatter(qkv_local.reshape(nf, -1, qkv_local.shape[1])))
    grad_normed = dot_bt(grad_projected, whole_qkv)
    scaled_one = gain_first * grad_normed
    gain_one_local = jnp.sum(grad_normed * inputs * inverse_one, 0)
    grad_inputs = (
        grad_middle
        + inverse_one * scaled_one
        - inputs
        * (inverse_one * inverse_one * inverse_one)
        * jnp.mean(scaled_one * inputs, -1, keepdims=True)
    )
    cut = q_width + k_width
    tiny = jnp.concatenate(
        [
            bias_local[:cut].reshape(nf, -1),
            bias_local[cut:].reshape(nf, -1),
            gain_one_local.reshape(nf, -1),
            gain_two_local.reshape(nf, -1),
        ],
        1,
    ).reshape(nf, 1, -1)
    tiny = plane_scatter(tiny).reshape(nz, -1)
    tiny = ctx_sum(tiny).reshape(-1)
    e1 = cut // nf
    e2 = e1 + k_width // nf
    e3 = e2 + ng
    return (
        hidden_out,
        grad_inputs.astype(BF)[None],
        grad_qkv,
        tiny[:e1],
        tiny[e1:e2],
        grad_out,
        grad_gate_up,
        grad_down,
        tiny[e2:e3],
        tiny[e3:],
    )


def solution(mesh):
    placed = (
        P("fsdp", "ctx", None),
        P("fsdp", None),
        P("fsdp"),
        P("fsdp", None),
        P("fsdp", None),
        P("fsdp", None),
        P("fsdp"),
        P("fsdp"),
        P("fsdp", None),
        P("fsdp", "ctx", None),
    )
    return jax.shard_map(
        shards,
        mesh=mesh,
        in_specs=placed,
        out_specs=(
            P("fsdp", "ctx", None),
            P("fsdp", "ctx", None),
            P("fsdp", None),
            P("fsdp"),
            P("fsdp"),
            P("fsdp", None),
            P("fsdp", None),
            P("fsdp", None),
            P("fsdp"),
            P("fsdp"),
        ),
        check_vma=False,
    )
```

```python
import functools

import jax
import jax.numpy as jnp
from jax import lax
from jax.experimental import pallas as pl
from jax.experimental.pallas import tpu as pltpu
from jax.sharding import PartitionSpec as P

HEADS = 12
KV_HEADS = 2
HEAD_DIM = 128
EPSILON = 1e-06
THETA = 1000000.0
MASKED = -1e30
BF = jnp.bfloat16
F32 = jnp.float32


def dot(a, b):
    return jnp.dot(a, b, preferred_element_type=F32)


def dot_bt(a, b):
    return lax.dot_general(a, b, (((1,), (1,)), ((), ())), preferred_element_type=F32)


def dot_at(a, b):
    return lax.dot_general(a, b, (((0,), (0,)), ((), ())), preferred_element_type=F32)


def angle_tables(places):
    half_dim = HEAD_DIM // 2
    freqs = THETA ** (-(jnp.arange(half_dim).astype(F32) * 2.0 / HEAD_DIM))
    angles = places.astype(F32)[:, None] * freqs[None, :]
    return (jnp.cos(angles), jnp.sin(angles))


def half_rows(rows):
    return -(-rows // 32) * 16


def pack_kernel(nz, nf, ff, unit, upad, z_ref, w_ref, out_ref):
    for k in range(nz):

        @pl.when(z_ref[0] == k)
        def _():
            for h in range(2):
                for f in range(nf):
                    src = h * ff + f * (ff // nf) + k * unit
                    dst = (h * nf + f) * upad
                    out_ref[:, dst : dst + unit] = w_ref[:, src : src + unit]
                    out_ref[:, dst + unit : dst + upad] = jnp.zeros(
                        (out_ref.shape[0], upad - unit), out_ref.dtype
                    )


def pack(w, nz, nf, z):
    rows, ff = w.shape[0], w.shape[1] // 2
    unit = ff // (nf * nz)
    upad = -(-unit // 16) * 16
    wide = nf * upad
    step = 32
    return pl.pallas_call(
        functools.partial(pack_kernel, nz, nf, ff, unit, upad),
        grid=(rows // step,),
        in_specs=[
            pl.BlockSpec(memory_space=pltpu.SMEM),
            pl.BlockSpec((step, 2 * ff), lambda i: (i, 0)),
        ],
        out_specs=pl.BlockSpec((step, 2 * wide), lambda i: (i, 0)),
        out_shape=jax.ShapeDtypeStruct((rows, 2 * wide), w.dtype),
    )(z.reshape(1).astype(jnp.int32), w)


def unpack_kernel(nz, nf, ff, unit, upad, *refs):
    out_ref = refs[-1]
    for k in range(nz):
        for h in range(2):
            for f in range(nf):
                src = f * upad
                dst = h * ff + f * (ff // nf) + k * unit
                part = refs[h * nz + k]
                out_ref[:, dst : dst + unit] = part[:, src : src + unit].astype(F32)


def unpack(gate, up, nz, nf, ff):
    rows, wide = gate.shape[0] // nz, gate.shape[1]
    step = 32
    specs = [
        pl.BlockSpec((step, wide), lambda i, k=k: (k * (rows // step) + i, 0)) for k in range(nz)
    ]
    return pl.pallas_call(
        functools.partial(unpack_kernel, nz, nf, ff, ff // (nf * nz), wide // nf),
        grid=(rows // step,),
        in_specs=specs * 2,
        out_specs=pl.BlockSpec((step, 2 * ff), lambda i: (i, 0)),
        out_shape=jax.ShapeDtypeStruct((rows, 2 * ff), F32),
    )(*[gate] * nz, *[up] * nz)


MESH = pl.DeviceIdType.MESH
VMEM_LIMIT = 63 * 2**20


def remote(src, dst, send, recv, z, f):
    return pltpu.make_async_remote_copy(
        src_ref=src, dst_ref=dst, send_sem=send, recv_sem=recv, device_id=(z, f), device_id_type=MESH
    )


def rows_at(ref, index, count):
    return ref.at[pl.ds(pl.multiple_of(index * count, count), count)]


class PlaneGather:
    def __init__(self, src, dst, rows, nf, z, me, send, recv, local, base):
        self.src, self.dst, self.rows, self.nf, self.z, self.me = src, dst, rows, nf, z, me
        self.send, self.recv, self.base = send, recv, base
        self.local = pltpu.make_async_copy(src, rows_at(dst, me, rows), local)
        self.sent = []
        self.cut = half_rows(rows)
        self.swaps = {}

    @staticmethod
    def sems(nf):
        return 2 * nf

    def slot(self, k, lo=0, hi=None):
        hi = self.rows if hi is None else hi
        start = pl.multiple_of((self.me ^ k) * self.rows, 16) + lo
        return self.dst.at[pl.ds(pl.multiple_of(start, 16), hi - lo)]

    def push(self, index, src, dst, flip_by):
        copy = remote(
            src, dst, self.send.at[self.base + index], self.recv.at[self.base + index],
            self.z, self.me ^ flip_by,
        )
        copy.start()
        self.sent.append(copy)
        return copy

    def begin(self):
        self.local.start()
        self.direct = {}
        for k in (2, 4) if self.nf == 8 else range(2, self.nf, 2):
            self.direct[k] = self.push(k, self.src, self.slot(0), k)
        self.swaps[0] = self.push(1, self.src, self.slot(0), 1)

    def swap(self, k):
        self.swaps[k] = self.push(k + 1, self.slot(k), self.slot(k), 1)

    def middle(self):
        for k, copy in self.direct.items():
            copy.wait_recv()
            if self.nf == 8:
                if k == 2:
                    self.far_a = self.push(6, self.slot(2, 0, self.cut), self.slot(2, 0, self.cut), 4)
                elif self.cut < self.rows:
                    self.far_b = self.push(
                        8, self.slot(4, self.cut), self.slot(4, self.cut), 2
                    )
            self.swap(k)

    def late(self):
        if self.nf == 8:
            self.far_a.wait_recv()
            if self.cut < self.rows:
                self.far_b.wait_recv()
            self.swap(6)

    def finish(self):
        self.local.wait()
        for copy in self.swaps.values():
            copy.wait_recv()

    def drain(self):
        for copy in self.sent:
            copy.wait_send()


class Chain:
    def __init__(self, buf, rows, nz, z, me, send, recv, base):
        self.buf, self.rows, self.nz, self.z, self.me = buf, rows, nz, z, me
        self.send, self.recv, self.base = send, recv, base

    @staticmethod
    def sems(nz):
        return nz + 2

    def copy(self, j, sem, step):
        slot = rows_at(self.buf, j, self.rows)
        return remote(
            slot, slot, self.send.at[self.base + sem], self.recv.at[self.base + j], self.z + step, self.me
        )

    def order(self, k):
        z, nz = self.z, self.nz
        below, above = z, nz - 1 - z
        m = jnp.minimum(below, above)
        near = jnp.where(k % 2 == 1, z - (k + 1) // 2, z + k // 2)
        far = jnp.where(above > below, z + (k - m), z - (k - m))
        return jnp.where(k <= 2 * m, near, far)

    def begin(self):
        z, nz = self.z, self.nz

        @pl.when(z < nz - 1)
        def _():
            self.copy(z, nz, 1).start()

        @pl.when(z > 0)
        def _():
            self.copy(z, nz + 1, -1).start()

    def passing(self, j):
        z, nz = self.z, self.nz
        return jnp.logical_and(j < z, z < nz - 1), jnp.logical_and(j > z, z > 0)

    def forward(self, k):
        j = self.order(k)
        up, down = self.passing(j)

        @pl.when(up)
        def _():
            self.copy(j, j, 1).wait_recv()
            self.copy(j, j, 1).start()

        @pl.when(down)
        def _():
            self.copy(j, j, -1).wait_recv()
            self.copy(j, j, -1).start()

    def arrive(self, k):
        j = self.order(k)
        up, down = self.passing(j)

        @pl.when(jnp.logical_not(jnp.logical_or(up, down)))
        def _():
            self.copy(j, j, 0).wait_recv()

    def drain(self):
        z, nz = self.z, self.nz

        @pl.when(z < nz - 1)
        def _():
            self.copy(z, nz, 1).wait_send()

        @pl.when(z > 0)
        def _():
            self.copy(z, nz + 1, -1).wait_send()

        def one(k, carry):
            j = self.order(k)
            up, down = self.passing(j)

            @pl.when(jnp.logical_or(up, down))
            def _():
                self.copy(j, j, 0).wait_send()

            return carry

        lax.fori_loop(1, nz, one, 0)


def greet_ctx_and_plane(nz, nf, z, me):
    barrier = pltpu.get_barrier_semaphore()
    flips = (1, 2, 4) if nf == 8 else (1,) + tuple(range(2, nf, 2))
    for k in flips:
        pl.semaphore_signal(barrier, inc=1, device_id=(z, me ^ k), device_id_type=MESH)

    @pl.when(z < nz - 1)
    def _():
        pl.semaphore_signal(barrier, inc=1, device_id=(z + 1, me), device_id_type=MESH)

    @pl.when(z > 0)
    def _():
        pl.semaphore_signal(barrier, inc=1, device_id=(z - 1, me), device_id_type=MESH)

    inner = jnp.logical_and(z > 0, z < nz - 1)

    @pl.when(inner)
    def _():
        pl.semaphore_wait(barrier, len(flips) + 2)

    @pl.when(jnp.logical_not(inner))
    def _():
        pl.semaphore_wait(barrier, len(flips) + 1)


def loop(n, body):
    def step(i, carry):
        body(i)
        return carry

    lax.fori_loop(0, n, step, 0)


def at128(i, n):
    return i * n if isinstance(i, int) else pl.multiple_of(i * n, n)


def turn(t, cos2, sin2):
    return t * cos2 + pltpu.roll(t, HEAD_DIM // 2, 1) * sin2


def front_kernel(
    dims,
    wq, sm, wo, wp, dn, x_ref, g_ref, cos_ref, sin_ref, qpos_ref, kpos_ref,
    wq_all, wo_all, q_ref, kv_out, o_ref, lse_ref, mid_ref, dx_ref, gain_ref, dwgu, dwd, dpart,
    stage, gu, dnb, g_all, x_all, act, dgu, smb, kv, bias, mask, send, recv, local,
):
    nz, nf, rows, d, wide, upad, nb, ng = dims
    z, me = lax.axis_index("ctx"), lax.axis_index("fsdp")
    q_width, k_width = HEADS * HEAD_DIM, KV_HEADS * HEAD_DIM
    qkv = q_width + 2 * k_width
    scale = HEAD_DIM ** (-0.5)
    wr = d // nf
    per = PlaneGather.sems(nf)
    plane = [
        PlaneGather(src, dst, r, nf, z, me, send, recv, local.at[i], i * per)
        for i, (src, dst, r) in enumerate(
            [(wq, wq_all, wr), (sm, smb, 16), (wo, wo_all, wr), (wp, gu, wr), (dn, dnb, upad)]
        )
    ]
    p_q, p_s, p_o, p_gu, p_d = plane
    base = len(plane) * per
    chain = [
        Chain(buf, rows, nz, z, me, send, recv, base + i * Chain.sems(nz))
        for i, buf in enumerate([g_all, kv, x_all])
    ]
    c_g, c_kv, c_x = chain
    base += len(chain) * Chain.sems(nz)
    spare = len(plane)

    g_copy = pltpu.make_async_copy(g_ref, rows_at(g_all, z, rows), local.at[spare])
    g_copy.start()
    greet_ctx_and_plane(nz, nf, z, me)
    p_s.begin()
    p_q.begin()
    g_copy.wait()
    c_g.begin()

    x = x_ref[...].astype(F32)
    inverse = lax.rsqrt(jnp.mean(x * x, -1, keepdims=True) + EPSILON)
    mask[...] = jnp.where(kpos_ref[...] <= qpos_ref[...], 0.0, MASKED)

    p_s.middle()
    p_q.middle()
    p_s.late()
    p_q.late()
    p_o.begin()
    p_s.finish()
    for f in range(nf):
        row = smb[f * 16 : (f + 1) * 16, :].astype(F32)[0:1]
        bias[0:1, f * nb : (f + 1) * nb] = row[:, :nb]
        gain_ref[0:1, f * ng : (f + 1) * ng] = row[:, nb : nb + ng]
        gain_ref[1:2, f * ng : (f + 1) * ng] = row[:, nb + ng : nb + 2 * ng]
    normed = (x * inverse * gain_ref[0:1, :]).astype(BF)
    x_all[pl.ds(at128(z, rows), rows), :] = normed
    p_q.finish()
    fetch = pltpu.make_async_copy(wq_all, stage.at[pl.ds(0, d)], local.at[spare])
    fetch.start()
    for k in range(1, nz - 1):
        c_g.forward(k)
    fetch.wait()

    def project(t):
        c0 = at128(t, 2 * HEAD_DIM)
        y = dot(
            x_all[pl.ds(at128(z, rows), rows), :], stage[pl.ds(0, d), pl.ds(c0, 2 * HEAD_DIM)]
        ) + bias[0:1, pl.ds(c0, 2 * HEAD_DIM)]
        return y, c0

    def project_v(t):
        y, c0 = project(t)
        kv[pl.ds(at128(z, rows), rows), pl.ds(pl.multiple_of(c0 - q_width, 256), 256)] = y.astype(BF)

    def turned(y):
        halves = [
            turn(y[:, h * HEAD_DIM : (h + 1) * HEAD_DIM], cos_ref[...], sin_ref[...]).astype(BF)
            for h in range(2)
        ]
        return jnp.concatenate(halves, 1)

    project_v((q_width + k_width) // 256)
    y, _ = project(q_width // 256)
    kv[pl.ds(at128(z, rows), rows), 0:k_width] = turned(y)
    c_kv.begin()
    p_gu.begin()

    def project_q(t):
        y, c0 = project(t)
        q_ref[:, pl.ds(c0, 256)] = turned(y)

    loop(q_width // 256, project_q)
    for k in range(1, nz):
        c_kv.forward(k)
        c_kv.arrive(k)
    c_g.forward(nz - 1)
    p_o.middle()

    lanes = lax.broadcasted_iota(jnp.int32, (rows, HEAD_DIM), 1)
    lse_ref[...] = jnp.zeros_like(lse_ref)

    def head(h):
        c0 = at128(h, HEAD_DIM)
        kc = at128(h // (HEADS // KV_HEADS), HEAD_DIM)
        vc = pl.multiple_of(kc + k_width, HEAD_DIM)
        s = dot_bt(q_ref[:, pl.ds(c0, HEAD_DIM)], kv[:, pl.ds(kc, HEAD_DIM)]) * scale + mask[...]
        top = jnp.max(s, -1, keepdims=True)
        p = jnp.exp(s - top)
        total = jnp.sum(p, -1, keepdims=True)
        o = dot(p.astype(BF), kv[:, pl.ds(vc, HEAD_DIM)]) / total
        o_ref[:, pl.ds(c0, HEAD_DIM)] = o.astype(BF)
        lse_ref[...] = jnp.where(lanes == h, top + jnp.log(total), lse_ref[...])

    half = HEADS // 2
    loop(half, head)
    p_o.late()
    loop(HEADS - half, lambda h: head(h + half))
    p_o.finish()
    fetch = pltpu.make_async_copy(wo_all, stage.at[pl.ds(0, q_width), pl.ds(0, d)], local.at[spare])
    fetch.start()
    p_gu.middle()
    fetch.wait()

    def out_proj(t):
        c0 = at128(t, 512)
        mid_ref[:, pl.ds(c0, 512)] = (
            dot(o_ref[...], stage[pl.ds(0, q_width), pl.ds(c0, 512)]) + x_ref[:, pl.ds(c0, 512)].astype(F32)
        )

    loop(d // 512, out_proj)
    mid = mid_ref[...]
    inverse_two = lax.rsqrt(jnp.mean(mid * mid, -1, keepdims=True) + EPSILON)
    x_all[pl.ds(at128(z, rows), rows), :] = (mid * inverse_two * gain_ref[1:2, :]).astype(BF)
    c_x.begin()
    for k in range(1, nz - 1):
        c_x.forward(k)
    p_gu.late()
    p_d.begin()
    p_gu.finish()

    cols = 768 if wide % 768 == 0 else 256

    def hidden(j):
        r0 = at128(j, rows)

        def one(t):
            c0 = at128(t, cols)
            xb = x_all[pl.ds(r0, rows), :]
            gate = dot(xb, gu[:, pl.ds(c0, cols)])
            up = dot(xb, gu[:, pl.ds(pl.multiple_of(wide + c0, 128), cols)])
            act[pl.ds(r0, rows), pl.ds(c0, cols)] = (gate * jax.nn.sigmoid(gate) * up).astype(BF)
            dgu[pl.ds(r0, rows), pl.ds(c0, cols)] = gate.astype(BF)
            dgu[pl.ds(r0, rows), pl.ds(pl.multiple_of(wide + c0, 128), cols)] = up.astype(BF)

        loop(wide // cols, one)

    hidden(z)

    def nearest(k):
        c_x.arrive(k)
        hidden(c_x.order(k))

    loop(nz - 2, lambda i: nearest(i + 1))
    c_x.forward(nz - 1)
    p_d.middle()
    nearest(nz - 1)
    for k in range(1, nz):
        c_g.arrive(k)
    p_d.late()
    p_d.finish()

    def back(j):
        r0 = at128(j, rows)

        def one(t):
            c0 = at128(t, cols)
            c1 = pl.multiple_of(wide + c0, 128)
            da = dot_bt(g_all[pl.ds(r0, rows), :], dnb[pl.ds(c0, cols), :])
            gate = dgu[pl.ds(r0, rows), pl.ds(c0, cols)].astype(F32)
            up = dgu[pl.ds(r0, rows), pl.ds(c1, cols)].astype(F32)
            sig = jax.nn.sigmoid(gate)
            dgu[pl.ds(r0, rows), pl.ds(c0, cols)] = (
                da * up * (sig * (1.0 + gate * (1.0 - sig)))
            ).astype(BF)
            dgu[pl.ds(r0, rows), pl.ds(c1, cols)] = (da * gate * sig).astype(BF)

        loop(wide // cols, one)

    rs = base

    slots = stage.at[:, pl.ds(0, d)]

    def slot_copy(src, dst, step):
        return remote(
            rows_at(slots, src, rows), rows_at(slots, dst, rows),
            send.at[rs + src], recv.at[rs + dst], z + step, me,
        )

    def give(j):
        r0 = at128(j, rows)
        back(j)
        below, above = j > z, j < z
        got = jnp.logical_or(
            jnp.logical_and(below, z > 0), jnp.logical_and(above, z < nz - 1)
        )

        @pl.when(got)
        def _():
            slot_copy(j, j, 0).wait_recv()

        def one(t):
            c0 = at128(t, 512)
            y = dot_bt(dgu[pl.ds(r0, rows), :], gu[pl.ds(c0, 512), :])
            where = (pl.ds(at128(j, rows), rows), pl.ds(c0, 512))
            y = y + jnp.where(got, stage[where].astype(F32), 0.0)
            stage[where] = y.astype(BF)

        loop(d // 512, one)

        @pl.when(below)
        def _():
            slot_copy(j, j, 1).start()

        @pl.when(above)
        def _():
            slot_copy(j, jnp.where(z - 1 == j, nz, j), -1).start()

    loop(nz - 1, lambda i: give(c_x.order(nz - 1 - i)))
    back(z)

    def own(t):
        c0 = at128(t, 512)
        dx_ref[:, pl.ds(c0, 512)] = dot_bt(
            dgu[pl.ds(at128(z, rows), rows), :], gu[pl.ds(c0, 512), :]
        )

    loop(d // 512, own)

    p_gu.drain()

    def w_gu_grad(t):
        c0 = at128(t, 256)
        gu[:, pl.ds(c0, 256)] = dot_at(x_all[...], dgu[:, pl.ds(c0, 256)]).astype(BF)

    loop(2 * wide // 256, w_gu_grad)
    out_gu = pltpu.make_async_copy(gu, dwgu, local.at[spare + 1])
    out_gu.start()

    c_x.drain()

    def down_part(t):
        c0 = at128(t, 256)
        x_all[:, pl.ds(c0, 256)] = dot(act[...], dnb[:, pl.ds(c0, 256)]).astype(BF)

    loop(d // 256, down_part)
    out_p = pltpu.make_async_copy(x_all, dpart, local.at[spare + 3])
    out_p.start()

    p_d.drain()

    def w_down_grad(t):
        c0 = at128(t, 512)
        dnb[:, pl.ds(c0, 512)] = dot_at(act[...], g_all[:, pl.ds(c0, 512)]).astype(BF)

    loop(d // 512, w_down_grad)
    out_d = pltpu.make_async_copy(dnb, dwd, local.at[spare])
    out_d.start()
    out_kv = pltpu.make_async_copy(kv, kv_out, local.at[spare + 2])
    out_kv.start()

    @pl.when(z > 0)
    def _():
        slot_copy(z, z, 0).wait_recv()
        dx_ref[...] += rows_at(slots, z, rows)[...].astype(F32)

    @pl.when(z < nz - 1)
    def _():
        slot_copy(z, nz, 0).wait_recv()
        dx_ref[...] += rows_at(slots, nz, rows)[...].astype(F32)

    for part in (p_q, p_s, p_o, c_g, c_kv):
        part.drain()

    def gave(i):
        j = c_x.order(i + 1)
        slot_copy(j, j, 0).wait_send()

    loop(nz - 1, gave)
    out_d.wait()
    out_gu.wait()
    out_kv.wait()
    out_p.wait()


def front(dims, wq, sm, wo, wp, dn, x, g, cos2, sin2, qpos, kpos):
    nz, nf, rows, d, wide, upad, nb, ng = dims
    q_width, k_width = HEADS * HEAD_DIM, KV_HEADS * HEAD_DIM
    qkv = q_width + 2 * k_width
    tokens = nz * rows
    any_, vm = pl.BlockSpec(memory_space=pl.ANY), pl.BlockSpec(memory_space=pltpu.VMEM)
    sems = 5 * PlaneGather.sems(nf) + 3 * Chain.sems(nz) + nz + 1
    out = jax.ShapeDtypeStruct
    return pl.pallas_call(
        functools.partial(front_kernel, dims),
        in_specs=[any_] * 5 + [vm, any_] + [vm] * 4,
        out_specs=[any_, any_, vm, any_] + [vm] * 5 + [any_] * 3,
        out_shape=[
            out((d, qkv), BF),
            out((q_width, d), BF),
            out((rows, q_width), BF),
            out((tokens, 2 * k_width), BF),
            out((rows, q_width), BF),
            out((rows, HEAD_DIM), F32),
            out((rows, d), F32),
            out((rows, d), F32),
            out((8, d), F32),
            out((d, 2 * wide), BF),
            out((wide, d), BF),
            out((tokens, d), BF),
        ],
        scratch_shapes=[
            pltpu.VMEM((max(d, (nz + 1) * rows), qkv), BF),
            pltpu.VMEM((d, 2 * wide), BF),
            pltpu.VMEM((wide, d), BF),
            pltpu.VMEM((tokens, d), BF),
            pltpu.VMEM((tokens, d), BF),
            pltpu.VMEM((tokens, wide), BF),
            pltpu.VMEM((tokens, 2 * wide), BF),
            pltpu.VMEM((nf * 16, sm.shape[1]), BF),
            pltpu.VMEM((tokens, 2 * k_width), BF),
            pltpu.VMEM((8, qkv), F32),
            pltpu.VMEM((rows, tokens), F32),
            pltpu.SemaphoreType.DMA((sems,)),
            pltpu.SemaphoreType.DMA((sems,)),
            pltpu.SemaphoreType.DMA((9,)),
        ],
        compiler_params=pltpu.CompilerParams(
            collective_id=0, has_side_effects=True, vmem_limit_bytes=VMEM_LIMIT
        ),
    )(wq, sm, wo, wp, dn, x, g, cos2, sin2, qpos, kpos)


class Scatter:
    def __init__(self, src, c0, rows, cols, recv4, land, inside, nf, z, me, send, recv, base):
        self.src, self.c0, self.rows, self.cols = src, c0, rows, cols
        self.recv4, self.land, self.inside = recv4, land, inside
        self.nf, self.z, self.me, self.send, self.recv, self.base = nf, z, me, send, recv, base
        self.chips, self.chip, self.core = nf // 2, me // 2, me % 2
        self.cut = half_rows(rows)
        self.sent = []
        self.got = {}

    @staticmethod
    def sems(nf):
        return nf

    def push(self, index, src, dst, flip_by):
        copy = remote(
            src, dst, self.send.at[self.base + index], self.recv.at[self.base + index],
            self.z, self.me ^ flip_by,
        )
        copy.start()
        self.sent.append(copy)
        self.got[index] = copy

    def mine(self, ref, start, n):
        return ref.at[pl.ds(pl.multiple_of(start, 16), n)]

    def block(self, k, lo=0, hi=None):
        hi = self.rows if hi is None else hi
        return self.mine(self.recv4, (self.chip ^ k) * self.rows + lo, hi - lo)

    def swap(self):
        for p in range(self.chips):
            start = pl.multiple_of((2 * p + 1 - self.core) * self.rows, 16)
            src = self.src.at[pl.ds(start, self.rows), pl.ds(self.c0, self.cols)]
            self.push(p, src, self.mine(self.recv4, p * self.rows, self.rows), 1)

    def merge(self):
        rows, cols = self.rows, self.cols
        for p in range(self.chips):
            self.got[p].wait_recv()
        if self.inside:
            for p in range(self.chips):
                start = pl.multiple_of((2 * p + self.core) * rows, 16)
                own = self.src[pl.ds(start, rows), pl.ds(self.c0, cols)]
                where = pl.ds(p * rows, rows)
                self.recv4[where, :] = (self.recv4[where, :].astype(F32) + own.astype(F32)).astype(BF)
            return
        step = rows if rows <= 96 else rows // 2
        n = rows // step
        core, col = self.core, self.c0 // cols
        own = pl.BlockSpec((step, cols), lambda p, i: ((2 * p + core) * n + i, col))
        held = pl.BlockSpec((step, cols), lambda p, i: (p * n + i, 0))
        pltpu.emit_pipeline(
            add_two, grid=(self.chips, n), in_specs=[own, held], out_specs=[held]
        )(self.src, self.recv4, self.recv4)

    def add(self, out, parts, n):
        if self.inside:
            total = parts[0][...].astype(F32)
            for part in parts[1:]:
                total = total + part[...].astype(F32)
            out[...] = total.astype(BF)
            return
        step = n if n <= 96 else n // 2
        spec = pl.BlockSpec((step, self.cols), lambda i: (i, 0))
        body = add_two if len(parts) == 2 else add_all
        pltpu.emit_pipeline(
            body, grid=(n // step,), in_specs=[spec] * len(parts), out_specs=[spec]
        )(*parts, out)

    def first(self):
        base, rows, cut = self.chips, self.rows, self.cut
        if self.nf == 8:
            self.push(base, self.block(3, 0, cut), self.land.at[pl.ds(0, cut)], 2)
            self.push(base + 1, self.block(3, cut), self.land.at[pl.ds(cut, rows - cut)], 4)
        else:
            for k in range(1, self.chips):
                self.push(base + k - 1, self.block(k), self.land.at[pl.ds((k - 1) * rows, rows)], 2 * k)

    def second(self):
        if self.nf != 8:
            return
        base, rows, cut = self.chips, self.rows, self.cut
        self.got[base].wait_recv()
        to_y = self.block(2, 0, cut)
        self.add(to_y, [to_y, self.land.at[pl.ds(0, cut)]], cut)
        self.push(base + 3, self.block(2), self.land.at[pl.ds(2 * rows, rows)], 4)
        self.got[base + 1].wait_recv()
        to_x = self.block(1, cut)
        self.add(to_x, [to_x, self.land.at[pl.ds(cut, rows - cut)]], rows - cut)
        self.push(base + 2, self.block(1), self.land.at[pl.ds(rows, rows)], 2)

    def last(self, out):
        base, rows = self.chips, self.rows
        if self.nf == 8:
            incoming = [(base + 2, rows), (base + 3, 2 * rows)]
        else:
            incoming = [(base + k - 1, (k - 1) * rows) for k in range(1, self.chips)]
        for index, _ in incoming:
            self.got[index].wait_recv()
        parts = [self.block(0)] + [self.land.at[pl.ds(at, rows)] for _, at in incoming]
        self.add(out, parts, rows)

    def drain(self):
        for copy in self.sent:
            copy.wait_send()


def add_two(a, b, out):
    out[...] = (a[...].astype(F32) + b[...].astype(F32)).astype(BF)


def add_all(*refs):
    total = refs[0][...].astype(F32)
    for ref in refs[1:-1]:
        total = total + ref[...].astype(F32)
    refs[-1][...] = total.astype(BF)


class Reduce:
    def __init__(self, slots, rows, nz, z, me, send, recv, base, order):
        self.slots, self.rows, self.nz, self.z, self.me = slots, rows, nz, z, me
        self.send, self.recv, self.base, self.order = send, recv, base, order

    @staticmethod
    def sems(nz):
        return nz + 1

    def copy(self, src, dst, step):
        return remote(
            rows_at(self.slots, src, self.rows), rows_at(self.slots, dst, self.rows),
            self.send.at[self.base + src], self.recv.at[self.base + dst], self.z + step, self.me,
        )

    def give(self, i, part):
        z, nz, rows = self.z, self.nz, self.rows
        j = self.order(nz - 1 - i)
        below, above = j > z, j < z
        got = jnp.logical_or(jnp.logical_and(below, z > 0), jnp.logical_and(above, z < nz - 1))
        where = pl.ds(at128(j, rows) if rows % 128 == 0 else pl.multiple_of(j * rows, 16), rows)
        own = part(j)

        @pl.when(got)
        def _():
            self.copy(j, j, 0).wait_recv()
            self.slots[where, :] = (self.slots[where, :].astype(F32) + own.astype(F32)).astype(BF)

        @pl.when(jnp.logical_not(got))
        def _():
            self.slots[where, :] = own.astype(BF)

        @pl.when(below)
        def _():
            self.copy(j, j, 1).start()

        @pl.when(above)
        def _():
            self.copy(j, jnp.where(z - 1 == j, nz, j), -1).start()

    def take(self, total):
        z, nz = self.z, self.nz

        @pl.when(z > 0)
        def _():
            self.copy(z, z, 0).wait_recv()
            total[...] += rows_at(self.slots, z, self.rows)[...].astype(F32)

        @pl.when(z < nz - 1)
        def _():
            self.copy(z, nz, 0).wait_recv()
            total[...] += rows_at(self.slots, nz, self.rows)[...].astype(F32)

    def drain(self):
        def gave(i):
            j = self.order(i + 1)
            self.copy(j, j, 0).wait_send()

        loop(self.nz - 1, gave)


def back_kernel(
    dims,
    dwgu, dwd, dpart, wq_all, wo_all, kv_hbm, mid_hbm, dx_hbm,
    x_ref, g_ref, q_ref, o_ref, lse_ref, gain_ref, cos_ref, sin_ref, qpos_ref, kpos_ref,
    hid_ref, gh_ref, all_d, all_g, all_u, z_out, tiny_out,
    r0, r1, r2, l0, l1, l2,
    stage, full, dslots, part, do_ref, kv, dkv, kslots, m32, dh, t32, dqkv, mask, normed,
    r3, l3, r4, l4, zsrc, zslots, zfull, zown, tiny, tin, zin, send, recv, local,
):
    nz, nf, rows, d, wide, upad, nb, ng, ch = dims
    z, me = lax.axis_index("ctx"), lax.axis_index("fsdp")
    q_width, k_width = HEADS * HEAD_DIM, KV_HEADS * HEAD_DIM
    qkv = q_width + 2 * k_width
    scale = HEAD_DIM ** (-0.5)
    wr = d // nf
    place = {"nf": nf, "z": z, "me": me, "send": send, "recv": recv}
    per = Scatter.sems(nf)
    s_d = Scatter(dwd, 0, upad, d, r0, l0, False, base=0, **place)
    s_g = Scatter(dwgu, 0, wr, wide, r1, l1, False, base=per, **place)
    s_u = Scatter(dwgu, wide, wr, wide, r2, l2, False, base=2 * per, **place)
    s_o = Scatter(full, 0, wr, d, r3, l3, True, base=3 * per, **place)
    s_q = Scatter(full, 0, wr, qkv, r4, l4, True, base=4 * per, **place)
    base = 5 * per
    line = {"nz": nz, "z": z, "me": me, "send": send, "recv": recv}
    per = Chain.sems(nz)
    a_d = Chain(all_d, upad, base=base, **line)
    a_g = Chain(all_g, wr, base=base + per, **line)
    a_u = Chain(all_u, wr, base=base + 2 * per, **line)
    a_z = Chain(zfull, ch, base=base + 3 * per, **line)
    base += 4 * per
    per = Reduce.sems(nz)
    d_kv = Reduce(kslots, rows, base=base, order=a_d.order, **line)
    d_h = Reduce(dslots, rows, base=base + per, order=a_d.order, **line)
    d_z = Reduce(zslots, ch, base=base + 2 * per, order=a_d.order, **line)
    base += 3 * per

    def fetch(src, dst, i):
        copy = pltpu.make_async_copy(src, dst, local.at[i])
        copy.start()
        return copy

    wo_in = fetch(wo_all, stage.at[pl.ds(0, q_width), pl.ds(0, d)], 0)
    mid_in = fetch(mid_hbm, m32, 1)
    dx_in = fetch(dx_hbm, dh, 2)
    kv_in = fetch(kv_hbm, kv, 3)

    barrier = pltpu.get_barrier_semaphore()
    for k in range(1, nf):
        pl.semaphore_signal(barrier, inc=1, device_id=(z, me ^ k), device_id_type=MESH)
    for k in range(1, nz):
        pl.semaphore_signal(barrier, inc=1, device_id=((z + k) % nz, me), device_id_type=MESH)
    pl.semaphore_wait(barrier, nf + nz - 2)

    s_d.swap()
    mask[...] = jnp.where(kpos_ref[...] <= qpos_ref[...], 0.0, MASKED)
    dkv[...] = jnp.zeros_like(dkv)
    mid_in.wait()
    dx_in.wait()

    mid, dxn = m32[...], dh[...]
    inverse_two = lax.rsqrt(jnp.mean(mid * mid, -1, keepdims=True) + EPSILON)
    scaled = gain_ref[1:2, :] * dxn
    gain_two = jnp.sum(dxn * mid * inverse_two, 0, keepdims=True)
    dh[...] = (
        g_ref[...].astype(F32)
        + inverse_two * scaled
        - mid
        * (inverse_two * inverse_two * inverse_two)
        * jnp.mean(scaled * mid, -1, keepdims=True)
    )
    da = dh[...].astype(BF)
    normed[...] = da
    wo_in.wait()

    def do_tile(t):
        c0 = at128(t, 512)
        do_ref[:, pl.ds(c0, 512)] = dot_bt(
            normed[...], stage[pl.ds(c0, 512), pl.ds(0, d)]
        ).astype(BF)

    loop(q_width // 512, do_tile)
    kv_in.wait()
    s_d.merge()
    s_d.first()
    s_g.swap()

    def w_out_grad(t):
        c0 = at128(t, 512)
        full[pl.ds(0, q_width), pl.ds(c0, 512)] = dot_at(
            o_ref[...], normed[:, pl.ds(c0, 512)]
        ).astype(BF)

    loop(d // 512, w_out_grad)
    lanes = lax.broadcasted_iota(jnp.int32, (rows, HEAD_DIM), 1)

    def head(h):
        c0 = at128(h, HEAD_DIM)
        kc = at128(h // (HEADS // KV_HEADS), HEAD_DIM)
        vc = pl.multiple_of(kc + k_width, HEAD_DIM)
        q, k, v = q_ref[:, pl.ds(c0, HEAD_DIM)], kv[:, pl.ds(kc, HEAD_DIM)], kv[:, pl.ds(vc, HEAD_DIM)]
        do = do_ref[:, pl.ds(c0, HEAD_DIM)]
        lse = jnp.sum(jnp.where(lanes == h, lse_ref[...], 0.0), -1, keepdims=True)
        delta = jnp.sum(
            do.astype(F32) * o_ref[:, pl.ds(c0, HEAD_DIM)].astype(F32), -1, keepdims=True
        )
        p = jnp.exp(dot_bt(q, k) * scale + mask[...] - lse)
        dkv[:, pl.ds(vc, HEAD_DIM)] += dot_at(p.astype(BF), do)
        ds = (p * (dot_bt(do, v) - delta)).astype(BF)
        dq = dot(ds, k) * scale
        dkv[:, pl.ds(kc, HEAD_DIM)] += dot_at(ds, q) * scale
        dqkv[:, pl.ds(c0, HEAD_DIM)] = turn(dq, cos_ref[...], -sin_ref[...]).astype(BF)

    third = HEADS // 3
    loop(third, head)
    s_d.second()
    s_g.merge()
    s_g.first()
    s_u.swap()
    loop(third, lambda h: head(h + third))
    s_d.last(rows_at(all_d, z, upad))
    a_d.begin()
    s_g.second()
    s_u.merge()
    s_u.first()
    s_o.swap()
    loop(third, lambda h: head(h + 2 * third))

    def kv_part(j):
        return dkv[pl.ds(at128(j, rows), rows), :]

    for i in range(nz - 1):
        d_kv.give(i, kv_part)
        if i == 0:
            s_o.merge()
            s_o.first()
            s_g.last(rows_at(all_g, z, wr))
            a_g.begin()
            s_u.second()
            a_d.forward(1)
    mine = dkv.at[pl.ds(at128(z, rows), rows)]
    d_kv.take(mine)
    for h in range(KV_HEADS):
        c0 = h * HEAD_DIM
        dqkv[:, q_width + c0 : q_width + c0 + HEAD_DIM] = turn(
            mine[:, c0 : c0 + HEAD_DIM], cos_ref[...], -sin_ref[...]
        ).astype(BF)
    dqkv[:, q_width + k_width :] = mine[:, k_width:].astype(BF)
    for k in range(2, nz - 1):
        a_d.forward(k)
    s_o.second()
    s_u.last(rows_at(all_u, z, wr))
    a_u.begin()
    wq_in = fetch(wq_all, stage.at[pl.ds(0, d)], 0)
    x = x_ref[...].astype(F32)
    inverse = lax.rsqrt(jnp.mean(x * x, -1, keepdims=True) + EPSILON)
    normed[...] = (x * inverse * gain_ref[0:1, :]).astype(BF)
    s_o.last(zsrc.at[pl.ds(0, wr), pl.ds(0, d)])
    s_o.drain()

    def w_qkv_grad(t):
        c0 = at128(t, 512)
        full[pl.ds(0, d), pl.ds(c0, 512)] = dot_at(normed[...], dqkv[:, pl.ds(c0, 512)]).astype(BF)

    loop(qkv // 512, w_qkv_grad)
    s_q.swap()
    wq_in.wait()
    for k in range(1, nz - 1):
        a_g.forward(k)
    a_d.forward(nz - 1)

    def dxn_tile(t):
        c0 = at128(t, 512)
        t32[:, pl.ds(c0, 512)] = dot_bt(dqkv[...], stage[pl.ds(c0, 512), :])

    loop(d // 512, dxn_tile)
    dxn = t32[...]
    scaled = gain_ref[0:1, :] * dxn
    gain_one = jnp.sum(dxn * x * inverse, 0, keepdims=True)
    bias = jnp.sum(dqkv[...].astype(F32), 0, keepdims=True)
    gh_ref[...] = (
        dh[...]
        + inverse * scaled
        - x * (inverse * inverse * inverse) * jnp.mean(scaled * x, -1, keepdims=True)
    ).astype(BF)

    cut = q_width + k_width
    qk, vb = cut // nf, k_width // nf
    tiny[...] = jnp.zeros_like(tiny)
    for f in range(nf):
        r = slice(8 * f, 8 * f + 1)
        tiny[r, 0:qk] = bias[:, f * qk : (f + 1) * qk]
        tiny[r, qk : qk + vb] = bias[:, cut + f * vb : cut + (f + 1) * vb]
        tiny[r, qk + vb : qk + vb + ng] = gain_one[:, f * ng : (f + 1) * ng]
        tiny[r, qk + vb + ng : qk + vb + 2 * ng] = gain_two[:, f * ng : (f + 1) * ng]
    tin[pl.ds(pl.multiple_of(me * 8, 8), 8), :] = tiny[pl.ds(pl.multiple_of(me * 8, 8), 8), :]
    tiny_copies = []
    for k in range(1, nf):
        copy = remote(
            rows_at(tiny, me ^ k, 8), rows_at(tin, me, 8), send.at[base + k], recv.at[base + k], z, me ^ k
        )
        copy.start()
        tiny_copies.append(copy)
    base += nf

    s_q.merge()
    s_q.first()
    for copy in tiny_copies:
        copy.wait_recv()
    total = tin[0:8, :]
    for f in range(1, nf):
        total = total + tin[8 * f : 8 * f + 8, :]
    zin[pl.ds(pl.multiple_of(z * 8, 8), 8), :] = total
    for k in range(1, nz):
        copy = remote(
            rows_at(zin, z, 8), rows_at(zin, z, 8), send.at[base + k], recv.at[base + k], (z + k) % nz, me
        )
        copy.start()
        tiny_copies.append(copy)

    def down_part(j):
        copy = pltpu.make_async_copy(rows_at(dpart, j, rows), part, local.at[1])
        copy.start()
        copy.wait()
        return part[...]

    for i in range(nz - 1):
        d_h.give(i, down_part)
        if i == 0:
            s_q.second()
        if i == 1:
            for k in range(1, nz - 1):
                a_u.forward(k)
    s_q.last(zsrc.at[pl.ds(0, wr), pl.ds(d, qkv)])

    def z_part(j):
        return zsrc[pl.ds(pl.multiple_of(j * ch, 16), ch), :]

    for i in range(nz - 1):
        d_z.give(i, z_part)
    zown[...] = z_part(z).astype(F32)
    d_z.take(zown)
    zfull[pl.ds(pl.multiple_of(z * ch, 16), ch), :] = zown[...].astype(BF)
    a_z.begin()
    for k in range(1, nz):
        a_z.forward(k)
        a_z.arrive(k)
    z_put = fetch(zfull, z_out, 2)
    m32[...] += down_part(z).astype(F32)
    d_h.take(m32)
    hid_ref[...] = m32[...].astype(BF)
    for copy in tiny_copies[nf - 1 :]:
        copy.wait_recv()
    total = zin[0:8, :]
    for j in range(1, nz):
        total = total + zin[8 * j : 8 * j + 8, :]
    tiny_out[...] = total
    a_g.forward(nz - 1)
    a_u.forward(nz - 1)
    for chain in (a_d, a_g, a_u):
        for k in range(1, nz):
            chain.arrive(k)
    for item in (s_d, s_g, s_u, s_q, a_d, a_g, a_u, a_z, d_kv, d_h, d_z):
        item.drain()
    for copy in tiny_copies:
        copy.wait_send()
    z_put.wait()


def back(dims, *args):
    nz, nf, rows, d, wide, upad, nb, ng, ch = dims
    q_width, k_width = HEADS * HEAD_DIM, KV_HEADS * HEAD_DIM
    qkv = q_width + 2 * k_width
    tokens, chips, wr = nz * rows, nf // 2, d // nf
    tiny = -(-((qkv + 2 * d) // nf) // 128) * 128
    any_, vm = pl.BlockSpec(memory_space=pl.ANY), pl.BlockSpec(memory_space=pltpu.VMEM)
    out = jax.ShapeDtypeStruct
    sems = 5 * Scatter.sems(nf) + 4 * Chain.sems(nz) + 3 * Reduce.sems(nz) + nf + nz
    pieces = [(upad, d), (wr, wide), (wr, wide)]
    return pl.pallas_call(
        functools.partial(back_kernel, dims),
        in_specs=[any_] * 8 + [vm] * 10,
        out_specs=[vm, vm] + [any_] * 4 + [vm] + [any_] * 6,
        out_shape=[out((rows, d), BF), out((rows, d), BF)]
        + [out((nz * r, c), BF) for r, c in pieces]
        + [out((nz * ch, d + qkv), BF), out((8, tiny), F32)]
        + [out((chips * r, c), BF) for r, c in pieces]
        + [out(((chips - 1) * r, c), BF) for r, c in pieces],
        scratch_shapes=[
            pltpu.VMEM((d, qkv), BF),
            pltpu.VMEM((d, qkv), BF),
            pltpu.VMEM(((nz + 1) * rows, d), BF),
            pltpu.VMEM((rows, d), BF),
            pltpu.VMEM((rows, q_width), BF),
            pltpu.VMEM((tokens, 2 * k_width), BF),
            pltpu.VMEM((tokens, 2 * k_width), F32),
            pltpu.VMEM(((nz + 1) * rows, 2 * k_width), BF),
            pltpu.VMEM((rows, d), F32),
            pltpu.VMEM((rows, d), F32),
            pltpu.VMEM((rows, d), F32),
            pltpu.VMEM((rows, qkv), BF),
            pltpu.VMEM((rows, tokens), F32),
            pltpu.VMEM((rows, d), BF),
            pltpu.VMEM((chips * wr, d), BF),
            pltpu.VMEM(((chips - 1) * wr, d), BF),
            pltpu.VMEM((chips * wr, qkv), BF),
            pltpu.VMEM(((chips - 1) * wr, qkv), BF),
            pltpu.VMEM((nz * ch, d + qkv), BF),
            pltpu.VMEM(((nz + 1) * ch, d + qkv), BF),
            pltpu.VMEM((nz * ch, d + qkv), BF),
            pltpu.VMEM((ch, d + qkv), F32),
            pltpu.VMEM((nf * 8, tiny), F32),
            pltpu.VMEM((nf * 8, tiny), F32),
            pltpu.VMEM((nz * 8, tiny), F32),
            pltpu.SemaphoreType.DMA((sems,)),
            pltpu.SemaphoreType.DMA((sems,)),
            pltpu.SemaphoreType.DMA((4,)),
        ],
        compiler_params=pltpu.CompilerParams(
            collective_id=1, has_side_effects=True, vmem_limit_bytes=VMEM_LIMIT
        ),
    )(*args)


def shards(
    hidden_in, w_qkv, b_qkv, w_out, w_gate_up, w_down, gain_attn, gain_mlp, block_order, cotangent
):
    nz, nf = lax.axis_size("ctx"), lax.axis_size("fsdp")
    z, me = lax.axis_index("ctx"), lax.axis_index("fsdp")
    q_width, k_width = HEADS * HEAD_DIM, KV_HEADS * HEAD_DIM
    rows = hidden_in.shape[1]
    piece_len = rows // 2
    ff = w_gate_up.shape[1] // 2
    unit = ff // (nf * nz)
    order_row = block_order[0]
    all_places = (
        order_row[:, None] * piece_len + jnp.arange(piece_len, dtype=jnp.int32)[None, :]
    ).reshape(-1)
    my_places = lax.dynamic_slice_in_dim(all_places, z * rows, rows)
    cosine, sine_table = angle_tables(my_places)
    cos2 = jnp.concatenate([cosine, cosine], 1)
    sin2 = jnp.concatenate([-sine_table, sine_table], 1)

    packed = pack(w_gate_up, nz, nf, z)
    wide = packed.shape[1] // 2
    upad = wide // nf
    down_mine = jnp.pad(
        lax.dynamic_slice_in_dim(w_down, z * unit, unit), ((0, upad - unit), (0, 0))
    )
    nb, ng = b_qkv.shape[0], gain_attn.shape[0]
    d = hidden_in.shape[2]
    small = jnp.concatenate([b_qkv, gain_attn, gain_mlp])
    small = jnp.pad(small[None], ((0, 15), (0, -small.shape[0] % 128)))
    grad_low = cotangent[0]
    (whole_qkv, whole_out, q_low, kv_all, attn_low, lse, middle, grad_normed_two, gains, gate_up_local, down_local,
     down_part) = front(
        (nz, nf, rows, d, wide, upad, nb, ng),
        w_qkv, small, w_out, packed, down_mine, hidden_in[0], grad_low, cos2, sin2,
        my_places[:, None], all_places[None, :],
    )
    ch = -(-(d // (nf * nz)) // 16) * 16
    hidden, grad_hidden, down_all, gate_all, up_all, attn_all, tiny = back(
        (nz, nf, rows, d, wide, upad, nb, ng, ch),
        gate_up_local, down_local, down_part, whole_qkv, whole_out, kv_all, middle, grad_normed_two,
        hidden_in[0], grad_low, q_low, attn_low, lse, gains, cos2, sin2, my_places[:, None], all_places[None, :],
    )[:7]
    e1 = (q_width + k_width) // nf
    e2 = e1 + k_width // nf
    e3 = e2 + ng
    shard = d // nf
    return (
        hidden[None],
        grad_hidden[None],
        attn_all[:shard, d:].astype(F32),
        tiny[0, :e1],
        tiny[0, e1:e2],
        attn_all[:shard, :d].astype(F32),
        unpack(gate_all, up_all, nz, nf, ff),
        down_all.reshape(nz, upad, d)[:, :unit].reshape(nz * unit, d).astype(F32),
        tiny[0, e2:e3],
        tiny[0, e3 : e3 + ng],
    )


def solution(mesh):
    placed = (
        P("fsdp", "ctx", None),
        P("fsdp", None),
        P("fsdp"),
        P("fsdp", None),
        P("fsdp", None),
        P("fsdp", None),
        P("fsdp"),
        P("fsdp"),
        P("fsdp", None),
        P("fsdp", "ctx", None),
    )
    return jax.shard_map(
        shards,
        mesh=mesh,
        in_specs=placed,
        out_specs=(
            P("fsdp", "ctx", None),
            P("fsdp", "ctx", None),
            P("fsdp", None),
            P("fsdp"),
            P("fsdp"),
            P("fsdp", None),
            P("fsdp", None),
            P("fsdp", None),
            P("fsdp"),
            P("fsdp"),
        ),
        check_vma=False,
    )
```

```python
import functools

import jax
import jax.numpy as jnp
from jax import lax
from jax.experimental import pallas as pl
from jax.experimental.pallas import tpu as pltpu
from jax.sharding import PartitionSpec as P

HEADS = 12
KV_HEADS = 2
HEAD_DIM = 128
EPSILON = 1e-06
THETA = 1000000.0
MASKED = -1e30
BF = jnp.bfloat16
F32 = jnp.float32


def dot(a, b):
    return jnp.dot(a, b, preferred_element_type=F32)


def dot_bt(a, b):
    return lax.dot_general(a, b, (((1,), (1,)), ((), ())), preferred_element_type=F32)


def dot_at(a, b):
    return lax.dot_general(a, b, (((0,), (0,)), ((), ())), preferred_element_type=F32)


def angle_tables(places):
    half_dim = HEAD_DIM // 2
    freqs = THETA ** (-(jnp.arange(half_dim).astype(F32) * 2.0 / HEAD_DIM))
    angles = places.astype(F32)[:, None] * freqs[None, :]
    return (jnp.cos(angles), jnp.sin(angles))


def half_rows(rows):
    return -(-rows // 32) * 16


def pack_kernel(nz, nf, ff, unit, upad, z_ref, w_ref, out_ref):
    for k in range(nz):

        @pl.when(z_ref[0] == k)
        def _():
            for h in range(2):
                for f in range(nf):
                    src = h * ff + f * (ff // nf) + k * unit
                    dst = (h * nf + f) * upad
                    out_ref[:, dst : dst + unit] = w_ref[:, src : src + unit]
                    out_ref[:, dst + unit : dst + upad] = jnp.zeros(
                        (out_ref.shape[0], upad - unit), out_ref.dtype
                    )


def pack(w, nz, nf, z):
    rows, ff = w.shape[0], w.shape[1] // 2
    unit = ff // (nf * nz)
    upad = -(-unit // 16) * 16
    wide = nf * upad
    step = 32
    return pl.pallas_call(
        functools.partial(pack_kernel, nz, nf, ff, unit, upad),
        grid=(rows // step,),
        in_specs=[
            pl.BlockSpec(memory_space=pltpu.SMEM),
            pl.BlockSpec((step, 2 * ff), lambda i: (i, 0)),
        ],
        out_specs=pl.BlockSpec((step, 2 * wide), lambda i: (i, 0)),
        out_shape=jax.ShapeDtypeStruct((rows, 2 * wide), w.dtype),
    )(z.reshape(1).astype(jnp.int32), w)


def unpack_kernel(nz, nf, ff, unit, upad, *refs):
    out_ref = refs[-1]
    for k in range(nz):
        for h in range(2):
            for f in range(nf):
                src = f * upad
                dst = h * ff + f * (ff // nf) + k * unit
                part = refs[h * nz + k]
                out_ref[:, dst : dst + unit] = part[:, src : src + unit].astype(F32)


def unpack(gate, up, nz, nf, ff):
    rows, wide = gate.shape[0] // nz, gate.shape[1]
    step = 32
    specs = [
        pl.BlockSpec((step, wide), lambda i, k=k: (k * (rows // step) + i, 0)) for k in range(nz)
    ]
    return pl.pallas_call(
        functools.partial(unpack_kernel, nz, nf, ff, ff // (nf * nz), wide // nf),
        grid=(rows // step,),
        in_specs=specs * 2,
        out_specs=pl.BlockSpec((step, 2 * ff), lambda i: (i, 0)),
        out_shape=jax.ShapeDtypeStruct((rows, 2 * ff), F32),
    )(*[gate] * nz, *[up] * nz)


MESH = pl.DeviceIdType.MESH
VMEM_LIMIT = 63 * 2**20


def remote(src, dst, send, recv, z, f):
    return pltpu.make_async_remote_copy(
        src_ref=src, dst_ref=dst, send_sem=send, recv_sem=recv, device_id=(z, f), device_id_type=MESH
    )


def rows_at(ref, index, count):
    return ref.at[pl.ds(pl.multiple_of(index * count, count), count)]


class PlaneGather:
    def __init__(self, src, dst, rows, nf, z, me, send, recv, local, base):
        self.src, self.dst, self.rows, self.nf, self.z, self.me = src, dst, rows, nf, z, me
        self.send, self.recv, self.base = send, recv, base
        self.local = pltpu.make_async_copy(src, rows_at(dst, me, rows), local)
        self.sent = []
        self.cut = half_rows(rows)
        self.swaps = {}

    @staticmethod
    def sems(nf):
        return 2 * nf

    def slot(self, k, lo=0, hi=None):
        hi = self.rows if hi is None else hi
        start = pl.multiple_of((self.me ^ k) * self.rows, 16) + lo
        return self.dst.at[pl.ds(pl.multiple_of(start, 16), hi - lo)]

    def push(self, index, src, dst, flip_by):
        copy = remote(
            src, dst, self.send.at[self.base + index], self.recv.at[self.base + index],
            self.z, self.me ^ flip_by,
        )
        copy.start()
        self.sent.append(copy)
        return copy

    def begin(self):
        self.local.start()
        self.direct = {}
        for k in (2, 4) if self.nf == 8 else range(2, self.nf, 2):
            self.direct[k] = self.push(k, self.src, self.slot(0), k)
        self.swaps[0] = self.push(1, self.src, self.slot(0), 1)

    def swap(self, k):
        self.swaps[k] = self.push(k + 1, self.slot(k), self.slot(k), 1)

    def middle(self):
        for k, copy in self.direct.items():
            copy.wait_recv()
            if self.nf == 8:
                if k == 2:
                    self.far_a = self.push(6, self.slot(2, 0, self.cut), self.slot(2, 0, self.cut), 4)
                elif self.cut < self.rows:
                    self.far_b = self.push(
                        8, self.slot(4, self.cut), self.slot(4, self.cut), 2
                    )
            self.swap(k)

    def late(self):
        if self.nf == 8:
            self.far_a.wait_recv()
            if self.cut < self.rows:
                self.far_b.wait_recv()
            self.swap(6)

    def finish(self):
        self.local.wait()
        for copy in self.swaps.values():
            copy.wait_recv()

    def drain(self):
        for copy in self.sent:
            copy.wait_send()


class Chain:
    def __init__(self, buf, rows, nz, z, me, send, recv, base):
        self.buf, self.rows, self.nz, self.z, self.me = buf, rows, nz, z, me
        self.send, self.recv, self.base = send, recv, base

    @staticmethod
    def sems(nz):
        return nz + 2

    def copy(self, j, sem, step):
        slot = rows_at(self.buf, j, self.rows)
        return remote(
            slot, slot, self.send.at[self.base + sem], self.recv.at[self.base + j], self.z + step, self.me
        )

    def order(self, k):
        z, nz = self.z, self.nz
        below, above = z, nz - 1 - z
        m = jnp.minimum(below, above)
        near = jnp.where(k % 2 == 1, z - (k + 1) // 2, z + k // 2)
        far = jnp.where(above > below, z + (k - m), z - (k - m))
        return jnp.where(k <= 2 * m, near, far)

    def begin(self):
        z, nz = self.z, self.nz

        @pl.when(z < nz - 1)
        def _():
            self.copy(z, nz, 1).start()

        @pl.when(z > 0)
        def _():
            self.copy(z, nz + 1, -1).start()

    def passing(self, j):
        z, nz = self.z, self.nz
        return jnp.logical_and(j < z, z < nz - 1), jnp.logical_and(j > z, z > 0)

    def forward(self, k):
        j = self.order(k)
        up, down = self.passing(j)

        @pl.when(up)
        def _():
            self.copy(j, j, 1).wait_recv()
            self.copy(j, j, 1).start()

        @pl.when(down)
        def _():
            self.copy(j, j, -1).wait_recv()
            self.copy(j, j, -1).start()

    def arrive(self, k):
        j = self.order(k)
        up, down = self.passing(j)

        @pl.when(jnp.logical_not(jnp.logical_or(up, down)))
        def _():
            self.copy(j, j, 0).wait_recv()

    def drain(self):
        z, nz = self.z, self.nz

        @pl.when(z < nz - 1)
        def _():
            self.copy(z, nz, 1).wait_send()

        @pl.when(z > 0)
        def _():
            self.copy(z, nz + 1, -1).wait_send()

        def one(k, carry):
            j = self.order(k)
            up, down = self.passing(j)

            @pl.when(jnp.logical_or(up, down))
            def _():
                self.copy(j, j, 0).wait_send()

            return carry

        lax.fori_loop(1, nz, one, 0)


class Scatter:
    def __init__(self, src, c0, rows, cols, recv4, land, inside, nf, z, me, send, recv, base, own=None, sems=None):
        self.src, self.c0, self.rows, self.cols = src, c0, rows, cols
        self.recv4, self.land, self.inside = recv4, land, inside
        self.nf, self.z, self.me, self.send, self.recv, self.base = nf, z, me, send, recv, base
        self.chips, self.chip, self.core = nf // 2, me // 2, me % 2
        self.cut = half_rows(rows)
        self.sent = []
        self.got = {}
        self.own, self.own_sems = own, sems

    @staticmethod
    def sems(nf):
        return nf

    def push(self, index, src, dst, flip_by):
        copy = remote(
            src, dst, self.send.at[self.base + index], self.recv.at[self.base + index],
            self.z, self.me ^ flip_by,
        )
        copy.start()
        self.sent.append(copy)
        self.got[index] = copy

    def mine(self, ref, start, n):
        return ref.at[pl.ds(pl.multiple_of(start, 16), n)]

    def block(self, k, lo=0, hi=None):
        hi = self.rows if hi is None else hi
        return self.mine(self.recv4, (self.chip ^ k) * self.rows + lo, hi - lo)

    def swap(self):
        for p in range(self.chips):
            start = pl.multiple_of((2 * p + 1 - self.core) * self.rows, 16)
            src = self.src.at[pl.ds(start, self.rows), pl.ds(self.c0, self.cols)]
            self.push(p, src, self.mine(self.recv4, p * self.rows, self.rows), 1)

    def merge(self):
        rows, cols = self.rows, self.cols
        if self.own is not None:
            for p in range(min(2, self.chips)):
                self.fetch(p).start()
        for p in range(self.chips):
            self.got[p].wait_recv()
        if self.inside:
            for p in range(self.chips):
                start = pl.multiple_of((2 * p + self.core) * rows, 16)
                if self.own is None:
                    own, first = self.src, start
                else:
                    self.fetch(p).wait()
                    own, first = self.own, p % 2 * rows
                step = rows if rows <= 96 else rows // 2
                for i in range(0, rows, step):
                    where = pl.ds(p * rows + i, step)
                    part = own[pl.ds(pl.multiple_of(first + i, 16), step), pl.ds(0, cols)]
                    self.recv4[where, :] = (
                        self.recv4[where, :].astype(F32) + part.astype(F32)
                    ).astype(BF)
                if self.own is not None and p + 2 < self.chips:
                    self.fetch(p + 2).start()
            return
        step = rows if rows <= 96 else rows // 2
        n = rows // step
        core, col = self.core, self.c0 // cols
        own = pl.BlockSpec((step, cols), lambda p, i: ((2 * p + core) * n + i, col))
        held = pl.BlockSpec((step, cols), lambda p, i: (p * n + i, 0))
        pltpu.emit_pipeline(
            add_two, grid=(self.chips, n), in_specs=[own, held], out_specs=[held]
        )(self.src, self.recv4, self.recv4)

    def fetch(self, p):
        start = pl.multiple_of((2 * p + self.core) * self.rows, 16)
        return pltpu.make_async_copy(
            self.src.at[pl.ds(start, self.rows), pl.ds(self.c0, self.cols)],
            self.own.at[pl.ds(p % 2 * self.rows, self.rows)],
            self.own_sems.at[p % 2],
        )

    def add(self, out, parts, n):
        if self.inside:
            total = parts[0][...].astype(F32)
            for part in parts[1:]:
                total = total + part[...].astype(F32)
            out[...] = total.astype(BF)
            return
        step = n if n <= 96 else n // 2
        spec = pl.BlockSpec((step, self.cols), lambda i: (i, 0))
        body = add_two if len(parts) == 2 else add_all
        pltpu.emit_pipeline(
            body, grid=(n // step,), in_specs=[spec] * len(parts), out_specs=[spec]
        )(*parts, out)

    def first(self):
        base, rows, cut = self.chips, self.rows, self.cut
        if self.nf == 8:
            self.push(base, self.block(3, 0, cut), self.land.at[pl.ds(0, cut)], 2)
            self.push(base + 1, self.block(3, cut), self.land.at[pl.ds(cut, rows - cut)], 4)
        else:
            for k in range(1, self.chips):
                self.push(base + k - 1, self.block(k), self.land.at[pl.ds((k - 1) * rows, rows)], 2 * k)

    def second(self):
        if self.nf != 8:
            return
        base, rows, cut = self.chips, self.rows, self.cut
        self.got[base].wait_recv()
        to_y = self.block(2, 0, cut)
        self.add(to_y, [to_y, self.land.at[pl.ds(0, cut)]], cut)
        self.push(base + 3, self.block(2), self.land.at[pl.ds(2 * rows, rows)], 4)
        self.got[base + 1].wait_recv()
        to_x = self.block(1, cut)
        self.add(to_x, [to_x, self.land.at[pl.ds(cut, rows - cut)]], rows - cut)
        self.push(base + 2, self.block(1), self.land.at[pl.ds(rows, rows)], 2)

    def last(self, out):
        base, rows = self.chips, self.rows
        if self.nf == 8:
            incoming = [(base + 2, rows), (base + 3, 2 * rows)]
        else:
            incoming = [(base + k - 1, (k - 1) * rows) for k in range(1, self.chips)]
        for index, _ in incoming:
            self.got[index].wait_recv()
        parts = [self.block(0)] + [self.land.at[pl.ds(at, rows)] for _, at in incoming]
        self.add(out, parts, rows)

    def drain(self):
        for copy in self.sent:
            copy.wait_send()
        self.sent = []


def add_two(a, b, out):
    out[...] = (a[...].astype(F32) + b[...].astype(F32)).astype(BF)


def add_all(*refs):
    total = refs[0][...].astype(F32)
    for ref in refs[1:-1]:
        total = total + ref[...].astype(F32)
    refs[-1][...] = total.astype(BF)


def greet_ctx_and_plane(nz, nf, z, me):
    barrier = pltpu.get_barrier_semaphore()
    flips = (1, 2, 4) if nf == 8 else (1,) + tuple(range(2, nf, 2))
    for k in flips:
        pl.semaphore_signal(barrier, inc=1, device_id=(z, me ^ k), device_id_type=MESH)

    @pl.when(z < nz - 1)
    def _():
        pl.semaphore_signal(barrier, inc=1, device_id=(z + 1, me), device_id_type=MESH)

    @pl.when(z > 0)
    def _():
        pl.semaphore_signal(barrier, inc=1, device_id=(z - 1, me), device_id_type=MESH)

    inner = jnp.logical_and(z > 0, z < nz - 1)

    @pl.when(inner)
    def _():
        pl.semaphore_wait(barrier, len(flips) + 2)

    @pl.when(jnp.logical_not(inner))
    def _():
        pl.semaphore_wait(barrier, len(flips) + 1)


def loop(n, body):
    def step(i, carry):
        body(i)
        return carry

    lax.fori_loop(0, n, step, 0)


def at128(i, n):
    return i * n if isinstance(i, int) else pl.multiple_of(i * n, n)


def turn(t, cos2, sin2):
    return t * cos2 + pltpu.roll(t, HEAD_DIM // 2, 1) * sin2


def front_kernel(
    dims,
    wq, sm, wo, wp, dn, x_ref, g_ref, cos_ref, sin_ref, qpos_ref, kpos_ref,
    wq_all, wo_all, q_ref, kv_out, o_ref, lse_ref, mid_ref, dx_ref, gain_ref, dwgu, dpart, d_own, dwd, r0, l0,
    stage, gu, dnb, g_all, x_all, act, dgu, smb, kv, bias, mask, ybuf, send, recv, local,
):
    nz, nf, rows, d, wide, upad, nb, ng = dims
    z, me = lax.axis_index("ctx"), lax.axis_index("fsdp")
    q_width, k_width = HEADS * HEAD_DIM, KV_HEADS * HEAD_DIM
    qkv = q_width + 2 * k_width
    scale = HEAD_DIM ** (-0.5)
    wr = d // nf
    per = PlaneGather.sems(nf)
    plane = [
        PlaneGather(src, dst, r, nf, z, me, send, recv, local.at[i], i * per)
        for i, (src, dst, r) in enumerate(
            [
                (wq.at[:, pl.ds(0, q_width)], wq_all.at[:, pl.ds(0, q_width)], wr),
                (wq.at[:, pl.ds(q_width, 2 * k_width)], wq_all.at[:, pl.ds(q_width, 2 * k_width)], wr),
                (sm, smb, 16),
                (wo, wo_all, wr),
                (wp, gu, wr),
                (dn, dnb, upad),
            ]
        )
    ]
    p_q, p_kv, p_s, p_o, p_gu, p_d = plane
    base = len(plane) * per
    chain = [
        Chain(buf, rows, nz, z, me, send, recv, base + i * Chain.sems(nz))
        for i, buf in enumerate([g_all, kv, x_all])
    ]
    c_g, c_kv, c_x = chain
    base += len(chain) * Chain.sems(nz)
    s_d = Scatter(dwd, 0, upad, d, r0, l0, False, nf, z, me, send, recv, base)
    base += Scatter.sems(nf)
    spare = len(plane)

    g_copy = pltpu.make_async_copy(g_ref, rows_at(g_all, z, rows), local.at[spare])
    g_copy.start()
    greet_ctx_and_plane(nz, nf, z, me)
    p_s.begin()
    p_kv.begin()
    g_copy.wait()
    c_g.begin()

    x = x_ref[...].astype(F32)
    inverse = lax.rsqrt(jnp.mean(x * x, -1, keepdims=True) + EPSILON)
    mask[...] = jnp.where(kpos_ref[...] <= qpos_ref[...], 0.0, MASKED)

    p_s.middle()
    p_kv.middle()
    p_q.begin()
    p_s.late()
    p_kv.late()
    p_s.finish()
    for f in range(nf):
        row = smb[f * 16 : (f + 1) * 16, :].astype(F32)[0:1]
        bias[0:1, f * nb : (f + 1) * nb] = row[:, :nb]
        gain_ref[0:1, f * ng : (f + 1) * ng] = row[:, nb : nb + ng]
        gain_ref[1:2, f * ng : (f + 1) * ng] = row[:, nb + ng : nb + 2 * ng]
    normed = (x * inverse * gain_ref[0:1, :]).astype(BF)
    x_all[pl.ds(at128(z, rows), rows), :] = normed

    def fetch_qkv(c0, n):
        copy = pltpu.make_async_copy(
            wq_all.at[:, pl.ds(c0, n)], stage.at[pl.ds(0, d), pl.ds(c0, n)], local.at[spare]
        )
        copy.start()
        copy.wait()

    p_kv.finish()
    fetch_qkv(q_width, 2 * k_width)

    def project(t):
        c0 = at128(t, 2 * HEAD_DIM)
        y = dot(
            x_all[pl.ds(at128(z, rows), rows), :], stage[pl.ds(0, d), pl.ds(c0, 2 * HEAD_DIM)]
        ) + bias[0:1, pl.ds(c0, 2 * HEAD_DIM)]
        return y, c0

    def project_v(t):
        y, c0 = project(t)
        kv[pl.ds(at128(z, rows), rows), pl.ds(pl.multiple_of(c0 - q_width, 256), 256)] = y.astype(BF)

    def turned(y):
        halves = [
            turn(y[:, h * HEAD_DIM : (h + 1) * HEAD_DIM], cos_ref[...], sin_ref[...]).astype(BF)
            for h in range(2)
        ]
        return jnp.concatenate(halves, 1)

    project_v((q_width + k_width) // 256)
    y, _ = project(q_width // 256)
    kv[pl.ds(at128(z, rows), rows), 0:k_width] = turned(y)
    c_kv.begin()
    p_q.middle()
    p_o.begin()
    for k in range(1, nz - 1):
        c_kv.forward(k)
    p_q.late()
    p_q.finish()
    fetch_qkv(0, q_width)
    c_kv.forward(nz - 1)

    def project_q(t):
        y, c0 = project(t)
        q_ref[:, pl.ds(c0, 256)] = turned(y)

    loop(q_width // 256, project_q)
    p_o.middle()
    p_gu.begin()
    for k in range(1, nz):
        c_kv.arrive(k)
    for k in range(1, nz - 1):
        c_g.forward(k)

    lanes = lax.broadcasted_iota(jnp.int32, (rows, HEAD_DIM), 1)
    lse_ref[...] = jnp.zeros_like(lse_ref)

    def head(h):
        c0 = at128(h, HEAD_DIM)
        kc = at128(h // (HEADS // KV_HEADS), HEAD_DIM)
        vc = pl.multiple_of(kc + k_width, HEAD_DIM)
        s = dot_bt(q_ref[:, pl.ds(c0, HEAD_DIM)], kv[:, pl.ds(kc, HEAD_DIM)]) * scale + mask[...]
        top = jnp.max(s, -1, keepdims=True)
        p = jnp.exp(s - top)
        total = jnp.sum(p, -1, keepdims=True)
        o = dot(p.astype(BF), kv[:, pl.ds(vc, HEAD_DIM)]) / total
        o_ref[:, pl.ds(c0, HEAD_DIM)] = o.astype(BF)
        lse_ref[...] = jnp.where(lanes == h, top + jnp.log(total), lse_ref[...])

    loop(HEADS, head)
    p_o.late()
    p_o.finish()
    fetch = pltpu.make_async_copy(wo_all, stage.at[pl.ds(0, q_width), pl.ds(0, d)], local.at[spare])
    fetch.start()
    fetch.wait()

    def out_proj(t):
        c0 = at128(t, 512)
        mid_ref[:, pl.ds(c0, 512)] = (
            dot(o_ref[...], stage[pl.ds(0, q_width), pl.ds(c0, 512)]) + x_ref[:, pl.ds(c0, 512)].astype(F32)
        )

    loop(d // 512, out_proj)
    mid = mid_ref[...]
    inverse_two = lax.rsqrt(jnp.mean(mid * mid, -1, keepdims=True) + EPSILON)
    x_all[pl.ds(at128(z, rows), rows), :] = (mid * inverse_two * gain_ref[1:2, :]).astype(BF)
    c_x.begin()
    c_g.forward(nz - 1)
    for k in range(1, nz - 1):
        c_x.forward(k)
    p_gu.middle()
    if nz <= 4:
        c_x.forward(nz - 1)
    p_gu.late()
    p_d.begin()
    p_gu.finish()

    cols = 768 if wide % 768 == 0 else 256

    def hidden(j):
        r0 = at128(j, rows)

        def one(t):
            c0 = at128(t, cols)
            xb = x_all[pl.ds(r0, rows), :]
            gate = dot(xb, gu[:, pl.ds(c0, cols)])
            up = dot(xb, gu[:, pl.ds(pl.multiple_of(wide + c0, 128), cols)])
            act[pl.ds(r0, rows), pl.ds(c0, cols)] = (gate * jax.nn.sigmoid(gate) * up).astype(BF)
            dgu[pl.ds(r0, rows), pl.ds(c0, cols)] = gate.astype(BF)
            dgu[pl.ds(r0, rows), pl.ds(pl.multiple_of(wide + c0, 128), cols)] = up.astype(BF)

        loop(wide // cols, one)

    hidden(z)
    if nz > 4:
        c_x.forward(nz - 1)

    def nearest(k):
        c_x.arrive(k)
        hidden(c_x.order(k))

    loop(nz - 2, lambda i: nearest(i + 1))
    p_d.middle()
    nearest(nz - 1)
    for k in range(1, nz):
        c_g.arrive(k)
    part = wide // 2
    tiles = [stage.at[pl.ds(0, part), pl.ds(d + i * 256, 256)] for i in range(2)]

    def put(t, i):
        c0 = at128(t, 256)
        return pltpu.make_async_copy(
            tiles[i], dwd.at[pl.ds(i * part, part), pl.ds(c0, 256)], local.at[spare + i]
        )

    def w_down_grad(t):
        for i in range(2):

            @pl.when(t > 0)
            def _():
                put(t - 1, i).wait()

            tiles[i][...] = dot_at(
                act[:, i * part : (i + 1) * part], g_all[:, pl.ds(at128(t, 256), 256)]
            ).astype(BF)
            put(t, i).start()

    loop(d // 256, w_down_grad)
    for i in range(2):
        put(d // 256 - 1, i).wait()
    s_d.swap()
    p_d.late()
    p_d.finish()

    def back(j):
        r0 = at128(j, rows)

        def one(t):
            c0 = at128(t, cols)
            c1 = pl.multiple_of(wide + c0, 128)
            da = dot_bt(g_all[pl.ds(r0, rows), :], dnb[pl.ds(c0, cols), :])
            gate = dgu[pl.ds(r0, rows), pl.ds(c0, cols)].astype(F32)
            up = dgu[pl.ds(r0, rows), pl.ds(c1, cols)].astype(F32)
            sig = jax.nn.sigmoid(gate)
            dgu[pl.ds(r0, rows), pl.ds(c0, cols)] = (
                da * up * (sig * (1.0 + gate * (1.0 - sig)))
            ).astype(BF)
            dgu[pl.ds(r0, rows), pl.ds(c1, cols)] = (da * gate * sig).astype(BF)

        loop(wide // cols, one)

    rs = base

    slots = stage.at[:, pl.ds(0, d)]

    def slot_copy(src, dst, step):
        return remote(
            rows_at(slots, src, rows), rows_at(slots, dst, rows),
            send.at[rs + src], recv.at[rs + dst], z + step, me,
        )

    hold = nz <= 4

    def sides(i):
        j = c_x.order(nz - 1 - i)
        below, above = j > z, j < z
        got = jnp.logical_or(jnp.logical_and(below, z > 0), jnp.logical_and(above, z < nz - 1))
        return j, below, above, got, (pl.ds(at128(j, rows), rows), pl.ds(0, d))

    def terms(i, at):
        j = sides(i)[0]
        back(j)

        def one(t):
            c0 = at128(t, 512)
            ybuf[at : at + rows, pl.ds(c0, 512)] = dot_bt(
                dgu[pl.ds(at128(j, rows), rows), :], gu[pl.ds(c0, 512), :]
            ).astype(BF)

        loop(d // 512, one)

    def ship(j, below, above):
        @pl.when(below)
        def _():
            slot_copy(j, j, 1).start()

        @pl.when(above)
        def _():
            slot_copy(j, jnp.where(z - 1 == j, nz, j), -1).start()

    def early(i, at):
        j, below, above, got, where = sides(i)

        @pl.when(jnp.logical_not(got))
        def _():
            stage[where] = ybuf[at : at + rows, :]
            ship(j, below, above)

    def late(i, at):
        j, below, above, got, where = sides(i)

        @pl.when(got)
        def _():
            slot_copy(j, j, 0).wait_recv()
            stage[where] = (
                stage[where].astype(F32) + ybuf[at : at + rows, :].astype(F32)
            ).astype(BF)
            ship(j, below, above)

    if hold:
        between = {0: (s_d.merge, s_d.first), 1: (s_d.second,)}
        for i in range(nz - 1):
            terms(i, i * rows)
            early(i, i * rows)
            for step in between.get(i, ()):
                step()
        late(0, 0)
    else:

        def at_once(i):
            terms(i, 0)
            early(i, 0)
            late(i, 0)

        loop(nz - 1, at_once)
        for step in (s_d.merge, s_d.first, s_d.second):
            step()
    back(z)

    def own(t):
        c0 = at128(t, 512)
        dx_ref[:, pl.ds(c0, 512)] = dot_bt(
            dgu[pl.ds(at128(z, rows), rows), :], gu[pl.ds(c0, 512), :]
        )

    loop(d // 512, own)

    c_x.drain()

    def down_terms(t):
        c0 = at128(t, 256)
        g_all[:, pl.ds(c0, 256)] = dot(act[...], dnb[:, pl.ds(c0, 256)]).astype(BF)

    c_g.drain()
    loop(d // 256, down_terms)
    out_p = pltpu.make_async_copy(g_all, dpart, local.at[spare + 3])
    out_p.start()
    if hold:
        for i in range(1, nz - 1):
            late(i, i * rows)
            if i == 1:
                s_d.last(d_own)
    else:
        s_d.last(d_own)
    p_gu.drain()

    def w_gu_grad(t):
        c0 = at128(t, 256)
        gu[:, pl.ds(c0, 256)] = dot_at(x_all[...], dgu[:, pl.ds(c0, 256)]).astype(BF)

    outs = []
    for i in range(2):
        loop(wide // 256, lambda t: w_gu_grad(t + i * (wide // 256)))
        half = pl.ds(i * wide, wide)
        outs.append(pltpu.make_async_copy(gu.at[:, half], dwgu.at[:, half], local.at[spare + i]))
        outs[-1].start()
    out_kv = pltpu.make_async_copy(kv, kv_out, local.at[spare + 2])
    out_kv.start()

    @pl.when(z > 0)
    def _():
        slot_copy(z, z, 0).wait_recv()
        dx_ref[...] += rows_at(slots, z, rows)[...].astype(F32)

    @pl.when(z < nz - 1)
    def _():
        slot_copy(z, nz, 0).wait_recv()
        dx_ref[...] += rows_at(slots, nz, rows)[...].astype(F32)

    for item in (p_q, p_kv, p_s, p_o, p_d, c_kv, s_d):
        item.drain()

    def gave(i):
        j = c_x.order(i + 1)
        slot_copy(j, j, 0).wait_send()

    loop(nz - 1, gave)
    for copy in outs + [out_kv, out_p]:
        copy.wait()


def front(dims, wq, sm, wo, wp, dn, x, g, cos2, sin2, qpos, kpos):
    nz, nf, rows, d, wide, upad, nb, ng = dims
    q_width, k_width = HEADS * HEAD_DIM, KV_HEADS * HEAD_DIM
    qkv = q_width + 2 * k_width
    tokens = nz * rows
    any_, vm = pl.BlockSpec(memory_space=pl.ANY), pl.BlockSpec(memory_space=pltpu.VMEM)
    sems = 6 * PlaneGather.sems(nf) + 3 * Chain.sems(nz) + Scatter.sems(nf) + nz + 1
    chips = nf // 2
    out = jax.ShapeDtypeStruct
    return pl.pallas_call(
        functools.partial(front_kernel, dims),
        in_specs=[any_] * 5 + [vm, any_] + [vm] * 4,
        out_specs=[any_, any_, vm, any_] + [vm] * 5 + [any_] * 6,
        out_shape=[
            out((d, qkv), BF),
            out((q_width, d), BF),
            out((rows, q_width), BF),
            out((tokens, 2 * k_width), BF),
            out((rows, q_width), BF),
            out((rows, HEAD_DIM), F32),
            out((rows, d), F32),
            out((rows, d), F32),
            out((8, d), F32),
            out((d, 2 * wide), BF),
            out((tokens, d), BF),
            out((upad, d), BF),
            out((wide, d), BF),
            out((chips * upad, d), BF),
            out(((chips - 1) * upad, d), BF),
        ],
        scratch_shapes=[
            pltpu.VMEM((max(d, (nz + 1) * rows), qkv), BF),
            pltpu.VMEM((d, 2 * wide), BF),
            pltpu.VMEM((wide, d), BF),
            pltpu.VMEM((tokens, d), BF),
            pltpu.VMEM((tokens, d), BF),
            pltpu.VMEM((tokens, wide), BF),
            pltpu.VMEM((tokens, 2 * wide), BF),
            pltpu.VMEM((nf * 16, sm.shape[1]), BF),
            pltpu.VMEM((tokens, 2 * k_width), BF),
            pltpu.VMEM((8, qkv), F32),
            pltpu.VMEM((rows, tokens), F32),
            pltpu.VMEM(((nz - 1 if nz <= 4 else 1) * rows, d), BF),
            pltpu.SemaphoreType.DMA((sems,)),
            pltpu.SemaphoreType.DMA((sems,)),
            pltpu.SemaphoreType.DMA((10,)),
        ],
        compiler_params=pltpu.CompilerParams(
            collective_id=0, has_side_effects=True, vmem_limit_bytes=VMEM_LIMIT
        ),
    )(wq, sm, wo, wp, dn, x, g, cos2, sin2, qpos, kpos)


class Reduce:
    def __init__(self, slots, rows, nz, z, me, send, recv, base, order):
        self.slots, self.rows, self.nz, self.z, self.me = slots, rows, nz, z, me
        self.send, self.recv, self.base, self.order = send, recv, base, order

    @staticmethod
    def sems(nz):
        return nz + 1

    def copy(self, src, dst, step):
        return remote(
            rows_at(self.slots, src, self.rows), rows_at(self.slots, dst, self.rows),
            self.send.at[self.base + src], self.recv.at[self.base + dst], self.z + step, self.me,
        )

    def give(self, i, part):
        z, nz, rows = self.z, self.nz, self.rows
        j = self.order(nz - 1 - i)
        below, above = j > z, j < z
        got = jnp.logical_or(jnp.logical_and(below, z > 0), jnp.logical_and(above, z < nz - 1))
        where = pl.ds(at128(j, rows) if rows % 128 == 0 else pl.multiple_of(j * rows, 16), rows)
        own = part(j)

        @pl.when(got)
        def _():
            self.copy(j, j, 0).wait_recv()
            self.slots[where, :] = (self.slots[where, :].astype(F32) + own.astype(F32)).astype(BF)

        @pl.when(jnp.logical_not(got))
        def _():
            self.slots[where, :] = own.astype(BF)

        @pl.when(below)
        def _():
            self.copy(j, j, 1).start()

        @pl.when(above)
        def _():
            self.copy(j, jnp.where(z - 1 == j, nz, j), -1).start()

    def take(self, total):
        z, nz = self.z, self.nz

        @pl.when(z > 0)
        def _():
            self.copy(z, z, 0).wait_recv()
            total[...] += rows_at(self.slots, z, self.rows)[...].astype(F32)

        @pl.when(z < nz - 1)
        def _():
            self.copy(z, nz, 0).wait_recv()
            total[...] += rows_at(self.slots, nz, self.rows)[...].astype(F32)

    def drain(self):
        def gave(i):
            j = self.order(i + 1)
            self.copy(j, j, 0).wait_send()

        loop(self.nz - 1, gave)


def back_kernel(
    dims,
    dwgu, d_own, dpart, wq_all, wo_all, kv_hbm, mid_hbm, dx_hbm,
    x_ref, g_ref, q_ref, o_ref, lse_ref, gain_ref, cos_ref, sin_ref, qpos_ref, kpos_ref,
    hid_ref, gh_ref, all_d, all_g, all_u, z_out, tiny_out,
    stage, full, dslots, do_ref, kv, dkv, kslots, m32, dh, t32, dqkv, mask, normed,
    r3, l3, r4, l4, zsrc, zslots, zlow, zown, gain_sums, tiny, tin, zin,
    r1, r2, l1, l2, own2, own_sems, send, recv, local,
):
    nz, nf, rows, d, wide, upad, nb, ng, ch = dims
    z, me = lax.axis_index("ctx"), lax.axis_index("fsdp")
    q_width, k_width = HEADS * HEAD_DIM, KV_HEADS * HEAD_DIM
    qkv = q_width + 2 * k_width
    scale = HEAD_DIM ** (-0.5)
    wr = d // nf
    place = {"nf": nf, "z": z, "me": me, "send": send, "recv": recv}
    per = Scatter.sems(nf)
    own = {"own": own2, "sems": own_sems}
    s_g = Scatter(dwgu, 0, wr, wide, r1, l1, True, base=per, **own, **place)
    s_u = Scatter(dwgu, wide, wr, wide, r2, l2, True, base=2 * per, **own, **place)
    s_o = Scatter(full, 0, wr, d, r3, l3, True, base=3 * per, **place)
    s_q = Scatter(full, 0, wr, qkv, r4, l4, True, base=4 * per, **place)
    base = 5 * per
    line = {"nz": nz, "z": z, "me": me, "send": send, "recv": recv}
    per = Chain.sems(nz)
    a_d = Chain(all_d, upad, base=base, **line)
    a_g = Chain(all_g, wr, base=base + per, **line)
    a_u = Chain(all_u, wr, base=base + 2 * per, **line)
    a_z = Chain(z_out, ch, base=base + 3 * per, **line)
    base += 4 * per
    per = Reduce.sems(nz)
    d_kv = Reduce(kslots, rows, base=base, order=a_d.order, **line)
    d_h = Reduce(dslots, rows, base=base + per, order=a_d.order, **line)
    d_z = Reduce(zslots, ch, base=base + 2 * per, order=a_d.order, **line)
    base += 3 * per

    def fetch(src, dst, i):
        copy = pltpu.make_async_copy(src, dst, local.at[i])
        copy.start()
        return copy

    def stream(src, cols, use):
        copies = []
        for t in range(src.shape[0] // 512):
            slot = stage.at[pl.ds(t % 2 * 512, 512), pl.ds(0, cols)]
            copies.append(
                pltpu.make_async_copy(src.at[pl.ds(t * 512, 512)], slot, local.at[6 + t % 2])
            )
        for copy in copies[:2]:
            copy.start()
        for t, copy in enumerate(copies):
            copy.wait()
            use(t, t % 2 * 512)
            if t + 2 < len(copies):
                copies[t + 2].start()

    mid_in = fetch(mid_hbm, m32, 1)
    dx_in = fetch(dx_hbm, dh, 2)
    kv_in = fetch(kv_hbm, kv, 3)
    d_in = fetch(d_own, rows_at(all_d, z, upad), 4)

    barrier = pltpu.get_barrier_semaphore()
    for k in range(1, nf):
        pl.semaphore_signal(barrier, inc=1, device_id=(z, me ^ k), device_id_type=MESH)
    for k in range(1, nz):
        pl.semaphore_signal(barrier, inc=1, device_id=((z + k) % nz, me), device_id_type=MESH)
    pl.semaphore_wait(barrier, nf + nz - 2)

    mask[...] = jnp.where(kpos_ref[...] <= qpos_ref[...], 0.0, MASKED).astype(BF)
    dkv[...] = jnp.zeros_like(dkv)
    lanes = lax.broadcasted_iota(jnp.int32, (rows, HEAD_DIM), 1)
    mine = dkv.at[pl.ds(at128(z, rows), rows)]
    third = HEADS // 3

    def norm_back():
        mid_in.wait()
        dx_in.wait()
        mid, dxn = m32[...], dh[...]
        inverse_two = lax.rsqrt(jnp.mean(mid * mid, -1, keepdims=True) + EPSILON)
        scaled = gain_ref[1:2, :] * dxn
        gain_sums[1:2, :] = jnp.sum(dxn * mid * inverse_two, 0, keepdims=True)
        dh[...] = (
            g_ref[...].astype(F32)
            + inverse_two * scaled
            - mid
            * (inverse_two * inverse_two * inverse_two)
            * jnp.mean(scaled * mid, -1, keepdims=True)
        )
        normed[...] = dh[...].astype(BF)

    def out_back():
        def one(t, r):
            do_ref[:, t * 512 : t * 512 + 512] = dot_bt(
                normed[...], stage[r : r + 512, 0:d]
            ).astype(BF)

        stream(wo_all, d, one)
        kv_in.wait()

    def w_out_grad():
        def one(t):
            c0 = at128(t, 512)
            full[pl.ds(0, q_width), pl.ds(c0, 512)] = dot_at(
                o_ref[...], normed[:, pl.ds(c0, 512)]
            ).astype(BF)

        loop(d // 512, one)

    def head(h):
        c0 = at128(h, HEAD_DIM)
        kc = at128(h // (HEADS // KV_HEADS), HEAD_DIM)
        vc = pl.multiple_of(kc + k_width, HEAD_DIM)
        q, k, v = q_ref[:, pl.ds(c0, HEAD_DIM)], kv[:, pl.ds(kc, HEAD_DIM)], kv[:, pl.ds(vc, HEAD_DIM)]
        do = do_ref[:, pl.ds(c0, HEAD_DIM)]
        lse = jnp.sum(jnp.where(lanes == h, lse_ref[...], 0.0), -1, keepdims=True)
        delta = jnp.sum(
            do.astype(F32) * o_ref[:, pl.ds(c0, HEAD_DIM)].astype(F32), -1, keepdims=True
        )
        p = jnp.exp(dot_bt(q, k) * scale + mask[...].astype(F32) - lse)
        dkv[:, pl.ds(vc, HEAD_DIM)] += dot_at(p.astype(BF), do)
        ds = (p * (dot_bt(do, v) - delta)).astype(BF)
        dq = dot(ds, k) * scale
        dkv[:, pl.ds(kc, HEAD_DIM)] += dot_at(ds, q) * scale
        dqkv[:, pl.ds(c0, HEAD_DIM)] = turn(dq, cos_ref[...], -sin_ref[...]).astype(BF)

    def kv_part(j):
        return dkv[pl.ds(at128(j, rows), rows), :]

    def down_part(j):
        part = stage.at[pl.ds(0, rows), pl.ds(0, d)]
        fetch(rows_at(dpart, j, rows), part, 1).wait()
        return part[...]

    def z_part(j):
        return zsrc[pl.ds(pl.multiple_of(j * ch, 16), ch), :]

    def project_back():
        for h in range(KV_HEADS):
            c0 = h * HEAD_DIM
            dqkv[:, q_width + c0 : q_width + c0 + HEAD_DIM] = turn(
                mine[:, c0 : c0 + HEAD_DIM], cos_ref[...], -sin_ref[...]
            ).astype(BF)
        dqkv[:, q_width + k_width :] = mine[:, k_width:].astype(BF)

    def w_qkv_grad():
        x = x_ref[...].astype(F32)
        inverse = lax.rsqrt(jnp.mean(x * x, -1, keepdims=True) + EPSILON)
        normed[...] = (x * inverse * gain_ref[0:1, :]).astype(BF)
        s_o.drain()

        def one(t):
            c0 = at128(t, 512)
            full[pl.ds(0, d), pl.ds(c0, 512)] = dot_at(
                normed[...], dqkv[:, pl.ds(c0, 512)]
            ).astype(BF)

        loop(qkv // 512, one)

    tiny_copies = []

    def input_back():
        def one(t, r):
            t32[:, t * 512 : t * 512 + 512] = dot_bt(dqkv[...], stage[r : r + 512, :])

        stream(wq_all, qkv, one)
        x = x_ref[...].astype(F32)
        inverse = lax.rsqrt(jnp.mean(x * x, -1, keepdims=True) + EPSILON)
        dxn = t32[...]
        scaled = gain_ref[0:1, :] * dxn
        gain_one = jnp.sum(dxn * x * inverse, 0, keepdims=True)
        gain_two = gain_sums[1:2, :]
        bias = jnp.sum(dqkv[...].astype(F32), 0, keepdims=True)
        gh_ref[...] = (
            dh[...]
            + inverse * scaled
            - x * (inverse * inverse * inverse) * jnp.mean(scaled * x, -1, keepdims=True)
        ).astype(BF)

        cut = q_width + k_width
        qk, vb = cut // nf, k_width // nf
        tiny[...] = jnp.zeros_like(tiny)
        for f in range(nf):
            r = slice(8 * f, 8 * f + 1)
            tiny[r, 0:qk] = bias[:, f * qk : (f + 1) * qk]
            tiny[r, qk : qk + vb] = bias[:, cut + f * vb : cut + (f + 1) * vb]
            tiny[r, qk + vb : qk + vb + ng] = gain_one[:, f * ng : (f + 1) * ng]
            tiny[r, qk + vb + ng : qk + vb + 2 * ng] = gain_two[:, f * ng : (f + 1) * ng]
        own = pl.ds(pl.multiple_of(me * 8, 8), 8)
        tin[own, :] = tiny[own, :]
        for k in range(1, nf):
            copy = remote(
                rows_at(tiny, me ^ k, 8), rows_at(tin, me, 8),
                send.at[base + k], recv.at[base + k], z, me ^ k,
            )
            copy.start()
            tiny_copies.append(copy)

    def tiny_along():
        for copy in tiny_copies:
            copy.wait_recv()
        total = tin[0:8, :]
        for f in range(1, nf):
            total = total + tin[8 * f : 8 * f + 8, :]
        zin[pl.ds(pl.multiple_of(z * 8, 8), 8), :] = total
        for k in range(1, nz):
            copy = remote(
                rows_at(zin, z, 8), rows_at(zin, z, 8),
                send.at[base + nf + k], recv.at[base + nf + k], (z + k) % nz, me,
            )
            copy.start()
            tiny_copies.append(copy)

    def z_take():
        zown[...] = z_part(z).astype(F32)
        d_z.take(zown)
        zlow[...] = zown[...].astype(BF)
        fetch(zlow, rows_at(z_out, z, ch), 2).wait()

    def h_take():
        m32[...] += down_part(z).astype(F32)
        d_h.take(m32)
        hid_ref[...] = m32[...].astype(BF)

    d_in.wait()
    a_d.begin()
    s_g.swap()
    norm_back()
    out_back()
    w_out_grad()
    s_o.swap()
    s_g.merge()
    s_g.first()
    s_u.swap()
    a_d.forward(1)
    for k in range(2, nz - 1):
        a_d.forward(k)
    loop(third, head)
    loop(third, lambda h: head(h + third))
    loop(third, lambda h: head(h + 2 * third))
    s_u.merge()
    s_g.second()
    s_u.first()
    a_d.forward(nz - 1)
    d_kv.give(0, kv_part)
    for i in range(1, nz - 2):
        d_kv.give(i, kv_part)
    d_kv.give(nz - 2, kv_part)
    s_o.merge()
    s_o.first()
    s_g.last(s_g.block(0))
    fetch(s_g.block(0), rows_at(all_g, z, wr), 4).wait()
    a_g.begin()
    s_u.second()
    a_g.forward(1)
    for k in range(2, nz - 1):
        a_g.forward(k)
    s_o.second()
    d_kv.take(mine)
    d_h.give(0, down_part)
    project_back()
    a_g.forward(nz - 1)
    w_qkv_grad()
    s_q.swap()
    s_o.last(zsrc.at[pl.ds(0, wr), pl.ds(0, d)])
    s_u.last(s_u.block(0))
    fetch(s_u.block(0), rows_at(all_u, z, wr), 5).wait()
    s_q.merge()
    s_q.first()
    a_u.begin()
    a_u.forward(1)
    s_q.second()
    for k in range(2, nz - 1):
        a_u.forward(k)
    a_u.forward(nz - 1)
    input_back()
    s_q.last(zsrc.at[pl.ds(0, wr), pl.ds(d, qkv)])
    d_z.give(0, z_part)
    tiny_along()
    for i in range(1, nz - 2):
        d_z.give(i, z_part)
    for i in range(1, nz - 2):
        d_h.give(i, down_part)
    d_z.give(nz - 2, z_part)
    d_h.give(nz - 2, down_part)
    for k in range(1, nz):
        a_u.arrive(k)
    z_take()
    for k in range(1, nz):
        a_g.arrive(k)
    a_z.begin()
    a_z.forward(1)
    for k in range(1, nz):
        a_d.arrive(k)
    for k in range(2, nz - 1):
        a_z.forward(k)
    a_z.forward(nz - 1)
    h_take()
    for k in range(1, nz):
        a_z.arrive(k)
    for copy in tiny_copies[nf - 1 :]:
        copy.wait_recv()
    total = zin[0:8, :]
    for j in range(1, nz):
        total = total + zin[8 * j : 8 * j + 8, :]
    tiny_out[...] = total
    for item in (s_g, s_u, s_o, s_q, a_d, a_g, a_u, a_z, d_kv, d_h, d_z):
        item.drain()
    for copy in tiny_copies:
        copy.wait_send()


def back(dims, *args):
    nz, nf, rows, d, wide, upad, nb, ng, ch = dims
    q_width, k_width = HEADS * HEAD_DIM, KV_HEADS * HEAD_DIM
    qkv = q_width + 2 * k_width
    tokens, chips, wr = nz * rows, nf // 2, d // nf
    tiny = -(-((qkv + 2 * d) // nf) // 128) * 128
    any_, vm = pl.BlockSpec(memory_space=pl.ANY), pl.BlockSpec(memory_space=pltpu.VMEM)
    out = jax.ShapeDtypeStruct
    sems = 5 * Scatter.sems(nf) + 4 * Chain.sems(nz) + 3 * Reduce.sems(nz) + nf + nz
    pieces = [(upad, d), (wr, wide), (wr, wide)]
    return pl.pallas_call(
        functools.partial(back_kernel, dims),
        in_specs=[any_] * 8 + [vm] * 10,
        out_specs=[vm, vm] + [any_] * 4 + [vm],
        out_shape=[out((rows, d), BF), out((rows, d), BF)]
        + [out((nz * r, c), BF) for r, c in pieces]
        + [out((nz * ch, d + qkv), BF), out((8, tiny), F32)],
        scratch_shapes=[
            pltpu.VMEM((1024, qkv), BF),
            pltpu.VMEM((d, qkv), BF),
            pltpu.VMEM(((nz + 1) * rows, d), BF),
            pltpu.VMEM((rows, q_width), BF),
            pltpu.VMEM((tokens, 2 * k_width), BF),
            pltpu.VMEM((tokens, 2 * k_width), F32),
            pltpu.VMEM(((nz + 1) * rows, 2 * k_width), BF),
            pltpu.VMEM((rows, d), F32),
            pltpu.VMEM((rows, d), F32),
            pltpu.VMEM((rows, d), F32),
            pltpu.VMEM((rows, qkv), BF),
            pltpu.VMEM((rows, tokens), BF),
            pltpu.VMEM((rows, d), BF),
            pltpu.VMEM((chips * wr, d), BF),
            pltpu.VMEM(((chips - 1) * wr, d), BF),
            pltpu.VMEM((chips * wr, qkv), BF),
            pltpu.VMEM(((chips - 1) * wr, qkv), BF),
            pltpu.VMEM((nz * ch, d + qkv), BF),
            pltpu.VMEM(((nz + 1) * ch, d + qkv), BF),
            pltpu.VMEM((ch, d + qkv), BF),
            pltpu.VMEM((ch, d + qkv), F32),
            pltpu.VMEM((8, d), F32),
            pltpu.VMEM((nf * 8, tiny), F32),
            pltpu.VMEM((nf * 8, tiny), F32),
            pltpu.VMEM((nz * 8, tiny), F32),
            pltpu.VMEM((chips * wr, wide), BF),
            pltpu.VMEM((chips * wr, wide), BF),
            pltpu.VMEM(((chips - 1) * wr, wide), BF),
            pltpu.VMEM(((chips - 1) * wr, wide), BF),
            pltpu.VMEM((2 * wr, wide), BF),
            pltpu.SemaphoreType.DMA((2,)),
            pltpu.SemaphoreType.DMA((sems,)),
            pltpu.SemaphoreType.DMA((sems,)),
            pltpu.SemaphoreType.DMA((8,)),
        ],
        compiler_params=pltpu.CompilerParams(
            collective_id=1, has_side_effects=True, vmem_limit_bytes=VMEM_LIMIT
        ),
    )(*args)


def shards(
    hidden_in, w_qkv, b_qkv, w_out, w_gate_up, w_down, gain_attn, gain_mlp, block_order, cotangent
):
    nz, nf = lax.axis_size("ctx"), lax.axis_size("fsdp")
    z, me = lax.axis_index("ctx"), lax.axis_index("fsdp")
    q_width, k_width = HEADS * HEAD_DIM, KV_HEADS * HEAD_DIM
    rows = hidden_in.shape[1]
    piece_len = rows // 2
    ff = w_gate_up.shape[1] // 2
    unit = ff // (nf * nz)
    order_row = block_order[0]
    all_places = (
        order_row[:, None] * piece_len + jnp.arange(piece_len, dtype=jnp.int32)[None, :]
    ).reshape(-1)
    my_places = lax.dynamic_slice_in_dim(all_places, z * rows, rows)
    cosine, sine_table = angle_tables(my_places)
    cos2 = jnp.concatenate([cosine, cosine], 1)
    sin2 = jnp.concatenate([-sine_table, sine_table], 1)

    packed = pack(w_gate_up, nz, nf, z)
    wide = packed.shape[1] // 2
    upad = wide // nf
    down_mine = jnp.pad(
        lax.dynamic_slice_in_dim(w_down, z * unit, unit), ((0, upad - unit), (0, 0))
    )
    nb, ng = b_qkv.shape[0], gain_attn.shape[0]
    d = hidden_in.shape[2]
    small = jnp.concatenate([b_qkv, gain_attn, gain_mlp])
    small = jnp.pad(small[None], ((0, 15), (0, -small.shape[0] % 128)))
    grad_low = cotangent[0]
    (whole_qkv, whole_out, q_low, kv_all, attn_low, lse, middle, grad_normed_two, gains, gate_up_local, down_part,
     down_own, *_) = front(
        (nz, nf, rows, d, wide, upad, nb, ng),
        w_qkv, small, w_out, packed, down_mine, hidden_in[0], grad_low, cos2, sin2,
        my_places[:, None], all_places[None, :],
    )
    ch = -(-(d // (nf * nz)) // 16) * 16
    hidden, grad_hidden, down_all, gate_all, up_all, attn_all, tiny = back(
        (nz, nf, rows, d, wide, upad, nb, ng, ch),
        gate_up_local, down_own, down_part, whole_qkv, whole_out, kv_all, middle, grad_normed_two,
        hidden_in[0], grad_low, q_low, attn_low, lse, gains, cos2, sin2, my_places[:, None], all_places[None, :],
    )
    e1 = (q_width + k_width) // nf
    e2 = e1 + k_width // nf
    e3 = e2 + ng
    shard = d // nf
    return (
        hidden[None],
        grad_hidden[None],
        attn_all[:shard, d:].astype(F32),
        tiny[0, :e1],
        tiny[0, e1:e2],
        attn_all[:shard, :d].astype(F32),
        unpack(gate_all, up_all, nz, nf, ff),
        down_all.reshape(nz, upad, d)[:, :unit].reshape(nz * unit, d).astype(F32),
        tiny[0, e2:e3],
        tiny[0, e3 : e3 + ng],
    )


def solution(mesh):
    placed = (
        P("fsdp", "ctx", None),
        P("fsdp", None),
        P("fsdp"),
        P("fsdp", None),
        P("fsdp", None),
        P("fsdp", None),
        P("fsdp"),
        P("fsdp"),
        P("fsdp", None),
        P("fsdp", "ctx", None),
    )
    return jax.shard_map(
        shards,
        mesh=mesh,
        in_specs=placed,
        out_specs=(
            P("fsdp", "ctx", None),
            P("fsdp", "ctx", None),
            P("fsdp", None),
            P("fsdp"),
            P("fsdp"),
            P("fsdp", None),
            P("fsdp", None),
            P("fsdp", None),
            P("fsdp"),
            P("fsdp"),
        ),
        check_vma=False,
    )
```

```python
import functools

import jax
import jax.numpy as jnp
from jax import lax
from jax.experimental import pallas as pl
from jax.experimental.pallas import tpu as pltpu
from jax.sharding import PartitionSpec as P

HEADS = 12
KV_HEADS = 2
HEAD_DIM = 128
EPSILON = 1e-06
THETA = 1000000.0
MASKED = -1e30
BF = jnp.bfloat16
F32 = jnp.float32


def dot(a, b):
    return jnp.dot(a, b, preferred_element_type=F32)


def dot_bt(a, b):
    return lax.dot_general(a, b, (((1,), (1,)), ((), ())), preferred_element_type=F32)


def dot_at(a, b):
    return lax.dot_general(a, b, (((0,), (0,)), ((), ())), preferred_element_type=F32)


def angle_tables(places):
    half_dim = HEAD_DIM // 2
    freqs = THETA ** (-(jnp.arange(half_dim).astype(F32) * 2.0 / HEAD_DIM))
    angles = places.astype(F32)[:, None] * freqs[None, :]
    return (jnp.cos(angles), jnp.sin(angles))


def half_rows(rows):
    return -(-rows // 32) * 16


def pieces_of(columns, width, rows, room):
    n = next(n for n in range(1, columns) if columns % (128 * n) == 0 and columns // n <= width)
    assert n * rows <= room
    return n


def pack(k, nz, nf, ff, unit, upad, rows, width, held, out):
    for h in range(2):
        for f in range(nf):
            src = h * ff + f * (ff // nf) + k * unit
            dst = (h * nf + f) * upad
            done = 0
            while done < unit:
                piece, at = divmod(src + done, width)
                n = min(unit - done, width - at)
                out[:, dst + done : dst + done + n] = held[
                    piece * rows : (piece + 1) * rows, at : at + n
                ]
                done += n
            if upad > unit:
                out[:, dst + unit : dst + upad] = jnp.zeros((rows, upad - unit), out.dtype)


def unpack_kernel(nz, nf, ff, unit, upad, *refs):
    out_ref = refs[-1]
    for k in range(nz):
        for h in range(2):
            for f in range(nf):
                src = f * upad
                dst = h * ff + f * (ff // nf) + k * unit
                part = refs[h * nz + k]
                out_ref[:, dst : dst + unit] = part[:, src : src + unit].astype(F32)


def unpack(gate, up, nz, nf, ff):
    rows, wide = gate.shape[0] // nz, gate.shape[1]
    step = 32
    specs = [
        pl.BlockSpec((step, wide), lambda i, k=k: (k * (rows // step) + i, 0)) for k in range(nz)
    ]
    return pl.pallas_call(
        functools.partial(unpack_kernel, nz, nf, ff, ff // (nf * nz), wide // nf),
        grid=(rows // step,),
        in_specs=specs * 2,
        out_specs=pl.BlockSpec((step, 2 * ff), lambda i: (i, 0)),
        out_shape=jax.ShapeDtypeStruct((rows, 2 * ff), F32),
    )(*[gate] * nz, *[up] * nz)


def finish_kernel(nz, nf, ff, unit, upad, cuts, *refs):
    gates, ups = refs[:nz], refs[nz : 2 * nz]
    down, attn, tiny, hid, gh = refs[2 * nz : 2 * nz + 5]
    gu_out, down_out, qkv_out, out_out, hid_out, gh_out, *tiny_outs = refs[2 * nz + 5 :]
    unpack_kernel(nz, nf, ff, unit, upad, *gates, *ups, gu_out)
    down_out[...] = down[0:unit, :].astype(F32)
    d = out_out.shape[1]
    qkv_out[...] = attn[:, d:].astype(F32)
    out_out[...] = attn[:, :d].astype(F32)
    hid_out[...] = hid[...]
    gh_out[...] = gh[...]

    @pl.when(pl.program_id(0) == 0)
    def _():
        for out, lo, hi in zip(tiny_outs, cuts, cuts[1:]):
            out[...] = tiny[0:1, lo:hi]


def finish(gate, up, down, attn, tiny, hid, gh, nz, nf, ff, cuts):
    rows, wide = gate.shape[0] // nz, gate.shape[1]
    unit, upad, d = ff // (nf * nz), wide // nf, hid.shape[1]
    step = rows // nz
    along = [
        pl.BlockSpec((step, wide), lambda i, k=k: (k * (rows // step) + i, 0)) for k in range(nz)
    ]
    part = hid.shape[0] // nz

    def by_step(r, c):
        return pl.BlockSpec((r, c), lambda i: (i, 0))

    def still(c):
        return pl.BlockSpec((1, c), lambda i: (0, 0))

    qkv = attn.shape[1] - d
    sizes = [hi - lo for lo, hi in zip(cuts, cuts[1:])]
    out = jax.ShapeDtypeStruct
    return pl.pallas_call(
        functools.partial(finish_kernel, nz, nf, ff, unit, upad, cuts),
        grid=(nz,),
        in_specs=along * 2
        + [
            by_step(upad, d),
            by_step(step, d + qkv),
            pl.BlockSpec(tiny.shape, lambda i: (0, 0)),
            by_step(part, d),
            by_step(part, d),
        ],
        out_specs=[
            by_step(step, 2 * ff),
            by_step(unit, d),
            by_step(step, qkv),
            by_step(step, d),
            by_step(part, d),
            by_step(part, d),
        ]
        + [still(n) for n in sizes],
        out_shape=[
            out((rows, 2 * ff), F32),
            out((nz * unit, d), F32),
            out((rows, qkv), F32),
            out((rows, d), F32),
            out(hid.shape, BF),
            out(hid.shape, BF),
        ]
        + [out((1, n), F32) for n in sizes],
        compiler_params=pltpu.CompilerParams(vmem_limit_bytes=VMEM_LIMIT),
    )(*[gate] * nz, *[up] * nz, down, attn, tiny, hid, gh)


MESH = pl.DeviceIdType.MESH
VMEM_LIMIT = 63 * 2**20


def remote(src, dst, send, recv, z, f):
    return pltpu.make_async_remote_copy(
        src_ref=src, dst_ref=dst, send_sem=send, recv_sem=recv, device_id=(z, f), device_id_type=MESH
    )


def rows_at(ref, index, count):
    return ref.at[pl.ds(pl.multiple_of(index * count, count), count)]


class PlaneGather:
    def __init__(self, src, dst, rows, nf, z, me, send, recv, local, base):
        self.src, self.dst, self.rows, self.nf, self.z, self.me = src, dst, rows, nf, z, me
        self.send, self.recv, self.base = send, recv, base
        self.local = pltpu.make_async_copy(src, rows_at(dst, me, rows), local)
        self.sent = []
        self.cut = half_rows(rows)
        self.swaps = {}

    @staticmethod
    def sems(nf):
        return 2 * nf

    def slot(self, k, lo=0, hi=None):
        hi = self.rows if hi is None else hi
        start = pl.multiple_of((self.me ^ k) * self.rows, 16) + lo
        return self.dst.at[pl.ds(pl.multiple_of(start, 16), hi - lo)]

    def push(self, index, src, dst, flip_by):
        copy = remote(
            src, dst, self.send.at[self.base + index], self.recv.at[self.base + index],
            self.z, self.me ^ flip_by,
        )
        copy.start()
        self.sent.append(copy)
        return copy

    def begin(self):
        self.local.start()
        self.direct = {}
        for k in (2, 4) if self.nf == 8 else range(2, self.nf, 2):
            self.direct[k] = self.push(k, self.src, self.slot(0), k)
        self.swaps[0] = self.push(1, self.src, self.slot(0), 1)

    def swap(self, k):
        self.swaps[k] = self.push(k + 1, self.slot(k), self.slot(k), 1)

    def middle(self):
        for k, copy in self.direct.items():
            copy.wait_recv()
            if self.nf == 8:
                if k == 2:
                    self.far_a = self.push(6, self.slot(2, 0, self.cut), self.slot(2, 0, self.cut), 4)
                elif self.cut < self.rows:
                    self.far_b = self.push(
                        8, self.slot(4, self.cut), self.slot(4, self.cut), 2
                    )
            self.swap(k)

    def late(self):
        if self.nf == 8:
            self.far_a.wait_recv()
            if self.cut < self.rows:
                self.far_b.wait_recv()
            self.swap(6)

    def finish(self):
        self.local.wait()
        for copy in self.swaps.values():
            copy.wait_recv()

    def drain(self):
        for copy in self.sent:
            copy.wait_send()


class Chain:
    def __init__(self, buf, rows, nz, z, me, send, recv, base):
        self.buf, self.rows, self.nz, self.z, self.me = buf, rows, nz, z, me
        self.send, self.recv, self.base = send, recv, base

    @staticmethod
    def sems(nz):
        return nz + 2

    def copy(self, j, sem, step, src=None):
        slot = rows_at(self.buf, j, self.rows)
        return remote(
            slot if src is None else src, slot, self.send.at[self.base + sem], self.recv.at[self.base + j], self.z + step, self.me
        )

    def order(self, k):
        z, nz = self.z, self.nz
        below, above = z, nz - 1 - z
        m = jnp.minimum(below, above)
        near = jnp.where(k % 2 == 1, z - (k + 1) // 2, z + k // 2)
        far = jnp.where(above > below, z + (k - m), z - (k - m))
        return jnp.where(k <= 2 * m, near, far)

    def begin(self, src=None):
        z, nz = self.z, self.nz

        @pl.when(z < nz - 1)
        def _():
            self.copy(z, nz, 1, src).start()

        @pl.when(z > 0)
        def _():
            self.copy(z, nz + 1, -1, src).start()

    def passing(self, j):
        z, nz = self.z, self.nz
        return jnp.logical_and(j < z, z < nz - 1), jnp.logical_and(j > z, z > 0)

    def forward(self, k):
        j = self.order(k)
        up, down = self.passing(j)

        @pl.when(up)
        def _():
            self.copy(j, j, 1).wait_recv()
            self.copy(j, j, 1).start()

        @pl.when(down)
        def _():
            self.copy(j, j, -1).wait_recv()
            self.copy(j, j, -1).start()

    def arrive(self, k):
        j = self.order(k)
        up, down = self.passing(j)

        @pl.when(jnp.logical_not(jnp.logical_or(up, down)))
        def _():
            self.copy(j, j, 0).wait_recv()

    def drain(self):
        z, nz = self.z, self.nz

        @pl.when(z < nz - 1)
        def _():
            self.copy(z, nz, 1).wait_send()

        @pl.when(z > 0)
        def _():
            self.copy(z, nz + 1, -1).wait_send()

        def one(k, carry):
            j = self.order(k)
            up, down = self.passing(j)

            @pl.when(jnp.logical_or(up, down))
            def _():
                self.copy(j, j, 0).wait_send()

            return carry

        lax.fori_loop(1, nz, one, 0)


class Scatter:
    def __init__(self, src, c0, rows, cols, recv4, land, inside, nf, z, me, send, recv, base, own=None, sems=None):
        self.src, self.c0, self.rows, self.cols = src, c0, rows, cols
        self.recv4, self.land, self.inside = recv4, land, inside
        self.nf, self.z, self.me, self.send, self.recv, self.base = nf, z, me, send, recv, base
        self.chips, self.chip, self.core = nf // 2, me // 2, me % 2
        self.cut = half_rows(rows)
        self.sent = []
        self.got = {}
        self.own, self.own_sems = own, sems

    @staticmethod
    def sems(nf):
        return nf

    def push(self, index, src, dst, flip_by):
        copy = remote(
            src, dst, self.send.at[self.base + index], self.recv.at[self.base + index],
            self.z, self.me ^ flip_by,
        )
        copy.start()
        self.sent.append(copy)
        self.got[index] = copy

    def mine(self, ref, start, n):
        return ref.at[pl.ds(pl.multiple_of(start, 16), n)]

    def block(self, k, lo=0, hi=None):
        hi = self.rows if hi is None else hi
        return self.mine(self.recv4, (self.chip ^ k) * self.rows + lo, hi - lo)

    def swap(self):
        for p in range(self.chips):
            start = pl.multiple_of((2 * p + 1 - self.core) * self.rows, 16)
            src = self.src.at[pl.ds(start, self.rows), pl.ds(self.c0, self.cols)]
            self.push(p, src, self.mine(self.recv4, p * self.rows, self.rows), 1)

    def merge(self):
        rows, cols = self.rows, self.cols
        if self.own is not None:
            for p in range(min(2, self.chips)):
                self.fetch(p).start()
        for p in range(self.chips):
            self.got[p].wait_recv()
        if self.inside:
            for p in range(self.chips):
                start = pl.multiple_of((2 * p + self.core) * rows, 16)
                if self.own is None:
                    own, first = self.src, start
                else:
                    self.fetch(p).wait()
                    own, first = self.own, p % 2 * rows
                step = rows if rows <= 96 else rows // 2
                for i in range(0, rows, step):
                    where = pl.ds(p * rows + i, step)
                    part = own[pl.ds(pl.multiple_of(first + i, 16), step), pl.ds(0, cols)]
                    self.recv4[where, :] = (
                        self.recv4[where, :].astype(F32) + part.astype(F32)
                    ).astype(BF)
                if self.own is not None and p + 2 < self.chips:
                    self.fetch(p + 2).start()
            return
        step = rows if rows <= 96 else rows // 2
        n = rows // step
        core, col = self.core, self.c0 // cols
        own = pl.BlockSpec((step, cols), lambda p, i: ((2 * p + core) * n + i, col))
        held = pl.BlockSpec((step, cols), lambda p, i: (p * n + i, 0))
        pltpu.emit_pipeline(
            add_two, grid=(self.chips, n), in_specs=[own, held], out_specs=[held]
        )(self.src, self.recv4, self.recv4)

    def fetch(self, p):
        start = pl.multiple_of((2 * p + self.core) * self.rows, 16)
        return pltpu.make_async_copy(
            self.src.at[pl.ds(start, self.rows), pl.ds(self.c0, self.cols)],
            self.own.at[pl.ds(p % 2 * self.rows, self.rows)],
            self.own_sems.at[p % 2],
        )

    def add(self, out, parts, n):
        if self.inside:
            total = parts[0][...].astype(F32)
            for part in parts[1:]:
                total = total + part[...].astype(F32)
            out[...] = total.astype(BF)
            return
        step = n if n <= 96 else n // 2
        spec = pl.BlockSpec((step, self.cols), lambda i: (i, 0))
        body = add_two if len(parts) == 2 else add_all
        pltpu.emit_pipeline(
            body, grid=(n // step,), in_specs=[spec] * len(parts), out_specs=[spec]
        )(*parts, out)

    def first(self):
        base, rows, cut = self.chips, self.rows, self.cut
        if self.nf == 8:
            self.push(base, self.block(3, 0, cut), self.land.at[pl.ds(0, cut)], 2)
            self.push(base + 1, self.block(3, cut), self.land.at[pl.ds(cut, rows - cut)], 4)
        else:
            for k in range(1, self.chips):
                self.push(base + k - 1, self.block(k), self.land.at[pl.ds((k - 1) * rows, rows)], 2 * k)

    def second(self):
        if self.nf != 8:
            return
        base, rows, cut = self.chips, self.rows, self.cut
        self.got[base].wait_recv()
        to_y = self.block(2, 0, cut)
        self.add(to_y, [to_y, self.land.at[pl.ds(0, cut)]], cut)
        self.push(base + 3, self.block(2), self.land.at[pl.ds(2 * rows, rows)], 4)
        self.got[base + 1].wait_recv()
        to_x = self.block(1, cut)
        self.add(to_x, [to_x, self.land.at[pl.ds(cut, rows - cut)]], rows - cut)
        self.push(base + 2, self.block(1), self.land.at[pl.ds(rows, rows)], 2)

    def last(self, out):
        base, rows = self.chips, self.rows
        if self.nf == 8:
            incoming = [(base + 2, rows), (base + 3, 2 * rows)]
        else:
            incoming = [(base + k - 1, (k - 1) * rows) for k in range(1, self.chips)]
        for index, _ in incoming:
            self.got[index].wait_recv()
        parts = [self.block(0)] + [self.land.at[pl.ds(at, rows)] for _, at in incoming]
        self.add(out, parts, rows)

    def drain(self):
        for copy in self.sent:
            copy.wait_send()
        self.sent = []


def add_two(a, b, out):
    out[...] = (a[...].astype(F32) + b[...].astype(F32)).astype(BF)


def add_all(*refs):
    total = refs[0][...].astype(F32)
    for ref in refs[1:-1]:
        total = total + ref[...].astype(F32)
    refs[-1][...] = total.astype(BF)


def greet_ctx_and_plane(nz, nf, z, me):
    barrier = pltpu.get_barrier_semaphore()
    flips = (1, 2, 4) if nf == 8 else (1,) + tuple(range(2, nf, 2))
    for k in flips:
        pl.semaphore_signal(barrier, inc=1, device_id=(z, me ^ k), device_id_type=MESH)

    @pl.when(z < nz - 1)
    def _():
        pl.semaphore_signal(barrier, inc=1, device_id=(z + 1, me), device_id_type=MESH)

    @pl.when(z > 0)
    def _():
        pl.semaphore_signal(barrier, inc=1, device_id=(z - 1, me), device_id_type=MESH)

    inner = jnp.logical_and(z > 0, z < nz - 1)

    @pl.when(inner)
    def _():
        pl.semaphore_wait(barrier, len(flips) + 2)

    @pl.when(jnp.logical_not(inner))
    def _():
        pl.semaphore_wait(barrier, len(flips) + 1)


def loop(n, body):
    def step(i, carry):
        body(i)
        return carry

    lax.fori_loop(0, n, step, 0)


def at128(i, n):
    return i * n if isinstance(i, int) else pl.multiple_of(i * n, n)


def turn(t, cos2, sin2):
    return t * cos2 + pltpu.roll(t, HEAD_DIM // 2, 1) * sin2


def front_kernel(
    dims,
    wq, sm, wo, w_gu, w_dn, x_ref, g_ref, cos_ref, sin_ref, qpos_ref, kpos_ref,
    wq_all, wo_all, q_ref, kv_out, o_ref, lse_ref, mid_ref, dx_ref, gain_ref, dwgu, dpart, d_own, dwd, r0, l0,
    stage, gu, dnb, g_all, x_all, act, dgu, smb, kv, bias, ybuf, packed, down, send, recv, local,
):
    nz, nf, rows, d, ff, wide, upad, nb, ng = dims
    z, me = lax.axis_index("ctx"), lax.axis_index("fsdp")
    q_width, k_width = HEADS * HEAD_DIM, KV_HEADS * HEAD_DIM
    qkv = q_width + 2 * k_width
    scale = HEAD_DIM ** (-0.5)
    wr = d // nf
    per = PlaneGather.sems(nf)
    plane = [
        PlaneGather(src, dst, r, nf, z, me, send, recv, local.at[i], i * per)
        for i, (src, dst, r) in enumerate(
            [
                (wq.at[:, pl.ds(0, q_width)], wq_all.at[:, pl.ds(0, q_width)], wr),
                (wq.at[:, pl.ds(q_width, 2 * k_width)], wq_all.at[:, pl.ds(q_width, 2 * k_width)], wr),
                (sm, smb, 16),
                (wo, wo_all, wr),
                (packed, gu, wr),
                (down, dnb, upad),
            ]
        )
    ]
    p_q, p_kv, p_s, p_o, p_gu, p_d = plane
    base = len(plane) * per
    chain = [
        Chain(buf, rows, nz, z, me, send, recv, base + i * Chain.sems(nz))
        for i, buf in enumerate([g_all, kv, x_all])
    ]
    c_g, c_kv, c_x = chain
    base += len(chain) * Chain.sems(nz)
    s_d = Scatter(dwd, 0, upad, d, r0, l0, False, nf, z, me, send, recv, base)
    base += Scatter.sems(nf)
    spare = len(plane)

    unit = ff // (nf * nz)
    n = pieces_of(2 * ff, 2 * wide, wr, nz * rows)
    width = 2 * ff // n
    loads = [
        pltpu.make_async_copy(
            w_gu.at[:, pl.ds(i * width, width)],
            dgu.at[pl.ds(i * wr, wr), pl.ds(0, width)],
            local.at[spare + 1 + i],
        )
        for i in range(n)
    ]
    fetched = upad + 16
    down_in = act.at[pl.ds(0, fetched), pl.ds(0, d)] if wide >= d else dgu.at[pl.ds(n * wr, fetched), pl.ds(0, d)]

    def down_load(k):
        start = min(unit * k // 16 * 16, ff // nf - fetched)
        copy = pltpu.make_async_copy(w_dn.at[pl.ds(start, fetched)], down_in, local.at[spare + 1 + n])
        return copy, unit * k - start

    def part_loads():
        for copy in loads:
            copy.start()
        for k in range(nz):

            @pl.when(z == k)
            def _():
                down_load(k)[0].start()

    def part_pack():
        for copy in loads:
            copy.wait()
        for k in range(nz):

            @pl.when(z == k)
            def _():
                pack(k, nz, nf, ff, unit, upad, wr, width, dgu, packed)
                copy, off = down_load(k)
                copy.wait()
                down[0:unit, :] = down_in[...].astype(F32)[off : off + unit].astype(BF)
                if upad > unit:
                    down[unit:upad, :] = jnp.zeros((upad - unit, d), BF)

    g_copy = pltpu.make_async_copy(g_ref, rows_at(g_all, z, rows), local.at[spare])
    g_copy.start()
    greet_ctx_and_plane(nz, nf, z, me)
    p_s.begin()
    p_kv.begin()
    g_copy.wait()
    c_g.begin()
    part_loads()

    x = x_ref[...].astype(F32)
    inverse = lax.rsqrt(jnp.mean(x * x, -1, keepdims=True) + EPSILON)

    p_s.middle()
    p_kv.middle()
    p_q.begin()
    p_s.late()
    p_kv.late()
    p_s.finish()
    for f in range(nf):
        row = smb[f * 16 : (f + 1) * 16, :].astype(F32)[0:1]
        bias[0:1, f * nb : (f + 1) * nb] = row[:, :nb]
        gain_ref[0:1, f * ng : (f + 1) * ng] = row[:, nb : nb + ng]
        gain_ref[1:2, f * ng : (f + 1) * ng] = row[:, nb + ng : nb + 2 * ng]
    normed = (x * inverse * gain_ref[0:1, :]).astype(BF)
    x_all[pl.ds(at128(z, rows), rows), :] = normed

    def fetch_qkv(c0, n):
        copy = pltpu.make_async_copy(
            wq_all.at[:, pl.ds(c0, n)], stage.at[pl.ds(0, d), pl.ds(c0, n)], local.at[spare]
        )
        copy.start()
        copy.wait()

    p_kv.finish()
    fetch_qkv(q_width, 2 * k_width)

    def project(t):
        c0 = at128(t, 2 * HEAD_DIM)
        y = dot(
            x_all[pl.ds(at128(z, rows), rows), :], stage[pl.ds(0, d), pl.ds(c0, 2 * HEAD_DIM)]
        ) + bias[0:1, pl.ds(c0, 2 * HEAD_DIM)]
        return y, c0

    def project_v(t):
        y, c0 = project(t)
        kv[pl.ds(at128(z, rows), rows), pl.ds(pl.multiple_of(c0 - q_width, 256), 256)] = y.astype(BF)

    def turned(y):
        halves = [
            turn(y[:, h * HEAD_DIM : (h + 1) * HEAD_DIM], cos_ref[...], sin_ref[...]).astype(BF)
            for h in range(2)
        ]
        return jnp.concatenate(halves, 1)

    project_v((q_width + k_width) // 256)
    y, _ = project(q_width // 256)
    kv[pl.ds(at128(z, rows), rows), 0:k_width] = turned(y)
    c_kv.begin()
    p_q.middle()
    p_o.begin()
    part_pack()
    for k in range(1, nz - 1):
        c_kv.forward(k)
    p_q.late()
    p_q.finish()
    fetch_qkv(0, q_width)
    c_kv.forward(nz - 1)

    def project_q(t):
        y, c0 = project(t)
        q_ref[:, pl.ds(c0, 256)] = turned(y)

    loop(q_width // 256, project_q)
    p_o.middle()
    p_gu.begin()
    for k in range(1, nz):
        c_kv.arrive(k)
    for k in range(1, nz - 1):
        c_g.forward(k)

    lanes = lax.broadcasted_iota(jnp.int32, (rows, HEAD_DIM), 1)
    lse_ref[...] = jnp.zeros_like(lse_ref)

    def head(h):
        c0 = at128(h, HEAD_DIM)
        kc = at128(h // (HEADS // KV_HEADS), HEAD_DIM)
        vc = pl.multiple_of(kc + k_width, HEAD_DIM)
        s = dot_bt(q_ref[:, pl.ds(c0, HEAD_DIM)], kv[:, pl.ds(kc, HEAD_DIM)]) * scale
        s = jnp.where(kpos_ref[...] <= qpos_ref[...], s, MASKED)
        top = jnp.max(s, -1, keepdims=True)
        p = jnp.exp(s - top)
        total = jnp.sum(p, -1, keepdims=True)
        o = dot(p.astype(BF), kv[:, pl.ds(vc, HEAD_DIM)]) / total
        o_ref[:, pl.ds(c0, HEAD_DIM)] = o.astype(BF)
        lse_ref[...] = jnp.where(lanes == h, top + jnp.log(total), lse_ref[...])

    loop(HEADS, head)
    p_o.late()
    p_o.finish()
    fetch = pltpu.make_async_copy(wo_all, stage.at[pl.ds(0, q_width), pl.ds(0, d)], local.at[spare])
    fetch.start()
    fetch.wait()

    def out_proj(t):
        c0 = at128(t, 512)
        mid_ref[:, pl.ds(c0, 512)] = (
            dot(o_ref[...], stage[pl.ds(0, q_width), pl.ds(c0, 512)]) + x_ref[:, pl.ds(c0, 512)].astype(F32)
        )

    loop(d // 512, out_proj)
    mid = mid_ref[...]
    inverse_two = lax.rsqrt(jnp.mean(mid * mid, -1, keepdims=True) + EPSILON)
    x_all[pl.ds(at128(z, rows), rows), :] = (mid * inverse_two * gain_ref[1:2, :]).astype(BF)
    c_x.begin()
    c_g.forward(nz - 1)
    for k in range(1, nz - 1):
        c_x.forward(k)
    p_gu.middle()
    if nz <= 4:
        c_x.forward(nz - 1)
    p_gu.late()
    p_d.begin()
    p_gu.finish()

    cols = 768 if wide % 768 == 0 else 256

    def hidden(j):
        r0 = at128(j, rows)

        def one(t):
            c0 = at128(t, cols)
            xb = x_all[pl.ds(r0, rows), :]
            gate = dot(xb, gu[:, pl.ds(c0, cols)])
            up = dot(xb, gu[:, pl.ds(pl.multiple_of(wide + c0, 128), cols)])
            act[pl.ds(r0, rows), pl.ds(c0, cols)] = (gate * jax.nn.sigmoid(gate) * up).astype(BF)
            dgu[pl.ds(r0, rows), pl.ds(c0, cols)] = gate.astype(BF)
            dgu[pl.ds(r0, rows), pl.ds(pl.multiple_of(wide + c0, 128), cols)] = up.astype(BF)

        loop(wide // cols, one)

    hidden(z)
    if nz > 4:
        c_x.forward(nz - 1)

    def nearest(k):
        c_x.arrive(k)
        hidden(c_x.order(k))

    loop(nz - 2, lambda i: nearest(i + 1))
    p_d.middle()
    nearest(nz - 1)
    for k in range(1, nz):
        c_g.arrive(k)
    part = wide // 2
    tiles = [stage.at[pl.ds(0, part), pl.ds(d + i * 256, 256)] for i in range(2)]

    def put(t, i):
        c0 = at128(t, 256)
        return pltpu.make_async_copy(
            tiles[i], dwd.at[pl.ds(i * part, part), pl.ds(c0, 256)], local.at[spare + i]
        )

    def w_down_grad(t):
        for i in range(2):

            @pl.when(t > 0)
            def _():
                put(t - 1, i).wait()

            tiles[i][...] = dot_at(
                act[:, i * part : (i + 1) * part], g_all[:, pl.ds(at128(t, 256), 256)]
            ).astype(BF)
            put(t, i).start()

    loop(d // 256, w_down_grad)
    for i in range(2):
        put(d // 256 - 1, i).wait()
    s_d.swap()
    p_d.late()
    p_d.finish()

    def back(j):
        r0 = at128(j, rows)

        def one(t):
            c0 = at128(t, cols)
            c1 = pl.multiple_of(wide + c0, 128)
            da = dot_bt(g_all[pl.ds(r0, rows), :], dnb[pl.ds(c0, cols), :])
            gate = dgu[pl.ds(r0, rows), pl.ds(c0, cols)].astype(F32)
            up = dgu[pl.ds(r0, rows), pl.ds(c1, cols)].astype(F32)
            sig = jax.nn.sigmoid(gate)
            dgu[pl.ds(r0, rows), pl.ds(c0, cols)] = (
                da * up * (sig * (1.0 + gate * (1.0 - sig)))
            ).astype(BF)
            dgu[pl.ds(r0, rows), pl.ds(c1, cols)] = (da * gate * sig).astype(BF)

        loop(wide // cols, one)

    rs = base

    slots = stage.at[:, pl.ds(0, d)]

    def slot_copy(src, dst, step):
        return remote(
            rows_at(slots, src, rows), rows_at(slots, dst, rows),
            send.at[rs + src], recv.at[rs + dst], z + step, me,
        )

    hold = nz <= 4

    def sides(i):
        j = c_x.order(nz - 1 - i)
        below, above = j > z, j < z
        got = jnp.logical_or(jnp.logical_and(below, z > 0), jnp.logical_and(above, z < nz - 1))
        return j, below, above, got, (pl.ds(at128(j, rows), rows), pl.ds(0, d))

    def terms(i, at):
        j = sides(i)[0]
        back(j)

        def one(t):
            c0 = at128(t, 512)
            ybuf[at : at + rows, pl.ds(c0, 512)] = dot_bt(
                dgu[pl.ds(at128(j, rows), rows), :], gu[pl.ds(c0, 512), :]
            ).astype(BF)

        loop(d // 512, one)

    def ship(j, below, above):
        @pl.when(below)
        def _():
            slot_copy(j, j, 1).start()

        @pl.when(above)
        def _():
            slot_copy(j, jnp.where(z - 1 == j, nz, j), -1).start()

    def early(i, at):
        j, below, above, got, where = sides(i)

        @pl.when(jnp.logical_not(got))
        def _():
            stage[where] = ybuf[at : at + rows, :]
            ship(j, below, above)

    def late(i, at):
        j, below, above, got, where = sides(i)

        @pl.when(got)
        def _():
            slot_copy(j, j, 0).wait_recv()
            stage[where] = (
                stage[where].astype(F32) + ybuf[at : at + rows, :].astype(F32)
            ).astype(BF)
            ship(j, below, above)

    if hold:
        between = {nz - 2: (s_d.merge, s_d.first)}
        for i in range(nz - 1):
            terms(i, i * rows)
            early(i, i * rows)
            for step in between.get(i, ()):
                step()
        late(0, 0)
    else:

        def at_once(i):
            terms(i, 0)
            early(i, 0)
            late(i, 0)

        loop(nz - 1, at_once)
        for step in (s_d.merge, s_d.first, s_d.second):
            step()
    back(z)

    def own(t):
        c0 = at128(t, 512)
        dx_ref[:, pl.ds(c0, 512)] = dot_bt(
            dgu[pl.ds(at128(z, rows), rows), :], gu[pl.ds(c0, 512), :]
        )

    loop(d // 512, own)

    c_x.drain()

    def down_terms(t):
        c0 = at128(t, 256)
        g_all[:, pl.ds(c0, 256)] = dot(act[...], dnb[:, pl.ds(c0, 256)]).astype(BF)

    c_g.drain()
    loop(d // 256, down_terms)
    out_p = pltpu.make_async_copy(g_all, dpart, local.at[spare + 3])
    out_p.start()
    if hold:
        s_d.second()
        for i in range(1, nz - 1):
            late(i, i * rows)
    p_gu.drain()

    def w_gu_grad(t):
        c0 = at128(t, 256)
        gu[:, pl.ds(c0, 256)] = dot_at(x_all[...], dgu[:, pl.ds(c0, 256)]).astype(BF)

    outs = []
    for i in range(2):
        loop(wide // 256, lambda t: w_gu_grad(t + i * (wide // 256)))
        half = pl.ds(i * wide, wide)
        outs.append(pltpu.make_async_copy(gu.at[:, half], dwgu.at[:, half], local.at[spare + i]))
        outs[-1].start()
    s_d.last(d_own)
    out_kv = pltpu.make_async_copy(kv, kv_out, local.at[spare + 2])
    out_kv.start()

    @pl.when(z > 0)
    def _():
        slot_copy(z, z, 0).wait_recv()
        dx_ref[...] += rows_at(slots, z, rows)[...].astype(F32)

    @pl.when(z < nz - 1)
    def _():
        slot_copy(z, nz, 0).wait_recv()
        dx_ref[...] += rows_at(slots, nz, rows)[...].astype(F32)

    for item in (p_q, p_kv, p_s, p_o, p_d, c_kv, s_d):
        item.drain()

    def gave(i):
        j = c_x.order(i + 1)
        slot_copy(j, j, 0).wait_send()

    loop(nz - 1, gave)
    for copy in outs + [out_kv, out_p]:
        copy.wait()


def front(dims, wq, sm, wo, w_gu, w_dn, x, g, cos2, sin2, qpos, kpos):
    nz, nf, rows, d, ff, wide, upad, nb, ng = dims
    q_width, k_width = HEADS * HEAD_DIM, KV_HEADS * HEAD_DIM
    qkv = q_width + 2 * k_width
    tokens = nz * rows
    any_, vm = pl.BlockSpec(memory_space=pl.ANY), pl.BlockSpec(memory_space=pltpu.VMEM)
    sems = 6 * PlaneGather.sems(nf) + 3 * Chain.sems(nz) + Scatter.sems(nf) + nz + 1
    chips = nf // 2
    out = jax.ShapeDtypeStruct
    return pl.pallas_call(
        functools.partial(front_kernel, dims),
        in_specs=[any_] * 5 + [vm, any_] + [vm] * 4,
        out_specs=[any_, any_, vm, any_] + [vm] * 5 + [any_] * 6,
        out_shape=[
            out((d, qkv), BF),
            out((q_width, d), BF),
            out((rows, q_width), BF),
            out((tokens, 2 * k_width), BF),
            out((rows, q_width), BF),
            out((rows, HEAD_DIM), F32),
            out((rows, d), F32),
            out((rows, d), F32),
            out((8, d), F32),
            out((d, 2 * wide), BF),
            out((tokens, d), BF),
            out((upad, d), BF),
            out((wide, d), BF),
            out((chips * upad, d), BF),
            out(((chips - 1) * upad, d), BF),
        ],
        scratch_shapes=[
            pltpu.VMEM((max(d, (nz + 1) * rows), qkv), BF),
            pltpu.VMEM((d, 2 * wide), BF),
            pltpu.VMEM((wide, d), BF),
            pltpu.VMEM((tokens, d), BF),
            pltpu.VMEM((tokens, d), BF),
            pltpu.VMEM((tokens, wide), BF),
            pltpu.VMEM((tokens, 2 * wide), BF),
            pltpu.VMEM((nf * 16, sm.shape[1]), BF),
            pltpu.VMEM((tokens, 2 * k_width), BF),
            pltpu.VMEM((8, qkv), F32),
            pltpu.VMEM(((nz - 1 if nz <= 4 else 1) * rows, d), BF),
            pltpu.VMEM((d // nf, 2 * wide), BF),
            pltpu.VMEM((upad, d), BF),
            pltpu.SemaphoreType.DMA((sems,)),
            pltpu.SemaphoreType.DMA((sems,)),
            pltpu.SemaphoreType.DMA((24,)),
        ],
        compiler_params=pltpu.CompilerParams(
            collective_id=0, has_side_effects=True, vmem_limit_bytes=VMEM_LIMIT
        ),
    )(wq, sm, wo, w_gu, w_dn, x, g, cos2, sin2, qpos, kpos)


class Reduce:
    def __init__(self, slots, rows, nz, z, me, send, recv, base, order):
        self.slots, self.rows, self.nz, self.z, self.me = slots, rows, nz, z, me
        self.send, self.recv, self.base, self.order = send, recv, base, order

    @staticmethod
    def sems(nz):
        return nz + 1

    def copy(self, src, dst, step):
        return remote(
            rows_at(self.slots, src, self.rows), rows_at(self.slots, dst, self.rows),
            self.send.at[self.base + src], self.recv.at[self.base + dst], self.z + step, self.me,
        )

    def give(self, i, part):
        z, nz, rows = self.z, self.nz, self.rows
        j = self.order(nz - 1 - i)
        below, above = j > z, j < z
        got = jnp.logical_or(jnp.logical_and(below, z > 0), jnp.logical_and(above, z < nz - 1))
        where = pl.ds(at128(j, rows) if rows % 128 == 0 else pl.multiple_of(j * rows, 16), rows)
        own = part(j)

        @pl.when(got)
        def _():
            self.copy(j, j, 0).wait_recv()
            self.slots[where, :] = (self.slots[where, :].astype(F32) + own.astype(F32)).astype(BF)

        @pl.when(jnp.logical_not(got))
        def _():
            self.slots[where, :] = own.astype(BF)

        @pl.when(below)
        def _():
            self.copy(j, j, 1).start()

        @pl.when(above)
        def _():
            self.copy(j, jnp.where(z - 1 == j, nz, j), -1).start()

    def take(self, total):
        z, nz = self.z, self.nz

        @pl.when(z > 0)
        def _():
            self.copy(z, z, 0).wait_recv()
            total[...] += rows_at(self.slots, z, self.rows)[...].astype(F32)

        @pl.when(z < nz - 1)
        def _():
            self.copy(z, nz, 0).wait_recv()
            total[...] += rows_at(self.slots, nz, self.rows)[...].astype(F32)

    def drain(self):
        def gave(i):
            j = self.order(i + 1)
            self.copy(j, j, 0).wait_send()

        loop(self.nz - 1, gave)


def back_kernel(
    dims,
    dwgu, d_own, dpart, wq_all, wo_all, kv_hbm, mid_hbm, dx_hbm,
    x_ref, g_ref, q_ref, o_ref, lse_ref, gain_ref, cos_ref, sin_ref, qpos_ref, kpos_ref,
    hid_ref, gh_ref, all_d, all_g, all_u, z_out, tiny_out,
    stage, full, dslots, do_ref, kv, dkv, kslots, m32, dh, t32, dqkv, normed,
    r3, l3, r4, l4, zsrc, zslots, zlow, zown, gain_sums, tiny, tin, zin,
    r1, r2, l1, l2, own2, own_sems, send, recv, local,
):
    nz, nf, rows, d, wide, upad, nb, ng, ch = dims
    z, me = lax.axis_index("ctx"), lax.axis_index("fsdp")
    q_width, k_width = HEADS * HEAD_DIM, KV_HEADS * HEAD_DIM
    qkv = q_width + 2 * k_width
    scale = HEAD_DIM ** (-0.5)
    wr = d // nf
    place = {"nf": nf, "z": z, "me": me, "send": send, "recv": recv}
    per = Scatter.sems(nf)
    own = {"own": own2, "sems": own_sems}
    s_g = Scatter(dwgu, 0, wr, wide, r1, l1, True, base=per, **own, **place)
    s_u = Scatter(dwgu, wide, wr, wide, r2, l2, True, base=2 * per, **own, **place)
    s_o = Scatter(full, 0, wr, d, r3, l3, True, base=3 * per, **place)
    s_q = Scatter(full, 0, wr, qkv, r4, l4, True, base=4 * per, **place)
    base = 5 * per
    line = {"nz": nz, "z": z, "me": me, "send": send, "recv": recv}
    per = Chain.sems(nz)
    a_d = Chain(all_d, upad, base=base, **line)
    a_g = Chain(all_g, wr, base=base + per, **line)
    a_u = Chain(all_u, wr, base=base + 2 * per, **line)
    a_z = Chain(z_out, ch, base=base + 3 * per, **line)
    base += 4 * per
    per = Reduce.sems(nz)
    d_kv = Reduce(kslots, rows, base=base, order=a_d.order, **line)
    d_h = Reduce(dslots, rows, base=base + per, order=a_d.order, **line)
    d_z = Reduce(zslots, ch, base=base + 2 * per, order=a_d.order, **line)
    base += 3 * per

    def fetch(src, dst, i):
        copy = pltpu.make_async_copy(src, dst, local.at[i])
        copy.start()
        return copy

    def stream(src, cols, use):
        copies = []
        for t in range(src.shape[0] // 512):
            slot = stage.at[pl.ds(t % 2 * 512, 512), pl.ds(0, cols)]
            copies.append(
                pltpu.make_async_copy(src.at[pl.ds(t * 512, 512)], slot, local.at[6 + t % 2])
            )
        for copy in copies[:2]:
            copy.start()
        for t, copy in enumerate(copies):
            copy.wait()
            use(t, t % 2 * 512)
            if t + 2 < len(copies):
                copies[t + 2].start()

    mid_in = fetch(mid_hbm, m32, 1)
    dx_in = fetch(dx_hbm, dh, 2)
    kv_in = fetch(kv_hbm, kv, 3)
    d_in = fetch(d_own, rows_at(all_d, z, upad), 8)

    barrier = pltpu.get_barrier_semaphore()
    for k in range(1, nf):
        pl.semaphore_signal(barrier, inc=1, device_id=(z, me ^ k), device_id_type=MESH)
    for k in range(1, nz):
        pl.semaphore_signal(barrier, inc=1, device_id=((z + k) % nz, me), device_id_type=MESH)
    pl.semaphore_wait(barrier, nf + nz - 2)

    dkv[...] = jnp.zeros_like(dkv)
    lanes = lax.broadcasted_iota(jnp.int32, (rows, HEAD_DIM), 1)
    mine = dkv.at[pl.ds(at128(z, rows), rows)]
    third = HEADS // 3

    def norm_back():
        mid_in.wait()
        dx_in.wait()
        mid, dxn = m32[...], dh[...]
        inverse_two = lax.rsqrt(jnp.mean(mid * mid, -1, keepdims=True) + EPSILON)
        scaled = gain_ref[1:2, :] * dxn
        gain_sums[1:2, :] = jnp.sum(dxn * mid * inverse_two, 0, keepdims=True)
        dh[...] = (
            g_ref[...].astype(F32)
            + inverse_two * scaled
            - mid
            * (inverse_two * inverse_two * inverse_two)
            * jnp.mean(scaled * mid, -1, keepdims=True)
        )
        normed[...] = dh[...].astype(BF)

    def out_back():
        def one(t, r):
            do_ref[:, t * 512 : t * 512 + 512] = dot_bt(
                normed[...], stage[r : r + 512, 0:d]
            ).astype(BF)

        stream(wo_all, d, one)
        kv_in.wait()

    def w_out_grad():
        def one(t):
            c0 = at128(t, 512)
            full[pl.ds(0, q_width), pl.ds(c0, 512)] = dot_at(
                o_ref[...], normed[:, pl.ds(c0, 512)]
            ).astype(BF)

        loop(d // 512, one)

    def head(h):
        c0 = at128(h, HEAD_DIM)
        kc = at128(h // (HEADS // KV_HEADS), HEAD_DIM)
        vc = pl.multiple_of(kc + k_width, HEAD_DIM)
        q, k, v = q_ref[:, pl.ds(c0, HEAD_DIM)], kv[:, pl.ds(kc, HEAD_DIM)], kv[:, pl.ds(vc, HEAD_DIM)]
        do = do_ref[:, pl.ds(c0, HEAD_DIM)]
        lse = jnp.sum(jnp.where(lanes == h, lse_ref[...], 0.0), -1, keepdims=True)
        delta = jnp.sum(
            do.astype(F32) * o_ref[:, pl.ds(c0, HEAD_DIM)].astype(F32), -1, keepdims=True
        )
        s = jnp.where(kpos_ref[...] <= qpos_ref[...], dot_bt(q, k) * scale, MASKED)
        p = jnp.exp(s - lse)
        dkv[:, pl.ds(vc, HEAD_DIM)] += dot_at(p.astype(BF), do)
        ds = (p * (dot_bt(do, v) - delta)).astype(BF)
        dq = dot(ds, k) * scale
        dkv[:, pl.ds(kc, HEAD_DIM)] += dot_at(ds, q) * scale
        dqkv[:, pl.ds(c0, HEAD_DIM)] = turn(dq, cos_ref[...], -sin_ref[...]).astype(BF)

    def kv_part(j):
        return dkv[pl.ds(at128(j, rows), rows), :]

    def down_part(j):
        part = stage.at[pl.ds(0, rows), pl.ds(0, d)]
        fetch(rows_at(dpart, j, rows), part, 1).wait()
        return part[...]

    def z_part(j):
        return zsrc[pl.ds(pl.multiple_of(j * ch, 16), ch), :]

    def project_back():
        for h in range(KV_HEADS):
            c0 = h * HEAD_DIM
            dqkv[:, q_width + c0 : q_width + c0 + HEAD_DIM] = turn(
                mine[:, c0 : c0 + HEAD_DIM], cos_ref[...], -sin_ref[...]
            ).astype(BF)
        dqkv[:, q_width + k_width :] = mine[:, k_width:].astype(BF)

    def w_qkv_grad():
        x = x_ref[...].astype(F32)
        inverse = lax.rsqrt(jnp.mean(x * x, -1, keepdims=True) + EPSILON)
        normed[...] = (x * inverse * gain_ref[0:1, :]).astype(BF)
        s_o.drain()

        def one(t):
            c0 = at128(t, 512)
            full[pl.ds(0, d), pl.ds(c0, 512)] = dot_at(
                normed[...], dqkv[:, pl.ds(c0, 512)]
            ).astype(BF)

        loop(qkv // 512, one)

    tiny_copies = []

    def input_back():
        def one(t, r):
            t32[:, t * 512 : t * 512 + 512] = dot_bt(dqkv[...], stage[r : r + 512, :])

        stream(wq_all, qkv, one)
        x = x_ref[...].astype(F32)
        inverse = lax.rsqrt(jnp.mean(x * x, -1, keepdims=True) + EPSILON)
        dxn = t32[...]
        scaled = gain_ref[0:1, :] * dxn
        gain_one = jnp.sum(dxn * x * inverse, 0, keepdims=True)
        gain_two = gain_sums[1:2, :]
        bias = jnp.sum(dqkv[...].astype(F32), 0, keepdims=True)
        gh_ref[...] = (
            dh[...]
            + inverse * scaled
            - x * (inverse * inverse * inverse) * jnp.mean(scaled * x, -1, keepdims=True)
        ).astype(BF)

        cut = q_width + k_width
        qk, vb = cut // nf, k_width // nf
        tiny[...] = jnp.zeros_like(tiny)
        for f in range(nf):
            r = slice(8 * f, 8 * f + 1)
            tiny[r, 0:qk] = bias[:, f * qk : (f + 1) * qk]
            tiny[r, qk : qk + vb] = bias[:, cut + f * vb : cut + (f + 1) * vb]
            tiny[r, qk + vb : qk + vb + ng] = gain_one[:, f * ng : (f + 1) * ng]
            tiny[r, qk + vb + ng : qk + vb + 2 * ng] = gain_two[:, f * ng : (f + 1) * ng]
        own = pl.ds(pl.multiple_of(me * 8, 8), 8)
        tin[own, :] = tiny[own, :]
        for k in range(1, nf):
            copy = remote(
                rows_at(tiny, me ^ k, 8), rows_at(tin, me, 8),
                send.at[base + k], recv.at[base + k], z, me ^ k,
            )
            copy.start()
            tiny_copies.append(copy)

    def tiny_along():
        for copy in tiny_copies:
            copy.wait_recv()
        total = tin[0:8, :]
        for f in range(1, nf):
            total = total + tin[8 * f : 8 * f + 8, :]
        zin[pl.ds(pl.multiple_of(z * 8, 8), 8), :] = total
        for k in range(1, nz):
            copy = remote(
                rows_at(zin, z, 8), rows_at(zin, z, 8),
                send.at[base + nf + k], recv.at[base + nf + k], (z + k) % nz, me,
            )
            copy.start()
            tiny_copies.append(copy)

    def z_take():
        zown[...] = z_part(z).astype(F32)
        d_z.take(zown)
        zlow[...] = zown[...].astype(BF)
        fetch(zlow, rows_at(z_out, z, ch), 2).wait()

    def h_take():
        m32[...] += down_part(z).astype(F32)
        d_h.take(m32)
        hid_ref[...] = m32[...].astype(BF)

    a_d.begin(d_own)
    s_g.swap()
    norm_back()
    out_back()
    w_out_grad()
    s_o.swap()
    s_g.merge()
    s_g.first()
    s_u.swap()
    a_d.forward(1)
    for k in range(2, nz - 1):
        a_d.forward(k)
    loop(third, head)
    loop(third, lambda h: head(h + third))
    loop(third, lambda h: head(h + 2 * third))
    s_u.merge()
    s_g.second()
    s_u.first()
    a_d.forward(nz - 1)
    d_kv.give(0, kv_part)
    for i in range(1, nz - 2):
        d_kv.give(i, kv_part)
    d_kv.give(nz - 2, kv_part)
    s_o.merge()
    s_o.first()
    s_g.last(s_g.block(0))
    fetch(s_g.block(0), rows_at(all_g, z, wr), 4).wait()
    a_g.begin()
    s_u.second()
    a_g.forward(1)
    for k in range(2, nz - 1):
        a_g.forward(k)
    s_o.second()
    d_kv.take(mine)
    d_h.give(0, down_part)
    project_back()
    a_g.forward(nz - 1)
    w_qkv_grad()
    s_q.swap()
    s_o.last(zsrc.at[pl.ds(0, wr), pl.ds(0, d)])
    s_u.last(s_u.block(0))
    fetch(s_u.block(0), rows_at(all_u, z, wr), 5).wait()
    s_q.merge()
    s_q.first()
    a_u.begin()
    a_u.forward(1)
    s_q.second()
    for k in range(2, nz - 1):
        a_u.forward(k)
    a_u.forward(nz - 1)
    input_back()
    s_q.last(zsrc.at[pl.ds(0, wr), pl.ds(d, qkv)])
    d_z.give(0, z_part)
    tiny_along()
    for i in range(1, nz - 2):
        d_z.give(i, z_part)
    for i in range(1, nz - 2):
        d_h.give(i, down_part)
    d_z.give(nz - 2, z_part)
    d_h.give(nz - 2, down_part)
    for k in range(1, nz):
        a_u.arrive(k)
    z_take()
    for k in range(1, nz):
        a_g.arrive(k)
    a_z.begin()
    a_z.forward(1)
    for k in range(1, nz):
        a_d.arrive(k)
    for k in range(2, nz - 1):
        a_z.forward(k)
    a_z.forward(nz - 1)
    h_take()
    for k in range(1, nz):
        a_z.arrive(k)
    for copy in tiny_copies[nf - 1 :]:
        copy.wait_recv()
    total = zin[0:8, :]
    for j in range(1, nz):
        total = total + zin[8 * j : 8 * j + 8, :]
    tiny_out[...] = total
    d_in.wait()
    for item in (s_g, s_u, s_o, s_q, a_d, a_g, a_u, a_z, d_kv, d_h, d_z):
        item.drain()
    for copy in tiny_copies:
        copy.wait_send()


def back(dims, *args):
    nz, nf, rows, d, wide, upad, nb, ng, ch = dims
    q_width, k_width = HEADS * HEAD_DIM, KV_HEADS * HEAD_DIM
    qkv = q_width + 2 * k_width
    tokens, chips, wr = nz * rows, nf // 2, d // nf
    tiny = -(-((qkv + 2 * d) // nf) // 128) * 128
    any_, vm = pl.BlockSpec(memory_space=pl.ANY), pl.BlockSpec(memory_space=pltpu.VMEM)
    out = jax.ShapeDtypeStruct
    sems = 5 * Scatter.sems(nf) + 4 * Chain.sems(nz) + 3 * Reduce.sems(nz) + nf + nz
    pieces = [(upad, d), (wr, wide), (wr, wide)]
    return pl.pallas_call(
        functools.partial(back_kernel, dims),
        in_specs=[any_] * 8 + [vm] * 10,
        out_specs=[vm, vm] + [any_] * 4 + [vm],
        out_shape=[out((rows, d), BF), out((rows, d), BF)]
        + [out((nz * r, c), BF) for r, c in pieces]
        + [out((nz * ch, d + qkv), BF), out((8, tiny), F32)],
        scratch_shapes=[
            pltpu.VMEM((1024, qkv), BF),
            pltpu.VMEM((d, qkv), BF),
            pltpu.VMEM(((nz + 1) * rows, d), BF),
            pltpu.VMEM((rows, q_width), BF),
            pltpu.VMEM((tokens, 2 * k_width), BF),
            pltpu.VMEM((tokens, 2 * k_width), F32),
            pltpu.VMEM(((nz + 1) * rows, 2 * k_width), BF),
            pltpu.VMEM((rows, d), F32),
            pltpu.VMEM((rows, d), F32),
            pltpu.VMEM((rows, d), F32),
            pltpu.VMEM((rows, qkv), BF),
            pltpu.VMEM((rows, d), BF),
            pltpu.VMEM((chips * wr, d), BF),
            pltpu.VMEM(((chips - 1) * wr, d), BF),
            pltpu.VMEM((chips * wr, qkv), BF),
            pltpu.VMEM(((chips - 1) * wr, qkv), BF),
            pltpu.VMEM((nz * ch, d + qkv), BF),
            pltpu.VMEM(((nz + 1) * ch, d + qkv), BF),
            pltpu.VMEM((ch, d + qkv), BF),
            pltpu.VMEM((ch, d + qkv), F32),
            pltpu.VMEM((8, d), F32),
            pltpu.VMEM((nf * 8, tiny), F32),
            pltpu.VMEM((nf * 8, tiny), F32),
            pltpu.VMEM((nz * 8, tiny), F32),
            pltpu.VMEM((chips * wr, wide), BF),
            pltpu.VMEM((chips * wr, wide), BF),
            pltpu.VMEM(((chips - 1) * wr, wide), BF),
            pltpu.VMEM(((chips - 1) * wr, wide), BF),
            pltpu.VMEM((2 * wr, wide), BF),
            pltpu.SemaphoreType.DMA((2,)),
            pltpu.SemaphoreType.DMA((sems,)),
            pltpu.SemaphoreType.DMA((sems,)),
            pltpu.SemaphoreType.DMA((9,)),
        ],
        compiler_params=pltpu.CompilerParams(
            collective_id=1, has_side_effects=True, vmem_limit_bytes=VMEM_LIMIT
        ),
    )(*args)


def shards(
    hidden_in, w_qkv, b_qkv, w_out, w_gate_up, w_down, gain_attn, gain_mlp, block_order, cotangent
):
    nz, nf = lax.axis_size("ctx"), lax.axis_size("fsdp")
    z, me = lax.axis_index("ctx"), lax.axis_index("fsdp")
    q_width, k_width = HEADS * HEAD_DIM, KV_HEADS * HEAD_DIM
    rows = hidden_in.shape[1]
    piece_len = rows // 2
    ff = w_gate_up.shape[1] // 2
    unit = ff // (nf * nz)
    order_row = block_order[0]
    all_places = (
        order_row[:, None] * piece_len + jnp.arange(piece_len, dtype=jnp.int32)[None, :]
    ).reshape(-1)
    my_places = lax.dynamic_slice_in_dim(all_places, z * rows, rows)
    cosine, sine_table = angle_tables(my_places)
    cos2 = jnp.concatenate([cosine, cosine], 1)
    sin2 = jnp.concatenate([-sine_table, sine_table], 1)

    upad = -(-unit // 16) * 16
    wide = nf * upad
    nb, ng = b_qkv.shape[0], gain_attn.shape[0]
    d = hidden_in.shape[2]
    small = jnp.concatenate([b_qkv, gain_attn, gain_mlp])
    small = jnp.pad(small[None], ((0, 15), (0, -small.shape[0] % 128)))
    grad_low = cotangent[0]
    (whole_qkv, whole_out, q_low, kv_all, attn_low, lse, middle, grad_normed_two, gains, gate_up_local, down_part,
     down_own, *_) = front(
        (nz, nf, rows, d, ff, wide, upad, nb, ng),
        w_qkv, small, w_out, w_gate_up, w_down, hidden_in[0], grad_low, cos2, sin2,
        my_places[:, None], all_places[None, :],
    )
    ch = -(-(d // (nf * nz)) // 16) * 16
    hidden, grad_hidden, down_all, gate_all, up_all, attn_all, tiny = back(
        (nz, nf, rows, d, wide, upad, nb, ng, ch),
        gate_up_local, down_own, down_part, whole_qkv, whole_out, kv_all, middle, grad_normed_two,
        hidden_in[0], grad_low, q_low, attn_low, lse, gains, cos2, sin2, my_places[:, None], all_places[None, :],
    )
    e1 = (q_width + k_width) // nf
    e2 = e1 + k_width // nf
    e3 = e2 + ng
    shard = d // nf
    cuts = (0, e1, e2, e3, e3 + ng)
    if unit % 8 == 0 and shard % (16 * nz) == 0 and ch * nz == shard:
        gu_grad, down_grad, qkv_grad, out_grad, hidden, grad_hidden, *smalls = finish(
            gate_all, up_all, down_all, attn_all, tiny, hidden, grad_hidden, nz, nf, ff, cuts
        )
        b_qk, b_v, g_one, g_two = (item[0] for item in smalls)
    else:
        gu_grad = unpack(gate_all, up_all, nz, nf, ff)
        down_grad = down_all.reshape(nz, upad, d)[:, :unit].reshape(nz * unit, d).astype(F32)
        qkv_grad = attn_all[:shard, d:].astype(F32)
        out_grad = attn_all[:shard, :d].astype(F32)
        b_qk, b_v, g_one, g_two = (tiny[0, lo:hi] for lo, hi in zip(cuts, cuts[1:]))
    return (
        hidden[None],
        grad_hidden[None],
        qkv_grad,
        b_qk,
        b_v,
        out_grad,
        gu_grad,
        down_grad,
        g_one,
        g_two,
    )


def solution(mesh):
    placed = (
        P("fsdp", "ctx", None),
        P("fsdp", None),
        P("fsdp"),
        P("fsdp", None),
        P("fsdp", None),
        P("fsdp", None),
        P("fsdp"),
        P("fsdp"),
        P("fsdp", None),
        P("fsdp", "ctx", None),
    )
    return jax.shard_map(
        shards,
        mesh=mesh,
        in_specs=placed,
        out_specs=(
            P("fsdp", "ctx", None),
            P("fsdp", "ctx", None),
            P("fsdp", None),
            P("fsdp"),
            P("fsdp"),
            P("fsdp", None),
            P("fsdp", None),
            P("fsdp", None),
            P("fsdp"),
            P("fsdp"),
        ),
        check_vma=False,
    )
```

```python
import functools

import jax
import jax.numpy as jnp
from jax import lax
from jax.experimental import pallas as pl
from jax.experimental.pallas import tpu as pltpu
from jax.sharding import PartitionSpec as P

HEADS = 12
KV_HEADS = 2
HEAD_DIM = 128
EPSILON = 1e-06
THETA = 1000000.0
MASKED = -1e30
BF = jnp.bfloat16
F32 = jnp.float32


def dot(a, b):
    return jnp.dot(a, b, preferred_element_type=F32)


def dot_bt(a, b):
    return lax.dot_general(a, b, (((1,), (1,)), ((), ())), preferred_element_type=F32)


def dot_at(a, b):
    return lax.dot_general(a, b, (((0,), (0,)), ((), ())), preferred_element_type=F32)


def angle_tables(places):
    half_dim = HEAD_DIM // 2
    freqs = THETA ** (-(jnp.arange(half_dim).astype(F32) * 2.0 / HEAD_DIM))
    angles = places.astype(F32)[:, None] * freqs[None, :]
    return (jnp.cos(angles), jnp.sin(angles))


def half_rows(rows):
    return -(-rows // 32) * 16


def pieces_of(columns, width, rows, room):
    n = next(n for n in range(1, columns) if columns % (128 * n) == 0 and columns // n <= width)
    assert n * rows <= room
    return n


def pack(k, nz, nf, ff, unit, upad, rows, width, held, out):
    for h in range(2):
        for f in range(nf):
            src = h * ff + f * (ff // nf) + k * unit
            dst = (h * nf + f) * upad
            done = 0
            while done < unit:
                piece, at = divmod(src + done, width)
                n = min(unit - done, width - at)
                out[:, dst + done : dst + done + n] = held[
                    piece * rows : (piece + 1) * rows, at : at + n
                ]
                done += n
            if upad > unit:
                out[:, dst + unit : dst + upad] = jnp.zeros((rows, upad - unit), out.dtype)


def unpack_kernel(nz, nf, ff, unit, upad, *refs):
    out_ref = refs[-1]
    for k in range(nz):
        for h in range(2):
            for f in range(nf):
                src = f * upad
                dst = h * ff + f * (ff // nf) + k * unit
                part = refs[h * nz + k]
                out_ref[:, dst : dst + unit] = part[:, src : src + unit].astype(F32)


def unpack(gate, up, nz, nf, ff):
    rows, wide = gate.shape[0] // nz, gate.shape[1]
    step = 32
    specs = [
        pl.BlockSpec((step, wide), lambda i, k=k: (k * (rows // step) + i, 0)) for k in range(nz)
    ]
    return pl.pallas_call(
        functools.partial(unpack_kernel, nz, nf, ff, ff // (nf * nz), wide // nf),
        grid=(rows // step,),
        in_specs=specs * 2,
        out_specs=pl.BlockSpec((step, 2 * ff), lambda i: (i, 0)),
        out_shape=jax.ShapeDtypeStruct((rows, 2 * ff), F32),
    )(*[gate] * nz, *[up] * nz)


def finish_kernel(nz, nf, ff, unit, upad, cuts, *refs):
    gates, ups = refs[:nz], refs[nz : 2 * nz]
    down, attn, tiny, hid, gh = refs[2 * nz : 2 * nz + 5]
    gu_out, down_out, qkv_out, out_out, hid_out, gh_out, *tiny_outs = refs[2 * nz + 5 :]
    unpack_kernel(nz, nf, ff, unit, upad, *gates, *ups, gu_out)
    down_out[...] = down[0:unit, :].astype(F32)
    d = out_out.shape[1]
    qkv_out[...] = attn[:, d:].astype(F32)
    out_out[...] = attn[:, :d].astype(F32)
    hid_out[...] = hid[...]
    gh_out[...] = gh[...]

    @pl.when(pl.program_id(0) == 0)
    def _():
        for out, lo, hi in zip(tiny_outs, cuts, cuts[1:]):
            out[...] = tiny[0:1, lo:hi]


def finish(gate, up, down, attn, tiny, hid, gh, nz, nf, ff, cuts):
    rows, wide = gate.shape[0] // nz, gate.shape[1]
    unit, upad, d = ff // (nf * nz), wide // nf, hid.shape[1]
    step = rows // nz
    along = [
        pl.BlockSpec((step, wide), lambda i, k=k: (k * (rows // step) + i, 0)) for k in range(nz)
    ]
    part = hid.shape[0] // nz

    def by_step(r, c):
        return pl.BlockSpec((r, c), lambda i: (i, 0))

    def still(c):
        return pl.BlockSpec((1, c), lambda i: (0, 0))

    qkv = attn.shape[1] - d
    sizes = [hi - lo for lo, hi in zip(cuts, cuts[1:])]
    out = jax.ShapeDtypeStruct
    return pl.pallas_call(
        functools.partial(finish_kernel, nz, nf, ff, unit, upad, cuts),
        grid=(nz,),
        in_specs=along * 2
        + [
            by_step(upad, d),
            by_step(step, d + qkv),
            pl.BlockSpec(tiny.shape, lambda i: (0, 0)),
            by_step(part, d),
            by_step(part, d),
        ],
        out_specs=[
            by_step(step, 2 * ff),
            by_step(unit, d),
            by_step(step, qkv),
            by_step(step, d),
            by_step(part, d),
            by_step(part, d),
        ]
        + [still(n) for n in sizes],
        out_shape=[
            out((rows, 2 * ff), F32),
            out((nz * unit, d), F32),
            out((rows, qkv), F32),
            out((rows, d), F32),
            out(hid.shape, BF),
            out(hid.shape, BF),
        ]
        + [out((1, n), F32) for n in sizes],
        compiler_params=pltpu.CompilerParams(vmem_limit_bytes=VMEM_LIMIT),
    )(*[gate] * nz, *[up] * nz, down, attn, tiny, hid, gh)


MESH = pl.DeviceIdType.MESH
VMEM_LIMIT = 63 * 2**20


def remote(src, dst, send, recv, z, f):
    return pltpu.make_async_remote_copy(
        src_ref=src, dst_ref=dst, send_sem=send, recv_sem=recv, device_id=(z, f), device_id_type=MESH
    )


def rows_at(ref, index, count):
    return ref.at[pl.ds(pl.multiple_of(index * count, count), count)]


class PlaneGather:
    def __init__(self, src, dst, rows, nf, z, me, send, recv, local, base, bounce=None):
        self.src, self.dst, self.rows, self.nf, self.z, self.me = src, dst, rows, nf, z, me
        self.send, self.recv, self.base = send, recv, base
        home = rows_at(dst, me, rows)
        if bounce is None:
            self.local = (pltpu.make_async_copy(src, home, local),)
        else:
            self.local = (
                pltpu.make_async_copy(src, bounce, local),
                pltpu.make_async_copy(bounce, home, local),
            )
        self.sent = []
        self.cut = half_rows(rows)
        self.swaps = {}

    @staticmethod
    def sems(nf):
        return 2 * nf

    def slot(self, k, lo=0, hi=None):
        hi = self.rows if hi is None else hi
        start = pl.multiple_of((self.me ^ k) * self.rows, 16) + lo
        return self.dst.at[pl.ds(pl.multiple_of(start, 16), hi - lo)]

    def push(self, index, src, dst, flip_by):
        copy = remote(
            src, dst, self.send.at[self.base + index], self.recv.at[self.base + index],
            self.z, self.me ^ flip_by,
        )
        copy.start()
        self.sent.append(copy)
        return copy

    def begin(self):
        self.local[0].start()
        self.direct = {}
        for k in (2, 4) if self.nf == 8 else range(2, self.nf, 2):
            self.direct[k] = self.push(k, self.src, self.slot(0), k)
        self.swaps[0] = self.push(1, self.src, self.slot(0), 1)

    def swap(self, k):
        self.swaps[k] = self.push(k + 1, self.slot(k), self.slot(k), 1)

    def middle(self):
        for one, two in zip(self.local, self.local[1:]):
            one.wait()
            two.start()
        for k, copy in self.direct.items():
            copy.wait_recv()
            if self.nf == 8:
                if k == 2:
                    self.far_a = self.push(6, self.slot(2, 0, self.cut), self.slot(2, 0, self.cut), 4)
                elif self.cut < self.rows:
                    self.far_b = self.push(
                        8, self.slot(4, self.cut), self.slot(4, self.cut), 2
                    )
            self.swap(k)

    def late(self):
        if self.nf == 8:
            self.far_a.wait_recv()
            if self.cut < self.rows:
                self.far_b.wait_recv()
            self.swap(6)

    def finish(self):
        self.local[-1].wait()
        for copy in self.swaps.values():
            copy.wait_recv()

    def drain(self):
        for copy in self.sent:
            copy.wait_send()


class Chain:
    def __init__(self, buf, rows, nz, z, me, send, recv, base):
        self.buf, self.rows, self.nz, self.z, self.me = buf, rows, nz, z, me
        self.send, self.recv, self.base = send, recv, base

    @staticmethod
    def sems(nz):
        return nz + 2

    def copy(self, j, sem, step, src=None):
        slot = rows_at(self.buf, j, self.rows)
        return remote(
            slot if src is None else src, slot, self.send.at[self.base + sem], self.recv.at[self.base + j], self.z + step, self.me
        )

    def order(self, k):
        z, nz = self.z, self.nz
        below, above = z, nz - 1 - z
        m = jnp.minimum(below, above)
        near = jnp.where(k % 2 == 1, z - (k + 1) // 2, z + k // 2)
        far = jnp.where(above > below, z + (k - m), z - (k - m))
        return jnp.where(k <= 2 * m, near, far)

    def begin(self, src=None):
        z, nz = self.z, self.nz

        @pl.when(z < nz - 1)
        def _():
            self.copy(z, nz, 1, src).start()

        @pl.when(z > 0)
        def _():
            self.copy(z, nz + 1, -1, src).start()

    def passing(self, j):
        z, nz = self.z, self.nz
        return jnp.logical_and(j < z, z < nz - 1), jnp.logical_and(j > z, z > 0)

    def forward(self, k):
        j = self.order(k)
        up, down = self.passing(j)

        @pl.when(up)
        def _():
            self.copy(j, j, 1).wait_recv()
            self.copy(j, j, 1).start()

        @pl.when(down)
        def _():
            self.copy(j, j, -1).wait_recv()
            self.copy(j, j, -1).start()

    def arrive(self, k):
        j = self.order(k)
        up, down = self.passing(j)

        @pl.when(jnp.logical_not(jnp.logical_or(up, down)))
        def _():
            self.copy(j, j, 0).wait_recv()

    def drain(self):
        z, nz = self.z, self.nz

        @pl.when(z < nz - 1)
        def _():
            self.copy(z, nz, 1).wait_send()

        @pl.when(z > 0)
        def _():
            self.copy(z, nz + 1, -1).wait_send()

        def one(k, carry):
            j = self.order(k)
            up, down = self.passing(j)

            @pl.when(jnp.logical_or(up, down))
            def _():
                self.copy(j, j, 0).wait_send()

            return carry

        lax.fori_loop(1, nz, one, 0)


class Scatter:
    def __init__(self, src, c0, rows, cols, recv4, land, inside, nf, z, me, send, recv, base, own=None, sems=None):
        self.src, self.c0, self.rows, self.cols = src, c0, rows, cols
        self.recv4, self.land, self.inside = recv4, land, inside
        self.nf, self.z, self.me, self.send, self.recv, self.base = nf, z, me, send, recv, base
        self.chips, self.chip, self.core = nf // 2, me // 2, me % 2
        self.cut = half_rows(rows)
        self.sent = []
        self.got = {}
        self.own, self.own_sems = own, sems

    @staticmethod
    def sems(nf):
        return nf

    def push(self, index, src, dst, flip_by):
        copy = remote(
            src, dst, self.send.at[self.base + index], self.recv.at[self.base + index],
            self.z, self.me ^ flip_by,
        )
        copy.start()
        self.sent.append(copy)
        self.got[index] = copy

    def mine(self, ref, start, n):
        return ref.at[pl.ds(pl.multiple_of(start, 16), n)]

    def block(self, k, lo=0, hi=None):
        hi = self.rows if hi is None else hi
        return self.mine(self.recv4, (self.chip ^ k) * self.rows + lo, hi - lo)

    def swap(self):
        for p in range(self.chips):
            start = pl.multiple_of((2 * p + 1 - self.core) * self.rows, 16)
            src = self.src.at[pl.ds(start, self.rows), pl.ds(self.c0, self.cols)]
            self.push(p, src, self.mine(self.recv4, p * self.rows, self.rows), 1)

    def merge(self):
        rows, cols = self.rows, self.cols
        if self.own is not None:
            for p in range(min(2, self.chips)):
                self.fetch(p).start()
        for p in range(self.chips):
            self.got[p].wait_recv()
        if self.inside:
            for p in range(self.chips):
                start = pl.multiple_of((2 * p + self.core) * rows, 16)
                if self.own is None:
                    own, first = self.src, start
                else:
                    self.fetch(p).wait()
                    own, first = self.own, p % 2 * rows
                step = rows if rows <= 96 else rows // 2
                for i in range(0, rows, step):
                    where = pl.ds(p * rows + i, step)
                    part = own[pl.ds(pl.multiple_of(first + i, 16), step), pl.ds(0, cols)]
                    self.recv4[where, :] = (
                        self.recv4[where, :].astype(F32) + part.astype(F32)
                    ).astype(BF)
                if self.own is not None and p + 2 < self.chips:
                    self.fetch(p + 2).start()
            return
        step = rows if rows <= 96 else rows // 2
        n = rows // step
        core, col = self.core, self.c0 // cols
        own = pl.BlockSpec((step, cols), lambda p, i: ((2 * p + core) * n + i, col))
        held = pl.BlockSpec((step, cols), lambda p, i: (p * n + i, 0))
        pltpu.emit_pipeline(
            add_two, grid=(self.chips, n), in_specs=[own, held], out_specs=[held]
        )(self.src, self.recv4, self.recv4)

    def fetch(self, p):
        start = pl.multiple_of((2 * p + self.core) * self.rows, 16)
        return pltpu.make_async_copy(
            self.src.at[pl.ds(start, self.rows), pl.ds(self.c0, self.cols)],
            self.own.at[pl.ds(p % 2 * self.rows, self.rows)],
            self.own_sems.at[p % 2],
        )

    def add(self, out, parts, n):
        if self.inside:
            total = parts[0][...].astype(F32)
            for part in parts[1:]:
                total = total + part[...].astype(F32)
            out[...] = total.astype(BF)
            return
        step = n if n <= 96 else n // 2
        spec = pl.BlockSpec((step, self.cols), lambda i: (i, 0))
        body = add_two if len(parts) == 2 else add_all
        pltpu.emit_pipeline(
            body, grid=(n // step,), in_specs=[spec] * len(parts), out_specs=[spec]
        )(*parts, out)

    def first(self):
        base, rows, cut = self.chips, self.rows, self.cut
        if self.nf == 8:
            self.push(base, self.block(3, 0, cut), self.land.at[pl.ds(0, cut)], 2)
            self.push(base + 1, self.block(3, cut), self.land.at[pl.ds(cut, rows - cut)], 4)
        else:
            for k in range(1, self.chips):
                self.push(base + k - 1, self.block(k), self.land.at[pl.ds((k - 1) * rows, rows)], 2 * k)

    def second(self):
        if self.nf != 8:
            return
        base, rows, cut = self.chips, self.rows, self.cut
        self.got[base].wait_recv()
        to_y = self.block(2, 0, cut)
        self.add(to_y, [to_y, self.land.at[pl.ds(0, cut)]], cut)
        self.push(base + 3, self.block(2), self.land.at[pl.ds(2 * rows, rows)], 4)
        self.got[base + 1].wait_recv()
        to_x = self.block(1, cut)
        self.add(to_x, [to_x, self.land.at[pl.ds(cut, rows - cut)]], rows - cut)
        self.push(base + 2, self.block(1), self.land.at[pl.ds(rows, rows)], 2)

    def last(self, out):
        base, rows = self.chips, self.rows
        if self.nf == 8:
            incoming = [(base + 2, rows), (base + 3, 2 * rows)]
        else:
            incoming = [(base + k - 1, (k - 1) * rows) for k in range(1, self.chips)]
        for index, _ in incoming:
            self.got[index].wait_recv()
        parts = [self.block(0)] + [self.land.at[pl.ds(at, rows)] for _, at in incoming]
        self.add(out, parts, rows)

    def drain(self):
        for copy in self.sent:
            copy.wait_send()
        self.sent = []


def add_two(a, b, out):
    out[...] = (a[...].astype(F32) + b[...].astype(F32)).astype(BF)


def add_all(*refs):
    total = refs[0][...].astype(F32)
    for ref in refs[1:-1]:
        total = total + ref[...].astype(F32)
    refs[-1][...] = total.astype(BF)


def greet_ctx_and_plane(nz, nf, z, me):
    barrier = pltpu.get_barrier_semaphore()
    flips = (1, 2, 4) if nf == 8 else (1,) + tuple(range(2, nf, 2))
    for k in flips:
        pl.semaphore_signal(barrier, inc=1, device_id=(z, me ^ k), device_id_type=MESH)

    @pl.when(z < nz - 1)
    def _():
        pl.semaphore_signal(barrier, inc=1, device_id=(z + 1, me), device_id_type=MESH)

    @pl.when(z > 0)
    def _():
        pl.semaphore_signal(barrier, inc=1, device_id=(z - 1, me), device_id_type=MESH)

    inner = jnp.logical_and(z > 0, z < nz - 1)

    @pl.when(inner)
    def _():
        pl.semaphore_wait(barrier, len(flips) + 2)

    @pl.when(jnp.logical_not(inner))
    def _():
        pl.semaphore_wait(barrier, len(flips) + 1)


def loop(n, body):
    def step(i, carry):
        body(i)
        return carry

    lax.fori_loop(0, n, step, 0)


def at128(i, n):
    return i * n if isinstance(i, int) else pl.multiple_of(i * n, n)


def turn(t, cos2, sin2):
    return t * cos2 + pltpu.roll(t, HEAD_DIM // 2, 1) * sin2


def front_kernel(
    dims,
    wq, sm, wo, w_gu, w_dn, x_ref, g_ref, cos_ref, sin_ref, qpos_ref, kpos_ref,
    wq_all, wo_all, q_ref, kv_out, o_ref, lse_ref, mid_ref, dx_ref, gain_ref, dwgu, dpart, d_own, dwd, r0, l0,
    stage, gu, dnb, g_all, x_all, act, dgu, smb, kv, bias, ybuf, packed, down, send, recv, local,
):
    nz, nf, rows, d, ff, wide, upad, nb, ng = dims
    z, me = lax.axis_index("ctx"), lax.axis_index("fsdp")
    q_width, k_width = HEADS * HEAD_DIM, KV_HEADS * HEAD_DIM
    qkv = q_width + 2 * k_width
    scale = HEAD_DIM ** (-0.5)
    wr = d // nf
    per = PlaneGather.sems(nf)
    q_cols, kv_cols = pl.ds(0, q_width), pl.ds(q_width, 2 * k_width)
    plane = [
        PlaneGather(src, dst, r, nf, z, me, send, recv, local.at[i], i * per, bounce)
        for i, (src, dst, r, bounce) in enumerate(
            [
                (wq.at[:, q_cols], wq_all.at[:, q_cols], wr, ybuf.at[pl.ds(wr, wr)]),
                (wq.at[:, kv_cols], wq_all.at[:, kv_cols], wr, ybuf.at[pl.ds(0, wr), pl.ds(0, 2 * k_width)]),
                (sm, smb, 16, None),
                (wo, wo_all, wr, ybuf.at[pl.ds(0, wr)]),
                (packed, gu, wr, None),
                (down, dnb, upad, None),
            ]
        )
    ]
    p_q, p_kv, p_s, p_o, p_gu, p_d = plane
    base = len(plane) * per
    chain = [
        Chain(buf, rows, nz, z, me, send, recv, base + i * Chain.sems(nz))
        for i, buf in enumerate([g_all, kv, x_all])
    ]
    c_g, c_kv, c_x = chain
    base += len(chain) * Chain.sems(nz)
    s_d = Scatter(dwd, 0, upad, d, r0, l0, False, nf, z, me, send, recv, base)
    base += Scatter.sems(nf)
    spare = len(plane)

    unit = ff // (nf * nz)
    n = pieces_of(2 * ff, 2 * wide, wr, nz * rows)
    width = 2 * ff // n
    loads = [
        pltpu.make_async_copy(
            w_gu.at[:, pl.ds(i * width, width)],
            dgu.at[pl.ds(i * wr, wr), pl.ds(0, width)],
            local.at[spare + 1 + i],
        )
        for i in range(n)
    ]
    fetched = upad + 16
    down_in = act.at[pl.ds(0, fetched), pl.ds(0, d)] if wide >= d else dgu.at[pl.ds(n * wr, fetched), pl.ds(0, d)]

    def down_load(k):
        start = min(unit * k // 16 * 16, ff // nf - fetched)
        copy = pltpu.make_async_copy(w_dn.at[pl.ds(start, fetched)], down_in, local.at[spare + 1 + n])
        return copy, unit * k - start

    def part_loads():
        for copy in loads:
            copy.start()
        for k in range(nz):

            @pl.when(z == k)
            def _():
                down_load(k)[0].start()

    def part_pack():
        for copy in loads:
            copy.wait()
        for k in range(nz):

            @pl.when(z == k)
            def _():
                pack(k, nz, nf, ff, unit, upad, wr, width, dgu, packed)
                copy, off = down_load(k)
                copy.wait()
                down[0:unit, :] = down_in[...].astype(F32)[off : off + unit].astype(BF)
                if upad > unit:
                    down[unit:upad, :] = jnp.zeros((upad - unit, d), BF)

    g_copy = pltpu.make_async_copy(g_ref, rows_at(g_all, z, rows), local.at[spare])
    g_copy.start()
    greet_ctx_and_plane(nz, nf, z, me)
    p_s.begin()
    p_kv.begin()
    g_copy.wait()
    c_g.begin()
    part_loads()

    x = x_ref[...].astype(F32)
    inverse = lax.rsqrt(jnp.mean(x * x, -1, keepdims=True) + EPSILON)

    p_s.middle()
    p_kv.middle()
    p_q.begin()
    p_s.late()
    p_kv.late()
    p_s.finish()
    for f in range(nf):
        row = smb[f * 16 : (f + 1) * 16, :].astype(F32)[0:1]
        bias[0:1, f * nb : (f + 1) * nb] = row[:, :nb]
        gain_ref[0:1, f * ng : (f + 1) * ng] = row[:, nb : nb + ng]
        gain_ref[1:2, f * ng : (f + 1) * ng] = row[:, nb + ng : nb + 2 * ng]
    normed = (x * inverse * gain_ref[0:1, :]).astype(BF)
    x_all[pl.ds(at128(z, rows), rows), :] = normed

    def fetch_qkv(c0, n):
        copy = pltpu.make_async_copy(
            wq_all.at[:, pl.ds(c0, n)], stage.at[pl.ds(0, d), pl.ds(c0, n)], local.at[spare]
        )
        copy.start()
        copy.wait()

    p_kv.finish()
    fetch_qkv(q_width, 2 * k_width)

    def project(t):
        c0 = at128(t, 2 * HEAD_DIM)
        y = dot(
            x_all[pl.ds(at128(z, rows), rows), :], stage[pl.ds(0, d), pl.ds(c0, 2 * HEAD_DIM)]
        ) + bias[0:1, pl.ds(c0, 2 * HEAD_DIM)]
        return y, c0

    def project_v(t):
        y, c0 = project(t)
        kv[pl.ds(at128(z, rows), rows), pl.ds(pl.multiple_of(c0 - q_width, 256), 256)] = y.astype(BF)

    def turned(y):
        halves = [
            turn(y[:, h * HEAD_DIM : (h + 1) * HEAD_DIM], cos_ref[...], sin_ref[...]).astype(BF)
            for h in range(2)
        ]
        return jnp.concatenate(halves, 1)

    project_v((q_width + k_width) // 256)
    y, _ = project(q_width // 256)
    kv[pl.ds(at128(z, rows), rows), 0:k_width] = turned(y)
    c_kv.begin()
    p_q.middle()
    p_o.begin()
    part_pack()
    for k in range(1, nz - 1):
        c_kv.forward(k)
    p_q.late()
    p_q.finish()
    fetch_qkv(0, q_width)
    c_kv.forward(nz - 1)

    def project_q(t):
        y, c0 = project(t)
        q_ref[:, pl.ds(c0, 256)] = turned(y)

    loop(q_width // 256, project_q)
    p_o.middle()
    p_gu.begin()
    for k in range(1, nz):
        c_kv.arrive(k)
    for k in range(1, nz - 1):
        c_g.forward(k)

    lanes = lax.broadcasted_iota(jnp.int32, (rows, HEAD_DIM), 1)
    lse_ref[...] = jnp.zeros_like(lse_ref)

    def head(h):
        c0 = at128(h, HEAD_DIM)
        kc = at128(h // (HEADS // KV_HEADS), HEAD_DIM)
        vc = pl.multiple_of(kc + k_width, HEAD_DIM)
        s = dot_bt(q_ref[:, pl.ds(c0, HEAD_DIM)], kv[:, pl.ds(kc, HEAD_DIM)]) * scale
        s = jnp.where(kpos_ref[...] <= qpos_ref[...], s, MASKED)
        top = jnp.max(s, -1, keepdims=True)
        p = jnp.exp(s - top)
        total = jnp.sum(p, -1, keepdims=True)
        o = dot(p.astype(BF), kv[:, pl.ds(vc, HEAD_DIM)]) / total
        o_ref[:, pl.ds(c0, HEAD_DIM)] = o.astype(BF)
        lse_ref[...] = jnp.where(lanes == h, top + jnp.log(total), lse_ref[...])

    loop(HEADS, head)
    p_o.late()
    p_o.finish()
    fetch = pltpu.make_async_copy(wo_all, stage.at[pl.ds(0, q_width), pl.ds(0, d)], local.at[spare])
    fetch.start()
    fetch.wait()

    def out_proj(t):
        c0 = at128(t, 512)
        mid_ref[:, pl.ds(c0, 512)] = (
            dot(o_ref[...], stage[pl.ds(0, q_width), pl.ds(c0, 512)]) + x_ref[:, pl.ds(c0, 512)].astype(F32)
        )

    loop(d // 512, out_proj)
    mid = mid_ref[...]
    inverse_two = lax.rsqrt(jnp.mean(mid * mid, -1, keepdims=True) + EPSILON)
    x_all[pl.ds(at128(z, rows), rows), :] = (mid * inverse_two * gain_ref[1:2, :]).astype(BF)
    c_x.begin()
    c_g.forward(nz - 1)
    for k in range(1, nz - 1):
        c_x.forward(k)
    p_gu.middle()
    if nz <= 4:
        c_x.forward(nz - 1)
    p_gu.late()
    p_d.begin()
    p_gu.finish()

    cols = 768 if wide % 768 == 0 else 256

    def hidden(j):
        r0 = at128(j, rows)

        def one(t):
            c0 = at128(t, cols)
            xb = x_all[pl.ds(r0, rows), :]
            gate = dot(xb, gu[:, pl.ds(c0, cols)])
            up = dot(xb, gu[:, pl.ds(pl.multiple_of(wide + c0, 128), cols)])
            act[pl.ds(r0, rows), pl.ds(c0, cols)] = (gate * jax.nn.sigmoid(gate) * up).astype(BF)
            dgu[pl.ds(r0, rows), pl.ds(c0, cols)] = gate.astype(BF)
            dgu[pl.ds(r0, rows), pl.ds(pl.multiple_of(wide + c0, 128), cols)] = up.astype(BF)

        loop(wide // cols, one)

    hidden(z)
    if nz > 4:
        c_x.forward(nz - 1)

    def nearest(k):
        c_x.arrive(k)
        hidden(c_x.order(k))

    loop(nz - 2, lambda i: nearest(i + 1))
    p_d.middle()
    nearest(nz - 1)
    for k in range(1, nz):
        c_g.arrive(k)
    high = 768 if nz <= 4 and wide % 768 == 0 else 256
    spots = [(r, c) for r in range(0, wide, high) for c in range(0, d, 768)]
    puts = []
    for i, (r, c) in enumerate(spots):
        if i >= 2:
            puts[i - 2].wait()
        slot = pl.ds(i % 2 * 768, 768)
        ybuf[0:high, slot] = dot_at(act[:, r : r + high], g_all[:, c : c + 768]).astype(BF)
        puts.append(
            pltpu.make_async_copy(
                ybuf.at[pl.ds(0, high), slot], dwd.at[pl.ds(r, high), pl.ds(c, 768)],
                local.at[spare + i % 2],
            )
        )
        puts[i].start()
        if i == len(spots) // 2:
            p_d.late()
    for put in puts[-2:]:
        put.wait()
    s_d.swap()
    p_d.finish()

    def back(j):
        r0 = at128(j, rows)

        def one(t):
            c0 = at128(t, cols)
            c1 = pl.multiple_of(wide + c0, 128)
            da = dot_bt(g_all[pl.ds(r0, rows), :], dnb[pl.ds(c0, cols), :])
            gate = dgu[pl.ds(r0, rows), pl.ds(c0, cols)].astype(F32)
            up = dgu[pl.ds(r0, rows), pl.ds(c1, cols)].astype(F32)
            sig = jax.nn.sigmoid(gate)
            dgu[pl.ds(r0, rows), pl.ds(c0, cols)] = (
                da * up * (sig * (1.0 + gate * (1.0 - sig)))
            ).astype(BF)
            dgu[pl.ds(r0, rows), pl.ds(c1, cols)] = (da * gate * sig).astype(BF)

        loop(wide // cols, one)

    rs = base

    slots = stage.at[:, pl.ds(0, d)]

    def slot_copy(src, dst, step):
        return remote(
            rows_at(slots, src, rows), rows_at(slots, dst, rows),
            send.at[rs + src], recv.at[rs + dst], z + step, me,
        )

    hold = nz <= 4

    def sides(i):
        j = c_x.order(nz - 1 - i)
        below, above = j > z, j < z
        got = jnp.logical_or(jnp.logical_and(below, z > 0), jnp.logical_and(above, z < nz - 1))
        return j, below, above, got, (pl.ds(at128(j, rows), rows), pl.ds(0, d))

    def terms(i, at):
        j = sides(i)[0]
        back(j)

        def one(t):
            c0 = at128(t, 768)
            ybuf[at : at + rows, pl.ds(c0, 768)] = dot_bt(
                dgu[pl.ds(at128(j, rows), rows), :], gu[pl.ds(c0, 768), :]
            ).astype(BF)

        loop(d // 768, one)

    def ship(j, below, above):
        @pl.when(below)
        def _():
            slot_copy(j, j, 1).start()

        @pl.when(above)
        def _():
            slot_copy(j, jnp.where(z - 1 == j, nz, j), -1).start()

    def early(i, at):
        j, below, above, got, where = sides(i)

        @pl.when(jnp.logical_not(got))
        def _():
            stage[where] = ybuf[at : at + rows, :]
            ship(j, below, above)

    def late(i, at):
        j, below, above, got, where = sides(i)

        @pl.when(got)
        def _():
            slot_copy(j, j, 0).wait_recv()
            stage[where] = (
                stage[where].astype(F32) + ybuf[at : at + rows, :].astype(F32)
            ).astype(BF)
            ship(j, below, above)

    if hold:
        between = {max(nz - 3, 0): (s_d.merge, s_d.first)}
        for i in range(nz - 1):
            terms(i, i * rows)
            early(i, i * rows)
            for step in between.get(i, ()):
                step()
        late(0, 0)
    else:

        def at_once(i):
            terms(i, 0)
            early(i, 0)
            late(i, 0)

        loop(nz - 1, at_once)
        for step in (s_d.merge, s_d.first, s_d.second):
            step()
    back(z)

    def own(t):
        c0 = at128(t, 512)
        dx_ref[:, pl.ds(c0, 512)] = dot_bt(
            dgu[pl.ds(at128(z, rows), rows), :], gu[pl.ds(c0, 512), :]
        )

    loop(d // 512, own)

    c_x.drain()

    def down_terms(t):
        c0 = at128(t, 512)
        g_all[:, pl.ds(c0, 512)] = dot(act[...], dnb[:, pl.ds(c0, 512)]).astype(BF)

    c_g.drain()
    loop(d // 512, down_terms)
    out_p = pltpu.make_async_copy(g_all, dpart, local.at[spare + 3])
    out_p.start()
    if hold:
        s_d.second()
        for i in range(1, nz - 1):
            late(i, i * rows)
    p_gu.drain()

    side = 768 if wide % 768 == 0 else 256

    def w_gu_grad(t):
        c0 = at128(t, side)
        for r in range(0, d, 768):
            gu[r : r + 768, pl.ds(c0, side)] = dot_at(
                x_all[:, r : r + 768], dgu[:, pl.ds(c0, side)]
            ).astype(BF)

    outs = []
    for i in range(2):
        loop(wide // side, lambda t: w_gu_grad(t + i * (wide // side)))
        half = pl.ds(i * wide, wide)
        outs.append(pltpu.make_async_copy(gu.at[:, half], dwgu.at[:, half], local.at[spare + i]))
        outs[-1].start()
    s_d.last(d_own)
    out_kv = pltpu.make_async_copy(kv, kv_out, local.at[spare + 2])
    out_kv.start()

    @pl.when(z > 0)
    def _():
        slot_copy(z, z, 0).wait_recv()
        dx_ref[...] += rows_at(slots, z, rows)[...].astype(F32)

    @pl.when(z < nz - 1)
    def _():
        slot_copy(z, nz, 0).wait_recv()
        dx_ref[...] += rows_at(slots, nz, rows)[...].astype(F32)

    for item in (p_q, p_kv, p_s, p_o, p_d, c_kv, s_d):
        item.drain()

    def gave(i):
        j = c_x.order(i + 1)
        slot_copy(j, j, 0).wait_send()

    loop(nz - 1, gave)
    for copy in outs + [out_kv, out_p]:
        copy.wait()


def front(dims, wq, sm, wo, w_gu, w_dn, x, g, cos2, sin2, qpos, kpos):
    nz, nf, rows, d, ff, wide, upad, nb, ng = dims
    q_width, k_width = HEADS * HEAD_DIM, KV_HEADS * HEAD_DIM
    qkv = q_width + 2 * k_width
    tokens = nz * rows
    any_, vm = pl.BlockSpec(memory_space=pl.ANY), pl.BlockSpec(memory_space=pltpu.VMEM)
    sems = 6 * PlaneGather.sems(nf) + 3 * Chain.sems(nz) + Scatter.sems(nf) + nz + 1
    chips = nf // 2
    out = jax.ShapeDtypeStruct
    return pl.pallas_call(
        functools.partial(front_kernel, dims),
        in_specs=[any_] * 5 + [vm, any_] + [vm] * 4,
        out_specs=[any_, any_, vm, any_] + [vm] * 5 + [any_] * 6,
        out_shape=[
            out((d, qkv), BF),
            out((q_width, d), BF),
            out((rows, q_width), BF),
            out((tokens, 2 * k_width), BF),
            out((rows, q_width), BF),
            out((rows, HEAD_DIM), F32),
            out((rows, d), F32),
            out((rows, d), F32),
            out((8, d), F32),
            out((d, 2 * wide), BF),
            out((tokens, d), BF),
            out((upad, d), BF),
            out((wide, d), BF),
            out((chips * upad, d), BF),
            out(((chips - 1) * upad, d), BF),
        ],
        scratch_shapes=[
            pltpu.VMEM((max(d, (nz + 1) * rows), qkv), BF),
            pltpu.VMEM((d, 2 * wide), BF),
            pltpu.VMEM((wide, d), BF),
            pltpu.VMEM((tokens, d), BF),
            pltpu.VMEM((tokens, d), BF),
            pltpu.VMEM((tokens, wide), BF),
            pltpu.VMEM((tokens, 2 * wide), BF),
            pltpu.VMEM((nf * 16, sm.shape[1]), BF),
            pltpu.VMEM((tokens, 2 * k_width), BF),
            pltpu.VMEM((8, qkv), F32),
            pltpu.VMEM(((nz - 1 if nz <= 4 else 1) * rows, d), BF),
            pltpu.VMEM((d // nf, 2 * wide), BF),
            pltpu.VMEM((upad, d), BF),
            pltpu.SemaphoreType.DMA((sems,)),
            pltpu.SemaphoreType.DMA((sems,)),
            pltpu.SemaphoreType.DMA((24,)),
        ],
        compiler_params=pltpu.CompilerParams(
            collective_id=0, has_side_effects=True, vmem_limit_bytes=VMEM_LIMIT
        ),
    )(wq, sm, wo, w_gu, w_dn, x, g, cos2, sin2, qpos, kpos)


class Reduce:
    def __init__(self, slots, rows, nz, z, me, send, recv, base, order):
        self.slots, self.rows, self.nz, self.z, self.me = slots, rows, nz, z, me
        self.send, self.recv, self.base, self.order = send, recv, base, order

    @staticmethod
    def sems(nz):
        return nz + 1

    def copy(self, src, dst, step):
        return remote(
            rows_at(self.slots, src, self.rows), rows_at(self.slots, dst, self.rows),
            self.send.at[self.base + src], self.recv.at[self.base + dst], self.z + step, self.me,
        )

    def give(self, i, part):
        z, nz, rows = self.z, self.nz, self.rows
        j = self.order(nz - 1 - i)
        below, above = j > z, j < z
        got = jnp.logical_or(jnp.logical_and(below, z > 0), jnp.logical_and(above, z < nz - 1))
        where = pl.ds(at128(j, rows) if rows % 128 == 0 else pl.multiple_of(j * rows, 16), rows)
        own = part(j)

        @pl.when(got)
        def _():
            self.copy(j, j, 0).wait_recv()
            self.slots[where, :] = (self.slots[where, :].astype(F32) + own.astype(F32)).astype(BF)

        @pl.when(jnp.logical_not(got))
        def _():
            self.slots[where, :] = own.astype(BF)

        @pl.when(below)
        def _():
            self.copy(j, j, 1).start()

        @pl.when(above)
        def _():
            self.copy(j, jnp.where(z - 1 == j, nz, j), -1).start()

    def take(self, total):
        z, nz = self.z, self.nz

        @pl.when(z > 0)
        def _():
            self.copy(z, z, 0).wait_recv()
            total[...] += rows_at(self.slots, z, self.rows)[...].astype(F32)

        @pl.when(z < nz - 1)
        def _():
            self.copy(z, nz, 0).wait_recv()
            total[...] += rows_at(self.slots, nz, self.rows)[...].astype(F32)

    def drain(self):
        def gave(i):
            j = self.order(i + 1)
            self.copy(j, j, 0).wait_send()

        loop(self.nz - 1, gave)


def back_kernel(
    dims,
    dwgu, d_own, dpart, wq_all, wo_all, kv_hbm, mid_hbm, dx_hbm,
    x_ref, g_ref, q_ref, o_ref, lse_ref, gain_ref, cos_ref, sin_ref, qpos_ref, kpos_ref,
    hid_ref, gh_ref, all_d, all_g, all_u, z_out, tiny_out,
    stage, full, dslots, do_ref, kv, dkv, kslots, m32, dh, t32, dqkv, normed,
    r3, l3, r4, l4, zsrc, zslots, zlow, zown, gain_sums, tiny, tin, zin,
    r1, r2, l1, l2, own2, own_sems, send, recv, local,
):
    nz, nf, rows, d, wide, upad, nb, ng, ch = dims
    z, me = lax.axis_index("ctx"), lax.axis_index("fsdp")
    q_width, k_width = HEADS * HEAD_DIM, KV_HEADS * HEAD_DIM
    qkv = q_width + 2 * k_width
    scale = HEAD_DIM ** (-0.5)
    wr = d // nf
    place = {"nf": nf, "z": z, "me": me, "send": send, "recv": recv}
    per = Scatter.sems(nf)
    own = {"own": own2, "sems": own_sems}
    s_g = Scatter(dwgu, 0, wr, wide, r1, l1, True, base=per, **own, **place)
    s_u = Scatter(dwgu, wide, wr, wide, r2, l2, True, base=2 * per, **own, **place)
    s_o = Scatter(full, 0, wr, d, r3, l3, True, base=3 * per, **place)
    s_q = Scatter(full, 0, wr, qkv, r4, l4, True, base=4 * per, **place)
    base = 5 * per
    line = {"nz": nz, "z": z, "me": me, "send": send, "recv": recv}
    per = Chain.sems(nz)
    a_d = Chain(all_d, upad, base=base, **line)
    a_g = Chain(all_g, wr, base=base + per, **line)
    a_u = Chain(all_u, wr, base=base + 2 * per, **line)
    a_z = Chain(z_out, ch, base=base + 3 * per, **line)
    base += 4 * per
    per = Reduce.sems(nz)
    d_kv = Reduce(kslots, rows, base=base, order=a_d.order, **line)
    d_h = Reduce(dslots, rows, base=base + per, order=a_d.order, **line)
    d_z = Reduce(zslots, ch, base=base + 2 * per, order=a_d.order, **line)
    base += 3 * per

    def fetch(src, dst, i):
        copy = pltpu.make_async_copy(src, dst, local.at[i])
        copy.start()
        return copy

    def stream(src, cols, use):
        copies = []
        for t in range(src.shape[0] // 512):
            slot = stage.at[pl.ds(t % 2 * 512, 512), pl.ds(0, cols)]
            copies.append(
                pltpu.make_async_copy(src.at[pl.ds(t * 512, 512)], slot, local.at[6 + t % 2])
            )
        for copy in copies[:2]:
            copy.start()
        for t, copy in enumerate(copies):
            copy.wait()
            use(t, t % 2 * 512)
            if t + 2 < len(copies):
                copies[t + 2].start()

    mid_in = fetch(mid_hbm, m32, 1)
    dx_in = fetch(dx_hbm, dh, 2)
    kv_in = fetch(kv_hbm, kv, 3)
    d_in = fetch(d_own, rows_at(all_d, z, upad), 8)

    barrier = pltpu.get_barrier_semaphore()
    for k in range(1, nf):
        pl.semaphore_signal(barrier, inc=1, device_id=(z, me ^ k), device_id_type=MESH)
    for k in range(1, nz):
        pl.semaphore_signal(barrier, inc=1, device_id=((z + k) % nz, me), device_id_type=MESH)
    pl.semaphore_wait(barrier, nf + nz - 2)

    dkv[...] = jnp.zeros_like(dkv)
    lanes = lax.broadcasted_iota(jnp.int32, (rows, HEAD_DIM), 1)
    mine = dkv.at[pl.ds(at128(z, rows), rows)]
    third = HEADS // 3

    def norm_back():
        mid_in.wait()
        dx_in.wait()
        mid, dxn = m32[...], dh[...]
        inverse_two = lax.rsqrt(jnp.mean(mid * mid, -1, keepdims=True) + EPSILON)
        scaled = gain_ref[1:2, :] * dxn
        gain_sums[1:2, :] = jnp.sum(dxn * mid * inverse_two, 0, keepdims=True)
        dh[...] = (
            g_ref[...].astype(F32)
            + inverse_two * scaled
            - mid
            * (inverse_two * inverse_two * inverse_two)
            * jnp.mean(scaled * mid, -1, keepdims=True)
        )
        normed[...] = dh[...].astype(BF)

    def out_back():
        def one(t, r):
            do_ref[:, t * 512 : t * 512 + 512] = dot_bt(
                normed[...], stage[r : r + 512, 0:d]
            ).astype(BF)

        stream(wo_all, d, one)
        kv_in.wait()

    def w_out_grad():
        def one(t):
            c0 = at128(t, 512)
            full[pl.ds(0, q_width), pl.ds(c0, 512)] = dot_at(
                o_ref[...], normed[:, pl.ds(c0, 512)]
            ).astype(BF)

        loop(d // 512, one)

    def head(h):
        c0 = at128(h, HEAD_DIM)
        kc = at128(h // (HEADS // KV_HEADS), HEAD_DIM)
        vc = pl.multiple_of(kc + k_width, HEAD_DIM)
        q, k, v = q_ref[:, pl.ds(c0, HEAD_DIM)], kv[:, pl.ds(kc, HEAD_DIM)], kv[:, pl.ds(vc, HEAD_DIM)]
        do = do_ref[:, pl.ds(c0, HEAD_DIM)]
        lse = jnp.sum(jnp.where(lanes == h, lse_ref[...], 0.0), -1, keepdims=True)
        delta = jnp.sum(
            do.astype(F32) * o_ref[:, pl.ds(c0, HEAD_DIM)].astype(F32), -1, keepdims=True
        )
        s = jnp.where(kpos_ref[...] <= qpos_ref[...], dot_bt(q, k) * scale, MASKED)
        p = jnp.exp(s - lse)
        dkv[:, pl.ds(vc, HEAD_DIM)] += dot_at(p.astype(BF), do)
        ds = (p * (dot_bt(do, v) - delta)).astype(BF)
        dq = dot(ds, k) * scale
        dkv[:, pl.ds(kc, HEAD_DIM)] += dot_at(ds, q) * scale
        dqkv[:, pl.ds(c0, HEAD_DIM)] = turn(dq, cos_ref[...], -sin_ref[...]).astype(BF)

    def kv_part(j):
        return dkv[pl.ds(at128(j, rows), rows), :]

    def down_part(j):
        part = stage.at[pl.ds(0, rows), pl.ds(0, d)]
        fetch(rows_at(dpart, j, rows), part, 1).wait()
        return part[...]

    def z_part(j):
        return zsrc[pl.ds(pl.multiple_of(j * ch, 16), ch), :]

    def project_back():
        for h in range(KV_HEADS):
            c0 = h * HEAD_DIM
            dqkv[:, q_width + c0 : q_width + c0 + HEAD_DIM] = turn(
                mine[:, c0 : c0 + HEAD_DIM], cos_ref[...], -sin_ref[...]
            ).astype(BF)
        dqkv[:, q_width + k_width :] = mine[:, k_width:].astype(BF)

    def w_qkv_grad():
        x = x_ref[...].astype(F32)
        inverse = lax.rsqrt(jnp.mean(x * x, -1, keepdims=True) + EPSILON)
        normed[...] = (x * inverse * gain_ref[0:1, :]).astype(BF)
        s_o.drain()

        def one(t):
            c0 = at128(t, 512)
            full[pl.ds(0, d), pl.ds(c0, 512)] = dot_at(
                normed[...], dqkv[:, pl.ds(c0, 512)]
            ).astype(BF)

        loop(qkv // 512, one)

    tiny_copies = []

    def input_back():
        def one(t, r):
            t32[:, t * 512 : t * 512 + 512] = dot_bt(dqkv[...], stage[r : r + 512, :])

        stream(wq_all, qkv, one)
        x = x_ref[...].astype(F32)
        inverse = lax.rsqrt(jnp.mean(x * x, -1, keepdims=True) + EPSILON)
        dxn = t32[...]
        scaled = gain_ref[0:1, :] * dxn
        gain_one = jnp.sum(dxn * x * inverse, 0, keepdims=True)
        gain_two = gain_sums[1:2, :]
        bias = jnp.sum(dqkv[...].astype(F32), 0, keepdims=True)
        gh_ref[...] = (
            dh[...]
            + inverse * scaled
            - x * (inverse * inverse * inverse) * jnp.mean(scaled * x, -1, keepdims=True)
        ).astype(BF)

        cut = q_width + k_width
        qk, vb = cut // nf, k_width // nf
        tiny[...] = jnp.zeros_like(tiny)
        for f in range(nf):
            r = slice(8 * f, 8 * f + 1)
            tiny[r, 0:qk] = bias[:, f * qk : (f + 1) * qk]
            tiny[r, qk : qk + vb] = bias[:, cut + f * vb : cut + (f + 1) * vb]
            tiny[r, qk + vb : qk + vb + ng] = gain_one[:, f * ng : (f + 1) * ng]
            tiny[r, qk + vb + ng : qk + vb + 2 * ng] = gain_two[:, f * ng : (f + 1) * ng]
        own = pl.ds(pl.multiple_of(me * 8, 8), 8)
        tin[own, :] = tiny[own, :]
        for k in range(1, nf):
            copy = remote(
                rows_at(tiny, me ^ k, 8), rows_at(tin, me, 8),
                send.at[base + k], recv.at[base + k], z, me ^ k,
            )
            copy.start()
            tiny_copies.append(copy)

    def tiny_along():
        for copy in tiny_copies:
            copy.wait_recv()
        total = tin[0:8, :]
        for f in range(1, nf):
            total = total + tin[8 * f : 8 * f + 8, :]
        zin[pl.ds(pl.multiple_of(z * 8, 8), 8), :] = total
        for k in range(1, nz):
            copy = remote(
                rows_at(zin, z, 8), rows_at(zin, z, 8),
                send.at[base + nf + k], recv.at[base + nf + k], (z + k) % nz, me,
            )
            copy.start()
            tiny_copies.append(copy)

    def z_take():
        zown[...] = z_part(z).astype(F32)
        d_z.take(zown)
        zlow[...] = zown[...].astype(BF)
        fetch(zlow, rows_at(z_out, z, ch), 2).wait()

    def h_take():
        m32[...] += down_part(z).astype(F32)
        d_h.take(m32)
        hid_ref[...] = m32[...].astype(BF)

    a_d.begin(d_own)
    s_g.swap()
    norm_back()
    out_back()
    w_out_grad()
    s_o.swap()
    s_g.merge()
    s_g.first()
    s_u.swap()
    a_d.forward(1)
    for k in range(2, nz - 1):
        a_d.forward(k)
    loop(third, head)
    loop(third, lambda h: head(h + third))
    loop(third, lambda h: head(h + 2 * third))
    s_u.merge()
    s_g.second()
    s_u.first()
    a_d.forward(nz - 1)
    d_kv.give(0, kv_part)
    for i in range(1, nz - 2):
        d_kv.give(i, kv_part)
    d_kv.give(nz - 2, kv_part)
    s_o.merge()
    s_o.first()
    s_g.last(s_g.block(0))
    fetch(s_g.block(0), rows_at(all_g, z, wr), 4).wait()
    a_g.begin()
    s_u.second()
    a_g.forward(1)
    for k in range(2, nz - 1):
        a_g.forward(k)
    s_o.second()
    d_kv.take(mine)
    d_h.give(0, down_part)
    project_back()
    a_g.forward(nz - 1)
    w_qkv_grad()
    s_q.swap()
    s_o.last(zsrc.at[pl.ds(0, wr), pl.ds(0, d)])
    s_u.last(s_u.block(0))
    fetch(s_u.block(0), rows_at(all_u, z, wr), 5).wait()
    s_q.merge()
    s_q.first()
    a_u.begin()
    a_u.forward(1)
    s_q.second()
    for k in range(2, nz - 1):
        a_u.forward(k)
    a_u.forward(nz - 1)
    input_back()
    s_q.last(zsrc.at[pl.ds(0, wr), pl.ds(d, qkv)])
    d_z.give(0, z_part)
    tiny_along()
    for i in range(1, nz - 2):
        d_z.give(i, z_part)
    for i in range(1, nz - 2):
        d_h.give(i, down_part)
    d_z.give(nz - 2, z_part)
    d_h.give(nz - 2, down_part)
    for k in range(1, nz):
        a_u.arrive(k)
    z_take()
    for k in range(1, nz):
        a_g.arrive(k)
    a_z.begin()
    a_z.forward(1)
    for k in range(1, nz):
        a_d.arrive(k)
    for k in range(2, nz - 1):
        a_z.forward(k)
    a_z.forward(nz - 1)
    h_take()
    for k in range(1, nz):
        a_z.arrive(k)
    for copy in tiny_copies[nf - 1 :]:
        copy.wait_recv()
    total = zin[0:8, :]
    for j in range(1, nz):
        total = total + zin[8 * j : 8 * j + 8, :]
    tiny_out[...] = total
    d_in.wait()
    for item in (s_g, s_u, s_o, s_q, a_d, a_g, a_u, a_z, d_kv, d_h, d_z):
        item.drain()
    for copy in tiny_copies:
        copy.wait_send()


def back(dims, *args):
    nz, nf, rows, d, wide, upad, nb, ng, ch = dims
    q_width, k_width = HEADS * HEAD_DIM, KV_HEADS * HEAD_DIM
    qkv = q_width + 2 * k_width
    tokens, chips, wr = nz * rows, nf // 2, d // nf
    tiny = -(-((qkv + 2 * d) // nf) // 128) * 128
    any_, vm = pl.BlockSpec(memory_space=pl.ANY), pl.BlockSpec(memory_space=pltpu.VMEM)
    out = jax.ShapeDtypeStruct
    sems = 5 * Scatter.sems(nf) + 4 * Chain.sems(nz) + 3 * Reduce.sems(nz) + nf + nz
    pieces = [(upad, d), (wr, wide), (wr, wide)]
    return pl.pallas_call(
        functools.partial(back_kernel, dims),
        in_specs=[any_] * 8 + [vm] * 10,
        out_specs=[vm, vm] + [any_] * 4 + [vm],
        out_shape=[out((rows, d), BF), out((rows, d), BF)]
        + [out((nz * r, c), BF) for r, c in pieces]
        + [out((nz * ch, d + qkv), BF), out((8, tiny), F32)],
        scratch_shapes=[
            pltpu.VMEM((1024, qkv), BF),
            pltpu.VMEM((d, qkv), BF),
            pltpu.VMEM(((nz + 1) * rows, d), BF),
            pltpu.VMEM((rows, q_width), BF),
            pltpu.VMEM((tokens, 2 * k_width), BF),
            pltpu.VMEM((tokens, 2 * k_width), F32),
            pltpu.VMEM(((nz + 1) * rows, 2 * k_width), BF),
            pltpu.VMEM((rows, d), F32),
            pltpu.VMEM((rows, d), F32),
            pltpu.VMEM((rows, d), F32),
            pltpu.VMEM((rows, qkv), BF),
            pltpu.VMEM((rows, d), BF),
            pltpu.VMEM((chips * wr, d), BF),
            pltpu.VMEM(((chips - 1) * wr, d), BF),
            pltpu.VMEM((chips * wr, qkv), BF),
            pltpu.VMEM(((chips - 1) * wr, qkv), BF),
            pltpu.VMEM((nz * ch, d + qkv), BF),
            pltpu.VMEM(((nz + 1) * ch, d + qkv), BF),
            pltpu.VMEM((ch, d + qkv), BF),
            pltpu.VMEM((ch, d + qkv), F32),
            pltpu.VMEM((8, d), F32),
            pltpu.VMEM((nf * 8, tiny), F32),
            pltpu.VMEM((nf * 8, tiny), F32),
            pltpu.VMEM((nz * 8, tiny), F32),
            pltpu.VMEM((chips * wr, wide), BF),
            pltpu.VMEM((chips * wr, wide), BF),
            pltpu.VMEM(((chips - 1) * wr, wide), BF),
            pltpu.VMEM(((chips - 1) * wr, wide), BF),
            pltpu.VMEM((2 * wr, wide), BF),
            pltpu.SemaphoreType.DMA((2,)),
            pltpu.SemaphoreType.DMA((sems,)),
            pltpu.SemaphoreType.DMA((sems,)),
            pltpu.SemaphoreType.DMA((9,)),
        ],
        compiler_params=pltpu.CompilerParams(
            collective_id=1, has_side_effects=True, vmem_limit_bytes=VMEM_LIMIT
        ),
    )(*args)


def shards(
    hidden_in, w_qkv, b_qkv, w_out, w_gate_up, w_down, gain_attn, gain_mlp, block_order, cotangent
):
    nz, nf = lax.axis_size("ctx"), lax.axis_size("fsdp")
    z, me = lax.axis_index("ctx"), lax.axis_index("fsdp")
    q_width, k_width = HEADS * HEAD_DIM, KV_HEADS * HEAD_DIM
    rows = hidden_in.shape[1]
    piece_len = rows // 2
    ff = w_gate_up.shape[1] // 2
    unit = ff // (nf * nz)
    order_row = block_order[0]
    all_places = (
        order_row[:, None] * piece_len + jnp.arange(piece_len, dtype=jnp.int32)[None, :]
    ).reshape(-1)
    my_places = lax.dynamic_slice_in_dim(all_places, z * rows, rows)
    cosine, sine_table = angle_tables(my_places)
    cos2 = jnp.concatenate([cosine, cosine], 1)
    sin2 = jnp.concatenate([-sine_table, sine_table], 1)

    upad = -(-unit // 16) * 16
    wide = nf * upad
    nb, ng = b_qkv.shape[0], gain_attn.shape[0]
    d = hidden_in.shape[2]
    small = jnp.concatenate([b_qkv, gain_attn, gain_mlp])
    small = jnp.pad(small[None], ((0, 15), (0, -small.shape[0] % 128)))
    grad_low = cotangent[0]
    (whole_qkv, whole_out, q_low, kv_all, attn_low, lse, middle, grad_normed_two, gains, gate_up_local, down_part,
     down_own, *_) = front(
        (nz, nf, rows, d, ff, wide, upad, nb, ng),
        w_qkv, small, w_out, w_gate_up, w_down, hidden_in[0], grad_low, cos2, sin2,
        my_places[:, None], all_places[None, :],
    )
    ch = -(-(d // (nf * nz)) // 16) * 16
    hidden, grad_hidden, down_all, gate_all, up_all, attn_all, tiny = back(
        (nz, nf, rows, d, wide, upad, nb, ng, ch),
        gate_up_local, down_own, down_part, whole_qkv, whole_out, kv_all, middle, grad_normed_two,
        hidden_in[0], grad_low, q_low, attn_low, lse, gains, cos2, sin2, my_places[:, None], all_places[None, :],
    )
    e1 = (q_width + k_width) // nf
    e2 = e1 + k_width // nf
    e3 = e2 + ng
    shard = d // nf
    cuts = (0, e1, e2, e3, e3 + ng)
    if unit % 8 == 0 and shard % (16 * nz) == 0 and ch * nz == shard:
        gu_grad, down_grad, qkv_grad, out_grad, hidden, grad_hidden, *smalls = finish(
            gate_all, up_all, down_all, attn_all, tiny, hidden, grad_hidden, nz, nf, ff, cuts
        )
        b_qk, b_v, g_one, g_two = (item[0] for item in smalls)
    else:
        gu_grad = unpack(gate_all, up_all, nz, nf, ff)
        down_grad = down_all.reshape(nz, upad, d)[:, :unit].reshape(nz * unit, d).astype(F32)
        qkv_grad = attn_all[:shard, d:].astype(F32)
        out_grad = attn_all[:shard, :d].astype(F32)
        b_qk, b_v, g_one, g_two = (tiny[0, lo:hi] for lo, hi in zip(cuts, cuts[1:]))
    return (
        hidden[None],
        grad_hidden[None],
        qkv_grad,
        b_qk,
        b_v,
        out_grad,
        gu_grad,
        down_grad,
        g_one,
        g_two,
    )


def solution(mesh):
    placed = (
        P("fsdp", "ctx", None),
        P("fsdp", None),
        P("fsdp"),
        P("fsdp", None),
        P("fsdp", None),
        P("fsdp", None),
        P("fsdp"),
        P("fsdp"),
        P("fsdp", None),
        P("fsdp", "ctx", None),
    )
    return jax.shard_map(
        shards,
        mesh=mesh,
        in_specs=placed,
        out_specs=(
            P("fsdp", "ctx", None),
            P("fsdp", "ctx", None),
            P("fsdp", None),
            P("fsdp"),
            P("fsdp"),
            P("fsdp", None),
            P("fsdp", None),
            P("fsdp", None),
            P("fsdp"),
            P("fsdp"),
        ),
        check_vma=False,
    )
```

```python
import functools

import jax
import jax.numpy as jnp
from jax import lax
from jax.experimental import pallas as pl
from jax.experimental.pallas import tpu as pltpu
from jax.sharding import PartitionSpec as P

HEADS = 12
KV_HEADS = 2
HEAD_DIM = 128
EPSILON = 1e-06
THETA = 1000000.0
MASKED = -1e30
BF = jnp.bfloat16
F32 = jnp.float32


def dot(a, b):
    return jnp.dot(a, b, preferred_element_type=F32)


def dot_bt(a, b):
    return lax.dot_general(a, b, (((1,), (1,)), ((), ())), preferred_element_type=F32)


def dot_at(a, b):
    return lax.dot_general(a, b, (((0,), (0,)), ((), ())), preferred_element_type=F32)


def positions(order_ref, z, rows, tokens):
    half = rows // 2
    row = lax.broadcasted_iota(jnp.int32, (rows, 1), 0)
    mine = jnp.where(
        row < half, order_ref[0, 2 * z] * half + row, order_ref[0, 2 * z + 1] * half + row - half
    )
    lane = lax.broadcasted_iota(jnp.int32, (1, tokens), 1)
    places = lane
    for i in range(tokens // half):
        places = jnp.where(lane >= i * half, order_ref[0, i] * half + lane - i * half, places)
    return mine, places


def half_rows(rows):
    return -(-rows // 32) * 16


def pieces_of(columns, width, rows, room):
    n = next(n for n in range(1, columns) if columns % (128 * n) == 0 and columns // n <= width)
    assert n * rows <= room
    return n


def pack(k, nz, nf, ff, unit, upad, rows, width, held, out):
    for h in range(2):
        for f in range(nf):
            src = h * ff + f * (ff // nf) + k * unit
            dst = (h * nf + f) * upad
            done = 0
            while done < unit:
                piece, at = divmod(src + done, width)
                n = min(unit - done, width - at)
                out[:, dst + done : dst + done + n] = held[
                    piece * rows : (piece + 1) * rows, at : at + n
                ]
                done += n
            if upad > unit:
                out[:, dst + unit : dst + upad] = jnp.zeros((rows, upad - unit), out.dtype)


def unpack_kernel(nz, nf, ff, unit, upad, *refs):
    out_ref = refs[-1]
    for k in range(nz):
        for h in range(2):
            for f in range(nf):
                src = f * upad
                dst = h * ff + f * (ff // nf) + k * unit
                part = refs[h * nz + k]
                out_ref[:, dst : dst + unit] = part[:, src : src + unit].astype(F32)


def unpack(gate, up, nz, nf, ff):
    rows, wide = gate.shape[0] // nz, gate.shape[1]
    step = 32
    specs = [
        pl.BlockSpec((step, wide), lambda i, k=k: (k * (rows // step) + i, 0)) for k in range(nz)
    ]
    return pl.pallas_call(
        functools.partial(unpack_kernel, nz, nf, ff, ff // (nf * nz), wide // nf),
        grid=(rows // step,),
        in_specs=specs * 2,
        out_specs=pl.BlockSpec((step, 2 * ff), lambda i: (i, 0)),
        out_shape=jax.ShapeDtypeStruct((rows, 2 * ff), F32),
    )(*[gate] * nz, *[up] * nz)


def finish_kernel(nz, nf, ff, unit, upad, cuts, *refs):
    gates, ups = refs[:nz], refs[nz : 2 * nz]
    down, attn, tiny, hid, gh = refs[2 * nz : 2 * nz + 5]
    gu_out, down_out, qkv_out, out_out, hid_out, gh_out, *tiny_outs = refs[2 * nz + 5 :]
    unpack_kernel(nz, nf, ff, unit, upad, *gates, *ups, gu_out)
    down_out[...] = down[...].astype(F32)[0:unit]
    d = out_out.shape[1]
    qkv_out[...] = attn[:, d:].astype(F32)
    out_out[...] = attn[:, :d].astype(F32)
    hid_out[...] = hid[...]
    gh_out[...] = gh[...]

    @pl.when(pl.program_id(0) == 0)
    def _():
        for out, lo, hi in zip(tiny_outs, cuts, cuts[1:]):
            out[...] = tiny[0:1, lo:hi]


def finish(gate, up, down, attn, tiny, hid, gh, nz, nf, ff, cuts):
    rows, wide = gate.shape[0] // nz, gate.shape[1]
    unit, upad, d = ff // (nf * nz), wide // nf, hid.shape[1]
    step = rows // nz
    along = [
        pl.BlockSpec((step, wide), lambda i, k=k: (k * (rows // step) + i, 0)) for k in range(nz)
    ]
    part = hid.shape[0] // nz

    def by_step(r, c):
        return pl.BlockSpec((r, c), lambda i: (i, 0))

    def still(c):
        return pl.BlockSpec((1, c), lambda i: (0, 0))

    qkv = attn.shape[1] - d
    sizes = [hi - lo for lo, hi in zip(cuts, cuts[1:])]
    out = jax.ShapeDtypeStruct
    return pl.pallas_call(
        functools.partial(finish_kernel, nz, nf, ff, unit, upad, cuts),
        grid=(nz,),
        in_specs=along * 2
        + [
            by_step(upad, d),
            by_step(step, d + qkv),
            pl.BlockSpec(tiny.shape, lambda i: (0, 0)),
            by_step(part, d),
            by_step(part, d),
        ],
        out_specs=[
            by_step(step, 2 * ff),
            by_step(unit, d),
            by_step(step, qkv),
            by_step(step, d),
            by_step(part, d),
            by_step(part, d),
        ]
        + [still(n) for n in sizes],
        out_shape=[
            out((rows, 2 * ff), F32),
            out((nz * unit, d), F32),
            out((rows, qkv), F32),
            out((rows, d), F32),
            out(hid.shape, BF),
            out(hid.shape, BF),
        ]
        + [out((1, n), F32) for n in sizes],
        compiler_params=pltpu.CompilerParams(vmem_limit_bytes=VMEM_LIMIT),
    )(*[gate] * nz, *[up] * nz, down, attn, tiny, hid, gh)


MESH = pl.DeviceIdType.MESH
VMEM_LIMIT = 63 * 2**20


def remote(src, dst, send, recv, z, f):
    return pltpu.make_async_remote_copy(
        src_ref=src, dst_ref=dst, send_sem=send, recv_sem=recv, device_id=(z, f), device_id_type=MESH
    )


def rows_at(ref, index, count):
    return ref.at[pl.ds(pl.multiple_of(index * count, count), count)]


class PlaneGather:
    def __init__(self, src, dst, rows, nf, z, me, send, recv, local, base, bounce=None):
        self.src, self.dst, self.rows, self.nf, self.z, self.me = src, dst, rows, nf, z, me
        self.send, self.recv, self.base = send, recv, base
        home = rows_at(dst, me, rows)
        if bounce is None:
            self.local = (pltpu.make_async_copy(src, home, local),)
        else:
            self.local = (
                pltpu.make_async_copy(src, bounce, local),
                pltpu.make_async_copy(bounce, home, local),
            )
        self.sent = []
        self.cut = half_rows(rows)
        self.swaps = {}

    @staticmethod
    def sems(nf):
        return 2 * nf

    def slot(self, k, lo=0, hi=None):
        hi = self.rows if hi is None else hi
        start = pl.multiple_of((self.me ^ k) * self.rows, 16) + lo
        return self.dst.at[pl.ds(pl.multiple_of(start, 16), hi - lo)]

    def push(self, index, src, dst, flip_by):
        copy = remote(
            src, dst, self.send.at[self.base + index], self.recv.at[self.base + index],
            self.z, self.me ^ flip_by,
        )
        copy.start()
        self.sent.append(copy)
        return copy

    def begin(self):
        self.local[0].start()
        self.direct = {}
        for k in (2, 4) if self.nf == 8 else range(2, self.nf, 2):
            self.direct[k] = self.push(k, self.src, self.slot(0), k)
        self.swaps[0] = self.push(1, self.src, self.slot(0), 1)

    def swap(self, k):
        self.swaps[k] = self.push(k + 1, self.slot(k), self.slot(k), 1)

    def middle(self):
        for one, two in zip(self.local, self.local[1:]):
            one.wait()
            two.start()
        for k, copy in self.direct.items():
            copy.wait_recv()
            if self.nf == 8:
                if k == 2:
                    self.far_a = self.push(6, self.slot(2, 0, self.cut), self.slot(2, 0, self.cut), 4)
                elif self.cut < self.rows:
                    self.far_b = self.push(
                        8, self.slot(4, self.cut), self.slot(4, self.cut), 2
                    )
            self.swap(k)

    def late(self):
        if self.nf == 8:
            self.far_a.wait_recv()
            if self.cut < self.rows:
                self.far_b.wait_recv()
            self.swap(6)

    def finish(self):
        self.local[-1].wait()
        for copy in self.swaps.values():
            copy.wait_recv()

    def drain(self):
        for copy in self.sent:
            copy.wait_send()


class Chain:
    def __init__(self, buf, rows, nz, z, me, send, recv, base):
        self.buf, self.rows, self.nz, self.z, self.me = buf, rows, nz, z, me
        self.send, self.recv, self.base = send, recv, base

    @staticmethod
    def sems(nz):
        return nz + 2

    def copy(self, j, sem, step, src=None):
        slot = rows_at(self.buf, j, self.rows)
        return remote(
            slot if src is None else src, slot, self.send.at[self.base + sem], self.recv.at[self.base + j], self.z + step, self.me
        )

    def order(self, k):
        z, nz = self.z, self.nz
        below, above = z, nz - 1 - z
        m = jnp.minimum(below, above)
        near = jnp.where(k % 2 == 1, z - (k + 1) // 2, z + k // 2)
        far = jnp.where(above > below, z + (k - m), z - (k - m))
        return jnp.where(k <= 2 * m, near, far)

    def begin(self, src=None):
        z, nz = self.z, self.nz

        @pl.when(z < nz - 1)
        def _():
            self.copy(z, nz, 1, src).start()

        @pl.when(z > 0)
        def _():
            self.copy(z, nz + 1, -1, src).start()

    def passing(self, j):
        z, nz = self.z, self.nz
        return jnp.logical_and(j < z, z < nz - 1), jnp.logical_and(j > z, z > 0)

    def forward(self, k):
        j = self.order(k)
        up, down = self.passing(j)

        @pl.when(up)
        def _():
            self.copy(j, j, 1).wait_recv()
            self.copy(j, j, 1).start()

        @pl.when(down)
        def _():
            self.copy(j, j, -1).wait_recv()
            self.copy(j, j, -1).start()

    def arrive(self, k):
        j = self.order(k)
        up, down = self.passing(j)

        @pl.when(jnp.logical_not(jnp.logical_or(up, down)))
        def _():
            self.copy(j, j, 0).wait_recv()

    def drain(self):
        z, nz = self.z, self.nz

        @pl.when(z < nz - 1)
        def _():
            self.copy(z, nz, 1).wait_send()

        @pl.when(z > 0)
        def _():
            self.copy(z, nz + 1, -1).wait_send()

        def one(k, carry):
            j = self.order(k)
            up, down = self.passing(j)

            @pl.when(jnp.logical_or(up, down))
            def _():
                self.copy(j, j, 0).wait_send()

            return carry

        lax.fori_loop(1, nz, one, 0)


class Scatter:
    def __init__(self, src, c0, rows, cols, recv4, land, inside, nf, z, me, send, recv, base, own=None, sems=None):
        self.src, self.c0, self.rows, self.cols = src, c0, rows, cols
        self.recv4, self.land, self.inside = recv4, land, inside
        self.nf, self.z, self.me, self.send, self.recv, self.base = nf, z, me, send, recv, base
        self.chips, self.chip, self.core = nf // 2, me // 2, me % 2
        self.cut = half_rows(rows)
        self.sent = []
        self.got = {}
        self.own, self.own_sems = own, sems

    @staticmethod
    def sems(nf):
        return nf

    def push(self, index, src, dst, flip_by):
        copy = remote(
            src, dst, self.send.at[self.base + index], self.recv.at[self.base + index],
            self.z, self.me ^ flip_by,
        )
        copy.start()
        self.sent.append(copy)
        self.got[index] = copy

    def mine(self, ref, start, n):
        return ref.at[pl.ds(pl.multiple_of(start, 16), n)]

    def block(self, k, lo=0, hi=None):
        hi = self.rows if hi is None else hi
        return self.mine(self.recv4, (self.chip ^ k) * self.rows + lo, hi - lo)

    def swap(self):
        for p in range(self.chips):
            start = pl.multiple_of((2 * p + 1 - self.core) * self.rows, 16)
            src = self.src.at[pl.ds(start, self.rows), pl.ds(self.c0, self.cols)]
            self.push(p, src, self.mine(self.recv4, p * self.rows, self.rows), 1)

    def merge(self):
        rows, cols = self.rows, self.cols
        if self.own is not None:
            for p in range(min(2, self.chips)):
                self.fetch(p).start()
        for p in range(self.chips):
            self.got[p].wait_recv()
        if self.inside:
            for p in range(self.chips):
                start = pl.multiple_of((2 * p + self.core) * rows, 16)
                if self.own is None:
                    own, first = self.src, start
                else:
                    self.fetch(p).wait()
                    own, first = self.own, p % 2 * rows
                step = rows if rows <= 96 else rows // 2
                for i in range(0, rows, step):
                    where = pl.ds(p * rows + i, step)
                    part = own[pl.ds(pl.multiple_of(first + i, 16), step), pl.ds(0, cols)]
                    self.recv4[where, :] = (
                        self.recv4[where, :].astype(F32) + part.astype(F32)
                    ).astype(BF)
                if self.own is not None and p + 2 < self.chips:
                    self.fetch(p + 2).start()
            return
        step = rows if rows <= 96 else rows // 2
        n = rows // step
        core, col = self.core, self.c0 // cols
        deep = {"pipeline_mode": pl.Buffered(3)}
        own = pl.BlockSpec((step, cols), lambda p, i: ((2 * p + core) * n + i, col), **deep)
        held_in = pl.BlockSpec((step, cols), lambda p, i: (p * n + i, 0), **deep)
        held = pl.BlockSpec((step, cols), lambda p, i: (p * n + i, 0))
        pltpu.emit_pipeline(
            add_two, grid=(self.chips, n), in_specs=[own, held_in], out_specs=[held]
        )(self.src, self.recv4, self.recv4)

    def fetch(self, p):
        start = pl.multiple_of((2 * p + self.core) * self.rows, 16)
        return pltpu.make_async_copy(
            self.src.at[pl.ds(start, self.rows), pl.ds(self.c0, self.cols)],
            self.own.at[pl.ds(p % 2 * self.rows, self.rows)],
            self.own_sems.at[p % 2],
        )

    def add(self, out, parts, n):
        if self.inside:
            total = parts[0][...].astype(F32)
            for part in parts[1:]:
                total = total + part[...].astype(F32)
            out[...] = total.astype(BF)
            return
        step = n // 2 if n % 32 == 0 and n > 144 else n
        spec = pl.BlockSpec((step, self.cols), lambda i: (i, 0))
        body = add_two if len(parts) == 2 else add_all
        pltpu.emit_pipeline(
            body, grid=(n // step,), in_specs=[spec] * len(parts), out_specs=[spec]
        )(*parts, out)

    def first(self):
        base, rows, cut = self.chips, self.rows, self.cut
        if self.nf == 8:
            self.push(base, self.block(3, 0, cut), self.land.at[pl.ds(0, cut)], 2)
            self.push(base + 1, self.block(3, cut), self.land.at[pl.ds(cut, rows - cut)], 4)
        else:
            for k in range(1, self.chips):
                self.push(base + k - 1, self.block(k), self.land.at[pl.ds((k - 1) * rows, rows)], 2 * k)

    def second(self):
        if self.nf != 8:
            return
        base, rows, cut = self.chips, self.rows, self.cut
        self.got[base].wait_recv()
        to_y = self.block(2, 0, cut)
        self.add(to_y, [to_y, self.land.at[pl.ds(0, cut)]], cut)
        self.push(base + 3, self.block(2), self.land.at[pl.ds(2 * rows, rows)], 4)
        self.got[base + 1].wait_recv()
        to_x = self.block(1, cut)
        self.add(to_x, [to_x, self.land.at[pl.ds(cut, rows - cut)]], rows - cut)
        self.push(base + 2, self.block(1), self.land.at[pl.ds(rows, rows)], 2)

    def last(self, out):
        base, rows = self.chips, self.rows
        if self.nf == 8:
            incoming = [(base + 2, rows), (base + 3, 2 * rows)]
        else:
            incoming = [(base + k - 1, (k - 1) * rows) for k in range(1, self.chips)]
        for index, _ in incoming:
            self.got[index].wait_recv()
        parts = [self.block(0)] + [self.land.at[pl.ds(at, rows)] for _, at in incoming]
        self.add(out, parts, rows)

    def drain(self):
        for copy in self.sent:
            copy.wait_send()
        self.sent = []


def add_two(a, b, out):
    out[...] = (a[...].astype(F32) + b[...].astype(F32)).astype(BF)


def add_all(*refs):
    total = refs[0][...].astype(F32)
    for ref in refs[1:-1]:
        total = total + ref[...].astype(F32)
    refs[-1][...] = total.astype(BF)


def greet_ctx_and_plane(nz, nf, z, me):
    barrier = pltpu.get_barrier_semaphore()
    flips = (1, 2, 4) if nf == 8 else (1,) + tuple(range(2, nf, 2))
    for k in flips:
        pl.semaphore_signal(barrier, inc=1, device_id=(z, me ^ k), device_id_type=MESH)

    @pl.when(z < nz - 1)
    def _():
        pl.semaphore_signal(barrier, inc=1, device_id=(z + 1, me), device_id_type=MESH)

    @pl.when(z > 0)
    def _():
        pl.semaphore_signal(barrier, inc=1, device_id=(z - 1, me), device_id_type=MESH)

    inner = jnp.logical_and(z > 0, z < nz - 1)

    @pl.when(inner)
    def _():
        pl.semaphore_wait(barrier, len(flips) + 2)

    @pl.when(jnp.logical_not(inner))
    def _():
        pl.semaphore_wait(barrier, len(flips) + 1)


def loop(n, body):
    def step(i, carry):
        body(i)
        return carry

    lax.fori_loop(0, n, step, 0)


def at128(i, n):
    return i * n if isinstance(i, int) else pl.multiple_of(i * n, n)


def turn(t, cos2, sin2):
    return t * cos2 + pltpu.roll(t, HEAD_DIM // 2, 1) * sin2


def front_kernel(
    dims,
    wq, sm, wo, w_gu, w_dn, x_ref, g_ref, order_ref, freq_ref,
    wq_all, wo_all, q_out, kv_out, o_out, lse_out, mid_out, dx_ref, gain_out, cos_out, sin_out, dwgu, dpart, d_own, dwd, r0, l0,
    q_ref, o_ref, lse_ref, mid_ref, gain_ref, cos_ref, sin_ref, qpos_ref, kpos_ref,
    stage, gu, dnb, g_all, x_all, act, dgu, smb, kv, bias, ybuf, packed, down, send, recv, local,
):
    nz, nf, rows, d, ff, wide, upad, nb, ng = dims
    z, me = lax.axis_index("ctx"), lax.axis_index("fsdp")
    q_width, k_width = HEADS * HEAD_DIM, KV_HEADS * HEAD_DIM
    qkv = q_width + 2 * k_width
    scale = HEAD_DIM ** (-0.5)
    wr = d // nf
    per = PlaneGather.sems(nf)
    q_cols, kv_cols = pl.ds(0, q_width), pl.ds(q_width, 2 * k_width)
    plane = [
        PlaneGather(src, dst, r, nf, z, me, send, recv, local.at[i], i * per, bounce)
        for i, (src, dst, r, bounce) in enumerate(
            [
                (wq.at[:, q_cols], wq_all.at[:, q_cols], wr, ybuf.at[pl.ds(wr, wr)]),
                (wq.at[:, kv_cols], wq_all.at[:, kv_cols], wr, ybuf.at[pl.ds(0, wr), pl.ds(0, 2 * k_width)]),
                (sm, smb, 16, None),
                (wo, wo_all, wr, ybuf.at[pl.ds(0, wr)]),
                (packed, gu, wr, None),
                (down, dnb, upad, None),
            ]
        )
    ]
    p_q, p_kv, p_s, p_o, p_gu, p_d = plane
    base = len(plane) * per
    chain = [
        Chain(buf, rows, nz, z, me, send, recv, base + i * Chain.sems(nz))
        for i, buf in enumerate([g_all, kv, x_all])
    ]
    c_g, c_kv, c_x = chain
    base += len(chain) * Chain.sems(nz)
    s_d = Scatter(dwd, 0, upad, d, r0, l0, False, nf, z, me, send, recv, base)
    base += Scatter.sems(nf)
    spare = len(plane)

    unit = ff // (nf * nz)
    n = pieces_of(2 * ff, 2 * wide, wr, nz * rows)
    width = 2 * ff // n
    loads = [
        pltpu.make_async_copy(
            w_gu.at[:, pl.ds(i * width, width)],
            dgu.at[pl.ds(i * wr, wr), pl.ds(0, width)],
            local.at[spare + 1 + i],
        )
        for i in range(n)
    ]
    fetched = upad + 16
    down_in = act.at[pl.ds(0, fetched), pl.ds(0, d)] if wide >= d else dgu.at[pl.ds(n * wr, fetched), pl.ds(0, d)]

    def down_load(k):
        start = min(unit * k // 16 * 16, ff // nf - fetched)
        copy = pltpu.make_async_copy(w_dn.at[pl.ds(start, fetched)], down_in, local.at[spare + 1 + n])
        return copy, unit * k - start

    def part_loads():
        for copy in loads:
            copy.start()
        for k in range(nz):

            @pl.when(z == k)
            def _():
                down_load(k)[0].start()

    def part_pack():
        for copy in loads:
            copy.wait()
        for k in range(nz):

            @pl.when(z == k)
            def _():
                pack(k, nz, nf, ff, unit, upad, wr, width, dgu, packed)
                copy, off = down_load(k)
                copy.wait()
                part = down_in[...].astype(F32)[off : off + unit]
                rest = jnp.zeros((upad - unit, d), F32)
                down[...] = jnp.concatenate([part, rest], 0).astype(BF)

    g_copy = pltpu.make_async_copy(g_ref, rows_at(g_all, z, rows), local.at[spare])
    g_copy.start()
    greet_ctx_and_plane(nz, nf, z, me)
    p_s.begin()
    p_kv.begin()
    g_copy.wait()
    c_g.begin()
    part_loads()

    given = []

    def give_out(src, dst):
        copy = pltpu.make_async_copy(src, dst, local.at[spare + 16 + len(given)])
        copy.start()
        given.append(copy)

    x = x_ref[...].astype(F32)
    inverse = lax.rsqrt(jnp.mean(x * x, -1, keepdims=True) + EPSILON)

    p_s.middle()
    p_kv.middle()
    p_q.begin()
    tokens = nz * rows
    qpos_ref[...], kpos_ref[...] = positions(order_ref, z, rows, tokens)
    angle = qpos_ref[...].astype(F32) * freq_ref[...]
    cos_ref[...] = jnp.cos(angle)
    first_half = lax.broadcasted_iota(jnp.int32, angle.shape, 1) < HEAD_DIM // 2
    sine = jnp.sin(angle)
    sin_ref[...] = jnp.where(first_half, -sine, sine)
    give_out(cos_ref, cos_out)
    give_out(sin_ref, sin_out)
    p_s.late()
    p_kv.late()
    p_s.finish()
    for f in range(nf):
        row = smb[f * 16 : (f + 1) * 16, :].astype(F32)[0:1]
        bias[0:1, f * nb : (f + 1) * nb] = row[:, :nb]
        gain_ref[0:1, f * ng : (f + 1) * ng] = row[:, nb : nb + ng]
        gain_ref[1:2, f * ng : (f + 1) * ng] = row[:, nb + ng : nb + 2 * ng]
    give_out(gain_ref, gain_out)
    normed = (x * inverse * gain_ref[0:1, :]).astype(BF)
    x_all[pl.ds(at128(z, rows), rows), :] = normed

    def fetch_qkv(c0, n):
        copy = pltpu.make_async_copy(
            wq_all.at[:, pl.ds(c0, n)], stage.at[pl.ds(0, d), pl.ds(c0, n)], local.at[spare]
        )
        copy.start()
        copy.wait()

    p_kv.finish()
    fetch_qkv(q_width, 2 * k_width)

    def project(t):
        c0 = at128(t, 2 * HEAD_DIM)
        y = dot(
            x_all[pl.ds(at128(z, rows), rows), :], stage[pl.ds(0, d), pl.ds(c0, 2 * HEAD_DIM)]
        ) + bias[0:1, pl.ds(c0, 2 * HEAD_DIM)]
        return y, c0

    def project_v(t):
        y, c0 = project(t)
        kv[pl.ds(at128(z, rows), rows), pl.ds(pl.multiple_of(c0 - q_width, 256), 256)] = y.astype(BF)

    def turned(y):
        halves = [
            turn(y[:, h * HEAD_DIM : (h + 1) * HEAD_DIM], cos_ref[...], sin_ref[...]).astype(BF)
            for h in range(2)
        ]
        return jnp.concatenate(halves, 1)

    project_v((q_width + k_width) // 256)
    y, _ = project(q_width // 256)
    kv[pl.ds(at128(z, rows), rows), 0:k_width] = turned(y)
    c_kv.begin()
    p_q.middle()
    p_o.begin()
    part_pack()
    for k in range(1, nz - 1):
        c_kv.forward(k)
    p_q.late()
    p_q.finish()
    fetch_qkv(0, q_width)
    c_kv.forward(nz - 1)

    def project_q(t):
        y, c0 = project(t)
        q_ref[:, pl.ds(c0, 256)] = turned(y)

    loop(q_width // 256, project_q)
    give_out(q_ref, q_out)
    p_o.middle()
    p_gu.begin()
    for k in range(1, nz):
        c_kv.arrive(k)
    for k in range(1, nz - 1):
        c_g.forward(k)

    lanes = lax.broadcasted_iota(jnp.int32, (rows, HEAD_DIM), 1)
    lse_ref[...] = jnp.zeros_like(lse_ref)

    def head(h):
        c0 = at128(h, HEAD_DIM)
        kc = at128(h // (HEADS // KV_HEADS), HEAD_DIM)
        vc = pl.multiple_of(kc + k_width, HEAD_DIM)
        s = dot_bt(q_ref[:, pl.ds(c0, HEAD_DIM)], kv[:, pl.ds(kc, HEAD_DIM)]) * scale
        s = jnp.where(kpos_ref[...] <= qpos_ref[...], s, MASKED)
        top = jnp.max(s, -1, keepdims=True)
        p = jnp.exp(s - top)
        total = jnp.sum(p, -1, keepdims=True)
        o = dot(p.astype(BF), kv[:, pl.ds(vc, HEAD_DIM)]) / total
        o_ref[:, pl.ds(c0, HEAD_DIM)] = o.astype(BF)
        lse_ref[...] = jnp.where(lanes == h, top + jnp.log(total), lse_ref[...])

    loop(HEADS, head)
    give_out(o_ref, o_out)
    give_out(lse_ref, lse_out)
    p_o.late()
    p_o.finish()
    fetch = pltpu.make_async_copy(wo_all, stage.at[pl.ds(0, q_width), pl.ds(0, d)], local.at[spare])
    fetch.start()
    fetch.wait()

    def out_proj(t):
        c0 = at128(t, 512)
        mid_ref[:, pl.ds(c0, 512)] = (
            dot(o_ref[...], stage[pl.ds(0, q_width), pl.ds(c0, 512)]) + x_ref[:, pl.ds(c0, 512)].astype(F32)
        )

    loop(d // 512, out_proj)
    give_out(mid_ref, mid_out)
    mid = mid_ref[...]
    inverse_two = lax.rsqrt(jnp.mean(mid * mid, -1, keepdims=True) + EPSILON)
    x_all[pl.ds(at128(z, rows), rows), :] = (mid * inverse_two * gain_ref[1:2, :]).astype(BF)
    c_x.begin()
    c_g.forward(nz - 1)
    for k in range(1, nz - 1):
        c_x.forward(k)
    p_gu.middle()
    p_d.begin()
    if nz <= 4:
        c_x.forward(nz - 1)
    p_gu.late()
    p_gu.finish()

    cols = 768 if wide % 768 == 0 else 256

    def hidden(j):
        r0 = at128(j, rows)

        def one(t):
            c0 = at128(t, cols)
            xb = x_all[pl.ds(r0, rows), :]
            gate = dot(xb, gu[:, pl.ds(c0, cols)])
            up = dot(xb, gu[:, pl.ds(pl.multiple_of(wide + c0, 128), cols)])
            act[pl.ds(r0, rows), pl.ds(c0, cols)] = (gate * jax.nn.sigmoid(gate) * up).astype(BF)
            dgu[pl.ds(r0, rows), pl.ds(c0, cols)] = gate.astype(BF)
            dgu[pl.ds(r0, rows), pl.ds(pl.multiple_of(wide + c0, 128), cols)] = up.astype(BF)

        loop(wide // cols, one)

    hidden(z)
    if nz > 4:
        c_x.forward(nz - 1)

    def nearest(k):
        c_x.arrive(k)
        hidden(c_x.order(k))

    loop(nz - 2, lambda i: nearest(i + 1))
    p_d.middle()
    nearest(nz - 1)
    for k in range(1, nz):
        c_g.arrive(k)
    high = 768 if nz <= 4 and wide % 768 == 0 else 256
    spots = [(r, c) for r in range(0, wide, high) for c in range(0, d, 768)]
    puts = []
    for i, (r, c) in enumerate(spots):
        if i >= 2:
            puts[i - 2].wait()
        slot = pl.ds(i % 2 * 768, 768)
        ybuf[0:high, slot] = dot_at(act[:, r : r + high], g_all[:, c : c + 768]).astype(BF)
        puts.append(
            pltpu.make_async_copy(
                ybuf.at[pl.ds(0, high), slot], dwd.at[pl.ds(r, high), pl.ds(c, 768)],
                local.at[spare + i % 2],
            )
        )
        puts[i].start()
        if i == len(spots) // 2:
            p_d.late()
    for put in puts[-2:]:
        put.wait()
    s_d.swap()
    p_d.finish()

    def back(j):
        r0 = at128(j, rows)

        def one(t):
            c0 = at128(t, cols)
            c1 = pl.multiple_of(wide + c0, 128)
            da = dot_bt(g_all[pl.ds(r0, rows), :], dnb[pl.ds(c0, cols), :])
            gate = dgu[pl.ds(r0, rows), pl.ds(c0, cols)].astype(F32)
            up = dgu[pl.ds(r0, rows), pl.ds(c1, cols)].astype(F32)
            sig = jax.nn.sigmoid(gate)
            dgu[pl.ds(r0, rows), pl.ds(c0, cols)] = (
                da * up * (sig * (1.0 + gate * (1.0 - sig)))
            ).astype(BF)
            dgu[pl.ds(r0, rows), pl.ds(c1, cols)] = (da * gate * sig).astype(BF)

        loop(wide // cols, one)

    rs = base

    slots = stage.at[:, pl.ds(0, d)]

    def slot_copy(src, dst, step):
        return remote(
            rows_at(slots, src, rows), rows_at(slots, dst, rows),
            send.at[rs + src], recv.at[rs + dst], z + step, me,
        )

    hold = nz <= 4

    def sides(i):
        j = c_x.order(nz - 1 - i)
        below, above = j > z, j < z
        got = jnp.logical_or(jnp.logical_and(below, z > 0), jnp.logical_and(above, z < nz - 1))
        return j, below, above, got, (pl.ds(at128(j, rows), rows), pl.ds(0, d))

    def terms(i, at):
        j = sides(i)[0]
        back(j)

        def one(t):
            c0 = at128(t, 768)
            ybuf[at : at + rows, pl.ds(c0, 768)] = dot_bt(
                dgu[pl.ds(at128(j, rows), rows), :], gu[pl.ds(c0, 768), :]
            ).astype(BF)

        loop(d // 768, one)

    def ship(j, below, above):
        @pl.when(below)
        def _():
            slot_copy(j, j, 1).start()

        @pl.when(above)
        def _():
            slot_copy(j, jnp.where(z - 1 == j, nz, j), -1).start()

    def early(i, at):
        j, below, above, got, where = sides(i)

        @pl.when(jnp.logical_not(got))
        def _():
            stage[where] = ybuf[at : at + rows, :]
            ship(j, below, above)

    def late(i, at):
        j, below, above, got, where = sides(i)

        @pl.when(got)
        def _():
            slot_copy(j, j, 0).wait_recv()
            stage[where] = (
                stage[where].astype(F32) + ybuf[at : at + rows, :].astype(F32)
            ).astype(BF)
            ship(j, below, above)

    if hold:
        between = {0: (s_d.merge, s_d.first)}
        for i in range(nz - 1):
            terms(i, i * rows)
            early(i, i * rows)
            for step in between.get(i, ()):
                step()
        late(0, 0)
        s_d.second()
    else:

        def at_once(i):
            terms(i, 0)
            early(i, 0)
            late(i, 0)

        loop(nz - 1, at_once)
        for step in (s_d.merge, s_d.first, s_d.second):
            step()
    back(z)

    def own(t):
        c0 = at128(t, 512)
        dx_ref[:, pl.ds(c0, 512)] = dot_bt(
            dgu[pl.ds(at128(z, rows), rows), :], gu[pl.ds(c0, 512), :]
        )

    loop(d // 512, own)

    c_x.drain()

    def down_terms(t):
        c0 = at128(t, 512)
        g_all[:, pl.ds(c0, 512)] = dot(act[...], dnb[:, pl.ds(c0, 512)]).astype(BF)

    c_g.drain()
    loop(d // 512, down_terms)
    out_p = pltpu.make_async_copy(g_all, dpart, local.at[spare + 3])
    out_p.start()
    if hold:
        for i in range(1, nz - 1):
            late(i, i * rows)
    p_gu.drain()

    side = 768 if wide % 768 == 0 else 256

    def w_gu_grad(t):
        c0 = at128(t, side)
        for r in range(0, d, 768):
            gu[r : r + 768, pl.ds(c0, side)] = dot_at(
                x_all[:, r : r + 768], dgu[:, pl.ds(c0, side)]
            ).astype(BF)

    outs = []
    for i in range(2):
        loop(wide // side, lambda t: w_gu_grad(t + i * (wide // side)))
        half = pl.ds(i * wide, wide)
        outs.append(pltpu.make_async_copy(gu.at[:, half], dwgu.at[:, half], local.at[spare + i]))
        outs[-1].start()
    s_d.last(d_own)
    out_kv = pltpu.make_async_copy(kv, kv_out, local.at[spare + 2])
    out_kv.start()

    @pl.when(z > 0)
    def _():
        slot_copy(z, z, 0).wait_recv()
        dx_ref[...] += rows_at(slots, z, rows)[...].astype(F32)

    @pl.when(z < nz - 1)
    def _():
        slot_copy(z, nz, 0).wait_recv()
        dx_ref[...] += rows_at(slots, nz, rows)[...].astype(F32)

    for item in (p_q, p_kv, p_s, p_o, p_d, c_kv, s_d):
        item.drain()

    def gave(i):
        j = c_x.order(i + 1)
        slot_copy(j, j, 0).wait_send()

    loop(nz - 1, gave)
    for copy in outs + given + [out_kv, out_p]:
        copy.wait()


def front(dims, wq, sm, wo, w_gu, w_dn, x, g, order, freq):
    nz, nf, rows, d, ff, wide, upad, nb, ng = dims
    q_width, k_width = HEADS * HEAD_DIM, KV_HEADS * HEAD_DIM
    qkv = q_width + 2 * k_width
    tokens = nz * rows
    any_, vm = pl.BlockSpec(memory_space=pl.ANY), pl.BlockSpec(memory_space=pltpu.VMEM)
    sems = 6 * PlaneGather.sems(nf) + 3 * Chain.sems(nz) + Scatter.sems(nf) + nz + 1
    chips = nf // 2
    out = jax.ShapeDtypeStruct
    return pl.pallas_call(
        functools.partial(front_kernel, dims),
        in_specs=[any_] * 5 + [vm, any_, pl.BlockSpec(memory_space=pltpu.SMEM), vm],
        out_specs=[any_] * 7 + [vm] + [any_] * 9,
        out_shape=[
            out((d, qkv), BF),
            out((q_width, d), BF),
            out((rows, q_width), BF),
            out((tokens, 2 * k_width), BF),
            out((rows, q_width), BF),
            out((rows, HEAD_DIM), F32),
            out((rows, d), F32),
            out((rows, d), F32),
            out((8, d), F32),
            out((rows, HEAD_DIM), F32),
            out((rows, HEAD_DIM), F32),
            out((d, 2 * wide), BF),
            out((tokens, d), BF),
            out((upad, d), BF),
            out((wide, d), BF),
            out((chips * upad, d), BF),
            out(((chips - 1) * upad, d), BF),
        ],
        scratch_shapes=[
            pltpu.VMEM((rows, q_width), BF),
            pltpu.VMEM((rows, q_width), BF),
            pltpu.VMEM((rows, HEAD_DIM), F32),
            pltpu.VMEM((rows, d), F32),
            pltpu.VMEM((8, d), F32),
            pltpu.VMEM((rows, HEAD_DIM), F32),
            pltpu.VMEM((rows, HEAD_DIM), F32),
            pltpu.VMEM((rows, 1), jnp.int32),
            pltpu.VMEM((1, tokens), jnp.int32),
            pltpu.VMEM((max(d, (nz + 1) * rows), qkv), BF),
            pltpu.VMEM((d, 2 * wide), BF),
            pltpu.VMEM((wide, d), BF),
            pltpu.VMEM((tokens, d), BF),
            pltpu.VMEM((tokens, d), BF),
            pltpu.VMEM((tokens, wide), BF),
            pltpu.VMEM((tokens, 2 * wide), BF),
            pltpu.VMEM((nf * 16, sm.shape[1]), BF),
            pltpu.VMEM((tokens, 2 * k_width), BF),
            pltpu.VMEM((8, qkv), F32),
            pltpu.VMEM(((nz - 1 if nz <= 4 else 1) * rows, d), BF),
            pltpu.VMEM((d // nf, 2 * wide), BF),
            pltpu.VMEM((upad, d), BF),
            pltpu.SemaphoreType.DMA((sems,)),
            pltpu.SemaphoreType.DMA((sems,)),
            pltpu.SemaphoreType.DMA((32,)),
        ],
        compiler_params=pltpu.CompilerParams(
            collective_id=0, has_side_effects=True, vmem_limit_bytes=VMEM_LIMIT
        ),
    )(wq, sm, wo, w_gu, w_dn, x, g, order, freq)


class Reduce:
    def __init__(self, slots, rows, nz, z, me, send, recv, base, order):
        self.slots, self.rows, self.nz, self.z, self.me = slots, rows, nz, z, me
        self.send, self.recv, self.base, self.order = send, recv, base, order

    @staticmethod
    def sems(nz):
        return nz + 1

    def copy(self, src, dst, step):
        return remote(
            rows_at(self.slots, src, self.rows), rows_at(self.slots, dst, self.rows),
            self.send.at[self.base + src], self.recv.at[self.base + dst], self.z + step, self.me,
        )

    def give(self, i, part):
        z, nz, rows = self.z, self.nz, self.rows
        j = self.order(nz - 1 - i)
        below, above = j > z, j < z
        got = jnp.logical_or(jnp.logical_and(below, z > 0), jnp.logical_and(above, z < nz - 1))
        where = pl.ds(at128(j, rows) if rows % 128 == 0 else pl.multiple_of(j * rows, 16), rows)
        own = part(j)

        @pl.when(got)
        def _():
            self.copy(j, j, 0).wait_recv()
            self.slots[where, :] = (self.slots[where, :].astype(F32) + own.astype(F32)).astype(BF)

        @pl.when(jnp.logical_not(got))
        def _():
            self.slots[where, :] = own.astype(BF)

        @pl.when(below)
        def _():
            self.copy(j, j, 1).start()

        @pl.when(above)
        def _():
            self.copy(j, jnp.where(z - 1 == j, nz, j), -1).start()

    def take(self, total):
        z, nz = self.z, self.nz

        @pl.when(z > 0)
        def _():
            self.copy(z, z, 0).wait_recv()
            total[...] += rows_at(self.slots, z, self.rows)[...].astype(F32)

        @pl.when(z < nz - 1)
        def _():
            self.copy(z, nz, 0).wait_recv()
            total[...] += rows_at(self.slots, nz, self.rows)[...].astype(F32)

    def drain(self):
        def gave(i):
            j = self.order(i + 1)
            self.copy(j, j, 0).wait_send()

        loop(self.nz - 1, gave)


def back_kernel(
    dims,
    dwgu, d_own, dpart, wq_all, wo_all, kv_hbm, mid_hbm, dx_hbm,
    x_hbm, g_hbm, q_hbm, o_hbm, lse_hbm, gain_hbm, cos_hbm, sin_hbm, order_ref,
    hid_ref, gh_ref, all_d, all_g, all_u, z_out, tiny_out,
    x_ref, g_ref, q_ref, o_ref, lse_ref, gain_ref, cos_ref, sin_ref, qpos_ref, kpos_ref,
    stage, full, dslots, do_ref, kv, dkv, kslots, m32, dh, t32, dqkv, normed,
    r3, l3, r4, l4, zsrc, zslots, zlow, zown, gain_sums, tiny, tin, zin,
    r1, r2, l1, l2, own2, own_sems, send, recv, local,
):
    nz, nf, rows, d, wide, upad, nb, ng, ch = dims
    z, me = lax.axis_index("ctx"), lax.axis_index("fsdp")
    q_width, k_width = HEADS * HEAD_DIM, KV_HEADS * HEAD_DIM
    qkv = q_width + 2 * k_width
    scale = HEAD_DIM ** (-0.5)
    wr = d // nf
    place = {"nf": nf, "z": z, "me": me, "send": send, "recv": recv}
    per = Scatter.sems(nf)
    own = {"own": own2, "sems": own_sems}
    s_g = Scatter(dwgu, 0, wr, wide, r1, l1, True, base=per, **own, **place)
    s_u = Scatter(dwgu, wide, wr, wide, r2, l2, True, base=2 * per, **own, **place)
    s_o = Scatter(full, 0, wr, d, r3, l3, True, base=3 * per, **place)
    s_q = Scatter(full, 0, wr, qkv, r4, l4, True, base=4 * per, **place)
    base = 5 * per
    line = {"nz": nz, "z": z, "me": me, "send": send, "recv": recv}
    per = Chain.sems(nz)
    a_d = Chain(all_d, upad, base=base, **line)
    a_g = Chain(all_g, wr, base=base + per, **line)
    a_u = Chain(all_u, wr, base=base + 2 * per, **line)
    a_z = Chain(z_out, ch, base=base + 3 * per, **line)
    base += 4 * per
    per = Reduce.sems(nz)
    d_kv = Reduce(kslots, rows, base=base, order=a_d.order, **line)
    d_h = Reduce(dslots, rows, base=base + per, order=a_d.order, **line)
    d_z = Reduce(zslots, ch, base=base + 2 * per, order=a_d.order, **line)
    base += 3 * per

    def fetch(src, dst, i):
        copy = pltpu.make_async_copy(src, dst, local.at[i])
        copy.start()
        return copy

    def stream(src, cols, use):
        copies = []
        for t in range(src.shape[0] // 512):
            slot = stage.at[pl.ds(t % 2 * 512, 512), pl.ds(0, cols)]
            copies.append(
                pltpu.make_async_copy(src.at[pl.ds(t * 512, 512)], slot, local.at[6 + t % 2])
            )
        for copy in copies[:2]:
            copy.start()
        for t, copy in enumerate(copies):
            copy.wait()
            use(t, t % 2 * 512)
            if t + 2 < len(copies):
                copies[t + 2].start()

    coming = {}

    def bring(name, src, dst):
        coming[name] = fetch(src, dst, 9 + len(coming))

    def need(*names):
        for name in names:
            if name in coming:
                coming.pop(name).wait()

    arrays = (
        ("mid", mid_hbm, m32), ("dx", dx_hbm, dh), ("g", g_hbm, g_ref), ("gain", gain_hbm, gain_ref),
        ("o", o_hbm, o_ref), ("kv", kv_hbm, kv), ("q", q_hbm, q_ref), ("lse", lse_hbm, lse_ref),
        ("cos", cos_hbm, cos_ref), ("sin", sin_hbm, sin_ref), ("x", x_hbm, x_ref),
    )
    for array in arrays:
        bring(*array)
    d_in = fetch(d_own, rows_at(all_d, z, upad), 8)

    barrier = pltpu.get_barrier_semaphore()
    for k in range(1, nf):
        pl.semaphore_signal(barrier, inc=1, device_id=(z, me ^ k), device_id_type=MESH)
    for k in range(1, nz):
        pl.semaphore_signal(barrier, inc=1, device_id=((z + k) % nz, me), device_id_type=MESH)
    pl.semaphore_wait(barrier, nf + nz - 2)

    dkv[...] = jnp.zeros_like(dkv)
    qpos_ref[...], kpos_ref[...] = positions(order_ref, z, rows, nz * rows)
    lanes = lax.broadcasted_iota(jnp.int32, (rows, HEAD_DIM), 1)
    mine = dkv.at[pl.ds(at128(z, rows), rows)]
    third = HEADS // 3

    def norm_back():
        need("mid", "dx", "g", "gain")
        mid, dxn = m32[...], dh[...]
        inverse_two = lax.rsqrt(jnp.mean(mid * mid, -1, keepdims=True) + EPSILON)
        scaled = gain_ref[1:2, :] * dxn
        gain_sums[1:2, :] = jnp.sum(dxn * mid * inverse_two, 0, keepdims=True)
        dh[...] = (
            g_ref[...].astype(F32)
            + inverse_two * scaled
            - mid
            * (inverse_two * inverse_two * inverse_two)
            * jnp.mean(scaled * mid, -1, keepdims=True)
        )
        normed[...] = dh[...].astype(BF)

    def out_back():
        def one(t, r):
            do_ref[:, t * 512 : t * 512 + 512] = dot_bt(
                normed[...], stage[r : r + 512, 0:d]
            ).astype(BF)

        stream(wo_all, d, one)

    def w_out_grad():
        need("o")

        def one(t):
            c0 = at128(t, 512)
            full[pl.ds(0, q_width), pl.ds(c0, 512)] = dot_at(
                o_ref[...], normed[:, pl.ds(c0, 512)]
            ).astype(BF)

        loop(d // 512, one)

    def heads(start, count):
        need("o", "kv", "q", "lse", "cos", "sin")
        loop(count, lambda i: head(i + start))

    def head(h):
        c0 = at128(h, HEAD_DIM)
        kc = at128(h // (HEADS // KV_HEADS), HEAD_DIM)
        vc = pl.multiple_of(kc + k_width, HEAD_DIM)
        q, k, v = q_ref[:, pl.ds(c0, HEAD_DIM)], kv[:, pl.ds(kc, HEAD_DIM)], kv[:, pl.ds(vc, HEAD_DIM)]
        do = do_ref[:, pl.ds(c0, HEAD_DIM)]
        lse = jnp.sum(jnp.where(lanes == h, lse_ref[...], 0.0), -1, keepdims=True)
        delta = jnp.sum(
            do.astype(F32) * o_ref[:, pl.ds(c0, HEAD_DIM)].astype(F32), -1, keepdims=True
        )
        s = jnp.where(kpos_ref[...] <= qpos_ref[...], dot_bt(q, k) * scale, MASKED)
        p = jnp.exp(s - lse)
        dkv[:, pl.ds(vc, HEAD_DIM)] += dot_at(p.astype(BF), do)
        ds = (p * (dot_bt(do, v) - delta)).astype(BF)
        dq = dot(ds, k) * scale
        dkv[:, pl.ds(kc, HEAD_DIM)] += dot_at(ds, q) * scale
        dqkv[:, pl.ds(c0, HEAD_DIM)] = turn(dq, cos_ref[...], -sin_ref[...]).astype(BF)

    def kv_part(j):
        return dkv[pl.ds(at128(j, rows), rows), :]

    def down_part(j):
        part = stage.at[pl.ds(0, rows), pl.ds(0, d)]
        fetch(rows_at(dpart, j, rows), part, 1).wait()
        return part[...]

    def z_part(j):
        return zsrc[pl.ds(pl.multiple_of(j * ch, 16), ch), :]

    def project_back():
        for h in range(KV_HEADS):
            c0 = h * HEAD_DIM
            dqkv[:, q_width + c0 : q_width + c0 + HEAD_DIM] = turn(
                mine[:, c0 : c0 + HEAD_DIM], cos_ref[...], -sin_ref[...]
            ).astype(BF)
        dqkv[:, q_width + k_width :] = mine[:, k_width:].astype(BF)

    def w_qkv_grad():
        need("x")
        x = x_ref[...].astype(F32)
        inverse = lax.rsqrt(jnp.mean(x * x, -1, keepdims=True) + EPSILON)
        normed[...] = (x * inverse * gain_ref[0:1, :]).astype(BF)
        s_o.drain()

        def one(t):
            c0 = at128(t, 512)
            full[pl.ds(0, d), pl.ds(c0, 512)] = dot_at(
                normed[...], dqkv[:, pl.ds(c0, 512)]
            ).astype(BF)

        loop(qkv // 512, one)

    tiny_copies = []

    def input_back():
        def one(t, r):
            t32[:, t * 512 : t * 512 + 512] = dot_bt(dqkv[...], stage[r : r + 512, :])

        stream(wq_all, qkv, one)
        x = x_ref[...].astype(F32)
        inverse = lax.rsqrt(jnp.mean(x * x, -1, keepdims=True) + EPSILON)
        dxn = t32[...]
        scaled = gain_ref[0:1, :] * dxn
        gain_one = jnp.sum(dxn * x * inverse, 0, keepdims=True)
        gain_two = gain_sums[1:2, :]
        bias = jnp.sum(dqkv[...].astype(F32), 0, keepdims=True)
        gh_ref[...] = (
            dh[...]
            + inverse * scaled
            - x * (inverse * inverse * inverse) * jnp.mean(scaled * x, -1, keepdims=True)
        ).astype(BF)

        cut = q_width + k_width
        qk, vb = cut // nf, k_width // nf
        tiny[...] = jnp.zeros_like(tiny)
        for f in range(nf):
            r = slice(8 * f, 8 * f + 1)
            tiny[r, 0:qk] = bias[:, f * qk : (f + 1) * qk]
            tiny[r, qk : qk + vb] = bias[:, cut + f * vb : cut + (f + 1) * vb]
            tiny[r, qk + vb : qk + vb + ng] = gain_one[:, f * ng : (f + 1) * ng]
            tiny[r, qk + vb + ng : qk + vb + 2 * ng] = gain_two[:, f * ng : (f + 1) * ng]
        own = pl.ds(pl.multiple_of(me * 8, 8), 8)
        tin[own, :] = tiny[own, :]
        for k in range(1, nf):
            copy = remote(
                rows_at(tiny, me ^ k, 8), rows_at(tin, me, 8),
                send.at[base + k], recv.at[base + k], z, me ^ k,
            )
            copy.start()
            tiny_copies.append(copy)

    def tiny_along():
        for copy in tiny_copies:
            copy.wait_recv()
        total = tin[0:8, :]
        for f in range(1, nf):
            total = total + tin[8 * f : 8 * f + 8, :]
        zin[pl.ds(pl.multiple_of(z * 8, 8), 8), :] = total
        for k in range(1, nz):
            copy = remote(
                rows_at(zin, z, 8), rows_at(zin, z, 8),
                send.at[base + nf + k], recv.at[base + nf + k], (z + k) % nz, me,
            )
            copy.start()
            tiny_copies.append(copy)

    def z_take():
        zown[...] = z_part(z).astype(F32)
        d_z.take(zown)
        zlow[...] = zown[...].astype(BF)
        fetch(zlow, rows_at(z_out, z, ch), 2).wait()

    def h_take():
        m32[...] += down_part(z).astype(F32)
        d_h.take(m32)
        hid_ref[...] = m32[...].astype(BF)

    a_d.begin(d_own)
    s_g.swap()
    norm_back()
    out_back()
    w_out_grad()
    s_o.swap()
    s_g.merge()
    s_g.first()
    s_u.swap()
    a_d.forward(1)
    for k in range(2, nz - 1):
        a_d.forward(k)
    heads(0, third)
    heads(third, third)
    heads(2 * third, third)
    s_u.merge()
    s_g.second()
    s_u.first()
    a_d.forward(nz - 1)
    d_kv.give(0, kv_part)
    for i in range(1, nz - 2):
        d_kv.give(i, kv_part)
    d_kv.give(nz - 2, kv_part)
    s_o.merge()
    s_o.first()
    s_g.last(s_g.block(0))
    fetch(s_g.block(0), rows_at(all_g, z, wr), 4).wait()
    a_g.begin()
    s_u.second()
    a_g.forward(1)
    for k in range(2, nz - 1):
        a_g.forward(k)
    s_o.second()
    d_kv.take(mine)
    d_h.give(0, down_part)
    project_back()
    a_g.forward(nz - 1)
    w_qkv_grad()
    s_q.swap()
    s_o.last(zsrc.at[pl.ds(0, wr), pl.ds(0, d)])
    s_u.last(s_u.block(0))
    fetch(s_u.block(0), rows_at(all_u, z, wr), 5).wait()
    s_q.merge()
    s_q.first()
    a_u.begin()
    a_u.forward(1)
    s_q.second()
    for k in range(2, nz - 1):
        a_u.forward(k)
    a_u.forward(nz - 1)
    input_back()
    s_q.last(zsrc.at[pl.ds(0, wr), pl.ds(d, qkv)])
    d_z.give(0, z_part)
    tiny_along()
    for i in range(1, nz - 2):
        d_z.give(i, z_part)
    for i in range(1, nz - 2):
        d_h.give(i, down_part)
    d_z.give(nz - 2, z_part)
    d_h.give(nz - 2, down_part)
    for k in range(1, nz):
        a_u.arrive(k)
    z_take()
    for k in range(1, nz):
        a_g.arrive(k)
    a_z.begin()
    a_z.forward(1)
    for k in range(1, nz):
        a_d.arrive(k)
    for k in range(2, nz - 1):
        a_z.forward(k)
    a_z.forward(nz - 1)
    h_take()
    for k in range(1, nz):
        a_z.arrive(k)
    for copy in tiny_copies[nf - 1 :]:
        copy.wait_recv()
    total = zin[0:8, :]
    for j in range(1, nz):
        total = total + zin[8 * j : 8 * j + 8, :]
    tiny_out[...] = total
    d_in.wait()
    for item in (s_g, s_u, s_o, s_q, a_d, a_g, a_u, a_z, d_kv, d_h, d_z):
        item.drain()
    for copy in tiny_copies:
        copy.wait_send()


def back(dims, *args):
    nz, nf, rows, d, wide, upad, nb, ng, ch = dims
    q_width, k_width = HEADS * HEAD_DIM, KV_HEADS * HEAD_DIM
    qkv = q_width + 2 * k_width
    tokens, chips, wr = nz * rows, nf // 2, d // nf
    tiny = -(-((qkv + 2 * d) // nf) // 128) * 128
    any_, vm = pl.BlockSpec(memory_space=pl.ANY), pl.BlockSpec(memory_space=pltpu.VMEM)
    out = jax.ShapeDtypeStruct
    sems = 5 * Scatter.sems(nf) + 4 * Chain.sems(nz) + 3 * Reduce.sems(nz) + nf + nz
    pieces = [(upad, d), (wr, wide), (wr, wide)]
    return pl.pallas_call(
        functools.partial(back_kernel, dims),
        in_specs=[any_] * 16 + [pl.BlockSpec(memory_space=pltpu.SMEM)],
        out_specs=[vm, vm] + [any_] * 4 + [vm],
        out_shape=[out((rows, d), BF), out((rows, d), BF)]
        + [out((nz * r, c), BF) for r, c in pieces]
        + [out((nz * ch, d + qkv), BF), out((8, tiny), F32)],
        scratch_shapes=[
            pltpu.VMEM((rows, d), BF),
            pltpu.VMEM((rows, d), BF),
            pltpu.VMEM((rows, q_width), BF),
            pltpu.VMEM((rows, q_width), BF),
            pltpu.VMEM((rows, HEAD_DIM), F32),
            pltpu.VMEM((8, d), F32),
            pltpu.VMEM((rows, HEAD_DIM), F32),
            pltpu.VMEM((rows, HEAD_DIM), F32),
            pltpu.VMEM((rows, 1), jnp.int32),
            pltpu.VMEM((1, tokens), jnp.int32),
            pltpu.VMEM((1024, qkv), BF),
            pltpu.VMEM((d, qkv), BF),
            pltpu.VMEM(((nz + 1) * rows, d), BF),
            pltpu.VMEM((rows, q_width), BF),
            pltpu.VMEM((tokens, 2 * k_width), BF),
            pltpu.VMEM((tokens, 2 * k_width), F32),
            pltpu.VMEM(((nz + 1) * rows, 2 * k_width), BF),
            pltpu.VMEM((rows, d), F32),
            pltpu.VMEM((rows, d), F32),
            pltpu.VMEM((rows, d), F32),
            pltpu.VMEM((rows, qkv), BF),
            pltpu.VMEM((rows, d), BF),
            pltpu.VMEM((chips * wr, d), BF),
            pltpu.VMEM(((chips - 1) * wr, d), BF),
            pltpu.VMEM((chips * wr, qkv), BF),
            pltpu.VMEM(((chips - 1) * wr, qkv), BF),
            pltpu.VMEM((nz * ch, d + qkv), BF),
            pltpu.VMEM(((nz + 1) * ch, d + qkv), BF),
            pltpu.VMEM((ch, d + qkv), BF),
            pltpu.VMEM((ch, d + qkv), F32),
            pltpu.VMEM((8, d), F32),
            pltpu.VMEM((nf * 8, tiny), F32),
            pltpu.VMEM((nf * 8, tiny), F32),
            pltpu.VMEM((nz * 8, tiny), F32),
            pltpu.VMEM((chips * wr, wide), BF),
            pltpu.VMEM((chips * wr, wide), BF),
            pltpu.VMEM(((chips - 1) * wr, wide), BF),
            pltpu.VMEM(((chips - 1) * wr, wide), BF),
            pltpu.VMEM((2 * wr, wide), BF),
            pltpu.SemaphoreType.DMA((2,)),
            pltpu.SemaphoreType.DMA((sems,)),
            pltpu.SemaphoreType.DMA((sems,)),
            pltpu.SemaphoreType.DMA((20,)),
        ],
        compiler_params=pltpu.CompilerParams(
            collective_id=1, has_side_effects=True, vmem_limit_bytes=VMEM_LIMIT
        ),
    )(*args)


def shards(
    hidden_in, w_qkv, b_qkv, w_out, w_gate_up, w_down, gain_attn, gain_mlp, block_order, cotangent
):
    nz, nf = lax.axis_size("ctx"), lax.axis_size("fsdp")
    q_width, k_width = HEADS * HEAD_DIM, KV_HEADS * HEAD_DIM
    rows = hidden_in.shape[1]
    ff = w_gate_up.shape[1] // 2
    unit = ff // (nf * nz)
    freqs = THETA ** (-(jnp.arange(HEAD_DIM // 2).astype(F32) * 2.0 / HEAD_DIM))
    freqs = jnp.concatenate([freqs, freqs])[None]
    upad = -(-unit // 16) * 16
    wide = nf * upad
    nb, ng = b_qkv.shape[0], gain_attn.shape[0]
    d = hidden_in.shape[2]
    small = jnp.concatenate([b_qkv, gain_attn, gain_mlp])
    small = jnp.pad(small[None], ((0, 15), (0, -small.shape[0] % 128)))
    grad_low = cotangent[0]
    (whole_qkv, whole_out, q_low, kv_all, attn_low, lse, middle, grad_normed_two, gains, cos2, sin2, gate_up_local, down_part,
     down_own, *_) = front(
        (nz, nf, rows, d, ff, wide, upad, nb, ng),
        w_qkv, small, w_out, w_gate_up, w_down, hidden_in[0], grad_low, block_order, freqs,
    )
    ch = -(-(d // (nf * nz)) // 16) * 16
    hidden, grad_hidden, down_all, gate_all, up_all, attn_all, tiny = back(
        (nz, nf, rows, d, wide, upad, nb, ng, ch),
        gate_up_local, down_own, down_part, whole_qkv, whole_out, kv_all, middle, grad_normed_two,
        hidden_in[0], grad_low, q_low, attn_low, lse, gains, cos2, sin2, block_order,
    )
    e1 = (q_width + k_width) // nf
    e2 = e1 + k_width // nf
    e3 = e2 + ng
    shard = d // nf
    cuts = (0, e1, e2, e3, e3 + ng)
    if unit % 8 == 0 and shard % (16 * nz) == 0 and ch * nz == shard:
        gu_grad, down_grad, qkv_grad, out_grad, hidden, grad_hidden, *smalls = finish(
            gate_all, up_all, down_all, attn_all, tiny, hidden, grad_hidden, nz, nf, ff, cuts
        )
        b_qk, b_v, g_one, g_two = (item[0] for item in smalls)
    else:
        gu_grad = unpack(gate_all, up_all, nz, nf, ff)
        down_grad = down_all.reshape(nz, upad, d)[:, :unit].reshape(nz * unit, d).astype(F32)
        qkv_grad = attn_all[:shard, d:].astype(F32)
        out_grad = attn_all[:shard, :d].astype(F32)
        b_qk, b_v, g_one, g_two = (tiny[0, lo:hi] for lo, hi in zip(cuts, cuts[1:]))
    return (
        hidden[None],
        grad_hidden[None],
        qkv_grad,
        b_qk,
        b_v,
        out_grad,
        gu_grad,
        down_grad,
        g_one,
        g_two,
    )


def solution(mesh):
    placed = (
        P("fsdp", "ctx", None),
        P("fsdp", None),
        P("fsdp"),
        P("fsdp", None),
        P("fsdp", None),
        P("fsdp", None),
        P("fsdp"),
        P("fsdp"),
        P("fsdp", None),
        P("fsdp", "ctx", None),
    )
    return jax.shard_map(
        shards,
        mesh=mesh,
        in_specs=placed,
        out_specs=(
            P("fsdp", "ctx", None),
            P("fsdp", "ctx", None),
            P("fsdp", None),
            P("fsdp"),
            P("fsdp"),
            P("fsdp", None),
            P("fsdp", None),
            P("fsdp", None),
            P("fsdp"),
            P("fsdp"),
        ),
        check_vma=False,
    )
```

```python
import functools

import jax
import jax.numpy as jnp
import numpy as np
from jax import lax
from jax.experimental import pallas as pl
from jax.experimental.pallas import tpu as pltpu
from jax.sharding import PartitionSpec as P

HEADS = 12
KV_HEADS = 2
HEAD_DIM = 128
EPSILON = 1e-06
THETA = 1000000.0
MASKED = -1e30
BF = jnp.bfloat16
F32 = jnp.float32


def dot(a, b):
    return jnp.dot(a, b, preferred_element_type=F32)


def dot_bt(a, b):
    return lax.dot_general(a, b, (((1,), (1,)), ((), ())), preferred_element_type=F32)


def dot_at(a, b):
    return lax.dot_general(a, b, (((0,), (0,)), ((), ())), preferred_element_type=F32)


def positions(order_ref, z, rows, tokens):
    half = rows // 2
    row = lax.broadcasted_iota(jnp.int32, (rows, 1), 0)
    mine = jnp.where(
        row < half, order_ref[0, 2 * z] * half + row, order_ref[0, 2 * z + 1] * half + row - half
    )
    lane = lax.broadcasted_iota(jnp.int32, (1, tokens), 1)
    places = lane
    for i in range(tokens // half):
        places = jnp.where(lane >= i * half, order_ref[0, i] * half + lane - i * half, places)
    return mine, places


def half_rows(rows):
    return -(-rows // 32) * 16


def pieces_of(columns, width, rows, room):
    n = next(n for n in range(1, columns) if columns % (128 * n) == 0 and columns // n <= width)
    assert n * rows <= room
    return n


def pack(k, nz, nf, ff, unit, upad, rows, width, held, out):
    for h in range(2):
        for f in range(nf):
            src = h * ff + f * (ff // nf) + k * unit
            dst = (h * nf + f) * upad
            done = 0
            while done < unit:
                piece, at = divmod(src + done, width)
                n = min(unit - done, width - at)
                out[:, dst + done : dst + done + n] = held[
                    piece * rows : (piece + 1) * rows, at : at + n
                ]
                done += n
            if upad > unit:
                out[:, dst + unit : dst + upad] = jnp.zeros((rows, upad - unit), out.dtype)


def unpack_kernel(nz, nf, ff, unit, upad, *refs):
    out_ref = refs[-1]
    for k in range(nz):
        for h in range(2):
            for f in range(nf):
                src = f * upad
                dst = h * ff + f * (ff // nf) + k * unit
                part = refs[h * nz + k]
                out_ref[:, dst : dst + unit] = part[:, src : src + unit].astype(F32)


def unpack(gate, up, nz, nf, ff):
    rows, wide = gate.shape[0] // nz, gate.shape[1]
    step = 32
    specs = [
        pl.BlockSpec((step, wide), lambda i, k=k: (k * (rows // step) + i, 0)) for k in range(nz)
    ]
    return pl.pallas_call(
        functools.partial(unpack_kernel, nz, nf, ff, ff // (nf * nz), wide // nf),
        grid=(rows // step,),
        in_specs=specs * 2,
        out_specs=pl.BlockSpec((step, 2 * ff), lambda i: (i, 0)),
        out_shape=jax.ShapeDtypeStruct((rows, 2 * ff), F32),
    )(*[gate] * nz, *[up] * nz)


def finish_kernel(nz, nf, ff, unit, upad, cuts, *refs):
    gates, ups = refs[:nz], refs[nz : 2 * nz]
    down, attn, tiny, hid, gh = refs[2 * nz : 2 * nz + 5]
    gu_out, down_out, qkv_out, out_out, hid_out, gh_out, *tiny_outs = refs[2 * nz + 5 :]
    unpack_kernel(nz, nf, ff, unit, upad, *gates, *ups, gu_out)
    down_out[...] = down[...].astype(F32)[0:unit]
    d = out_out.shape[1]
    qkv_out[...] = attn[:, d:].astype(F32)
    out_out[...] = attn[:, :d].astype(F32)
    hid_out[...] = hid[...]
    gh_out[...] = gh[...]

    @pl.when(pl.program_id(0) == 0)
    def _():
        for out, lo, hi in zip(tiny_outs, cuts, cuts[1:]):
            out[...] = tiny[0:1, lo:hi]


def finish(gate, up, down, attn, tiny, hid, gh, nz, nf, ff, cuts):
    rows, wide = gate.shape[0] // nz, gate.shape[1]
    unit, upad, d = ff // (nf * nz), wide // nf, hid.shape[1]
    step = rows // nz
    along = [
        pl.BlockSpec((step, wide), lambda i, k=k: (k * (rows // step) + i, 0)) for k in range(nz)
    ]
    part = hid.shape[0] // nz

    def by_step(r, c):
        return pl.BlockSpec((r, c), lambda i: (i, 0))

    def still(c):
        return pl.BlockSpec((1, c), lambda i: (0, 0))

    qkv = attn.shape[1] - d
    sizes = [hi - lo for lo, hi in zip(cuts, cuts[1:])]
    out = jax.ShapeDtypeStruct
    return pl.pallas_call(
        functools.partial(finish_kernel, nz, nf, ff, unit, upad, cuts),
        grid=(nz,),
        in_specs=along * 2
        + [
            by_step(upad, d),
            by_step(step, d + qkv),
            pl.BlockSpec(tiny.shape, lambda i: (0, 0)),
            by_step(part, d),
            by_step(part, d),
        ],
        out_specs=[
            by_step(step, 2 * ff),
            by_step(unit, d),
            by_step(step, qkv),
            by_step(step, d),
            by_step(part, d),
            by_step(part, d),
        ]
        + [still(n) for n in sizes],
        out_shape=[
            out((rows, 2 * ff), F32),
            out((nz * unit, d), F32),
            out((rows, qkv), F32),
            out((rows, d), F32),
            out(hid.shape, BF),
            out(hid.shape, BF),
        ]
        + [out((1, n), F32) for n in sizes],
        compiler_params=pltpu.CompilerParams(vmem_limit_bytes=VMEM_LIMIT),
    )(*[gate] * nz, *[up] * nz, down, attn, tiny, hid, gh)


MESH = pl.DeviceIdType.MESH
VMEM_LIMIT = 63 * 2**20


def remote(src, dst, send, recv, z, f):
    return pltpu.make_async_remote_copy(
        src_ref=src, dst_ref=dst, send_sem=send, recv_sem=recv, device_id=(z, f), device_id_type=MESH
    )


def rows_at(ref, index, count):
    return ref.at[pl.ds(pl.multiple_of(index * count, count), count)]


class PlaneGather:
    def __init__(self, src, dst, rows, nf, z, me, send, recv, local, base, bounce=None):
        self.src, self.dst, self.rows, self.nf, self.z, self.me = src, dst, rows, nf, z, me
        self.send, self.recv, self.base = send, recv, base
        home = rows_at(dst, me, rows)
        if bounce is None:
            self.local = (pltpu.make_async_copy(src, home, local),)
        else:
            self.local = (
                pltpu.make_async_copy(src, bounce, local),
                pltpu.make_async_copy(bounce, home, local),
            )
        self.sent = []
        self.cut = half_rows(rows)
        self.swaps = {}

    @staticmethod
    def sems(nf):
        return 2 * nf

    def slot(self, k, lo=0, hi=None):
        hi = self.rows if hi is None else hi
        start = pl.multiple_of((self.me ^ k) * self.rows, 16) + lo
        return self.dst.at[pl.ds(pl.multiple_of(start, 16), hi - lo)]

    def push(self, index, src, dst, flip_by):
        copy = remote(
            src, dst, self.send.at[self.base + index], self.recv.at[self.base + index],
            self.z, self.me ^ flip_by,
        )
        copy.start()
        self.sent.append(copy)
        return copy

    def begin(self):
        self.local[0].start()
        self.direct = {}
        for k in (2, 4) if self.nf == 8 else range(2, self.nf, 2):
            self.direct[k] = self.push(k, self.src, self.slot(0), k)
        self.swaps[0] = self.push(1, self.src, self.slot(0), 1)

    def swap(self, k):
        self.swaps[k] = self.push(k + 1, self.slot(k), self.slot(k), 1)

    def middle(self):
        for one, two in zip(self.local, self.local[1:]):
            one.wait()
            two.start()
        for k, copy in self.direct.items():
            copy.wait_recv()
            if self.nf == 8:
                if k == 2:
                    self.far_a = self.push(6, self.slot(2, 0, self.cut), self.slot(2, 0, self.cut), 4)
                elif self.cut < self.rows:
                    self.far_b = self.push(
                        8, self.slot(4, self.cut), self.slot(4, self.cut), 2
                    )
            self.swap(k)

    def late(self):
        if self.nf == 8:
            self.far_a.wait_recv()
            if self.cut < self.rows:
                self.far_b.wait_recv()
            self.swap(6)

    def finish(self):
        self.local[-1].wait()
        for copy in self.swaps.values():
            copy.wait_recv()

    def drain(self):
        for copy in self.sent:
            copy.wait_send()


class Chain:
    def __init__(self, buf, rows, nz, z, me, send, recv, base):
        self.buf, self.rows, self.nz, self.z, self.me = buf, rows, nz, z, me
        self.send, self.recv, self.base = send, recv, base

    @staticmethod
    def sems(nz):
        return nz + 2

    def copy(self, j, sem, step, src=None):
        slot = rows_at(self.buf, j, self.rows)
        return remote(
            slot if src is None else src, slot, self.send.at[self.base + sem], self.recv.at[self.base + j], self.z + step, self.me
        )

    def order(self, k):
        z, nz = self.z, self.nz
        below, above = z, nz - 1 - z
        m = jnp.minimum(below, above)
        near = jnp.where(k % 2 == 1, z - (k + 1) // 2, z + k // 2)
        far = jnp.where(above > below, z + (k - m), z - (k - m))
        return jnp.where(k <= 2 * m, near, far)

    def begin(self, src=None):
        z, nz = self.z, self.nz

        @pl.when(z < nz - 1)
        def _():
            self.copy(z, nz, 1, src).start()

        @pl.when(z > 0)
        def _():
            self.copy(z, nz + 1, -1, src).start()

    def passing(self, j):
        z, nz = self.z, self.nz
        return jnp.logical_and(j < z, z < nz - 1), jnp.logical_and(j > z, z > 0)

    def forward(self, k):
        j = self.order(k)
        up, down = self.passing(j)

        @pl.when(up)
        def _():
            self.copy(j, j, 1).wait_recv()
            self.copy(j, j, 1).start()

        @pl.when(down)
        def _():
            self.copy(j, j, -1).wait_recv()
            self.copy(j, j, -1).start()

    def arrive(self, k):
        j = self.order(k)
        up, down = self.passing(j)

        @pl.when(jnp.logical_not(jnp.logical_or(up, down)))
        def _():
            self.copy(j, j, 0).wait_recv()

    def drain(self):
        z, nz = self.z, self.nz

        @pl.when(z < nz - 1)
        def _():
            self.copy(z, nz, 1).wait_send()

        @pl.when(z > 0)
        def _():
            self.copy(z, nz + 1, -1).wait_send()

        def one(k, carry):
            j = self.order(k)
            up, down = self.passing(j)

            @pl.when(jnp.logical_or(up, down))
            def _():
                self.copy(j, j, 0).wait_send()

            return carry

        lax.fori_loop(1, nz, one, 0)


class Scatter:
    def __init__(self, src, c0, rows, cols, recv4, land, inside, nf, z, me, send, recv, base, own=None, sems=None):
        self.src, self.c0, self.rows, self.cols = src, c0, rows, cols
        self.recv4, self.land, self.inside = recv4, land, inside
        self.nf, self.z, self.me, self.send, self.recv, self.base = nf, z, me, send, recv, base
        self.chips, self.chip, self.core = nf // 2, me // 2, me % 2
        self.cut = half_rows(rows)
        self.sent = []
        self.got = {}
        self.own, self.own_sems = own, sems

    @staticmethod
    def sems(nf):
        return nf

    def push(self, index, src, dst, flip_by):
        copy = remote(
            src, dst, self.send.at[self.base + index], self.recv.at[self.base + index],
            self.z, self.me ^ flip_by,
        )
        copy.start()
        self.sent.append(copy)
        self.got[index] = copy

    def mine(self, ref, start, n):
        return ref.at[pl.ds(pl.multiple_of(start, 16), n)]

    def block(self, k, lo=0, hi=None):
        hi = self.rows if hi is None else hi
        return self.mine(self.recv4, (self.chip ^ k) * self.rows + lo, hi - lo)

    def swap(self):
        for p in range(self.chips):
            start = pl.multiple_of((2 * p + 1 - self.core) * self.rows, 16)
            src = self.src.at[pl.ds(start, self.rows), pl.ds(self.c0, self.cols)]
            self.push(p, src, self.mine(self.recv4, p * self.rows, self.rows), 1)

    def merge(self):
        rows, cols = self.rows, self.cols
        if self.own is not None:
            for p in range(min(2, self.chips)):
                self.fetch(p).start()
        for p in range(self.chips):
            self.got[p].wait_recv()
        if self.inside:
            for p in range(self.chips):
                start = pl.multiple_of((2 * p + self.core) * rows, 16)
                if self.own is None:
                    own, first = self.src, start
                else:
                    self.fetch(p).wait()
                    own, first = self.own, p % 2 * rows
                step = rows if rows <= 96 else rows // 2
                for i in range(0, rows, step):
                    where = pl.ds(p * rows + i, step)
                    part = own[pl.ds(pl.multiple_of(first + i, 16), step), pl.ds(0, cols)]
                    self.recv4[where, :] = (
                        self.recv4[where, :].astype(F32) + part.astype(F32)
                    ).astype(BF)
                if self.own is not None and p + 2 < self.chips:
                    self.fetch(p + 2).start()
            return
        step = rows if rows <= 96 else rows // 2
        n = rows // step
        core, col = self.core, self.c0 // cols
        deep = {"pipeline_mode": pl.Buffered(3)}
        own = pl.BlockSpec((step, cols), lambda p, i: ((2 * p + core) * n + i, col), **deep)
        held_in = pl.BlockSpec((step, cols), lambda p, i: (p * n + i, 0), **deep)
        held = pl.BlockSpec((step, cols), lambda p, i: (p * n + i, 0))
        pltpu.emit_pipeline(
            add_two, grid=(self.chips, n), in_specs=[own, held_in], out_specs=[held]
        )(self.src, self.recv4, self.recv4)

    def fetch(self, p):
        start = pl.multiple_of((2 * p + self.core) * self.rows, 16)
        return pltpu.make_async_copy(
            self.src.at[pl.ds(start, self.rows), pl.ds(self.c0, self.cols)],
            self.own.at[pl.ds(p % 2 * self.rows, self.rows)],
            self.own_sems.at[p % 2],
        )

    def add(self, out, parts, n):
        if self.inside:
            total = parts[0][...].astype(F32)
            for part in parts[1:]:
                total = total + part[...].astype(F32)
            out[...] = total.astype(BF)
            return
        step = n // 2 if n % 32 == 0 and n > 144 else n
        spec = pl.BlockSpec((step, self.cols), lambda i: (i, 0))
        body = add_two if len(parts) == 2 else add_all
        pltpu.emit_pipeline(
            body, grid=(n // step,), in_specs=[spec] * len(parts), out_specs=[spec]
        )(*parts, out)

    def first(self):
        base, rows, cut = self.chips, self.rows, self.cut
        if self.nf == 8:
            self.push(base, self.block(3, 0, cut), self.land.at[pl.ds(0, cut)], 2)
            self.push(base + 1, self.block(3, cut), self.land.at[pl.ds(cut, rows - cut)], 4)
        else:
            for k in range(1, self.chips):
                self.push(base + k - 1, self.block(k), self.land.at[pl.ds((k - 1) * rows, rows)], 2 * k)

    def second(self):
        if self.nf != 8:
            return
        base, rows, cut = self.chips, self.rows, self.cut
        self.got[base].wait_recv()
        to_y = self.block(2, 0, cut)
        self.add(to_y, [to_y, self.land.at[pl.ds(0, cut)]], cut)
        self.push(base + 3, self.block(2), self.land.at[pl.ds(2 * rows, rows)], 4)
        self.got[base + 1].wait_recv()
        to_x = self.block(1, cut)
        self.add(to_x, [to_x, self.land.at[pl.ds(cut, rows - cut)]], rows - cut)
        self.push(base + 2, self.block(1), self.land.at[pl.ds(rows, rows)], 2)

    def last(self, out):
        base, rows = self.chips, self.rows
        if self.nf == 8:
            incoming = [(base + 2, rows), (base + 3, 2 * rows)]
        else:
            incoming = [(base + k - 1, (k - 1) * rows) for k in range(1, self.chips)]
        for index, _ in incoming:
            self.got[index].wait_recv()
        parts = [self.block(0)] + [self.land.at[pl.ds(at, rows)] for _, at in incoming]
        self.add(out, parts, rows)

    def drain(self):
        for copy in self.sent:
            copy.wait_send()
        self.sent = []


def add_two(a, b, out):
    out[...] = (a[...].astype(F32) + b[...].astype(F32)).astype(BF)


def add_all(*refs):
    total = refs[0][...].astype(F32)
    for ref in refs[1:-1]:
        total = total + ref[...].astype(F32)
    refs[-1][...] = total.astype(BF)


def greet_ctx_and_plane(nz, nf, z, me):
    barrier = pltpu.get_barrier_semaphore()
    flips = (1, 2, 4) if nf == 8 else (1,) + tuple(range(2, nf, 2))
    for k in flips:
        pl.semaphore_signal(barrier, inc=1, device_id=(z, me ^ k), device_id_type=MESH)

    @pl.when(z < nz - 1)
    def _():
        pl.semaphore_signal(barrier, inc=1, device_id=(z + 1, me), device_id_type=MESH)

    @pl.when(z > 0)
    def _():
        pl.semaphore_signal(barrier, inc=1, device_id=(z - 1, me), device_id_type=MESH)

    inner = jnp.logical_and(z > 0, z < nz - 1)

    @pl.when(inner)
    def _():
        pl.semaphore_wait(barrier, len(flips) + 2)

    @pl.when(jnp.logical_not(inner))
    def _():
        pl.semaphore_wait(barrier, len(flips) + 1)


def loop(n, body):
    def step(i, carry):
        body(i)
        return carry

    lax.fori_loop(0, n, step, 0)


def at128(i, n):
    return i * n if isinstance(i, int) else pl.multiple_of(i * n, n)


def turn(t, cos2, sin2):
    return t * cos2 + pltpu.roll(t, HEAD_DIM // 2, 1) * sin2


def front_kernel(
    dims,
    wq, sm, wo, w_gu, w_dn, x_ref, g_ref, order_ref, freq_ref,
    wq_all, wo_all, q_out, kv_out, o_out, lse_out, mid_out, dx_ref, gain_out, cos_out, sin_out, dwgu, dpart, d_own, dwd, r0, l0,
    q_ref, o_ref, lse_ref, mid_ref, gain_ref, cos_ref, sin_ref, qpos_ref, kpos_ref,
    stage, gu, dnb, g_all, x_all, act, dgu, smb, kv, bias, ybuf, packed, down, send, recv, local,
):
    nz, nf, rows, d, ff, wide, upad, nb, ng = dims
    z, me = lax.axis_index("ctx"), lax.axis_index("fsdp")
    q_width, k_width = HEADS * HEAD_DIM, KV_HEADS * HEAD_DIM
    qkv = q_width + 2 * k_width
    scale = HEAD_DIM ** (-0.5)
    wr = d // nf
    per = PlaneGather.sems(nf)
    q_cols, kv_cols = pl.ds(0, q_width), pl.ds(q_width, 2 * k_width)
    plane = [
        PlaneGather(src, dst, r, nf, z, me, send, recv, local.at[i], i * per, bounce)
        for i, (src, dst, r, bounce) in enumerate(
            [
                (wq.at[:, q_cols], wq_all.at[:, q_cols], wr, ybuf.at[pl.ds(wr, wr)]),
                (wq.at[:, kv_cols], wq_all.at[:, kv_cols], wr, ybuf.at[pl.ds(0, wr), pl.ds(0, 2 * k_width)]),
                (sm, smb, 16, None),
                (wo, wo_all, wr, ybuf.at[pl.ds(0, wr)]),
                (packed, gu, wr, None),
                (down, dnb, upad, None),
            ]
        )
    ]
    p_q, p_kv, p_s, p_o, p_gu, p_d = plane
    base = len(plane) * per
    chain = [
        Chain(buf, rows, nz, z, me, send, recv, base + i * Chain.sems(nz))
        for i, buf in enumerate([g_all, kv, x_all])
    ]
    c_g, c_kv, c_x = chain
    base += len(chain) * Chain.sems(nz)
    s_d = Scatter(dwd, 0, upad, d, r0, l0, False, nf, z, me, send, recv, base)
    base += Scatter.sems(nf)
    spare = len(plane)

    unit = ff // (nf * nz)
    n = pieces_of(2 * ff, 2 * wide, wr, nz * rows)
    width = 2 * ff // n
    loads = [
        pltpu.make_async_copy(
            w_gu.at[:, pl.ds(i * width, width)],
            dgu.at[pl.ds(i * wr, wr), pl.ds(0, width)],
            local.at[spare + 1 + i],
        )
        for i in range(n)
    ]
    fetched = upad + 16
    down_in = act.at[pl.ds(0, fetched), pl.ds(0, d)] if wide >= d else dgu.at[pl.ds(n * wr, fetched), pl.ds(0, d)]

    def down_load(k):
        start = min(unit * k // 16 * 16, ff // nf - fetched)
        copy = pltpu.make_async_copy(w_dn.at[pl.ds(start, fetched)], down_in, local.at[spare + 1 + n])
        return copy, unit * k - start

    def part_loads():
        for copy in loads:
            copy.start()
        for k in range(nz):

            @pl.when(z == k)
            def _():
                down_load(k)[0].start()

    def part_pack():
        for copy in loads:
            copy.wait()
        for k in range(nz):

            @pl.when(z == k)
            def _():
                pack(k, nz, nf, ff, unit, upad, wr, width, dgu, packed)
                copy, off = down_load(k)
                copy.wait()
                part = down_in[...].astype(F32)[off : off + unit]
                rest = jnp.zeros((upad - unit, d), F32)
                down[...] = jnp.concatenate([part, rest], 0).astype(BF)

    g_copy = pltpu.make_async_copy(g_ref, rows_at(g_all, z, rows), local.at[spare])
    g_copy.start()
    greet_ctx_and_plane(nz, nf, z, me)
    p_s.begin()
    p_kv.begin()
    g_copy.wait()
    c_g.begin()
    part_loads()

    given = []

    def give_out(src, dst):
        copy = pltpu.make_async_copy(src, dst, local.at[spare + 16 + len(given)])
        copy.start()
        given.append(copy)

    x = x_ref[...].astype(F32)
    inverse = lax.rsqrt(jnp.mean(x * x, -1, keepdims=True) + EPSILON)

    p_s.middle()
    p_kv.middle()
    p_q.begin()
    tokens = nz * rows
    qpos_ref[...], kpos_ref[...] = positions(order_ref, z, rows, tokens)
    angle = qpos_ref[...].astype(F32) * freq_ref[...]
    cos_ref[...] = jnp.cos(angle)
    first_half = lax.broadcasted_iota(jnp.int32, angle.shape, 1) < HEAD_DIM // 2
    sine = jnp.sin(angle)
    sin_ref[...] = jnp.where(first_half, -sine, sine)
    give_out(cos_ref, cos_out)
    give_out(sin_ref, sin_out)
    p_s.late()
    p_kv.late()
    p_s.finish()
    for f in range(nf):
        row = smb[f * 16 : (f + 1) * 16, :].astype(F32)[0:1]
        bias[0:1, f * nb : (f + 1) * nb] = row[:, :nb]
        gain_ref[0:1, f * ng : (f + 1) * ng] = row[:, nb : nb + ng]
        gain_ref[1:2, f * ng : (f + 1) * ng] = row[:, nb + ng : nb + 2 * ng]
    give_out(gain_ref, gain_out)
    normed = (x * inverse * gain_ref[0:1, :]).astype(BF)
    x_all[pl.ds(at128(z, rows), rows), :] = normed

    def fetch_qkv(c0, n):
        copy = pltpu.make_async_copy(
            wq_all.at[:, pl.ds(c0, n)], stage.at[pl.ds(0, d), pl.ds(c0, n)], local.at[spare]
        )
        copy.start()
        copy.wait()

    p_kv.finish()
    fetch_qkv(q_width, 2 * k_width)

    def project(t):
        c0 = at128(t, 2 * HEAD_DIM)
        y = dot(
            x_all[pl.ds(at128(z, rows), rows), :], stage[pl.ds(0, d), pl.ds(c0, 2 * HEAD_DIM)]
        ) + bias[0:1, pl.ds(c0, 2 * HEAD_DIM)]
        return y, c0

    def project_v(t):
        y, c0 = project(t)
        kv[pl.ds(at128(z, rows), rows), pl.ds(pl.multiple_of(c0 - q_width, 256), 256)] = y.astype(BF)

    def turned(y):
        halves = [
            turn(y[:, h * HEAD_DIM : (h + 1) * HEAD_DIM], cos_ref[...], sin_ref[...]).astype(BF)
            for h in range(2)
        ]
        return jnp.concatenate(halves, 1)

    project_v((q_width + k_width) // 256)
    y, _ = project(q_width // 256)
    kv[pl.ds(at128(z, rows), rows), 0:k_width] = turned(y)
    c_kv.begin()
    p_q.middle()
    p_o.begin()
    part_pack()
    for k in range(1, nz - 1):
        c_kv.forward(k)
    p_q.late()
    p_q.finish()
    fetch_qkv(0, q_width)
    c_kv.forward(nz - 1)

    def project_q(t):
        y, c0 = project(t)
        q_ref[:, pl.ds(c0, 256)] = turned(y)

    loop(q_width // 256, project_q)
    give_out(q_ref, q_out)
    p_o.middle()
    p_gu.begin()
    for k in range(1, nz):
        c_kv.arrive(k)
    for k in range(1, nz - 1):
        c_g.forward(k)

    lanes = lax.broadcasted_iota(jnp.int32, (rows, HEAD_DIM), 1)
    lse_ref[...] = jnp.zeros_like(lse_ref)

    def head(h):
        c0 = at128(h, HEAD_DIM)
        kc = at128(h // (HEADS // KV_HEADS), HEAD_DIM)
        vc = pl.multiple_of(kc + k_width, HEAD_DIM)
        s = dot_bt(q_ref[:, pl.ds(c0, HEAD_DIM)], kv[:, pl.ds(kc, HEAD_DIM)]) * scale
        s = jnp.where(kpos_ref[...] <= qpos_ref[...], s, MASKED)
        top = jnp.max(s, -1, keepdims=True)
        p = jnp.exp(s - top)
        total = jnp.sum(p, -1, keepdims=True)
        o = dot(p.astype(BF), kv[:, pl.ds(vc, HEAD_DIM)]) / total
        o_ref[:, pl.ds(c0, HEAD_DIM)] = o.astype(BF)
        lse_ref[...] = jnp.where(lanes == h, top + jnp.log(total), lse_ref[...])

    loop(HEADS, head)
    give_out(o_ref, o_out)
    give_out(lse_ref, lse_out)
    p_o.late()
    p_o.finish()
    fetch = pltpu.make_async_copy(wo_all, stage.at[pl.ds(0, q_width), pl.ds(0, d)], local.at[spare])
    fetch.start()
    fetch.wait()

    def out_proj(t):
        c0 = at128(t, 512)
        mid_ref[:, pl.ds(c0, 512)] = (
            dot(o_ref[...], stage[pl.ds(0, q_width), pl.ds(c0, 512)]) + x_ref[:, pl.ds(c0, 512)].astype(F32)
        )

    loop(d // 512, out_proj)
    give_out(mid_ref, mid_out)
    mid = mid_ref[...]
    inverse_two = lax.rsqrt(jnp.mean(mid * mid, -1, keepdims=True) + EPSILON)
    x_all[pl.ds(at128(z, rows), rows), :] = (mid * inverse_two * gain_ref[1:2, :]).astype(BF)
    c_x.begin()
    c_g.forward(nz - 1)
    for k in range(1, nz - 1):
        c_x.forward(k)
    p_gu.middle()
    p_d.begin()
    if nz <= 4:
        c_x.forward(nz - 1)
    p_gu.late()
    p_gu.finish()

    cols = 768 if wide % 768 == 0 else 256

    def hidden(j):
        r0 = at128(j, rows)

        def one(t):
            c0 = at128(t, cols)
            xb = x_all[pl.ds(r0, rows), :]
            gate = dot(xb, gu[:, pl.ds(c0, cols)])
            up = dot(xb, gu[:, pl.ds(pl.multiple_of(wide + c0, 128), cols)])
            act[pl.ds(r0, rows), pl.ds(c0, cols)] = (gate * jax.nn.sigmoid(gate) * up).astype(BF)
            dgu[pl.ds(r0, rows), pl.ds(c0, cols)] = gate.astype(BF)
            dgu[pl.ds(r0, rows), pl.ds(pl.multiple_of(wide + c0, 128), cols)] = up.astype(BF)

        loop(wide // cols, one)

    hidden(z)
    if nz > 4:
        c_x.forward(nz - 1)

    def nearest(k):
        c_x.arrive(k)
        hidden(c_x.order(k))

    loop(nz - 2, lambda i: nearest(i + 1))
    p_d.middle()
    nearest(nz - 1)
    for k in range(1, nz):
        c_g.arrive(k)
    high = 768 if nz <= 4 and wide % 768 == 0 else 256
    spots = [(r, c) for r in range(0, wide, high) for c in range(0, d, 768)]
    puts = []
    for i, (r, c) in enumerate(spots):
        if i >= 2:
            puts[i - 2].wait()
        slot = pl.ds(i % 2 * 768, 768)
        ybuf[0:high, slot] = dot_at(act[:, r : r + high], g_all[:, c : c + 768]).astype(BF)
        puts.append(
            pltpu.make_async_copy(
                ybuf.at[pl.ds(0, high), slot], dwd.at[pl.ds(r, high), pl.ds(c, 768)],
                local.at[spare + i % 2],
            )
        )
        puts[i].start()
        if i == len(spots) // 2:
            p_d.late()
    for put in puts[-2:]:
        put.wait()
    s_d.swap()
    p_d.finish()

    def back(j):
        r0 = at128(j, rows)

        def one(t):
            c0 = at128(t, cols)
            c1 = pl.multiple_of(wide + c0, 128)
            da = dot_bt(g_all[pl.ds(r0, rows), :], dnb[pl.ds(c0, cols), :])
            gate = dgu[pl.ds(r0, rows), pl.ds(c0, cols)].astype(F32)
            up = dgu[pl.ds(r0, rows), pl.ds(c1, cols)].astype(F32)
            sig = jax.nn.sigmoid(gate)
            dgu[pl.ds(r0, rows), pl.ds(c0, cols)] = (
                da * up * (sig * (1.0 + gate * (1.0 - sig)))
            ).astype(BF)
            dgu[pl.ds(r0, rows), pl.ds(c1, cols)] = (da * gate * sig).astype(BF)

        loop(wide // cols, one)

    rs = base

    slots = stage.at[:, pl.ds(0, d)]

    def slot_copy(src, dst, step):
        return remote(
            rows_at(slots, src, rows), rows_at(slots, dst, rows),
            send.at[rs + src], recv.at[rs + dst], z + step, me,
        )

    hold = nz <= 4

    def sides(i):
        j = c_x.order(nz - 1 - i)
        below, above = j > z, j < z
        got = jnp.logical_or(jnp.logical_and(below, z > 0), jnp.logical_and(above, z < nz - 1))
        return j, below, above, got, (pl.ds(at128(j, rows), rows), pl.ds(0, d))

    def terms(i, at):
        j = sides(i)[0]
        back(j)

        def one(t):
            c0 = at128(t, 768)
            ybuf[at : at + rows, pl.ds(c0, 768)] = dot_bt(
                dgu[pl.ds(at128(j, rows), rows), :], gu[pl.ds(c0, 768), :]
            ).astype(BF)

        loop(d // 768, one)

    def ship(j, below, above):
        @pl.when(below)
        def _():
            slot_copy(j, j, 1).start()

        @pl.when(above)
        def _():
            slot_copy(j, jnp.where(z - 1 == j, nz, j), -1).start()

    def early(i, at):
        j, below, above, got, where = sides(i)

        @pl.when(jnp.logical_not(got))
        def _():
            stage[where] = ybuf[at : at + rows, :]
            ship(j, below, above)

    def late(i, at):
        j, below, above, got, where = sides(i)

        @pl.when(got)
        def _():
            slot_copy(j, j, 0).wait_recv()
            stage[where] = (
                stage[where].astype(F32) + ybuf[at : at + rows, :].astype(F32)
            ).astype(BF)
            ship(j, below, above)

    if hold:
        between = {0: (s_d.merge, s_d.first)}
        for i in range(nz - 1):
            terms(i, i * rows)
            early(i, i * rows)
            for step in between.get(i, ()):
                step()
        late(0, 0)
        s_d.second()
    else:

        def at_once(i):
            terms(i, 0)
            early(i, 0)
            late(i, 0)

        loop(nz - 1, at_once)
        for step in (s_d.merge, s_d.first, s_d.second):
            step()
    back(z)

    def own(t):
        c0 = at128(t, 512)
        dx_ref[:, pl.ds(c0, 512)] = dot_bt(
            dgu[pl.ds(at128(z, rows), rows), :], gu[pl.ds(c0, 512), :]
        )

    loop(d // 512, own)

    c_x.drain()

    def down_terms(t):
        c0 = at128(t, 512)
        g_all[:, pl.ds(c0, 512)] = dot(act[...], dnb[:, pl.ds(c0, 512)]).astype(BF)

    c_g.drain()
    loop(d // 512, down_terms)
    out_p = pltpu.make_async_copy(g_all, dpart, local.at[spare + 3])
    out_p.start()
    if hold:
        for i in range(1, nz - 1):
            late(i, i * rows)
    p_gu.drain()

    side = 768 if wide % 768 == 0 else 256

    def w_gu_grad(t):
        c0 = at128(t, side)
        for r in range(0, d, 768):
            gu[r : r + 768, pl.ds(c0, side)] = dot_at(
                x_all[:, r : r + 768], dgu[:, pl.ds(c0, side)]
            ).astype(BF)

    outs = []
    for i in range(2):
        loop(wide // side, lambda t: w_gu_grad(t + i * (wide // side)))
        half = pl.ds(i * wide, wide)
        outs.append(pltpu.make_async_copy(gu.at[:, half], dwgu.at[:, half], local.at[spare + i]))
        outs[-1].start()
    s_d.last(d_own)
    out_kv = pltpu.make_async_copy(kv, kv_out, local.at[spare + 2])
    out_kv.start()

    @pl.when(z > 0)
    def _():
        slot_copy(z, z, 0).wait_recv()
        dx_ref[...] += rows_at(slots, z, rows)[...].astype(F32)

    @pl.when(z < nz - 1)
    def _():
        slot_copy(z, nz, 0).wait_recv()
        dx_ref[...] += rows_at(slots, nz, rows)[...].astype(F32)

    for item in (p_q, p_kv, p_s, p_o, p_d, c_kv, s_d):
        item.drain()

    def gave(i):
        j = c_x.order(i + 1)
        slot_copy(j, j, 0).wait_send()

    loop(nz - 1, gave)
    for copy in outs + given + [out_kv, out_p]:
        copy.wait()


def front(dims, wq, sm, wo, w_gu, w_dn, x, g, order, freq):
    nz, nf, rows, d, ff, wide, upad, nb, ng = dims
    q_width, k_width = HEADS * HEAD_DIM, KV_HEADS * HEAD_DIM
    qkv = q_width + 2 * k_width
    tokens = nz * rows
    any_, vm = pl.BlockSpec(memory_space=pl.ANY), pl.BlockSpec(memory_space=pltpu.VMEM)
    sems = 6 * PlaneGather.sems(nf) + 3 * Chain.sems(nz) + Scatter.sems(nf) + nz + 1
    chips = nf // 2
    out = jax.ShapeDtypeStruct
    return pl.pallas_call(
        functools.partial(front_kernel, dims),
        in_specs=[any_] * 5 + [vm, any_, pl.BlockSpec(memory_space=pltpu.SMEM), vm],
        out_specs=[any_] * 7 + [vm] + [any_] * 9,
        out_shape=[
            out((d, qkv), BF),
            out((q_width, d), BF),
            out((rows, q_width), BF),
            out((tokens, 2 * k_width), BF),
            out((rows, q_width), BF),
            out((rows, HEAD_DIM), F32),
            out((rows, d), F32),
            out((rows, d), F32),
            out((8, d), F32),
            out((rows, HEAD_DIM), F32),
            out((rows, HEAD_DIM), F32),
            out((d, 2 * wide), BF),
            out((tokens, d), BF),
            out((upad, d), BF),
            out((wide, d), BF),
            out((chips * upad, d), BF),
            out(((chips - 1) * upad, d), BF),
        ],
        scratch_shapes=[
            pltpu.VMEM((rows, q_width), BF),
            pltpu.VMEM((rows, q_width), BF),
            pltpu.VMEM((rows, HEAD_DIM), F32),
            pltpu.VMEM((rows, d), F32),
            pltpu.VMEM((8, d), F32),
            pltpu.VMEM((rows, HEAD_DIM), F32),
            pltpu.VMEM((rows, HEAD_DIM), F32),
            pltpu.VMEM((rows, 1), jnp.int32),
            pltpu.VMEM((1, tokens), jnp.int32),
            pltpu.VMEM((max(d, (nz + 1) * rows), qkv), BF),
            pltpu.VMEM((d, 2 * wide), BF),
            pltpu.VMEM((wide, d), BF),
            pltpu.VMEM((tokens, d), BF),
            pltpu.VMEM((tokens, d), BF),
            pltpu.VMEM((tokens, wide), BF),
            pltpu.VMEM((tokens, 2 * wide), BF),
            pltpu.VMEM((nf * 16, sm.shape[1]), BF),
            pltpu.VMEM((tokens, 2 * k_width), BF),
            pltpu.VMEM((8, qkv), F32),
            pltpu.VMEM(((nz - 1 if nz <= 4 else 1) * rows, d), BF),
            pltpu.VMEM((d // nf, 2 * wide), BF),
            pltpu.VMEM((upad, d), BF),
            pltpu.SemaphoreType.DMA((sems,)),
            pltpu.SemaphoreType.DMA((sems,)),
            pltpu.SemaphoreType.DMA((32,)),
        ],
        compiler_params=pltpu.CompilerParams(
            collective_id=0, has_side_effects=True, vmem_limit_bytes=VMEM_LIMIT
        ),
    )(wq, sm, wo, w_gu, w_dn, x, g, order, freq)


class Reduce:
    def __init__(self, slots, rows, nz, z, me, send, recv, base, order):
        self.slots, self.rows, self.nz, self.z, self.me = slots, rows, nz, z, me
        self.send, self.recv, self.base, self.order = send, recv, base, order

    @staticmethod
    def sems(nz):
        return nz + 1

    def copy(self, src, dst, step):
        return remote(
            rows_at(self.slots, src, self.rows), rows_at(self.slots, dst, self.rows),
            self.send.at[self.base + src], self.recv.at[self.base + dst], self.z + step, self.me,
        )

    def give(self, i, part):
        z, nz, rows = self.z, self.nz, self.rows
        j = self.order(nz - 1 - i)
        below, above = j > z, j < z
        got = jnp.logical_or(jnp.logical_and(below, z > 0), jnp.logical_and(above, z < nz - 1))
        where = pl.ds(at128(j, rows) if rows % 128 == 0 else pl.multiple_of(j * rows, 16), rows)
        own = part(j)

        @pl.when(got)
        def _():
            self.copy(j, j, 0).wait_recv()
            self.slots[where, :] = (self.slots[where, :].astype(F32) + own.astype(F32)).astype(BF)

        @pl.when(jnp.logical_not(got))
        def _():
            self.slots[where, :] = own.astype(BF)

        @pl.when(below)
        def _():
            self.copy(j, j, 1).start()

        @pl.when(above)
        def _():
            self.copy(j, jnp.where(z - 1 == j, nz, j), -1).start()

    def take(self, total):
        z, nz = self.z, self.nz

        @pl.when(z > 0)
        def _():
            self.copy(z, z, 0).wait_recv()
            total[...] += rows_at(self.slots, z, self.rows)[...].astype(F32)

        @pl.when(z < nz - 1)
        def _():
            self.copy(z, nz, 0).wait_recv()
            total[...] += rows_at(self.slots, nz, self.rows)[...].astype(F32)

    def drain(self):
        def gave(i):
            j = self.order(i + 1)
            self.copy(j, j, 0).wait_send()

        loop(self.nz - 1, gave)


def back_kernel(
    dims,
    dwgu, d_own, dpart, wq_all, wo_all, kv_hbm, mid_hbm, dx_hbm,
    x_hbm, g_hbm, q_hbm, o_hbm, lse_hbm, gain_hbm, cos_hbm, sin_hbm, order_ref,
    hid_ref, gh_ref, all_d, all_g, all_u, z_out, tiny_out,
    x_ref, g_ref, q_ref, o_ref, lse_ref, gain_ref, cos_ref, sin_ref, qpos_ref, kpos_ref,
    stage, full, dslots, do_ref, kv, dkv, kslots, m32, dh, t32, dqkv, normed,
    r3, l3, r4, l4, zsrc, zslots, zlow, zown, gain_sums, tiny, tin, zin,
    r1, r2, l1, l2, own2, own_sems, send, recv, local,
):
    nz, nf, rows, d, wide, upad, nb, ng, ch = dims
    z, me = lax.axis_index("ctx"), lax.axis_index("fsdp")
    q_width, k_width = HEADS * HEAD_DIM, KV_HEADS * HEAD_DIM
    qkv = q_width + 2 * k_width
    scale = HEAD_DIM ** (-0.5)
    wr = d // nf
    place = {"nf": nf, "z": z, "me": me, "send": send, "recv": recv}
    per = Scatter.sems(nf)
    own = {"own": own2, "sems": own_sems}
    s_g = Scatter(dwgu, 0, wr, wide, r1, l1, True, base=per, **own, **place)
    s_u = Scatter(dwgu, wide, wr, wide, r2, l2, True, base=2 * per, **own, **place)
    s_o = Scatter(full, 0, wr, d, r3, l3, True, base=3 * per, **place)
    s_q = Scatter(full, 0, wr, qkv, r4, l4, True, base=4 * per, **place)
    base = 5 * per
    line = {"nz": nz, "z": z, "me": me, "send": send, "recv": recv}
    per = Chain.sems(nz)
    a_d = Chain(all_d, upad, base=base, **line)
    a_g = Chain(all_g, wr, base=base + per, **line)
    a_u = Chain(all_u, wr, base=base + 2 * per, **line)
    a_z = Chain(z_out, ch, base=base + 3 * per, **line)
    base += 4 * per
    per = Reduce.sems(nz)
    d_kv = Reduce(kslots, rows, base=base, order=a_d.order, **line)
    d_h = Reduce(dslots, rows, base=base + per, order=a_d.order, **line)
    d_z = Reduce(zslots, ch, base=base + 2 * per, order=a_d.order, **line)
    base += 3 * per

    def fetch(src, dst, i):
        copy = pltpu.make_async_copy(src, dst, local.at[i])
        copy.start()
        return copy

    def stream(src, cols, use):
        copies = []
        for t in range(src.shape[0] // 512):
            slot = stage.at[pl.ds(t % 2 * 512, 512), pl.ds(0, cols)]
            copies.append(
                pltpu.make_async_copy(src.at[pl.ds(t * 512, 512)], slot, local.at[6 + t % 2])
            )
        for copy in copies[:2]:
            copy.start()
        for t, copy in enumerate(copies):
            copy.wait()
            use(t, t % 2 * 512)
            if t + 2 < len(copies):
                copies[t + 2].start()

    coming = {}

    def bring(name, src, dst):
        coming[name] = fetch(src, dst, 9 + len(coming))

    def need(*names):
        for name in names:
            if name in coming:
                coming.pop(name).wait()

    arrays = (
        ("mid", mid_hbm, m32), ("dx", dx_hbm, dh), ("g", g_hbm, g_ref), ("gain", gain_hbm, gain_ref),
        ("o", o_hbm, o_ref), ("kv", kv_hbm, kv), ("q", q_hbm, q_ref), ("lse", lse_hbm, lse_ref),
        ("cos", cos_hbm, cos_ref), ("sin", sin_hbm, sin_ref), ("x", x_hbm, x_ref),
    )
    for array in arrays:
        bring(*array)
    d_in = fetch(d_own, rows_at(all_d, z, upad), 8)

    barrier = pltpu.get_barrier_semaphore()
    for k in range(1, nf):
        pl.semaphore_signal(barrier, inc=1, device_id=(z, me ^ k), device_id_type=MESH)
    for k in range(1, nz):
        pl.semaphore_signal(barrier, inc=1, device_id=((z + k) % nz, me), device_id_type=MESH)
    pl.semaphore_wait(barrier, nf + nz - 2)

    dkv[...] = jnp.zeros_like(dkv)
    qpos_ref[...], kpos_ref[...] = positions(order_ref, z, rows, nz * rows)
    lanes = lax.broadcasted_iota(jnp.int32, (rows, HEAD_DIM), 1)
    mine = dkv.at[pl.ds(at128(z, rows), rows)]
    third = HEADS // 3

    def norm_back():
        need("mid", "dx", "g", "gain")
        mid, dxn = m32[...], dh[...]
        inverse_two = lax.rsqrt(jnp.mean(mid * mid, -1, keepdims=True) + EPSILON)
        scaled = gain_ref[1:2, :] * dxn
        gain_sums[1:2, :] = jnp.sum(dxn * mid * inverse_two, 0, keepdims=True)
        dh[...] = (
            g_ref[...].astype(F32)
            + inverse_two * scaled
            - mid
            * (inverse_two * inverse_two * inverse_two)
            * jnp.mean(scaled * mid, -1, keepdims=True)
        )
        normed[...] = dh[...].astype(BF)

    def out_back():
        def one(t, r):
            do_ref[:, t * 512 : t * 512 + 512] = dot_bt(
                normed[...], stage[r : r + 512, 0:d]
            ).astype(BF)

        stream(wo_all, d, one)

    def w_out_grad():
        need("o")

        def one(t):
            c0 = at128(t, 512)
            full[pl.ds(0, q_width), pl.ds(c0, 512)] = dot_at(
                o_ref[...], normed[:, pl.ds(c0, 512)]
            ).astype(BF)

        loop(d // 512, one)

    def heads(start, count):
        need("o", "kv", "q", "lse", "cos", "sin")
        loop(count, lambda i: head(i + start))

    def head(h):
        c0 = at128(h, HEAD_DIM)
        kc = at128(h // (HEADS // KV_HEADS), HEAD_DIM)
        vc = pl.multiple_of(kc + k_width, HEAD_DIM)
        q, k, v = q_ref[:, pl.ds(c0, HEAD_DIM)], kv[:, pl.ds(kc, HEAD_DIM)], kv[:, pl.ds(vc, HEAD_DIM)]
        do = do_ref[:, pl.ds(c0, HEAD_DIM)]
        lse = jnp.sum(jnp.where(lanes == h, lse_ref[...], 0.0), -1, keepdims=True)
        delta = jnp.sum(
            do.astype(F32) * o_ref[:, pl.ds(c0, HEAD_DIM)].astype(F32), -1, keepdims=True
        )
        s = jnp.where(kpos_ref[...] <= qpos_ref[...], dot_bt(q, k) * scale, MASKED)
        p = jnp.exp(s - lse)
        dkv[:, pl.ds(vc, HEAD_DIM)] += dot_at(p.astype(BF), do)
        ds = (p * (dot_bt(do, v) - delta)).astype(BF)
        dq = dot(ds, k) * scale
        dkv[:, pl.ds(kc, HEAD_DIM)] += dot_at(ds, q) * scale
        dqkv[:, pl.ds(c0, HEAD_DIM)] = turn(dq, cos_ref[...], -sin_ref[...]).astype(BF)

    def kv_part(j):
        return dkv[pl.ds(at128(j, rows), rows), :]

    def down_part(j):
        part = stage.at[pl.ds(0, rows), pl.ds(0, d)]
        fetch(rows_at(dpart, j, rows), part, 1).wait()
        return part[...]

    def z_part(j):
        return zsrc[pl.ds(pl.multiple_of(j * ch, 16), ch), :]

    def project_back():
        for h in range(KV_HEADS):
            c0 = h * HEAD_DIM
            dqkv[:, q_width + c0 : q_width + c0 + HEAD_DIM] = turn(
                mine[:, c0 : c0 + HEAD_DIM], cos_ref[...], -sin_ref[...]
            ).astype(BF)
        dqkv[:, q_width + k_width :] = mine[:, k_width:].astype(BF)

    def w_qkv_grad():
        need("x")
        x = x_ref[...].astype(F32)
        inverse = lax.rsqrt(jnp.mean(x * x, -1, keepdims=True) + EPSILON)
        normed[...] = (x * inverse * gain_ref[0:1, :]).astype(BF)
        s_o.drain()

        def one(t):
            c0 = at128(t, 512)
            full[pl.ds(0, d), pl.ds(c0, 512)] = dot_at(
                normed[...], dqkv[:, pl.ds(c0, 512)]
            ).astype(BF)

        loop(qkv // 512, one)

    tiny_copies = []

    def input_back():
        def one(t, r):
            t32[:, t * 512 : t * 512 + 512] = dot_bt(dqkv[...], stage[r : r + 512, :])

        stream(wq_all, qkv, one)
        x = x_ref[...].astype(F32)
        inverse = lax.rsqrt(jnp.mean(x * x, -1, keepdims=True) + EPSILON)
        dxn = t32[...]
        scaled = gain_ref[0:1, :] * dxn
        gain_one = jnp.sum(dxn * x * inverse, 0, keepdims=True)
        gain_two = gain_sums[1:2, :]
        bias = jnp.sum(dqkv[...].astype(F32), 0, keepdims=True)
        gh_ref[...] = (
            dh[...]
            + inverse * scaled
            - x * (inverse * inverse * inverse) * jnp.mean(scaled * x, -1, keepdims=True)
        ).astype(BF)

        cut = q_width + k_width
        qk, vb = cut // nf, k_width // nf
        tiny[...] = jnp.zeros_like(tiny)
        for f in range(nf):
            r = slice(8 * f, 8 * f + 1)
            tiny[r, 0:qk] = bias[:, f * qk : (f + 1) * qk]
            tiny[r, qk : qk + vb] = bias[:, cut + f * vb : cut + (f + 1) * vb]
            tiny[r, qk + vb : qk + vb + ng] = gain_one[:, f * ng : (f + 1) * ng]
            tiny[r, qk + vb + ng : qk + vb + 2 * ng] = gain_two[:, f * ng : (f + 1) * ng]
        own = pl.ds(pl.multiple_of(me * 8, 8), 8)
        tin[own, :] = tiny[own, :]
        for k in range(1, nf):
            copy = remote(
                rows_at(tiny, me ^ k, 8), rows_at(tin, me, 8),
                send.at[base + k], recv.at[base + k], z, me ^ k,
            )
            copy.start()
            tiny_copies.append(copy)

    def tiny_along():
        for copy in tiny_copies:
            copy.wait_recv()
        total = tin[0:8, :]
        for f in range(1, nf):
            total = total + tin[8 * f : 8 * f + 8, :]
        zin[pl.ds(pl.multiple_of(z * 8, 8), 8), :] = total
        for k in range(1, nz):
            copy = remote(
                rows_at(zin, z, 8), rows_at(zin, z, 8),
                send.at[base + nf + k], recv.at[base + nf + k], (z + k) % nz, me,
            )
            copy.start()
            tiny_copies.append(copy)

    def z_take():
        zown[...] = z_part(z).astype(F32)
        d_z.take(zown)
        zlow[...] = zown[...].astype(BF)
        fetch(zlow, rows_at(z_out, z, ch), 2).wait()

    def h_take():
        m32[...] += down_part(z).astype(F32)
        d_h.take(m32)
        hid_ref[...] = m32[...].astype(BF)

    a_d.begin(d_own)
    s_g.swap()
    norm_back()
    out_back()
    w_out_grad()
    s_o.swap()
    s_g.merge()
    s_g.first()
    s_u.swap()
    a_d.forward(1)
    for k in range(2, nz - 1):
        a_d.forward(k)
    heads(0, third)
    heads(third, third)
    heads(2 * third, third)
    s_u.merge()
    s_g.second()
    s_u.first()
    a_d.forward(nz - 1)
    d_kv.give(0, kv_part)
    for i in range(1, nz - 2):
        d_kv.give(i, kv_part)
    d_kv.give(nz - 2, kv_part)
    s_o.merge()
    s_o.first()
    s_g.last(s_g.block(0))
    fetch(s_g.block(0), rows_at(all_g, z, wr), 4).wait()
    a_g.begin()
    s_u.second()
    a_g.forward(1)
    for k in range(2, nz - 1):
        a_g.forward(k)
    s_o.second()
    d_kv.take(mine)
    d_h.give(0, down_part)
    project_back()
    a_g.forward(nz - 1)
    w_qkv_grad()
    s_q.swap()
    s_o.last(zsrc.at[pl.ds(0, wr), pl.ds(0, d)])
    s_u.last(s_u.block(0))
    fetch(s_u.block(0), rows_at(all_u, z, wr), 5).wait()
    s_q.merge()
    s_q.first()
    a_u.begin()
    a_u.forward(1)
    s_q.second()
    for k in range(2, nz - 1):
        a_u.forward(k)
    a_u.forward(nz - 1)
    input_back()
    s_q.last(zsrc.at[pl.ds(0, wr), pl.ds(d, qkv)])
    d_z.give(0, z_part)
    tiny_along()
    for i in range(1, nz - 2):
        d_z.give(i, z_part)
    for i in range(1, nz - 2):
        d_h.give(i, down_part)
    d_z.give(nz - 2, z_part)
    d_h.give(nz - 2, down_part)
    for k in range(1, nz):
        a_u.arrive(k)
    z_take()
    for k in range(1, nz):
        a_g.arrive(k)
    a_z.begin()
    a_z.forward(1)
    for k in range(1, nz):
        a_d.arrive(k)
    for k in range(2, nz - 1):
        a_z.forward(k)
    a_z.forward(nz - 1)
    h_take()
    for k in range(1, nz):
        a_z.arrive(k)
    for copy in tiny_copies[nf - 1 :]:
        copy.wait_recv()
    total = zin[0:8, :]
    for j in range(1, nz):
        total = total + zin[8 * j : 8 * j + 8, :]
    tiny_out[...] = total
    d_in.wait()
    for item in (s_g, s_u, s_o, s_q, a_d, a_g, a_u, a_z, d_kv, d_h, d_z):
        item.drain()
    for copy in tiny_copies:
        copy.wait_send()


def back(dims, *args):
    nz, nf, rows, d, wide, upad, nb, ng, ch = dims
    q_width, k_width = HEADS * HEAD_DIM, KV_HEADS * HEAD_DIM
    qkv = q_width + 2 * k_width
    tokens, chips, wr = nz * rows, nf // 2, d // nf
    tiny = -(-((qkv + 2 * d) // nf) // 128) * 128
    any_, vm = pl.BlockSpec(memory_space=pl.ANY), pl.BlockSpec(memory_space=pltpu.VMEM)
    out = jax.ShapeDtypeStruct
    sems = 5 * Scatter.sems(nf) + 4 * Chain.sems(nz) + 3 * Reduce.sems(nz) + nf + nz
    pieces = [(upad, d), (wr, wide), (wr, wide)]
    return pl.pallas_call(
        functools.partial(back_kernel, dims),
        in_specs=[any_] * 16 + [pl.BlockSpec(memory_space=pltpu.SMEM)],
        out_specs=[vm, vm] + [any_] * 4 + [vm],
        out_shape=[out((rows, d), BF), out((rows, d), BF)]
        + [out((nz * r, c), BF) for r, c in pieces]
        + [out((nz * ch, d + qkv), BF), out((8, tiny), F32)],
        scratch_shapes=[
            pltpu.VMEM((rows, d), BF),
            pltpu.VMEM((rows, d), BF),
            pltpu.VMEM((rows, q_width), BF),
            pltpu.VMEM((rows, q_width), BF),
            pltpu.VMEM((rows, HEAD_DIM), F32),
            pltpu.VMEM((8, d), F32),
            pltpu.VMEM((rows, HEAD_DIM), F32),
            pltpu.VMEM((rows, HEAD_DIM), F32),
            pltpu.VMEM((rows, 1), jnp.int32),
            pltpu.VMEM((1, tokens), jnp.int32),
            pltpu.VMEM((1024, qkv), BF),
            pltpu.VMEM((d, qkv), BF),
            pltpu.VMEM(((nz + 1) * rows, d), BF),
            pltpu.VMEM((rows, q_width), BF),
            pltpu.VMEM((tokens, 2 * k_width), BF),
            pltpu.VMEM((tokens, 2 * k_width), F32),
            pltpu.VMEM(((nz + 1) * rows, 2 * k_width), BF),
            pltpu.VMEM((rows, d), F32),
            pltpu.VMEM((rows, d), F32),
            pltpu.VMEM((rows, d), F32),
            pltpu.VMEM((rows, qkv), BF),
            pltpu.VMEM((rows, d), BF),
            pltpu.VMEM((chips * wr, d), BF),
            pltpu.VMEM(((chips - 1) * wr, d), BF),
            pltpu.VMEM((chips * wr, qkv), BF),
            pltpu.VMEM(((chips - 1) * wr, qkv), BF),
            pltpu.VMEM((nz * ch, d + qkv), BF),
            pltpu.VMEM(((nz + 1) * ch, d + qkv), BF),
            pltpu.VMEM((ch, d + qkv), BF),
            pltpu.VMEM((ch, d + qkv), F32),
            pltpu.VMEM((8, d), F32),
            pltpu.VMEM((nf * 8, tiny), F32),
            pltpu.VMEM((nf * 8, tiny), F32),
            pltpu.VMEM((nz * 8, tiny), F32),
            pltpu.VMEM((chips * wr, wide), BF),
            pltpu.VMEM((chips * wr, wide), BF),
            pltpu.VMEM(((chips - 1) * wr, wide), BF),
            pltpu.VMEM(((chips - 1) * wr, wide), BF),
            pltpu.VMEM((2 * wr, wide), BF),
            pltpu.SemaphoreType.DMA((2,)),
            pltpu.SemaphoreType.DMA((sems,)),
            pltpu.SemaphoreType.DMA((sems,)),
            pltpu.SemaphoreType.DMA((20,)),
        ],
        compiler_params=pltpu.CompilerParams(
            collective_id=1, has_side_effects=True, vmem_limit_bytes=VMEM_LIMIT
        ),
    )(*args)


def shards(
    hidden_in, w_qkv, b_qkv, w_out, w_gate_up, w_down, gain_attn, gain_mlp, block_order, cotangent
):
    nz, nf = lax.axis_size("ctx"), lax.axis_size("fsdp")
    q_width, k_width = HEADS * HEAD_DIM, KV_HEADS * HEAD_DIM
    rows = hidden_in.shape[1]
    ff = w_gate_up.shape[1] // 2
    unit = ff // (nf * nz)
    freqs = THETA ** (-(np.arange(HEAD_DIM) % (HEAD_DIM // 2) * 2.0 / HEAD_DIM))
    freqs = jnp.asarray(freqs[None].astype(np.float32))
    upad = -(-unit // 16) * 16
    wide = nf * upad
    nb, ng = b_qkv.shape[0], gain_attn.shape[0]
    d = hidden_in.shape[2]
    small = jnp.concatenate([b_qkv, gain_attn, gain_mlp])
    small = jnp.pad(small, (0, -small.shape[0] % 128))
    small = jnp.broadcast_to(small[None], (16, small.shape[0]))
    grad_low = cotangent[0]
    (whole_qkv, whole_out, q_low, kv_all, attn_low, lse, middle, grad_normed_two, gains, cos2, sin2, gate_up_local, down_part,
     down_own, *_) = front(
        (nz, nf, rows, d, ff, wide, upad, nb, ng),
        w_qkv, small, w_out, w_gate_up, w_down, hidden_in[0], grad_low, block_order, freqs,
    )
    ch = -(-(d // (nf * nz)) // 16) * 16
    hidden, grad_hidden, down_all, gate_all, up_all, attn_all, tiny = back(
        (nz, nf, rows, d, wide, upad, nb, ng, ch),
        gate_up_local, down_own, down_part, whole_qkv, whole_out, kv_all, middle, grad_normed_two,
        hidden_in[0], grad_low, q_low, attn_low, lse, gains, cos2, sin2, block_order,
    )
    e1 = (q_width + k_width) // nf
    e2 = e1 + k_width // nf
    e3 = e2 + ng
    shard = d // nf
    cuts = (0, e1, e2, e3, e3 + ng)
    if unit % 8 == 0 and shard % (16 * nz) == 0 and ch * nz == shard:
        gu_grad, down_grad, qkv_grad, out_grad, hidden, grad_hidden, *smalls = finish(
            gate_all, up_all, down_all, attn_all, tiny, hidden, grad_hidden, nz, nf, ff, cuts
        )
        b_qk, b_v, g_one, g_two = (item[0] for item in smalls)
    else:
        gu_grad = unpack(gate_all, up_all, nz, nf, ff)
        down_grad = down_all.reshape(nz, upad, d)[:, :unit].reshape(nz * unit, d).astype(F32)
        qkv_grad = attn_all[:shard, d:].astype(F32)
        out_grad = attn_all[:shard, :d].astype(F32)
        b_qk, b_v, g_one, g_two = (tiny[0, lo:hi] for lo, hi in zip(cuts, cuts[1:]))
    return (
        hidden[None],
        grad_hidden[None],
        qkv_grad,
        b_qk,
        b_v,
        out_grad,
        gu_grad,
        down_grad,
        g_one,
        g_two,
    )


def solution(mesh):
    placed = (
        P("fsdp", "ctx", None),
        P("fsdp", None),
        P("fsdp"),
        P("fsdp", None),
        P("fsdp", None),
        P("fsdp", None),
        P("fsdp"),
        P("fsdp"),
        P("fsdp", None),
        P("fsdp", "ctx", None),
    )
    return jax.shard_map(
        shards,
        mesh=mesh,
        in_specs=placed,
        out_specs=(
            P("fsdp", "ctx", None),
            P("fsdp", "ctx", None),
            P("fsdp", None),
            P("fsdp"),
            P("fsdp"),
            P("fsdp", None),
            P("fsdp", None),
            P("fsdp", None),
            P("fsdp"),
            P("fsdp"),
        ),
        check_vma=False,
    )
```
